32 devices in a mesh: region: 4 (over z), cell: 8 (over y, x, core).
Axes of the slice: x: 2, y: 2, z: 4, core: 2. Of those that a mesh axis runs over, the one named last changes fastest.
Arguments:
- positions: float32 [3, 128, 512], P(None, ('region', 'cell')), may hold values from 0 to 1
- velocities: float32 [3, 128, 512], P(None, ('region', 'cell')), may hold values from -6 to 6
- mass: float32 [128, 512], P(('region', 'cell')), may hold values from 0.0002 to 0.001
- smoothing: float32 [128, 512], P(('region', 'cell')), may hold values from 0.25 to 0.5
- energy: float32 [128, 512], P(('region', 'cell')), may hold values from 0.5 to 2
- counts: int32 [128], P(('region', 'cell')), may hold values from 128 to 512
- send_cells: int32 [4, 8, 8, 1], P('region', 'cell'), may hold values from -1 to 3, as said below
- local_pairs: int32 [4, 8, 4, 2], P('region', 'cell'), may hold values from 0 to 3, as said below
- edge_cells: int32 [4, 8, 2], P('region', 'cell'), may hold values from 0 to 3
Outputs:
- density: float32 [128, 512], P(('region', 'cell'))
- accel: float32 [3, 128, 512], P(None, ('region', 'cell'))
- energy_rate: float32 [128, 512], P(('region', 'cell'))
The draws below stay inside these ranges and needn't reach their ends.
Inputs may be any that keep to these rules, and one draw needn't show every extreme that they name: send_cells[r, c, c2, s] is a local cell index of device (r, c), or -1 for an empty slot; slot s is empty from c to c2 exactly when it is empty from c2 to c, and always empty for c2 = c. `local_pairs`: each row holds two different local cell indices of the device.
All inputs are finite; a program needn't handle non-finite values.
Results may differ from the reference program's by a relative error of at most 0.0003.
Values sent between devices are 32-bit elements; how exact they have to be, the bound alone decides.
No kernel may reach another device: no remote copies, remote signals or barrier semaphores. Data moves between devices by JAX's collectives and lax.ppermute only.
A program may use at most 64 MiB of HBM per device.

```python
import math
import jax
import jax.numpy as jnp
from jax import lax

P_SIZE = 512
C_DEV = 4
SLOT = 1
EB = 1
CELLS = 128
N_REGION = 4
N_CELL = 8
DEVICES = 32


def draw_send_cells(key, part):
    key = jax.random.fold_in(key, 11)
    key_live, key_pick = jax.random.split(key)
    shape = (N_REGION, N_CELL, N_CELL, SLOT)
    chance = jax.random.randint(key_live, shape, 0, 10)
    row_ids = jnp.arange(N_CELL)[:, None, None]
    col_ids = jnp.arange(N_CELL)[None, :, None]
    mirrored = jnp.where(row_ids < col_ids, chance, jnp.swapaxes(chance, 1, 2))
    alive = (mirrored < 6) & (row_ids != col_ids)
    picked = jax.random.randint(key_pick, shape, 0, C_DEV)
    return jnp.where(alive, picked, -1).astype(jnp.int32)


def draw_local_pairs(key, part):
    key = jax.random.fold_in(key, 12)
    key_first, key_step = jax.random.split(key)
    shape = (N_REGION, N_CELL, C_DEV)
    first = jax.random.randint(key_first, shape, 0, C_DEV)
    second = (first + jax.random.randint(key_step, shape, 1, C_DEV)) % C_DEV
    return jnp.stack([first, second], axis=-1).astype(jnp.int32)


def with_ends(entries, key, smallest, top_value):
    place = [jax.random.randint(jax.random.fold_in(key, axis), (), 0, length) for axis, length in enumerate(entries.shape)]
    longest = entries.shape.index(max(entries.shape))
    next_to = place[:longest] + [(place[longest] + 1) % entries.shape[longest]] + place[longest + 1:]
    return entries.at[tuple(place)].set(smallest).at[tuple(next_to)].set(top_value)


def shard_levels(stream_key, extent, cuts, smallest, largest):
    factor_of = 1.0
    for axis_at, parts in cuts:
        heights = jax.random.uniform(jax.random.fold_in(jax.random.fold_in(stream_key, 6), axis_at), (parts,), jnp.float32, smallest / len(cuts), largest / len(cuts))
        factor_of = factor_of * jnp.repeat(jnp.exp(heights), extent[axis_at] // parts).reshape((-1,) + (1,) * (len(extent) - 1 - axis_at))
    return factor_of


def gaussian(stream_key, dims, spread, bound, cuts=(), kind=jnp.bfloat16):
    gain = shard_levels(stream_key, dims, cuts, -0.22, 0.18) if cuts else 1.0
    array = jax.random.normal(stream_key, dims, jnp.float32) * spread * gain
    return jnp.minimum(jnp.maximum(array, -bound), bound).astype(kind)


def setup_inputs(seed: int = 0) -> dict:
    splits = jax.random.split(jax.random.key(seed), 10)
    return {
        "positions": jnp.clip(1.0 * jax.random.uniform(splits[0], (3, CELLS, P_SIZE), jnp.float32) ** shard_levels(splits[0], (3, CELLS, P_SIZE), ((1, 32),), -0.2, 0.2), 0.0, 1.0),
        "velocities": gaussian(splits[1], (3, CELLS, P_SIZE), 1.0, 6.0, ((1, 32),), jnp.float32),
        "mass": jnp.clip(jnp.exp(math.log(0.001) - 1.609438 * jax.random.uniform(splits[2], (CELLS, P_SIZE), jnp.float32) ** shard_levels(splits[2], (CELLS, P_SIZE), ((0, 32),), -0.2, 0.2)), 0.0002, 0.001),
        "smoothing": jnp.clip(jnp.exp(math.log(0.5) - 0.6931472 * jax.random.uniform(splits[3], (CELLS, P_SIZE), jnp.float32) ** shard_levels(splits[3], (CELLS, P_SIZE), ((0, 32),), -0.2, 0.2)), 0.25, 0.5),
        "energy": jnp.clip(jnp.exp(math.log(2.0) - 1.3862944 * jax.random.uniform(splits[4], (CELLS, P_SIZE), jnp.float32) ** shard_levels(splits[4], (CELLS, P_SIZE), ((0, 32),), -0.2, 0.2)), 0.5, 2.0),
        "counts": with_ends(jax.random.randint(splits[5], (CELLS,), P_SIZE // 4, P_SIZE + 1), jax.random.fold_in(splits[5], 1), P_SIZE // 4, P_SIZE).astype(jnp.int32),
        "send_cells": draw_send_cells(jax.random.fold_in(splits[9], 71), 0),
        "local_pairs": draw_local_pairs(jax.random.fold_in(splits[9], 71), 0),
        "edge_cells": with_ends(jax.random.randint(splits[8], (N_REGION, N_CELL, 2 * EB), 0, C_DEV), jax.random.fold_in(splits[8], 1), 0, C_DEV - 1).astype(jnp.int32),
    }


GAMMA = 5.0 / 3.0

def spline(distance, support_raw):
    support = jnp.where(support_raw > 0.0, support_raw, 1.0)
    scaled = distance / support
    norm_factor = 8.0 / (math.pi * support * support * support)
    inside = scaled < 0.5
    within = scaled < 1.0
    profile = jnp.where(inside, 1.0 - 6.0 * scaled * scaled + 6.0 * scaled * scaled * scaled, jnp.where(within, 2.0 * (1.0 - scaled) ** 3, 0.0))
    slope_term = jnp.where(inside, -12.0 + 18.0 * scaled, jnp.where(within, -6.0 * (1.0 - scaled) ** 2 / jnp.maximum(scaled, 0.5), 0.0))
    return (norm_factor * profile, norm_factor * slope_term / (support * support))

def separation(target, source):
    apart_x = target[0][:, None] - source[0][None, :]
    apart_y = target[1][:, None] - source[1][None, :]
    apart_z = target[2][:, None] - source[2][None, :]
    distance = jnp.sqrt(apart_x * apart_x + apart_y * apart_y + apart_z * apart_z)
    return (apart_x, apart_y, apart_z, distance)

def density_tile(target, source):
    apart_x, apart_y, apart_z, distance = separation(target, source)
    kernel_value, _ = spline(distance, target[7][:, None])
    return lax.optimization_barrier(jnp.sum(kernel_value * source[6][None, :], axis=1))

def force_tile(target, source):
    apart_x, apart_y, apart_z, distance = separation(target, source)
    _, own_slope = spline(distance, target[7][:, None])
    _, other_slope = spline(distance, source[7][None, :])
    weighted = source[6][None, :] * 0.5 * (own_slope + other_slope)
    coupled = weighted * (target[8][:, None] + source[8][None, :])
    accel_x = -lax.optimization_barrier(jnp.sum(coupled * apart_x, axis=1))
    accel_y = -lax.optimization_barrier(jnp.sum(coupled * apart_y, axis=1))
    accel_z = -lax.optimization_barrier(jnp.sum(coupled * apart_z, axis=1))
    closing = (target[3][:, None] - source[3][None, :]) * apart_x + (target[4][:, None] - source[4][None, :]) * apart_y + (target[5][:, None] - source[5][None, :]) * apart_z
    heating = target[8] * lax.optimization_barrier(jnp.sum(weighted * closing, axis=1))
    return jnp.stack([accel_x, accel_y, accel_z, heating])

def run_tiles(worker, targets, sources):
    total = targets.shape[0]
    block_count = total // 4
    target_blocks = targets.reshape((block_count, 4) + targets.shape[1:])
    source_blocks = sources.reshape((block_count, 4) + sources.shape[1:])
    results = lax.map(lambda block_pair: jax.vmap(worker)(block_pair[0], block_pair[1]), (target_blocks, source_blocks))
    return results.reshape((total,) + results.shape[2:])

def tile_index(cell_pairs, send_list, edge_list, cell_count, peer_count):
    own_cells = jnp.arange(cell_count, dtype=jnp.int32)
    picked = jnp.clip(send_list, 0, cell_count - 1).reshape(-1).astype(jnp.int32)
    edge_base = cell_count + peer_count * SLOT
    edge_slots = jnp.arange(EB, dtype=jnp.int32)
    target_ids = jnp.concatenate([own_cells, cell_pairs[:, 0], cell_pairs[:, 1], picked, jnp.repeat(edge_list[:EB], EB), jnp.repeat(edge_list[EB:], EB)])
    source_ids = jnp.concatenate([own_cells, cell_pairs[:, 1], cell_pairs[:, 0], cell_count + jnp.arange(peer_count * SLOT, dtype=jnp.int32), edge_base + jnp.tile(edge_slots, EB), edge_base + EB + jnp.tile(edge_slots, EB)])
    used = 3 * cell_count + peer_count * SLOT + 2 * EB * EB
    padding = -used % 4
    weights = jnp.concatenate([jnp.ones((used,), jnp.float32), jnp.zeros((padding,), jnp.float32)])
    target_ids = jnp.concatenate([target_ids, jnp.zeros((padding,), jnp.int32)]).astype(jnp.int32)
    source_ids = jnp.concatenate([source_ids, jnp.zeros((padding,), jnp.int32)]).astype(jnp.int32)
    return (target_ids, source_ids, weights)

def reference(positions, velocities, mass, smoothing, energy, counts, send_cells, local_pairs, edge_cells):
    slot_ids = lax.broadcasted_iota(jnp.int32, (CELLS, P_SIZE), 1)
    occupied = (slot_ids < counts[:, None]).astype(jnp.float32)
    state_rows = jnp.concatenate([jnp.transpose(positions, (1, 0, 2)), jnp.transpose(velocities, (1, 0, 2)), (mass * occupied)[:, None], smoothing[:, None]], axis=1)
    device_ids = jnp.arange(DEVICES, dtype=jnp.int32)

    def device_table(rows_all, device):
        region_id = device // N_CELL
        cell_id = device % N_CELL
        own_rows = lax.dynamic_slice_in_dim(rows_all, (device * C_DEV).astype(jnp.int32), C_DEV, 0)
        mine = send_cells[region_id, cell_id]
        theirs = send_cells[region_id, :, cell_id, :]
        alive = (mine >= 0).astype(jnp.float32).reshape(-1)
        peer_cells = ((region_id * N_CELL + jnp.arange(N_CELL, dtype=jnp.int32))[:, None] * C_DEV + jnp.clip(theirs, 0, C_DEV - 1)).reshape(-1).astype(jnp.int32)
        received = rows_all[peer_cells] * alive[:, None, None]
        lower = jnp.maximum(region_id - 1, 0)
        upper = jnp.minimum(region_id + 1, N_REGION - 1)
        lower_ids = ((lower * N_CELL + cell_id) * C_DEV + edge_cells[lower, cell_id, EB:]).astype(jnp.int32)
        upper_ids = ((upper * N_CELL + cell_id) * C_DEV + edge_cells[upper, cell_id, :EB]).astype(jnp.int32)
        lower_ok = (region_id > 0).astype(jnp.float32)
        upper_ok = (region_id < N_REGION - 1).astype(jnp.float32)
        outside = jnp.concatenate([rows_all[lower_ids] * lower_ok, rows_all[upper_ids] * upper_ok])
        table = jnp.concatenate([own_rows, received, outside])
        target_ids, source_ids, weights = tile_index(local_pairs[region_id, cell_id], mine, edge_cells[region_id, cell_id], C_DEV, N_CELL)
        assign = (target_ids[:, None] == jnp.arange(C_DEV, dtype=jnp.int32)[None, :]).astype(jnp.float32) * weights[:, None]
        return (own_rows[target_ids], table[source_ids], assign)

    def density_device(device):
        targets, sources, assign = device_table(state_rows, device)
        terms = run_tiles(density_tile, targets, sources)
        return jnp.dot(assign.T, terms, precision=lax.Precision.HIGHEST)
    rho = lax.map(density_device, device_ids).reshape(CELLS, P_SIZE)
    pressure_term = occupied * (GAMMA - 1.0) * energy / (rho + 1.0 - occupied)
    force_rows = jnp.concatenate([state_rows, pressure_term[:, None]], axis=1)

    def force_device(device):
        targets, sources, assign = device_table(force_rows, device)
        terms = run_tiles(force_tile, targets, sources)
        return jnp.einsum('tc,tkp->kcp', assign, terms, precision=lax.Precision.HIGHEST)
    forces = lax.map(force_device, device_ids)
    forces = jnp.transpose(forces, (1, 0, 2, 3)).reshape(4, CELLS, P_SIZE)
    return (rho * occupied, forces[:3] * occupied[None], forces[3] * occupied)
```

```python
import functools
import math

import jax
import jax.numpy as jnp
from jax import lax
from jax.experimental import pallas as pl
from jax.experimental.pallas import tpu as pltpu
from jax.sharding import PartitionSpec as P

GAMMA = 5.0 / 3.0
LANES = 128
BF16 = jnp.bfloat16
F32 = jnp.float32

ROWS = 8
TINY = 1e-12
DOT_K = 48

VMEM = pl.BlockSpec(memory_space=pltpu.VMEM)
SMEM = pl.BlockSpec(memory_space=pltpu.SMEM)


def row_ids(shape):
    return lax.broadcasted_iota(jnp.int32, shape, 0)


def split3(value):
    first = value.astype(BF16).astype(F32)
    rest = value - first
    second = rest.astype(BF16).astype(F32)
    return first, second, rest - second


def left_parts(value):
    a, b, c = split3(value)
    return jnp.concatenate([a, a, b, b, a, c], axis=0)


def right_parts(value):
    a, b, c = split3(value)
    return jnp.concatenate([a, b, a, b, c, a], axis=0).astype(BF16)


def norm_row(rows):
    return rows[0:1] * rows[0:1] + rows[1:2] * rows[1:2] + rows[2:3] * rows[2:3]


def left_comps(rows):
    ids = row_ids(rows.shape)
    return jnp.where(ids < 3, rows, jnp.where(ids == 3, norm_row(rows), jnp.where(ids == 4, 1.0, 0.0)))


def right_comps(rows):
    ids = row_ids(rows.shape)
    return jnp.where(ids < 3, -2.0 * rows, jnp.where(ids == 3, 1.0, jnp.where(ids == 4, norm_row(rows), 0.0)))


def store_left(left_ref, cell, comps):
    parts = left_parts(comps)
    pad = jnp.zeros((LANES - DOT_K, LANES), F32)
    for at in range(parts.shape[1] // LANES):
        block = jnp.concatenate([parts[:, at * LANES : (at + 1) * LANES], pad], axis=0)
        left_ref[cell, pl.ds(at * LANES, LANES), :] = block.T.astype(BF16)


def prep_kernel(counts, send, edge, pos, vel, mass, smooth, own, pay, up, down):
    cells = mass.shape[0]
    slots = mass.shape[1]
    peers = pay.shape[0]
    lane = lax.broadcasted_iota(jnp.int32, (1, slots), 1)
    for k in range(cells):
        live = lane < counts[k]
        for d in range(3):
            own[k, d : d + 1, :] = pos[d, k : k + 1, :] - 0.5
            own[k, 5 + d : 6 + d, :] = vel[d, k : k + 1, :]
        own[k, 3:4, :] = smooth[k : k + 1, :]
        own[k, 4:5, :] = jnp.where(live, mass[k : k + 1, :], 0.0)

    def fill(k, carry):
        picked = send[k]
        pay[k] = jnp.where(picked >= 0, own[jnp.maximum(picked, 0)], 0.0)
        return carry

    lax.fori_loop(0, peers, fill, 0)
    down[0] = own[edge[0, 0, 0]]
    up[0] = own[edge[0, 0, 1]]


def list_tiles(icut, jcut, counts, send, pairs, edge, own, rec, low, high, live, tgt, src, wgt, both):
    cells = own.shape[0]
    peers = rec.shape[0]
    for k in range(cells):
        live[k] = counts[k]

    def occupied_of(rows):
        return jnp.sum(jnp.where(rows[4:5] > 0.0, 1.0, 0.0)).astype(jnp.int32)

    def remote(k, carry):
        live[cells + k] = occupied_of(rec[k])
        return carry

    lax.fori_loop(0, peers, remote, 0)
    live[cells + peers] = occupied_of(low[0])
    live[cells + peers + 1] = occupied_of(high[0])

    def push(state, a, b, w, ok):
        n, blocks = state

        @pl.when(ok)
        def _():
            tgt[n] = a
            src[n] = b
            wgt[n] = w

        more = chunks(live[a], icut) * chunks(live[b], jcut)
        return n + ok.astype(jnp.int32), blocks + jnp.where(ok, more, 0)

    state = (jnp.int32(0), jnp.int32(0))
    for a in range(cells):
        for b in range(a + 1, cells):
            mult = jnp.int32(0)
            for row in range(pairs.shape[3]):
                one = pairs[0, 0, 0, row]
                two = pairs[0, 0, 1, row]
                hit = ((one == a) & (two == b)) | ((one == b) & (two == a))
                mult = mult + hit.astype(jnp.int32)
            state = push(state, a, b, mult, mult > 0)
            if not both:
                state = push(state, b, a, mult, mult > 0)
    local = state[1]
    for a in range(cells):
        state = push(state, a, a, jnp.int32(1), counts[a] > 0)

    def remote_tile(k, state):
        picked = send[k]
        return push(
            state, jnp.maximum(picked, 0), cells + k, jnp.int32(1), (picked >= 0) & (live[cells + k] > 0)
        )

    state = lax.fori_loop(0, peers, remote_tile, state)
    state = push(state, edge[0, 0, 0], cells + peers, jnp.int32(1), live[cells + peers] > 0)
    state = push(state, edge[0, 0, 1], cells + peers + 1, jnp.int32(1), live[cells + peers + 1] > 0)
    tgt[state[0]] = 0
    src[state[0]] = 0
    wgt[state[0]] = 0
    return state[0], state[1], local


def chunks(count, size):
    return lax.shift_right_logical(count + (size - 1), jnp.int32(size.bit_length() - 1))


class Blocks:
    def __init__(self, icut, jcut, live, tgt, src, wgt, ring, total):
        self.icut, self.jcut = icut, jcut
        self.live, self.tgt, self.src, self.wgt = live, tgt, src, wgt
        self.ring, self.total = ring, total

    def clear(self, entries):
        for k in range(entries):
            for field in range(5):
                self.ring[5 * k + field] = 0

    def write(self, slot, state):
        n, ii, jj = state
        a, b = self.tgt[n], self.src[n]
        at = 5 * slot
        self.ring[at] = a
        self.ring[at + 1] = b
        self.ring[at + 2] = ii
        self.ring[at + 3] = jj
        self.ring[at + 4] = self.wgt[n]
        jnext = jj + 1
        jwrap = jnext >= chunks(self.live[b], self.jcut)
        inext = jnp.where(jwrap, ii + 1, ii)
        iwrap = inext >= chunks(self.live[a], self.icut)
        return (
            jnp.minimum(jnp.where(iwrap, n + 1, n), self.total),
            jnp.where(iwrap, 0, inext),
            jnp.where(jwrap, 0, jnext),
        )

    def read(self, slot):
        at = 5 * slot
        return (
            self.ring[at],
            self.ring[at + 1],
            pl.multiple_of(self.ring[at + 2] * self.icut, self.icut),
            pl.multiple_of(self.ring[at + 3] * self.jcut, self.jcut),
            self.ring[at + 4].astype(F32),
        )


def density_kernel(
    icut, jcut, group,
    counts, send, pairs, edge, own, rec, low, high, energy,
    rho_out, term_out, pay,
    live, tgt, src, wgt, ring, left, right, mrow, acc, *dist,
):
    cells = own.shape[0]
    peers = rec.shape[0]
    slots = own.shape[2]
    tiles, total, _ = list_tiles(
        icut, jcut, counts, send, pairs, edge, own, rec, low, high, live, tgt, src, wgt, False
    )

    def source(rows, at):
        right[at] = right_parts(right_comps(rows))
        mrow[at] = jnp.broadcast_to(rows[4:5], (8, slots))

    def own_cell(k, carry):
        rows = own[k]
        inv = 1.0 / rows[3:4]
        store_left(left, k, left_comps(rows) * (inv * inv))
        source(rows, k)
        acc[k] = jnp.zeros((slots, LANES), F32)
        return carry

    lax.fori_loop(0, cells, own_cell, 0)

    def rec_cell(k, carry):
        source(rec[k], cells + k)
        return carry

    lax.fori_loop(0, peers, rec_cell, 0)
    source(low[0], cells + peers)
    source(high[0], cells + peers + 1)

    blocks = Blocks(icut, jcut, live, tgt, src, wgt, ring, tiles)
    blocks.clear(group)
    for ref in dist:
        ref[...] = jnp.ones_like(ref)
    zero = jnp.int32(0)
    state = (zero, zero, zero)
    for g in range(group):
        state = blocks.write(group + g, state)

    def step(k, state):
        for g in range(group):
            a, b, istart, jstart, w = blocks.read(k * group + g)
            s = jnp.maximum(dist[g][...], TINY)
            q = s * lax.rsqrt(s)
            e = 1.0 - q
            u = jnp.maximum(e, 0.0)
            t = jnp.minimum(0.5 - (s * 3.0) * e, u * u * u)
            t = t * (mrow[b, 0:1, pl.ds(jstart, jcut)] * w)
            part = t[:, :LANES]
            for at in range(1, jcut // LANES):
                part = part + t[:, at * LANES : (at + 1) * LANES]
            acc[a, pl.ds(istart, icut), :] += part

            state = blocks.write((k + 2) * group + g, state)
            a, b, istart, jstart, _ = blocks.read((k + 1) * group + g)
            dist[g][...] = jnp.dot(
                left[a, pl.ds(istart, icut), :DOT_K],
                right[b, :, pl.ds(jstart, jcut)],
                preferred_element_type=F32,
            )
        return state

    lax.fori_loop(0, chunks(total, group) + 1, step, state)

    lane = lax.broadcasted_iota(jnp.int32, (1, slots), 1)
    ones = jnp.ones((8, LANES), BF16)
    for k in range(cells):
        one, two, three = split3(acc[k])
        total_row = jnp.zeros((8, slots), F32)
        for part in (three, two, one):
            total_row = total_row + lax.dot_general(
                ones, part.astype(BF16), (((1,), (1,)), ((), ())), preferred_element_type=F32
            )
        inv = 1.0 / own[k, 3:4, :]
        rho = total_row[0:1] * (16.0 / math.pi) * (inv * inv * inv)
        occupied = jnp.where(lane < counts[k], 1.0, 0.0)
        rho_out[k : k + 1, :] = rho * occupied
        term_out[k] = occupied * (GAMMA - 1.0) * energy[k : k + 1, :] / (rho + 1.0 - occupied)

    def fill(k, carry):
        pay[k] = term_out[jnp.maximum(send[k], 0)]
        return carry

    lax.fori_loop(0, peers, fill, 0)
    pay[peers] = term_out[edge[0, 0, 0]]
    pay[peers + 1] = term_out[edge[0, 0, 1]]


def force_kernel(
    icut, jcut, group,
    counts, send, pairs, edge, own, rec, low, high, term, rterm, lterm, hterm,
    accel_out, heat_out,
    live, tgt, src, wgt, ring, left, right, weights, scale, bcol, ccol, acc, *work,
):
    cells = own.shape[0]
    peers = rec.shape[0]
    slots = own.shape[2]
    dist, upper, lower = work[:group], work[group : 2 * group], work[2 * group :]
    tiles, total, local = list_tiles(
        icut, jcut, counts, send, pairs, edge, own, rec, low, high, live, tgt, src, wgt, True
    )
    strength = math.sqrt(24.0 / math.pi)

    def source(rows, pressure, at):
        right[at] = right_parts(right_comps(rows))
        h = rows[3:4]
        inv = 1.0 / jnp.where(h > 0.0, h, 1.0)
        b = strength * (inv * inv)
        ids = row_ids((8, slots))
        scale[at] = jnp.where(ids == 0, b, b * inv)
        m = rows[4:5]
        mp = m * pressure
        xv = rows[0:1] * rows[5:6] + rows[1:2] * rows[6:7] + rows[2:3] * rows[7:8]
        base = jnp.where(ids == 3, 1.0, jnp.where(ids == 4, xv, rows))
        sums = jnp.concatenate([base * m, jnp.where(ids < 4, base, 0.0) * mp], axis=0)
        one, two, three = split3(sums)
        weights[at] = jnp.concatenate([one, two, three], axis=0).astype(BF16)

    def own_cell(k, carry):
        rows = own[k]
        store_left(left, k, left_comps(rows))
        source(rows, term[k], k)
        acc[k] = jnp.zeros((DOT_K, slots), F32)
        pair = jnp.concatenate([scale[k], jnp.zeros((LANES - 8, slots), F32)], axis=0)
        for at in range(slots // LANES):
            cols = pair[:, at * LANES : (at + 1) * LANES].T
            bcol[k, pl.ds(at * LANES, LANES), :] = jnp.broadcast_to(cols[:, 0:1], (LANES, LANES))
            ccol[k, pl.ds(at * LANES, LANES), :] = jnp.broadcast_to(cols[:, 1:2], (LANES, LANES))
        return carry

    lax.fori_loop(0, cells, own_cell, 0)

    def rec_cell(k, carry):
        source(rec[k], rterm[k], cells + k)
        return carry

    lax.fori_loop(0, peers, rec_cell, 0)
    source(low[0], lterm[0], cells + peers)
    source(high[0], hterm[0], cells + peers + 1)

    blocks = Blocks(icut, jcut, live, tgt, src, wgt, ring, tiles)
    blocks.clear(2 * group)
    for ref in work:
        ref[...] = jnp.ones_like(ref)
    zero = jnp.int32(0)
    state = (zero, zero, zero)
    for g in range(group):
        state = blocks.write(2 * group + g, state)

    def step(mutual, k, state):
        for g in range(group):
            a, b, istart, jstart, w = blocks.read(k * group + g)
            wt = weights[b, :, pl.ds(jstart, jcut)]
            spec = (((1,), (1,)), ((), ()))
            part = lax.dot_general(wt, upper[g][...], spec, preferred_element_type=F32)
            part = part + lax.dot_general(wt, lower[g][...], spec, preferred_element_type=F32)
            acc[a, :, pl.ds(istart, icut)] += part * w
            if mutual:
                wt = weights[a, :, pl.ds(istart, icut)]
                part = jnp.dot(wt, upper[g][...], preferred_element_type=F32)
                part = part + jnp.dot(wt, lower[g][...], preferred_element_type=F32)
                w = jnp.where(k * group + g < local + 2 * group, w, 0.0)
                acc[b, :, pl.ds(jstart, jcut)] += part * w

            a, b, istart, jstart, _ = blocks.read((k + 1) * group + g)
            s = jnp.maximum(dist[g][...], TINY)
            r = lax.rsqrt(s)
            d = s * r
            bi = bcol[a, pl.ds(istart, icut), :]
            ci = ccol[a, pl.ds(istart, icut), :]
            bi = jnp.concatenate([bi] * (jcut // LANES), axis=1)
            ci = jnp.concatenate([ci] * (jcut // LANES), axis=1)
            t = ci * d
            u = jnp.maximum(bi - t, 0.0)
            v = jnp.minimum(t, u)
            slope = (u + u - v) * v
            t = scale[b, 1:2, pl.ds(jstart, jcut)] * d
            u = jnp.maximum(scale[b, 0:1, pl.ds(jstart, jcut)] - t, 0.0)
            v = jnp.minimum(t, u)
            slope = (slope + (u + u - v) * v) * r
            rounded = slope.astype(BF16)
            upper[g][...] = rounded
            lower[g][...] = (slope - rounded.astype(F32)).astype(BF16)

            state = blocks.write((k + 3) * group + g, state)
            a, b, istart, jstart, _ = blocks.read((k + 2) * group + g)
            dist[g][...] = jnp.dot(
                left[a, pl.ds(istart, icut), :DOT_K],
                right[b, :, pl.ds(jstart, jcut)],
                preferred_element_type=F32,
            )
        return state

    first = jnp.minimum(chunks(local, group) + 2, chunks(total, group) + 2)
    state = lax.fori_loop(0, first, functools.partial(step, True), state)
    lax.fori_loop(first, chunks(total, group) + 2, functools.partial(step, False), state)

    lane = lax.broadcasted_iota(jnp.int32, (1, slots), 1)
    for k in range(cells):
        occupied = jnp.where(lane < counts[k], 1.0, 0.0)
        sums = acc[k, 0:16, :] + (acc[k, 16:32, :] + acc[k, 32:48, :])
        pressure = term[k]
        x = [own[k, d : d + 1, :] for d in range(3)]
        v = [own[k, 5 + d : 6 + d, :] for d in range(3)]
        both = pressure * sums[3:4] + sums[11:12]
        for d in range(3):
            accel_out[d, k : k + 1, :] = occupied * (
                x[d] * both - pressure * sums[d : d + 1] - sums[8 + d : 9 + d]
            )
        xv = x[0] * v[0] + x[1] * v[1] + x[2] * v[2]
        total_heat = xv * sums[3:4] + sums[4:5]
        for d in range(3):
            total_heat = total_heat - v[d] * sums[d : d + 1] - x[d] * sums[5 + d : 6 + d]
        heat_out[k : k + 1, :] = -occupied * pressure * total_heat


def on_device(positions, velocities, mass, smoothing, energy, counts, send, pairs, edge):
    cells, slots = mass.shape
    peers = send.shape[2]
    table = cells + peers + 2
    tiles = cells * cells + peers + 3
    icut, jcut, group = 128, 256, 4
    entries = 5 * (tiles * (slots // icut) * (slots // jcut) + 6 * group)
    send = send.reshape(peers)
    pairs = jnp.transpose(pairs, (0, 1, 3, 2))
    shape = jax.ShapeDtypeStruct
    params = pltpu.CompilerParams(vmem_limit_bytes=40 * 1024 * 1024)
    own, pay, up, down = pl.pallas_call(
        prep_kernel,
        out_shape=[
            shape((cells, ROWS, slots), F32),
            shape((peers, ROWS, slots), F32),
            shape((1, ROWS, slots), F32),
            shape((1, ROWS, slots), F32),
        ],
        in_specs=[SMEM] * 3 + [VMEM] * 4,
        out_specs=[VMEM] * 4,
        compiler_params=params,
        name="prep",
    )(counts, send, edge, positions, velocities, mass, smoothing)

    regions = lax.axis_size("region")
    upward = [(i, i + 1) for i in range(regions - 1)]
    downward = [(i + 1, i) for i in range(regions - 1)]

    def exchange(cell_pay, up, down):
        low = lax.ppermute(up, "region", upward)
        high = lax.ppermute(down, "region", downward)
        rec = lax.all_to_all(cell_pay, "cell", split_axis=0, concat_axis=0, tiled=True)
        return rec, low, high

    rec, low, high = exchange(pay, up, down)

    lists = [
        pltpu.SMEM((table,), jnp.int32),
        pltpu.SMEM((tiles,), jnp.int32),
        pltpu.SMEM((tiles,), jnp.int32),
        pltpu.SMEM((tiles,), jnp.int32),
        pltpu.SMEM((entries,), jnp.int32),
    ]
    density, term, term_pay = pl.pallas_call(
        functools.partial(density_kernel, icut, jcut, group),
        out_shape=[
            shape((cells, slots), F32),
            shape((cells, 1, slots), F32),
            shape((peers + 2, 1, slots), F32),
        ],
        in_specs=[SMEM] * 4 + [VMEM] * 5,
        out_specs=[VMEM] * 3,
        scratch_shapes=lists
        + [
            pltpu.VMEM((cells, slots, LANES), BF16),
            pltpu.VMEM((table, DOT_K, slots), BF16),
            pltpu.VMEM((table, 8, slots), F32),
            pltpu.VMEM((cells, slots, LANES), F32),
        ]
        + [pltpu.VMEM((icut, jcut), F32)] * group,
        compiler_params=params,
        name="density",
    )(counts, send, pairs, edge, own, rec, low, high, energy)

    rterm, lterm, hterm = exchange(
        term_pay[:peers], term_pay[peers + 1 : peers + 2], term_pay[peers : peers + 1]
    )

    accel, heat = pl.pallas_call(
        functools.partial(force_kernel, icut, jcut, group),
        out_shape=[shape((3, cells, slots), F32), shape((cells, slots), F32)],
        in_specs=[SMEM] * 4 + [VMEM] * 8,
        out_specs=[VMEM] * 2,
        scratch_shapes=lists
        + [
            pltpu.VMEM((cells, slots, LANES), BF16),
            pltpu.VMEM((table, DOT_K, slots), BF16),
            pltpu.VMEM((table, DOT_K, slots), BF16),
            pltpu.VMEM((table, 8, slots), F32),
            pltpu.VMEM((cells, slots, LANES), F32),
            pltpu.VMEM((cells, slots, LANES), F32),
            pltpu.VMEM((cells, DOT_K, slots), F32),
        ]
        + [pltpu.VMEM((icut, jcut), F32)] * group
        + [pltpu.VMEM((icut, jcut), BF16)] * (2 * group),
        compiler_params=params,
        name="force",
    )(counts, send, pairs, edge, own, rec, low, high, term, rterm, lterm, hterm)
    return density, accel, heat


def solution(mesh):
    placed = (
        P(None, ("region", "cell"), None),
        P(None, ("region", "cell"), None),
        P(("region", "cell"), None),
        P(("region", "cell"), None),
        P(("region", "cell"), None),
        P(("region", "cell")),
        P("region", "cell", None, None),
        P("region", "cell", None, None),
        P("region", "cell", None),
    )
    return jax.shard_map(
        on_device,
        mesh=mesh,
        in_specs=placed,
        out_specs=(
            P(("region", "cell"), None),
            P(None, ("region", "cell"), None),
            P(("region", "cell"), None),
        ),
        check_vma=False,
    )
```

```python
import functools
import math

import jax
import jax.numpy as jnp
from jax import lax
from jax.experimental import pallas as pl
from jax.experimental.pallas import tpu as pltpu
from jax.sharding import PartitionSpec as P

GAMMA = 5.0 / 3.0
LANES = 128
BF16 = jnp.bfloat16
F32 = jnp.float32

ROWS = 8
TINY = 1e-12
DOT_K = 48
STRIP = 16

VMEM = pl.BlockSpec(memory_space=pltpu.VMEM)
SMEM = pl.BlockSpec(memory_space=pltpu.SMEM)


def row_ids(shape):
    return lax.broadcasted_iota(jnp.int32, shape, 0)


def split3(value):
    first = value.astype(BF16).astype(F32)
    rest = value - first
    second = rest.astype(BF16).astype(F32)
    return first, second, rest - second


def left_parts(value):
    a, b, c = split3(value)
    return jnp.concatenate([a, a, b, b, a, c], axis=0)


def right_parts(value):
    a, b, c = split3(value)
    return jnp.concatenate([a, b, a, b, c, a], axis=0).astype(BF16)


def norm_row(rows):
    return rows[0:1] * rows[0:1] + rows[1:2] * rows[1:2] + rows[2:3] * rows[2:3]


def left_comps(rows):
    ids = row_ids(rows.shape)
    return jnp.where(ids < 3, rows, jnp.where(ids == 3, norm_row(rows), jnp.where(ids == 4, 1.0, 0.0)))


def right_comps(rows):
    ids = row_ids(rows.shape)
    return jnp.where(ids < 3, -2.0 * rows, jnp.where(ids == 3, 1.0, jnp.where(ids == 4, norm_row(rows), 0.0)))


def store_left(left_ref, cell, comps):
    parts = left_parts(comps)
    pad = jnp.zeros((LANES - DOT_K, LANES), F32)
    for at in range(parts.shape[1] // LANES):
        block = jnp.concatenate([parts[:, at * LANES : (at + 1) * LANES], pad], axis=0)
        left_ref[cell, pl.ds(at * LANES, LANES), :] = block.T.astype(BF16)


def prep_kernel(counts, send, edge, pos, vel, mass, smooth, own, pay, faces):
    cells = mass.shape[0]
    slots = mass.shape[1]
    peers = pay.shape[0]
    lane = lax.broadcasted_iota(jnp.int32, (1, slots), 1)
    for k in range(cells):
        live = lane < counts[k]
        for d in range(3):
            own[k, d : d + 1, :] = pos[d, k : k + 1, :] - 0.5
            own[k, 5 + d : 6 + d, :] = vel[d, k : k + 1, :]
        own[k, 3:4, :] = smooth[k : k + 1, :]
        own[k, 4:5, :] = jnp.where(live, mass[k : k + 1, :], 0.0)

    def fill(k, carry):
        picked = send[k]
        pay[k] = jnp.where(picked >= 0, own[jnp.maximum(picked, 0)], 0.0)
        return carry

    lax.fori_loop(0, peers, fill, 0)
    for side in range(2):
        faces[side] = own[edge[0, 0, side]]


def neighbours(met):
    region = lax.axis_index("region")
    last = met.shape[0] // 2 - 1
    return (
        jnp.maximum(2 * region - 1, 0),
        jnp.minimum(2 * region + 2, 2 * last),
        region > 0,
        region < last,
    )


def list_tiles(icut, jcut, counts, send, pairs, edge, own, rec, met, live, tgt, src, wgt, both):
    cells = own.shape[0]
    peers = rec.shape[0]
    for k in range(cells):
        live[k] = counts[k]

    low, high, has_low, has_high = neighbours(met)
    occupied = jnp.sum(jnp.where(rec[:, 4, :] > 0.0, 1.0, 0.0), axis=1, keepdims=True)
    for k in range(peers):
        live[cells + k] = occupied[k, 0].astype(jnp.int32)
    for at, face, there in ((0, low, has_low), (1, high, has_high)):
        count = jnp.sum(jnp.where(met[face, 4:5, :] > 0.0, 1.0, 0.0)).astype(jnp.int32)
        live[cells + peers + at] = jnp.where(there, count, 0)

    def push(state, a, b, w, ok):
        n, blocks = state

        @pl.when(ok)
        def _():
            tgt[n] = a
            src[n] = b
            wgt[n] = w

        more = chunks(live[a], icut) * chunks(live[b], jcut)
        return n + ok.astype(jnp.int32), blocks + jnp.where(ok, more, 0)

    state = (jnp.int32(0), jnp.int32(0))
    for a in range(cells):
        for b in range(a + 1, cells):
            mult = jnp.int32(0)
            for row in range(pairs.shape[3]):
                one = pairs[0, 0, 0, row]
                two = pairs[0, 0, 1, row]
                hit = ((one == a) & (two == b)) | ((one == b) & (two == a))
                mult = mult + hit.astype(jnp.int32)
            state = push(state, a, b, mult, mult > 0)
            if not both:
                state = push(state, b, a, mult, mult > 0)
    local = state[1]
    for a in range(cells):
        state = push(state, a, a, jnp.int32(1), counts[a] > 0)

    def remote_tile(k, state):
        picked = send[k]
        return push(
            state, jnp.maximum(picked, 0), cells + k, jnp.int32(1), (picked >= 0) & (live[cells + k] > 0)
        )

    state = lax.fori_loop(0, peers, remote_tile, state)
    state = push(state, edge[0, 0, 0], cells + peers, jnp.int32(1), live[cells + peers] > 0)
    state = push(state, edge[0, 0, 1], cells + peers + 1, jnp.int32(1), live[cells + peers + 1] > 0)
    tgt[state[0]] = 0
    src[state[0]] = 0
    wgt[state[0]] = 0
    return state[0], state[1], local


def chunks(count, size):
    return lax.shift_right_logical(count + (size - 1), jnp.int32(size.bit_length() - 1))


class Blocks:
    def __init__(self, icut, jcut, live, tgt, src, wgt, ring, total):
        self.icut, self.jcut = icut, jcut
        self.live, self.tgt, self.src, self.wgt = live, tgt, src, wgt
        self.ring, self.total = ring, total

    def clear(self, entries):
        for k in range(entries):
            for field in range(5):
                self.ring[5 * k + field] = 0

    def write(self, slot, state):
        n, ii, jj = state
        a, b = self.tgt[n], self.src[n]
        at = 5 * slot
        self.ring[at] = a
        self.ring[at + 1] = b
        self.ring[at + 2] = ii
        self.ring[at + 3] = jj
        self.ring[at + 4] = self.wgt[n]
        jnext = jj + 1
        jwrap = jnext >= chunks(self.live[b], self.jcut)
        inext = jnp.where(jwrap, ii + 1, ii)
        iwrap = inext >= chunks(self.live[a], self.icut)
        return (
            jnp.minimum(jnp.where(iwrap, n + 1, n), self.total),
            jnp.where(iwrap, 0, inext),
            jnp.where(jwrap, 0, jnext),
        )

    def read(self, slot):
        at = 5 * slot
        return (
            self.ring[at],
            self.ring[at + 1],
            pl.multiple_of(self.ring[at + 2] * self.icut, self.icut),
            pl.multiple_of(self.ring[at + 3] * self.jcut, self.jcut),
            self.ring[at + 4].astype(F32),
        )


def density_kernel(
    icut, jcut, group,
    counts, send, pairs, edge, own, rec, met, energy,
    rho_out, term_out, pay, faces,
    live, tgt, src, wgt, ring, left, right, mrow, acc, *work,
):
    cells = own.shape[0]
    peers = rec.shape[0]
    slots = own.shape[2]
    dist, parts = work[:group], work[group:]
    tiles, total, _ = list_tiles(
        icut, jcut, counts, send, pairs, edge, own, rec, met, live, tgt, src, wgt, False
    )

    def source(rows, at):
        right[at] = right_parts(right_comps(rows))
        mrow[at] = jnp.broadcast_to(rows[4:5], (8, slots))

    def own_cell(k, carry):
        rows = own[k]
        inv = 1.0 / rows[3:4]
        store_left(left, k, left_comps(rows) * (inv * inv))
        source(rows, k)
        acc[k] = jnp.zeros((slots, LANES), F32)
        return carry

    lax.fori_loop(0, cells, own_cell, 0, unroll=True)

    def rec_cell(k, carry):
        source(rec[k], cells + k)
        return carry

    lax.fori_loop(0, peers, rec_cell, 0, unroll=4)
    low, high, _, _ = neighbours(met)
    source(met[low], cells + peers)
    source(met[high], cells + peers + 1)

    blocks = Blocks(icut, jcut, live, tgt, src, wgt, ring, tiles)
    blocks.clear(group)
    for ref in dist:
        ref[...] = jnp.ones_like(ref)
    zero = jnp.int32(0)
    state = (zero, zero, zero)
    for g in range(group):
        state = blocks.write(group + g, state)

    def step(k, state):
        for g in range(group):
            _, b, _, jstart, w = blocks.read(k * group + g)
            weight = mrow[b, 0:1, pl.ds(jstart, jcut)] * w
            for row in range(0, icut, STRIP):
                s = jnp.maximum(dist[g][row : row + STRIP, :], TINY)
                q = s * lax.rsqrt(s)
                e = 1.0 - q
                u = jnp.maximum(e, 0.0)
                t = jnp.minimum(0.5 - (s * 3.0) * e, u * u * u) * weight
                part = t[:, :LANES]
                for at in range(1, jcut // LANES):
                    part = part + t[:, at * LANES : (at + 1) * LANES]
                parts[g][row : row + STRIP, :] = part

            state = blocks.write((k + 2) * group + g, state)
            a, b, istart, jstart, _ = blocks.read((k + 1) * group + g)
            dist[g][...] = jnp.dot(
                left[a, pl.ds(istart, icut), :DOT_K],
                right[b, :, pl.ds(jstart, jcut)],
                preferred_element_type=F32,
            )
        for g in range(group):
            a, _, istart, _, _ = blocks.read(k * group + g)
            acc[a, pl.ds(istart, icut), :] += parts[g][...]
        return state

    lax.fori_loop(0, chunks(total, group) + 1, step, state)

    lane = lax.broadcasted_iota(jnp.int32, (1, slots), 1)
    ones = jnp.ones((8, LANES), BF16)
    for k in range(cells):
        one, two, three = split3(acc[k])
        total_row = jnp.zeros((8, slots), F32)
        for part in (three, two, one):
            total_row = total_row + lax.dot_general(
                ones, part.astype(BF16), (((1,), (1,)), ((), ())), preferred_element_type=F32
            )
        inv = 1.0 / own[k, 3:4, :]
        rho = total_row[0:1] * (16.0 / math.pi) * (inv * inv * inv)
        occupied = jnp.where(lane < counts[k], 1.0, 0.0)
        rho_out[k : k + 1, :] = rho * occupied
        term_out[k] = occupied * (GAMMA - 1.0) * energy[k : k + 1, :] / (rho + 1.0 - occupied)

    def fill(k, carry):
        pay[k] = term_out[jnp.maximum(send[k], 0)]
        return carry

    lax.fori_loop(0, peers, fill, 0)
    for side in range(2):
        faces[side] = term_out[edge[0, 0, side]]


def force_kernel(
    icut, jcut, group,
    counts, send, pairs, edge, own, rec, met, term, rterm, mterm,
    accel_out, heat_out,
    live, tgt, src, wgt, ring, left, right, weights, scale, bcol, ccol, acc, *work,
):
    cells = own.shape[0]
    peers = rec.shape[0]
    slots = own.shape[2]
    dist, upper, lower = work[:group], work[group : 2 * group], work[2 * group :]
    tiles, total, local = list_tiles(
        icut, jcut, counts, send, pairs, edge, own, rec, met, live, tgt, src, wgt, True
    )
    strength = math.sqrt(24.0 / math.pi)

    def source(rows, pressure, at):
        right[at] = right_parts(right_comps(rows))
        h = rows[3:4]
        inv = 1.0 / jnp.where(h > 0.0, h, 1.0)
        b = strength * (inv * inv)
        ids = row_ids((8, slots))
        scale[at] = jnp.where(ids == 0, b, b * inv)
        m = rows[4:5]
        mp = m * pressure
        xv = rows[0:1] * rows[5:6] + rows[1:2] * rows[6:7] + rows[2:3] * rows[7:8]
        base = jnp.where(ids == 3, 1.0, jnp.where(ids == 4, xv, rows))
        sums = jnp.concatenate([base * m, jnp.where(ids < 4, base, 0.0) * mp], axis=0)
        one, two, three = split3(sums)
        weights[at] = jnp.concatenate([one, two, three], axis=0).astype(BF16)

    def own_cell(k, carry):
        rows = own[k]
        store_left(left, k, left_comps(rows))
        source(rows, term[k], k)
        acc[k] = jnp.zeros((DOT_K, slots), F32)
        pair = jnp.concatenate([scale[k], jnp.zeros((LANES - 8, slots), F32)], axis=0)
        for at in range(slots // LANES):
            cols = pair[:, at * LANES : (at + 1) * LANES].T
            bcol[k, pl.ds(at * LANES, LANES), :] = jnp.broadcast_to(cols[:, 0:1], (LANES, LANES))
            ccol[k, pl.ds(at * LANES, LANES), :] = jnp.broadcast_to(cols[:, 1:2], (LANES, LANES))
        return carry

    lax.fori_loop(0, cells, own_cell, 0, unroll=True)

    def rec_cell(k, carry):
        source(rec[k], rterm[k], cells + k)
        return carry

    lax.fori_loop(0, peers, rec_cell, 0, unroll=4)
    low, high, _, _ = neighbours(met)
    source(met[low], mterm[low], cells + peers)
    source(met[high], mterm[high], cells + peers + 1)

    blocks = Blocks(icut, jcut, live, tgt, src, wgt, ring, tiles)
    blocks.clear(2 * group)
    for ref in work:
        ref[...] = jnp.ones_like(ref)
    zero = jnp.int32(0)
    state = (zero, zero, zero)
    for g in range(group):
        state = blocks.write(2 * group + g, state)

    def step(mutual, k, state):
        adds = []
        for g in range(group):
            a, b, istart, jstart, w = blocks.read(k * group + g)
            wt = weights[b, :, pl.ds(jstart, jcut)]
            spec = (((1,), (1,)), ((), ()))
            part = lax.dot_general(wt, upper[g][...], spec, preferred_element_type=F32)
            part = part + lax.dot_general(wt, lower[g][...], spec, preferred_element_type=F32)
            later = [(a, istart, part * w)]
            if mutual:
                wt = weights[a, :, pl.ds(istart, icut)]
                part = jnp.dot(wt, upper[g][...], preferred_element_type=F32)
                part = part + jnp.dot(wt, lower[g][...], preferred_element_type=F32)
                w = jnp.where(k * group + g < local + 2 * group, w, 0.0)
                later.append((b, jstart, part * w))
            adds += later

            a, b, istart, jstart, _ = blocks.read((k + 1) * group + g)
            bj = scale[b, 0:1, pl.ds(jstart, jcut)]
            cj = scale[b, 1:2, pl.ds(jstart, jcut)]
            for row in range(0, icut, STRIP):
                s = jnp.maximum(dist[g][row : row + STRIP, :], TINY)
                r = lax.rsqrt(s)
                d = s * r
                bi = bcol[a, pl.ds(istart + row, STRIP), :]
                ci = ccol[a, pl.ds(istart + row, STRIP), :]
                bi = jnp.concatenate([bi] * (jcut // LANES), axis=1)
                ci = jnp.concatenate([ci] * (jcut // LANES), axis=1)
                t = ci * d
                u = jnp.maximum(bi - t, 0.0)
                v = jnp.minimum(t, u)
                slope = (u + u - v) * v
                t = cj * d
                u = jnp.maximum(bj - t, 0.0)
                v = jnp.minimum(t, u)
                slope = (slope + (u + u - v) * v) * r
                rounded = slope.astype(BF16)
                upper[g][row : row + STRIP, :] = rounded
                lower[g][row : row + STRIP, :] = (slope - rounded.astype(F32)).astype(BF16)

            state = blocks.write((k + 3) * group + g, state)
            a, b, istart, jstart, _ = blocks.read((k + 2) * group + g)
            dist[g][...] = jnp.dot(
                left[a, pl.ds(istart, icut), :DOT_K],
                right[b, :, pl.ds(jstart, jcut)],
                preferred_element_type=F32,
            )
        for cell, start, part in adds:
            acc[cell, :, pl.ds(start, part.shape[1])] += part
        return state

    first = jnp.minimum(chunks(local, group) + 2, chunks(total, group) + 2)
    state = lax.fori_loop(0, first, functools.partial(step, True), state)
    lax.fori_loop(first, chunks(total, group) + 2, functools.partial(step, False), state)

    lane = lax.broadcasted_iota(jnp.int32, (1, slots), 1)
    for k in range(cells):
        occupied = jnp.where(lane < counts[k], 1.0, 0.0)
        sums = acc[k, 0:16, :] + (acc[k, 16:32, :] + acc[k, 32:48, :])
        pressure = term[k]
        x = [own[k, d : d + 1, :] for d in range(3)]
        v = [own[k, 5 + d : 6 + d, :] for d in range(3)]
        both = pressure * sums[3:4] + sums[11:12]
        for d in range(3):
            accel_out[d, k : k + 1, :] = occupied * (
                x[d] * both - pressure * sums[d : d + 1] - sums[8 + d : 9 + d]
            )
        xv = x[0] * v[0] + x[1] * v[1] + x[2] * v[2]
        total_heat = xv * sums[3:4] + sums[4:5]
        for d in range(3):
            total_heat = total_heat - v[d] * sums[d : d + 1] - x[d] * sums[5 + d : 6 + d]
        heat_out[k : k + 1, :] = -occupied * pressure * total_heat


def on_device(positions, velocities, mass, smoothing, energy, counts, send, pairs, edge):
    cells, slots = mass.shape
    peers = send.shape[2]
    table = cells + peers + 2
    tiles = cells * cells + peers + 3
    icut, jcut, group = 128, 256, 4
    entries = 5 * (tiles * (slots // icut) * (slots // jcut) + 6 * group)
    send = send.reshape(peers)
    pairs = jnp.transpose(pairs, (0, 1, 3, 2))
    shape = jax.ShapeDtypeStruct
    params = pltpu.CompilerParams(vmem_limit_bytes=40 * 1024 * 1024)
    own, pay, faces = pl.pallas_call(
        prep_kernel,
        out_shape=[
            shape((cells, ROWS, slots), F32),
            shape((peers, ROWS, slots), F32),
            shape((2, ROWS, slots), F32),
        ],
        in_specs=[SMEM] * 3 + [VMEM] * 4,
        out_specs=[VMEM] * 3,
        compiler_params=params,
        name="prep",
    )(counts, send, edge, positions, velocities, mass, smoothing)

    def exchange(pay, faces):
        met = lax.all_gather(faces, "region", axis=0, tiled=True)
        return lax.all_to_all(pay, "cell", split_axis=0, concat_axis=0, tiled=True), met

    rec, met = exchange(pay, faces)

    lists = [
        pltpu.SMEM((table,), jnp.int32),
        pltpu.SMEM((tiles,), jnp.int32),
        pltpu.SMEM((tiles,), jnp.int32),
        pltpu.SMEM((tiles,), jnp.int32),
        pltpu.SMEM((entries,), jnp.int32),
    ]
    density, term, pay, faces = pl.pallas_call(
        functools.partial(density_kernel, icut, jcut, group),
        out_shape=[
            shape((cells, slots), F32),
            shape((cells, 1, slots), F32),
            shape((peers, 1, slots), F32),
            shape((2, 1, slots), F32),
        ],
        in_specs=[SMEM] * 4 + [VMEM] * 4,
        out_specs=[VMEM] * 4,
        scratch_shapes=lists
        + [
            pltpu.VMEM((cells, slots, LANES), BF16),
            pltpu.VMEM((table, DOT_K, slots), BF16),
            pltpu.VMEM((table, 8, slots), F32),
            pltpu.VMEM((cells, slots, LANES), F32),
        ]
        + [pltpu.VMEM((icut, jcut), F32)] * group
        + [pltpu.VMEM((icut, LANES), F32)] * group,
        compiler_params=params,
        name="density",
    )(counts, send, pairs, edge, own, rec, met, energy)

    rterm, mterm = exchange(pay, faces)

    accel, heat = pl.pallas_call(
        functools.partial(force_kernel, icut, jcut, group),
        out_shape=[shape((3, cells, slots), F32), shape((cells, slots), F32)],
        in_specs=[SMEM] * 4 + [VMEM] * 6,
        out_specs=[VMEM] * 2,
        scratch_shapes=lists
        + [
            pltpu.VMEM((cells, slots, LANES), BF16),
            pltpu.VMEM((table, DOT_K, slots), BF16),
            pltpu.VMEM((table, DOT_K, slots), BF16),
            pltpu.VMEM((table, 8, slots), F32),
            pltpu.VMEM((cells, slots, LANES), F32),
            pltpu.VMEM((cells, slots, LANES), F32),
            pltpu.VMEM((cells, DOT_K, slots), F32),
        ]
        + [pltpu.VMEM((icut, jcut), F32)] * group
        + [pltpu.VMEM((icut, jcut), BF16)] * (2 * group),
        compiler_params=params,
        name="force",
    )(counts, send, pairs, edge, own, rec, met, term, rterm, mterm)
    return density, accel, heat


def solution(mesh):
    placed = (
        P(None, ("region", "cell"), None),
        P(None, ("region", "cell"), None),
        P(("region", "cell"), None),
        P(("region", "cell"), None),
        P(("region", "cell"), None),
        P(("region", "cell")),
        P("region", "cell", None, None),
        P("region", "cell", None, None),
        P("region", "cell", None),
    )
    return jax.shard_map(
        on_device,
        mesh=mesh,
        in_specs=placed,
        out_specs=(
            P(("region", "cell"), None),
            P(None, ("region", "cell"), None),
            P(("region", "cell"), None),
        ),
        check_vma=False,
    )
```

```python
import functools
import math

import jax
import jax.numpy as jnp
from jax import lax
from jax.experimental import pallas as pl
from jax.experimental.pallas import tpu as pltpu
from jax.sharding import PartitionSpec as P

GAMMA = 5.0 / 3.0
LANES = 128
BF16 = jnp.bfloat16
F32 = jnp.float32

ROWS = 8
TINY = 1e-12
DOT_K = 48
STRIP = 16

VMEM = pl.BlockSpec(memory_space=pltpu.VMEM)
SMEM = pl.BlockSpec(memory_space=pltpu.SMEM)


def row_ids(shape):
    return lax.broadcasted_iota(jnp.int32, shape, 0)


def split3(value):
    first = value.astype(BF16).astype(F32)
    rest = value - first
    second = rest.astype(BF16).astype(F32)
    return first, second, rest - second


def left_parts(value):
    a, b, c = split3(value)
    return jnp.concatenate([a, a, b, b, a, c], axis=0)


def right_parts(value):
    a, b, c = split3(value)
    return jnp.concatenate([a, b, a, b, c, a], axis=0).astype(BF16)


def norm_row(rows):
    return rows[0:1] * rows[0:1] + rows[1:2] * rows[1:2] + rows[2:3] * rows[2:3]


def left_comps(rows):
    ids = row_ids(rows.shape)
    return jnp.where(ids < 3, rows, jnp.where(ids == 3, norm_row(rows), jnp.where(ids == 4, 1.0, 0.0)))


def right_comps(rows):
    ids = row_ids(rows.shape)
    return jnp.where(ids < 3, -2.0 * rows, jnp.where(ids == 3, 1.0, jnp.where(ids == 4, norm_row(rows), 0.0)))


def store_left(left_ref, cell, comps):
    parts = left_parts(comps)
    pad = jnp.zeros((LANES - DOT_K, LANES), F32)
    for at in range(parts.shape[1] // LANES):
        block = jnp.concatenate([parts[:, at * LANES : (at + 1) * LANES], pad], axis=0)
        left_ref[cell, pl.ds(at * LANES, LANES), :] = block.T.astype(BF16)


def prep_kernel(counts, send, edge, pos_in, vel_in, mass_in, smooth_in, own, pay, faces, pos, vel, mass, smooth, sems):
    copies = [
        pltpu.make_async_copy(source, target, sems.at[k])
        for k, (source, target) in enumerate(
            ((pos_in, pos), (vel_in, vel), (mass_in, mass), (smooth_in, smooth))
        )
    ]
    for copy in copies:
        copy.start()
    for copy in copies:
        copy.wait()
    cells = mass.shape[0]
    slots = mass.shape[1]
    peers = pay.shape[0]
    lane = lax.broadcasted_iota(jnp.int32, (1, slots), 1)
    for k in range(cells):
        live = lane < counts[k]
        for d in range(3):
            own[k, d : d + 1, :] = pos[d, k : k + 1, :] - 0.5
            own[k, 5 + d : 6 + d, :] = vel[d, k : k + 1, :]
        own[k, 3:4, :] = smooth[k : k + 1, :]
        own[k, 4:5, :] = jnp.where(live, mass[k : k + 1, :], 0.0)

    def fill(k, carry):
        picked = send[k]
        pay[k] = jnp.where(picked >= 0, own[jnp.maximum(picked, 0)], 0.0)
        return carry

    lax.fori_loop(0, peers, fill, 0)
    for side in range(2):
        faces[side] = own[edge[0, 0, side]]


def list_tiles(icut, jcut, counts, send, pairs, edge, own, rec, low, high, live, tgt, src, wgt, both):
    cells = own.shape[0]
    peers = rec.shape[0]
    for k in range(cells):
        live[k] = counts[k]

    occupied = jnp.sum(jnp.where(rec[:, 4, :] > 0.0, 1.0, 0.0), axis=1, keepdims=True)
    for k in range(peers):
        live[cells + k] = occupied[k, 0].astype(jnp.int32)
    for at, face in ((0, low), (1, high)):
        count = jnp.sum(jnp.where(face[0, 4:5, :] > 0.0, 1.0, 0.0))
        live[cells + peers + at] = count.astype(jnp.int32)

    def push(state, a, b, w, ok):
        n, blocks = state

        @pl.when(ok)
        def _():
            tgt[n] = a
            src[n] = b
            wgt[n] = w

        more = chunks(live[a], icut) * chunks(live[b], jcut)
        return n + ok.astype(jnp.int32), blocks + jnp.where(ok, more, 0)

    state = (jnp.int32(0), jnp.int32(0))
    for a in range(cells):
        for b in range(a + 1, cells):
            mult = jnp.int32(0)
            for row in range(pairs.shape[3]):
                one = pairs[0, 0, 0, row]
                two = pairs[0, 0, 1, row]
                hit = ((one == a) & (two == b)) | ((one == b) & (two == a))
                mult = mult + hit.astype(jnp.int32)
            state = push(state, a, b, mult, mult > 0)
            if not both:
                state = push(state, b, a, mult, mult > 0)
    local = state[1]
    for a in range(cells):
        state = push(state, a, a, jnp.int32(1), counts[a] > 0)

    def remote_tile(k, state):
        picked = send[k]
        return push(
            state, jnp.maximum(picked, 0), cells + k, jnp.int32(1), (picked >= 0) & (live[cells + k] > 0)
        )

    state = lax.fori_loop(0, peers, remote_tile, state)
    state = push(state, edge[0, 0, 0], cells + peers, jnp.int32(1), live[cells + peers] > 0)
    state = push(state, edge[0, 0, 1], cells + peers + 1, jnp.int32(1), live[cells + peers + 1] > 0)
    tgt[state[0]] = 0
    src[state[0]] = 0
    wgt[state[0]] = 0
    return state[0], state[1], local


def chunks(count, size):
    return lax.shift_right_logical(count + (size - 1), jnp.int32(size.bit_length() - 1))


class Blocks:
    def __init__(self, icut, jcut, live, tgt, src, wgt, ring, total):
        self.icut, self.jcut = icut, jcut
        self.live, self.tgt, self.src, self.wgt = live, tgt, src, wgt
        self.ring, self.total = ring, total

    def clear(self, entries):
        for k in range(entries):
            for field in range(5):
                self.ring[5 * k + field] = 0

    def write(self, slot, state):
        n, ii, jj = state
        a, b = self.tgt[n], self.src[n]
        at = 5 * slot
        self.ring[at] = a
        self.ring[at + 1] = b
        self.ring[at + 2] = ii
        self.ring[at + 3] = jj
        self.ring[at + 4] = self.wgt[n]
        jnext = jj + 1
        jwrap = jnext >= chunks(self.live[b], self.jcut)
        inext = jnp.where(jwrap, ii + 1, ii)
        iwrap = inext >= chunks(self.live[a], self.icut)
        return (
            jnp.minimum(jnp.where(iwrap, n + 1, n), self.total),
            jnp.where(iwrap, 0, inext),
            jnp.where(jwrap, 0, jnext),
        )

    def read(self, slot):
        at = 5 * slot
        return (
            self.ring[at],
            self.ring[at + 1],
            pl.multiple_of(self.ring[at + 2] * self.icut, self.icut),
            pl.multiple_of(self.ring[at + 3] * self.jcut, self.jcut),
            self.ring[at + 4].astype(F32),
        )


def density_kernel(
    icut, jcut, group,
    counts, send, pairs, edge, own, rec, low, high, energy,
    rho_out, term_out, pay,
    live, tgt, src, wgt, ring, left, right, mrow, acc, *work,
):
    cells = own.shape[0]
    peers = rec.shape[0]
    slots = own.shape[2]
    dist, parts = work[:group], work[group:]
    tiles, total, _ = list_tiles(
        icut, jcut, counts, send, pairs, edge, own, rec, low, high, live, tgt, src, wgt, False
    )

    def source(rows, at):
        right[at] = right_parts(right_comps(rows))
        mrow[at] = jnp.broadcast_to(rows[4:5], (8, slots))

    def own_cell(k, carry):
        rows = own[k]
        inv = 1.0 / rows[3:4]
        store_left(left, k, left_comps(rows) * (inv * inv))
        source(rows, k)
        acc[k] = jnp.zeros((slots, LANES), F32)
        return carry

    lax.fori_loop(0, cells, own_cell, 0, unroll=True)

    def rec_cell(k, carry):
        source(rec[k], cells + k)
        return carry

    lax.fori_loop(0, peers, rec_cell, 0, unroll=4)
    source(low[0], cells + peers)
    source(high[0], cells + peers + 1)

    blocks = Blocks(icut, jcut, live, tgt, src, wgt, ring, tiles)
    blocks.clear(group)
    for ref in dist:
        ref[...] = jnp.ones_like(ref)
    zero = jnp.int32(0)
    state = (zero, zero, zero)
    for g in range(group):
        state = blocks.write(group + g, state)

    def step(k, state):
        for g in range(group):
            _, b, _, jstart, w = blocks.read(k * group + g)
            weight = mrow[b, :, pl.ds(jstart, jcut)] * w
            weight = jnp.concatenate([weight] * (STRIP // 8), axis=0)
            for row in range(0, icut, STRIP):
                s = jnp.maximum(dist[g][row : row + STRIP, :], TINY)
                q = s * lax.rsqrt(s)
                e = 1.0 - q
                u = jnp.maximum(e, 0.0)
                t = jnp.minimum(0.5 - (s * 3.0) * e, u * u * u) * weight
                part = t[:, :LANES]
                for at in range(1, jcut // LANES):
                    part = part + t[:, at * LANES : (at + 1) * LANES]
                parts[g][row : row + STRIP, :] = part

            state = blocks.write((k + 2) * group + g, state)
            a, b, istart, jstart, _ = blocks.read((k + 1) * group + g)
            dist[g][...] = jnp.dot(
                left[a, pl.ds(istart, icut), :DOT_K],
                right[b, :, pl.ds(jstart, jcut)],
                preferred_element_type=F32,
            )
        for g in range(group):
            a, _, istart, _, _ = blocks.read(k * group + g)
            acc[a, pl.ds(istart, icut), :] += parts[g][...]
        return state

    lax.fori_loop(0, chunks(total, group) + 1, step, state)

    lane = lax.broadcasted_iota(jnp.int32, (1, slots), 1)
    ones = jnp.ones((8, LANES), BF16)
    for k in range(cells):
        one, two, three = split3(acc[k])
        total_row = jnp.zeros((8, slots), F32)
        for part in (three, two, one):
            total_row = total_row + lax.dot_general(
                ones, part.astype(BF16), (((1,), (1,)), ((), ())), preferred_element_type=F32
            )
        inv = 1.0 / own[k, 3:4, :]
        rho = total_row[0:1] * (16.0 / math.pi) * (inv * inv * inv)
        occupied = jnp.where(lane < counts[k], 1.0, 0.0)
        rho_out[k : k + 1, :] = rho * occupied
        term_out[k] = occupied * (GAMMA - 1.0) * energy[k : k + 1, :] / (rho + 1.0 - occupied)

    region = lax.axis_index("region")
    here = lax.axis_index("cell")
    first = region * peers

    def fill(k, carry):
        pay[first + k] = term_out[jnp.maximum(send[k], 0)]
        return carry

    pay[...] = jnp.zeros_like(pay)
    lax.fori_loop(0, peers, fill, 0)

    @pl.when(region > 0)
    def _():
        pay[first - peers + here] = term_out[edge[0, 0, 0]]

    @pl.when(first + peers < pay.shape[0])
    def _():
        pay[first + peers + here] = term_out[edge[0, 0, 1]]


def force_kernel(
    icut, jcut, group,
    counts, send, pairs, edge, own, rec, low, high, term, rterm,
    accel_out, heat_out,
    live, tgt, src, wgt, ring, left, right, weights, scale, bcol, ccol, acc, *work,
):
    cells = own.shape[0]
    peers = rec.shape[0]
    slots = own.shape[2]
    dist, upper, lower = work[:group], work[group : 2 * group], work[2 * group :]
    tiles, total, local = list_tiles(
        icut, jcut, counts, send, pairs, edge, own, rec, low, high, live, tgt, src, wgt, True
    )
    strength = math.sqrt(24.0 / math.pi)

    def source(rows, pressure, at):
        right[at] = right_parts(right_comps(rows))
        h = rows[3:4]
        inv = 1.0 / jnp.where(h > 0.0, h, 1.0)
        b = strength * (inv * inv)
        ids = row_ids((8, slots))
        scale[at] = jnp.concatenate(
            [jnp.broadcast_to(b, (8, slots)), jnp.broadcast_to(b * inv, (8, slots))], axis=0
        )
        m = rows[4:5]
        mp = m * pressure
        xv = rows[0:1] * rows[5:6] + rows[1:2] * rows[6:7] + rows[2:3] * rows[7:8]
        base = jnp.where(ids == 3, 1.0, jnp.where(ids == 4, xv, rows))
        sums = jnp.concatenate([base * m, jnp.where(ids < 4, base, 0.0) * mp], axis=0)
        one, two, three = split3(sums)
        weights[at] = jnp.concatenate([one, two, three], axis=0).astype(BF16)

    def own_cell(k, carry):
        rows = own[k]
        store_left(left, k, left_comps(rows))
        source(rows, term[k], k)
        acc[k] = jnp.zeros((DOT_K, slots), F32)
        pair = jnp.concatenate([scale[k], jnp.zeros((LANES - 16, slots), F32)], axis=0)
        for at in range(slots // LANES):
            cols = pair[:, at * LANES : (at + 1) * LANES].T
            bcol[k, pl.ds(at * LANES, LANES), :] = jnp.broadcast_to(cols[:, 0:1], (LANES, LANES))
            ccol[k, pl.ds(at * LANES, LANES), :] = jnp.broadcast_to(cols[:, 8:9], (LANES, LANES))
        return carry

    lax.fori_loop(0, cells, own_cell, 0, unroll=True)

    def rec_cell(k, carry):
        source(rec[k], rterm[lax.axis_index("region") * peers + k], cells + k)
        return carry

    lax.fori_loop(0, peers, rec_cell, 0, unroll=4)
    region = lax.axis_index("region")
    here = lax.axis_index("cell")
    first = region * peers
    below = jnp.maximum(first - peers, 0) + here
    above = jnp.minimum(first + peers, rterm.shape[0] - peers) + here
    source(low[0], rterm[below], cells + peers)
    source(high[0], rterm[above], cells + peers + 1)

    blocks = Blocks(icut, jcut, live, tgt, src, wgt, ring, tiles)
    blocks.clear(2 * group)
    for ref in work:
        ref[...] = jnp.ones_like(ref)
    zero = jnp.int32(0)
    state = (zero, zero, zero)
    for g in range(group):
        state = blocks.write(2 * group + g, state)

    def step(mutual, k, state):
        adds = []
        for g in range(group):
            a, b, istart, jstart, w = blocks.read(k * group + g)
            wt = weights[b, :, pl.ds(jstart, jcut)]
            spec = (((1,), (1,)), ((), ()))
            part = lax.dot_general(wt, upper[g][...], spec, preferred_element_type=F32)
            part = part + lax.dot_general(wt, lower[g][...], spec, preferred_element_type=F32)
            later = [(a, istart, part * w)]
            if mutual:
                wt = weights[a, :, pl.ds(istart, icut)]
                part = jnp.dot(wt, upper[g][...], preferred_element_type=F32)
                part = part + jnp.dot(wt, lower[g][...], preferred_element_type=F32)
                w = jnp.where(k * group + g < local + 2 * group, w, 0.0)
                later.append((b, jstart, part * w))
            adds += later

            a, b, istart, jstart, _ = blocks.read((k + 1) * group + g)
            bj = jnp.concatenate([scale[b, 0:8, pl.ds(jstart, jcut)]] * (STRIP // 8), axis=0)
            cj = jnp.concatenate([scale[b, 8:16, pl.ds(jstart, jcut)]] * (STRIP // 8), axis=0)
            for row in range(0, icut, STRIP):
                s = jnp.maximum(dist[g][row : row + STRIP, :], TINY)
                r = lax.rsqrt(s)
                d = s * r
                bi = bcol[a, pl.ds(istart + row, STRIP), :]
                ci = ccol[a, pl.ds(istart + row, STRIP), :]
                bi = jnp.concatenate([bi] * (jcut // LANES), axis=1)
                ci = jnp.concatenate([ci] * (jcut // LANES), axis=1)
                t = ci * d
                u = jnp.maximum(bi - t, 0.0)
                v = jnp.minimum(t, u)
                slope = (u + u - v) * v
                t = cj * d
                u = jnp.maximum(bj - t, 0.0)
                v = jnp.minimum(t, u)
                slope = (slope + (u + u - v) * v) * r
                rounded = slope.astype(BF16)
                upper[g][row : row + STRIP, :] = rounded
                lower[g][row : row + STRIP, :] = (slope - rounded.astype(F32)).astype(BF16)

            state = blocks.write((k + 3) * group + g, state)
            a, b, istart, jstart, _ = blocks.read((k + 2) * group + g)
            dist[g][...] = jnp.dot(
                left[a, pl.ds(istart, icut), :DOT_K],
                right[b, :, pl.ds(jstart, jcut)],
                preferred_element_type=F32,
            )
        for cell, start, part in adds:
            acc[cell, :, pl.ds(start, part.shape[1])] += part
        return state

    first = jnp.minimum(chunks(local, group) + 2, chunks(total, group) + 2)
    state = lax.fori_loop(0, first, functools.partial(step, True), state)
    lax.fori_loop(first, chunks(total, group) + 2, functools.partial(step, False), state)

    lane = lax.broadcasted_iota(jnp.int32, (1, slots), 1)
    for k in range(cells):
        occupied = jnp.where(lane < counts[k], 1.0, 0.0)
        sums = acc[k, 0:16, :] + (acc[k, 16:32, :] + acc[k, 32:48, :])
        pressure = term[k]
        x = [own[k, d : d + 1, :] for d in range(3)]
        v = [own[k, 5 + d : 6 + d, :] for d in range(3)]
        both = pressure * sums[3:4] + sums[11:12]
        for d in range(3):
            accel_out[d, k : k + 1, :] = occupied * (
                x[d] * both - pressure * sums[d : d + 1] - sums[8 + d : 9 + d]
            )
        xv = x[0] * v[0] + x[1] * v[1] + x[2] * v[2]
        total_heat = xv * sums[3:4] + sums[4:5]
        for d in range(3):
            total_heat = total_heat - v[d] * sums[d : d + 1] - x[d] * sums[5 + d : 6 + d]
        heat_out[k : k + 1, :] = -occupied * pressure * total_heat


def on_device(positions, velocities, mass, smoothing, energy, counts, send, pairs, edge):
    cells, slots = mass.shape
    peers = send.shape[2]
    table = cells + peers + 2
    tiles = cells * cells + peers + 3
    icut, jcut, group = 128, 512, 2
    entries = 5 * (tiles * (slots // icut) * (slots // jcut) + 6 * group)
    send = send.reshape(peers)
    pairs = jnp.transpose(pairs, (0, 1, 3, 2))
    shape = jax.ShapeDtypeStruct
    params = pltpu.CompilerParams(vmem_limit_bytes=40 * 1024 * 1024)
    own, pay, faces = pl.pallas_call(
        prep_kernel,
        out_shape=[
            shape((cells, ROWS, slots), F32),
            shape((peers, ROWS, slots), F32),
            shape((2, ROWS, slots), F32),
        ],
        in_specs=[SMEM] * 3 + [pl.BlockSpec(memory_space=pl.ANY)] * 4,
        out_specs=[VMEM] * 3,
        scratch_shapes=[
            pltpu.VMEM(positions.shape, F32),
            pltpu.VMEM(velocities.shape, F32),
            pltpu.VMEM(mass.shape, F32),
            pltpu.VMEM(smoothing.shape, F32),
            pltpu.SemaphoreType.DMA((4,)),
        ],
        compiler_params=params,
        name="prep",
    )(counts, send, edge, positions, velocities, mass, smoothing)

    regions = lax.axis_size("region")
    low = lax.ppermute(faces[1:], "region", [(i, i + 1) for i in range(regions - 1)])
    high = lax.ppermute(faces[:1], "region", [(i + 1, i) for i in range(regions - 1)])
    rec = lax.all_to_all(pay, "cell", split_axis=0, concat_axis=0, tiled=True)

    lists = [
        pltpu.SMEM((table,), jnp.int32),
        pltpu.SMEM((tiles,), jnp.int32),
        pltpu.SMEM((tiles,), jnp.int32),
        pltpu.SMEM((tiles,), jnp.int32),
        pltpu.SMEM((entries,), jnp.int32),
    ]
    density, term, pay = pl.pallas_call(
        functools.partial(density_kernel, icut, jcut, group),
        out_shape=[
            shape((cells, slots), F32),
            shape((cells, 1, slots), F32),
            shape((regions * peers, 1, slots), F32),
        ],
        in_specs=[SMEM] * 4 + [VMEM] * 5,
        out_specs=[VMEM] * 3,
        scratch_shapes=lists
        + [
            pltpu.VMEM((cells, slots, LANES), BF16),
            pltpu.VMEM((table, DOT_K, slots), BF16),
            pltpu.VMEM((table, 8, slots), F32),
            pltpu.VMEM((cells, slots, LANES), F32),
        ]
        + [pltpu.VMEM((icut, jcut), F32)] * group
        + [pltpu.VMEM((icut, LANES), F32)] * group,
        compiler_params=params,
        name="density",
    )(counts, send, pairs, edge, own, rec, low, high, energy)

    rterm = lax.all_to_all(pay, ("region", "cell"), split_axis=0, concat_axis=0, tiled=True)

    accel, heat = pl.pallas_call(
        functools.partial(force_kernel, icut, jcut, group),
        out_shape=[shape((3, cells, slots), F32), shape((cells, slots), F32)],
        in_specs=[SMEM] * 4 + [VMEM] * 6,
        out_specs=[VMEM] * 2,
        scratch_shapes=lists
        + [
            pltpu.VMEM((cells, slots, LANES), BF16),
            pltpu.VMEM((table, DOT_K, slots), BF16),
            pltpu.VMEM((table, DOT_K, slots), BF16),
            pltpu.VMEM((table, 16, slots), F32),
            pltpu.VMEM((cells, slots, LANES), F32),
            pltpu.VMEM((cells, slots, LANES), F32),
            pltpu.VMEM((cells, DOT_K, slots), F32),
        ]
        + [pltpu.VMEM((icut, jcut), F32)] * group
        + [pltpu.VMEM((icut, jcut), BF16)] * (2 * group),
        compiler_params=params,
        name="force",
    )(counts, send, pairs, edge, own, rec, low, high, term, rterm)
    return density, accel, heat


def solution(mesh):
    placed = (
        P(None, ("region", "cell"), None),
        P(None, ("region", "cell"), None),
        P(("region", "cell"), None),
        P(("region", "cell"), None),
        P(("region", "cell"), None),
        P(("region", "cell")),
        P("region", "cell", None, None),
        P("region", "cell", None, None),
        P("region", "cell", None),
    )
    return jax.shard_map(
        on_device,
        mesh=mesh,
        in_specs=placed,
        out_specs=(
            P(("region", "cell"), None),
            P(None, ("region", "cell"), None),
            P(("region", "cell"), None),
        ),
        check_vma=False,
    )
```

```python
import functools
import math

import jax
import jax.numpy as jnp
from jax import lax
from jax.experimental import pallas as pl
from jax.experimental.pallas import tpu as pltpu
from jax.sharding import PartitionSpec as P

GAMMA = 5.0 / 3.0
LANES = 128
BF16 = jnp.bfloat16
F32 = jnp.float32

ROWS = 8
TINY = 1e-12
DOT_K = 48
COLS = 64
STRIP = 16
SENT = 5
SENT_LATER = 4

VMEM = pl.BlockSpec(memory_space=pltpu.VMEM)
SMEM = pl.BlockSpec(memory_space=pltpu.SMEM)
HBM = pl.BlockSpec(memory_space=pltpu.HBM)


def row_ids(shape):
    return lax.broadcasted_iota(jnp.int32, shape, 0)


def split3(value):
    first = value.astype(BF16).astype(F32)
    rest = value - first
    second = rest.astype(BF16).astype(F32)
    return first, second, rest - second


def left_parts(value):
    a, b, c = split3(value)
    return jnp.concatenate([a, a, b, b, a, c], axis=0)


def right_parts(value):
    a, b, c = split3(value)
    return jnp.concatenate([a, b, a, b, c, a], axis=0).astype(BF16)


def norm_row(rows):
    return rows[0:1] * rows[0:1] + rows[1:2] * rows[1:2] + rows[2:3] * rows[2:3]


def left_comps(rows):
    ids = row_ids(rows.shape)
    return jnp.where(ids < 3, rows, jnp.where(ids == 3, norm_row(rows), jnp.where(ids == 4, 1.0, 0.0)))


def right_comps(rows):
    ids = row_ids(rows.shape)
    return jnp.where(ids < 3, -2.0 * rows, jnp.where(ids == 3, 1.0, jnp.where(ids == 4, norm_row(rows), 0.0)))


def chunks(count, size):
    return lax.shift_right_logical(count + (size - 1), jnp.int32(size.bit_length() - 1))


class Meta:
    def __init__(self, cells, peers, pairs):
        self.cells, self.peers, self.pairs = cells, peers, pairs
        self.send = cells
        self.pair = cells + peers
        self.edge = self.pair + 2 * pairs
        self.size = self.edge + 2


def prep_kernel(
    lay,
    counts_in, send_in, pairs_in, edge_in, pos_in, vel_in, mass_in, smooth_in,
    own, pay, meta,
    counts, send, pairs, edge, pos, vel, mass, smooth, sems,
):
    inputs = (counts_in, send_in, pairs_in, edge_in, pos_in, vel_in, mass_in, smooth_in)
    buffers = (counts, send, pairs, edge, pos, vel, mass, smooth)
    copies = [
        pltpu.make_async_copy(source, target, sems.at[k])
        for k, (source, target) in enumerate(zip(inputs, buffers))
    ]
    for copy in copies:
        copy.start()
    for copy in copies:
        copy.wait()
    cells = mass.shape[0]
    slots = mass.shape[1]
    for k in range(cells):
        meta[k] = counts[k]
    for k in range(lay.peers):
        meta[lay.send + k] = send[k]
    for k in range(lay.pairs):
        for side in range(2):
            meta[lay.pair + 2 * k + side] = pairs[0, 0, side, k]
    for side in range(2):
        meta[lay.edge + side] = edge[0, 0, side]

    lane = lax.broadcasted_iota(jnp.int32, (1, slots), 1)
    for k in range(cells):
        live = lane < counts[k]
        for d in range(3):
            own[k, d : d + 1, :] = pos[d, k : k + 1, :] - 0.5
            own[k, 5 + d : 6 + d, :] = vel[d, k : k + 1, :]
        own[k, 3:4, :] = smooth[k : k + 1, :]
        own[k, 4:5, :] = jnp.where(live, mass[k : k + 1, :], 0.0)

    def row(cell, r):
        return own[cell, r : r + 1, :]

    fill(lay, pay, meta, SENT, row)


def fill(lay, pay, meta, count, row):
    slots = pay.shape[2] // count
    region = lax.axis_index("region")
    here = lax.axis_index("cell")
    first = region * lay.peers
    pay[...] = jnp.zeros_like(pay)

    def put(at, cell, keep):
        for r in range(count):
            value = row(cell, r)
            if keep is not None:
                value = jnp.where(keep, value, 0.0)
            pay[at, :, r * slots : (r + 1) * slots] = value

    def peer(k, carry):
        picked = meta[lay.send + k]
        put(first + k, jnp.maximum(picked, 0), picked >= 0)
        return carry

    lax.fori_loop(0, lay.peers, peer, 0)

    @pl.when(region > 0)
    def _():
        put(first - lay.peers + here, meta[lay.edge], None)

    @pl.when(first + lay.peers < pay.shape[0])
    def _():
        put(first + lay.peers + here, meta[lay.edge + 1], None)


def arrivals(lay, got):
    region = lax.axis_index("region")
    here = lax.axis_index("cell")
    last = got.shape[0] // lay.peers - 1
    return (
        region * lay.peers,
        jnp.maximum(region - 1, 0) * lay.peers + here,
        jnp.minimum(region + 1, last) * lay.peers + here,
    )


class Tiles:
    def __init__(self, icut, jcut, tgt, src, wgt):
        self.icut, self.jcut = icut, jcut
        self.tgt, self.src, self.wgt = tgt, src, wgt
        self.count = self.blocks = jnp.int32(0)

    def push(self, a, b, w, ok, alive, blive):
        n = self.count
        self.tgt[n] = a
        self.src[n] = b
        self.wgt[n] = w
        more = chunks(alive, self.icut) * chunks(blive, self.jcut)
        self.count = n + ok.astype(jnp.int32)
        self.blocks = self.blocks + jnp.where(ok, more, 0)

    def close(self):
        self.push(0, 0, 0, jnp.bool_(False), 0, 0)


def local_tiles(tiles, lay, meta, both):
    cells = lay.cells

    def key(row):
        one = meta[lay.pair + 2 * row]
        two = meta[lay.pair + 2 * row + 1]
        return jnp.minimum(one, two) * cells + jnp.maximum(one, two)

    keys = [key(row) for row in range(lay.pairs)]
    for a in range(cells):
        for b in range(a + 1, cells):
            mult = jnp.int32(0)
            for one in keys:
                mult = mult + (one == a * cells + b).astype(jnp.int32)
            tiles.push(a, b, mult, mult > 0, meta[a], meta[b])
            if not both:
                tiles.push(b, a, mult, mult > 0, meta[b], meta[a])
    local = tiles.blocks
    for a in range(cells):
        tiles.push(a, a, jnp.int32(1), meta[a] > 0, meta[a], meta[a])
    tiles.close()
    return local


def remote_tiles(tiles, lay, meta, live):
    for k in range(lay.peers):
        picked = meta[lay.send + k]
        a = jnp.maximum(picked, 0)
        tiles.push(a, k, jnp.int32(1), (picked >= 0) & (live[k] > 0), meta[a], live[k])
    for side in range(2):
        a = meta[lay.edge + side]
        b = lay.peers + side
        tiles.push(a, b, jnp.int32(1), live[b] > 0, meta[a], live[b])
    tiles.close()


class Blocks:
    def __init__(self, tiles, alive, blive, ring):
        self.icut, self.jcut = tiles.icut, tiles.jcut
        self.alive, self.blive = alive, blive
        self.tgt, self.src, self.wgt = tiles.tgt, tiles.src, tiles.wgt
        self.ring, self.total = ring, tiles.count

    def clear(self, entries):
        for k in range(entries):
            for field in range(5):
                self.ring[5 * k + field] = 0

    def write(self, slot, state):
        n, ii, jj = state
        a, b = self.tgt[n], self.src[n]
        at = 5 * slot
        self.ring[at] = a
        self.ring[at + 1] = b
        self.ring[at + 2] = ii
        self.ring[at + 3] = jj
        self.ring[at + 4] = self.wgt[n]
        jnext = jj + 1
        jwrap = jnext >= chunks(self.blive[b], self.jcut)
        inext = jnp.where(jwrap, ii + 1, ii)
        iwrap = inext >= chunks(self.alive[a], self.icut)
        return (
            jnp.minimum(jnp.where(iwrap, n + 1, n), self.total),
            jnp.where(iwrap, 0, inext),
            jnp.where(jwrap, 0, jnext),
        )

    def read(self, slot):
        at = 5 * slot
        return (
            self.ring[at],
            self.ring[at + 1],
            pl.multiple_of(self.ring[at + 2] * self.icut, self.icut),
            pl.multiple_of(self.ring[at + 3] * self.jcut, self.jcut),
            self.ring[at + 4].astype(F32),
        )

    def distances(self, slot, left, right, out):
        a, b, istart, jstart, _ = self.read(slot)
        out[...] = jnp.dot(
            left[a, pl.ds(istart, self.icut), :DOT_K],
            right[b, :, pl.ds(jstart, self.jcut)],
            preferred_element_type=F32,
        )


def density_loop(group, blocks, total, left, right, mrow, acc, work):
    icut, jcut = blocks.icut, blocks.jcut
    dist, parts = work[:group], work[group:]
    zero = jnp.int32(0)
    state = (zero, zero, zero)
    for g in range(2 * group):
        state = blocks.write(g, state)
    for g in range(group):
        blocks.distances(g, left, right, dist[g])

    def step(k, state):
        for g in range(group):
            _, b, _, jstart, w = blocks.read(k * group + g)
            weight = mrow[b, :, pl.ds(jstart, jcut)] * w
            weight = jnp.concatenate([weight] * (STRIP // 8), axis=0)
            for row in range(0, icut, STRIP):
                s = jnp.maximum(dist[g][row : row + STRIP, :], TINY)
                q = s * lax.rsqrt(s)
                e = 1.0 - q
                u = jnp.maximum(e, 0.0)
                t = jnp.minimum(0.5 - (s * 3.0) * e, u * u * u) * weight
                part = t[:, :LANES]
                for at in range(1, jcut // LANES):
                    part = part + t[:, at * LANES : (at + 1) * LANES]
                parts[g][row : row + STRIP, :] = part

            state = blocks.write((k + 2) * group + g, state)
            blocks.distances((k + 1) * group + g, left, right, dist[g])
        for g in range(group):
            a, _, istart, _, _ = blocks.read(k * group + g)
            acc[a, pl.ds(istart, icut), :] += parts[g][...]
        return state

    lax.fori_loop(0, chunks(total, group), step, state)


def density_source(rows, right, mrow, at):
    right[at] = right_parts(right_comps(rows))
    mrow[at] = jnp.broadcast_to(rows[4:5], mrow.shape[1:])


def density_local_kernel(
    icut, jcut, group, lay, meta, own, acc, left, right, tgt, src, wgt, ring, mrow, *work
):
    slots = own.shape[2]
    for k in range(lay.cells):
        rows = own[k]
        inv = 1.0 / rows[3:4]
        parts = left_parts(left_comps(rows) * (inv * inv))
        pad = jnp.zeros((COLS - DOT_K, LANES), F32)
        for at in range(slots // LANES):
            block = jnp.concatenate([parts[:, at * LANES : (at + 1) * LANES], pad], axis=0)
            left[k, pl.ds(at * LANES, LANES), :] = block.T.astype(BF16)
        density_source(rows, right, mrow, k)
        acc[k] = jnp.zeros((slots, LANES), F32)
    tiles = Tiles(icut, jcut, tgt, src, wgt)
    local_tiles(tiles, lay, meta, False)
    blocks = Blocks(tiles, meta, meta, ring)
    density_loop(group, blocks, tiles.blocks, left, right, mrow, acc, work)


def density_remote_kernel(
    icut, jcut, group, lay,
    meta, own, rec, acc_in, left, energy_in,
    rho_out, term_out, pay, far, right, live,
    tgt, src, wgt, ring, mrow, acc, energy, sem, *work,
):
    cells, peers = lay.cells, lay.peers
    slots = own.shape[2]
    copy = pltpu.make_async_copy(energy_in, energy, sem)
    copy.start()
    first, below, above = arrivals(lay, rec)
    ids = row_ids((8, slots))

    def receive(at, k):
        rows = jnp.zeros((8, slots), F32)
        for r in range(SENT):
            rows = jnp.where(ids == r, rec[at, :, r * slots : (r + 1) * slots], rows)
        far[k] = rows
        density_source(rows, right, mrow, k)

    def rec_cell(k, carry):
        receive(first + k, k)
        return carry

    lax.fori_loop(0, peers, rec_cell, 0, unroll=4)
    receive(below, peers)
    receive(above, peers + 1)
    occupied = jnp.sum(jnp.where(far[:, 4, :] > 0.0, 1.0, 0.0), axis=1, keepdims=True)
    for k in range(peers + 2):
        live[k] = occupied[k, 0].astype(jnp.int32)
    acc[...] = acc_in[...]
    tiles = Tiles(icut, jcut, tgt, src, wgt)
    remote_tiles(tiles, lay, meta, live)
    blocks = Blocks(tiles, meta, live, ring)
    density_loop(group, blocks, tiles.blocks, left, right, mrow, acc, work)

    copy.wait()
    lane = lax.broadcasted_iota(jnp.int32, (1, slots), 1)
    ones = jnp.ones((8, LANES), BF16)
    for k in range(cells):
        one, two, three = split3(acc[k])
        total_row = jnp.zeros((8, slots), F32)
        for part in (three, two, one):
            total_row = total_row + lax.dot_general(
                ones, part.astype(BF16), (((1,), (1,)), ((), ())), preferred_element_type=F32
            )
        inv = 1.0 / own[k, 3:4, :]
        rho = total_row[0:1] * (16.0 / math.pi) * (inv * inv * inv)
        occupied = jnp.where(lane < meta[k], 1.0, 0.0)
        rho_out[k : k + 1, :] = rho * occupied
        term_out[k] = occupied * (GAMMA - 1.0) * energy[k : k + 1, :] / (rho + 1.0 - occupied)

    def row(cell, r):
        return term_out[cell] if r == 0 else own[cell, 4 + r : 5 + r, :]

    fill(lay, pay, meta, SENT_LATER, row)


def force_source(rows, pressure, weights, scale, at):
    slots = rows.shape[1]
    h = rows[3:4]
    inv = 1.0 / jnp.where(h > 0.0, h, 1.0)
    b = math.sqrt(24.0 / math.pi) * (inv * inv)
    scales = jnp.concatenate(
        [jnp.broadcast_to(b, (8, slots)), jnp.broadcast_to(b * inv, (8, slots))], axis=0
    )
    scale[at] = scales
    m = rows[4:5]
    mp = m * pressure
    xv = rows[0:1] * rows[5:6] + rows[1:2] * rows[6:7] + rows[2:3] * rows[7:8]
    ids = row_ids((8, slots))
    base = jnp.where(ids == 3, 1.0, jnp.where(ids == 4, xv, rows))
    sums = jnp.concatenate([base * m, jnp.where(ids < 4, base, 0.0) * mp], axis=0)
    one, two, three = split3(sums)
    weights[at] = jnp.concatenate([one, two, three], axis=0).astype(BF16)
    return scales


def force_loop(group, blocks, total, local, left, right, own_weights, weights, scale, bcol, ccol, acc, work):
    icut, jcut = blocks.icut, blocks.jcut
    dist, upper, lower = work[:group], work[group : 2 * group], work[2 * group :]
    blocks.clear(group)
    for ref in (*upper, *lower):
        ref[...] = jnp.zeros_like(ref)
    zero = jnp.int32(0)
    state = (zero, zero, zero)
    for g in range(2 * group):
        state = blocks.write(group + g, state)
    for g in range(group):
        blocks.distances(group + g, left, right, dist[g])

    def sums_of(mutual, k, g):
        a, b, istart, jstart, w = blocks.read(k * group + g)
        wt = weights[b, :, pl.ds(jstart, jcut)]
        spec = (((1,), (1,)), ((), ()))
        part = lax.dot_general(wt, upper[g][...], spec, preferred_element_type=F32)
        part = part + lax.dot_general(wt, lower[g][...], spec, preferred_element_type=F32)
        adds = [(a, istart, part * w)]
        if mutual:
            wt = own_weights[a, :, pl.ds(istart, icut)]
            part = jnp.dot(wt, upper[g][...], preferred_element_type=F32)
            part = part + jnp.dot(wt, lower[g][...], preferred_element_type=F32)
            w = jnp.where(k * group + g < local + group, w, 0.0)
            adds.append((b, jstart, part * w))
        return adds

    def store(adds):
        for cell, start, part in adds:
            acc[cell, :, pl.ds(start, part.shape[1])] += part

    def step(mutual, k, state):
        adds = []
        for g in range(group):
            adds += sums_of(mutual, k, g)

            a, b, istart, jstart, _ = blocks.read((k + 1) * group + g)
            bj = jnp.concatenate([scale[b, 0:8, pl.ds(jstart, jcut)]] * (STRIP // 8), axis=0)
            cj = jnp.concatenate([scale[b, 8:16, pl.ds(jstart, jcut)]] * (STRIP // 8), axis=0)
            for row in range(0, icut, STRIP):
                s = jnp.maximum(dist[g][row : row + STRIP, :], TINY)
                r = lax.rsqrt(s)
                d = s * r
                bi = bcol[a, pl.ds(istart + row, STRIP), :]
                ci = ccol[a, pl.ds(istart + row, STRIP), :]
                bi = jnp.concatenate([bi] * (jcut // LANES), axis=1)
                ci = jnp.concatenate([ci] * (jcut // LANES), axis=1)
                t = ci * d
                u = jnp.maximum(bi - t, 0.0)
                v = jnp.minimum(t, u)
                slope = (u + u - v) * v
                t = cj * d
                u = jnp.maximum(bj - t, 0.0)
                v = jnp.minimum(t, u)
                slope = (slope + (u + u - v) * v) * r
                rounded = slope.astype(BF16)
                upper[g][row : row + STRIP, :] = rounded
                lower[g][row : row + STRIP, :] = (slope - rounded.astype(F32)).astype(BF16)

            state = blocks.write((k + 3) * group + g, state)
            blocks.distances((k + 2) * group + g, left, right, dist[g])
        store(adds)
        return state

    steps = chunks(total, group)
    first = 0
    if local is not None:
        first = jnp.minimum(chunks(local, group) + 1, steps)
        state = lax.fori_loop(0, first, functools.partial(step, True), state)
    lax.fori_loop(first, steps, functools.partial(step, False), state)
    adds = []
    for g in range(group):
        adds += sums_of(local is not None, steps, g)
    store(adds)


def force_local_kernel(
    icut, jcut, group, lay,
    meta, own, right, term,
    acc, left, bcol, ccol,
    tgt, src, wgt, ring, weights, scale, *work,
):
    slots = own.shape[2]
    for k in range(lay.cells):
        rows = own[k]
        scales = force_source(rows, term[k], weights, scale, k)
        parts = left_parts(left_comps(rows))
        acc[k] = jnp.zeros((DOT_K, slots), F32)
        block = jnp.concatenate([parts, scales], axis=0)
        for at in range(slots // LANES):
            cols = block[:, at * LANES : (at + 1) * LANES].T
            here = pl.ds(at * LANES, LANES)
            left[k, here, :] = cols.astype(BF16)
            bcol[k, here, :] = jnp.broadcast_to(cols[:, DOT_K : DOT_K + 1], (LANES, LANES))
            ccol[k, here, :] = jnp.broadcast_to(cols[:, DOT_K + 8 : DOT_K + 9], (LANES, LANES))
    tiles = Tiles(icut, jcut, tgt, src, wgt)
    local = local_tiles(tiles, lay, meta, True)
    blocks = Blocks(tiles, meta, meta, ring)
    force_loop(
        group, blocks, tiles.blocks, local, left, right, weights, weights, scale, bcol, ccol, acc, work
    )


def force_remote_kernel(
    icut, jcut, group, lay,
    meta, live, own, far, right, term, rterm, acc_in, left, bcol, ccol,
    accel_out, heat_out,
    tgt, src, wgt, ring, weights, scale, acc, *work,
):
    cells, peers = lay.cells, lay.peers
    slots = own.shape[2]
    first, below, above = arrivals(lay, rterm)
    ids = row_ids((8, slots))

    def receive(at, k):
        rows = far[k]
        for d in range(3):
            rows = jnp.where(ids == 5 + d, rterm[at, :, (1 + d) * slots : (2 + d) * slots], rows)
        force_source(rows, rterm[at, :, :slots], weights, scale, k)

    def rec_cell(k, carry):
        receive(first + k, k)
        return carry

    lax.fori_loop(0, peers, rec_cell, 0, unroll=4)
    receive(below, peers)
    receive(above, peers + 1)
    acc[...] = acc_in[...]
    tiles = Tiles(icut, jcut, tgt, src, wgt)
    remote_tiles(tiles, lay, meta, live)
    blocks = Blocks(tiles, meta, live, ring)
    force_loop(
        group, blocks, tiles.blocks, None, left, right, None, weights, scale, bcol, ccol, acc, work
    )

    lane = lax.broadcasted_iota(jnp.int32, (1, slots), 1)
    for k in range(cells):
        occupied = jnp.where(lane < meta[k], 1.0, 0.0)
        sums = acc[k, 0:16, :] + (acc[k, 16:32, :] + acc[k, 32:48, :])
        pressure = term[k]
        x = [own[k, d : d + 1, :] for d in range(3)]
        v = [own[k, 5 + d : 6 + d, :] for d in range(3)]
        both = pressure * sums[3:4] + sums[11:12]
        for d in range(3):
            accel_out[d, k : k + 1, :] = occupied * (
                x[d] * both - pressure * sums[d : d + 1] - sums[8 + d : 9 + d]
            )
        xv = x[0] * v[0] + x[1] * v[1] + x[2] * v[2]
        total_heat = xv * sums[3:4] + sums[4:5]
        for d in range(3):
            total_heat = total_heat - v[d] * sums[d : d + 1] - x[d] * sums[5 + d : 6 + d]
        heat_out[k : k + 1, :] = -occupied * pressure * total_heat


def on_device(positions, velocities, mass, smoothing, energy, counts, send, pairs, edge):
    cells, slots = mass.shape
    peers = send.shape[2]
    regions = lax.axis_size("region")
    lay = Meta(cells, peers, pairs.shape[2])
    others = peers + 2
    most = max(cells * cells, others) + 1
    icut, jcut, group = 128, 256, 4
    ring = 5 * (most * (slots // icut) * (slots // jcut) + 6 * group)
    shape = jax.ShapeDtypeStruct
    params = pltpu.CompilerParams(vmem_limit_bytes=20 * 1024 * 1024)
    send = send.reshape(peers)
    pairs = jnp.transpose(pairs, (0, 1, 3, 2))
    integers = (counts, send, pairs, edge)
    floats = (positions, velocities, mass, smoothing)
    integers, floats, energy = jax.tree.map(
        lambda x: pltpu.with_memory_space_constraint(x, pltpu.HBM), (integers, floats, energy)
    )
    lists = [pltpu.SMEM((most,), jnp.int32)] * 3 + [pltpu.SMEM((ring,), jnp.int32)]
    density_work = [pltpu.VMEM((icut, jcut), F32)] * group + [pltpu.VMEM((icut, LANES), F32)] * group
    force_work = [pltpu.VMEM((icut, jcut), F32)] * group + [pltpu.VMEM((icut, jcut), BF16)] * (2 * group)
    wide = shape((cells, slots, LANES), F32)
    left_shape = shape((cells, slots, COLS), BF16)
    weight_shape = lambda count: pltpu.VMEM((count, DOT_K, slots), BF16)

    own, pay, meta = pl.pallas_call(
        functools.partial(prep_kernel, lay),
        out_shape=[
            shape((cells, ROWS, slots), F32),
            shape((regions * peers, 1, SENT * slots), F32),
            shape((lay.size,), jnp.int32),
        ],
        in_specs=[HBM] * 8,
        out_specs=[VMEM] * 2 + [SMEM],
        scratch_shapes=[pltpu.SMEM(x.shape, jnp.int32) for x in integers]
        + [pltpu.VMEM(x.shape, F32) for x in floats]
        + [pltpu.SemaphoreType.DMA((8,))],
        compiler_params=params,
        name="prep",
    )(*integers, *floats)

    rec = lax.all_to_all(pay, ("region", "cell"), split_axis=0, concat_axis=0, tiled=True)

    acc, left, right = pl.pallas_call(
        functools.partial(density_local_kernel, icut, jcut, group, lay),
        out_shape=[wide, left_shape, shape((cells, DOT_K, slots), BF16)],
        in_specs=[SMEM, VMEM],
        out_specs=[VMEM] * 3,
        scratch_shapes=lists + [pltpu.VMEM((cells, 8, slots), F32)] + density_work,
        compiler_params=params,
        name="density_local",
    )(meta, own)

    density, term, pay, far, far_right, live = pl.pallas_call(
        functools.partial(density_remote_kernel, icut, jcut, group, lay),
        out_shape=[
            shape((cells, slots), F32),
            shape((cells, 1, slots), F32),
            shape((regions * peers, 1, SENT_LATER * slots), F32),
            shape((others, ROWS, slots), F32),
            shape((others, DOT_K, slots), BF16),
            shape((others,), jnp.int32),
        ],
        in_specs=[SMEM] + [VMEM] * 4 + [HBM],
        out_specs=[VMEM] * 5 + [SMEM],
        scratch_shapes=lists
        + [
            pltpu.VMEM((others, 8, slots), F32),
            pltpu.VMEM((cells, slots, LANES), F32),
            pltpu.VMEM(energy.shape, F32),
            pltpu.SemaphoreType.DMA,
        ]
        + density_work,
        compiler_params=params,
        name="density_remote",
    )(meta, own, rec, acc, left, energy)

    rterm = lax.all_to_all(pay, ("region", "cell"), split_axis=0, concat_axis=0, tiled=True)

    acc, left, bcol, ccol = pl.pallas_call(
        functools.partial(force_local_kernel, icut, jcut, group, lay),
        out_shape=[shape((cells, DOT_K, slots), F32), left_shape, wide, wide],
        in_specs=[SMEM] + [VMEM] * 3,
        out_specs=[VMEM] * 4,
        scratch_shapes=lists + [weight_shape(cells), pltpu.VMEM((cells, 16, slots), F32)] + force_work,
        compiler_params=params,
        name="force_local",
    )(meta, own, right, term)

    accel, heat = pl.pallas_call(
        functools.partial(force_remote_kernel, icut, jcut, group, lay),
        out_shape=[shape((3, cells, slots), F32), shape((cells, slots), F32)],
        in_specs=[SMEM] * 2 + [VMEM] * 9,
        out_specs=[VMEM] * 2,
        scratch_shapes=lists
        + [
            weight_shape(others),
            pltpu.VMEM((others, 16, slots), F32),
            pltpu.VMEM((cells, DOT_K, slots), F32),
        ]
        + force_work,
        compiler_params=params,
        name="force_remote",
    )(meta, live, own, far, far_right, term, rterm, acc, left, bcol, ccol)
    return density, accel, heat


def solution(mesh):
    placed = (
        P(None, ("region", "cell"), None),
        P(None, ("region", "cell"), None),
        P(("region", "cell"), None),
        P(("region", "cell"), None),
        P(("region", "cell"), None),
        P(("region", "cell")),
        P("region", "cell", None, None),
        P("region", "cell", None, None),
        P("region", "cell", None),
    )
    return jax.shard_map(
        on_device,
        mesh=mesh,
        in_specs=placed,
        out_specs=(
            P(("region", "cell"), None),
            P(None, ("region", "cell"), None),
            P(("region", "cell"), None),
        ),
        check_vma=False,
    )
```

```python
import functools
import math

import jax
import jax.numpy as jnp
from jax import lax
from jax.experimental import pallas as pl
from jax.experimental.pallas import tpu as pltpu
from jax.sharding import PartitionSpec as P

GAMMA = 5.0 / 3.0
LANES = 128
BF16 = jnp.bfloat16
F32 = jnp.float32

ROWS = 8
TINY = 1e-12
DOT_K = 48
COLS = 64
STRIP = 16
SENT = 4
SENT_LATER = 5

VMEM = pl.BlockSpec(memory_space=pltpu.VMEM)
SMEM = pl.BlockSpec(memory_space=pltpu.SMEM)
HBM = pl.BlockSpec(memory_space=pltpu.HBM)


def row_ids(shape):
    return lax.broadcasted_iota(jnp.int32, shape, 0)


def split3(value):
    first = value.astype(BF16).astype(F32)
    rest = value - first
    second = rest.astype(BF16).astype(F32)
    return first, second, rest - second


def left_parts(value):
    a, b, c = split3(value)
    return jnp.concatenate([a, a, b, b, a, c], axis=0)


def right_parts(value):
    a, b, c = split3(value)
    return jnp.concatenate([a, b, a, b, c, a], axis=0).astype(BF16)


def norm_row(rows):
    return rows[0:1] * rows[0:1] + rows[1:2] * rows[1:2] + rows[2:3] * rows[2:3]


def left_comps(rows):
    ids = row_ids(rows.shape)
    return jnp.where(ids < 3, rows, jnp.where(ids == 3, norm_row(rows), jnp.where(ids == 4, 1.0, 0.0)))


def right_comps(rows):
    ids = row_ids(rows.shape)
    return jnp.where(ids < 3, -2.0 * rows, jnp.where(ids == 3, 1.0, jnp.where(ids == 4, norm_row(rows), 0.0)))


def chunks(count, size):
    return lax.shift_right_logical(count + (size - 1), jnp.int32(size.bit_length() - 1))


class Meta:
    def __init__(self, cells, peers, pairs):
        self.cells, self.peers, self.pairs = cells, peers, pairs
        self.send = cells
        self.pair = cells + peers
        self.edge = self.pair + 2 * pairs
        self.size = self.edge + 2


def prep_kernel(
    lay,
    counts_in, send_in, pairs_in, edge_in, pos_in, vel_in, mass_in, smooth_in,
    own, pay, meta,
    counts, send, pairs, edge, pos, vel, mass, smooth, sems,
):
    inputs = (counts_in, send_in, pairs_in, edge_in, pos_in, vel_in, mass_in, smooth_in)
    buffers = (counts, send, pairs, edge, pos, vel, mass, smooth)
    copies = [
        pltpu.make_async_copy(source, target, sems.at[k])
        for k, (source, target) in enumerate(zip(inputs, buffers))
    ]
    for copy in copies:
        copy.start()
    for copy in copies:
        copy.wait()
    cells = mass.shape[0]
    slots = mass.shape[1]
    for k in range(cells):
        meta[k] = counts[k]
    for k in range(lay.peers):
        meta[lay.send + k] = send[k]
    for k in range(lay.pairs):
        for side in range(2):
            meta[lay.pair + 2 * k + side] = pairs[0, 0, side, k]
    for side in range(2):
        meta[lay.edge + side] = edge[0, 0, side]

    lane = lax.broadcasted_iota(jnp.int32, (1, slots), 1)
    for k in range(cells):
        live = lane < counts[k]
        for d in range(3):
            own[k, d : d + 1, :] = pos[d, k : k + 1, :] - 0.5
            own[k, 5 + d : 6 + d, :] = vel[d, k : k + 1, :]
        own[k, 3:4, :] = jnp.where(live, mass[k : k + 1, :], 0.0)
        own[k, 4:5, :] = smooth[k : k + 1, :]

    def row(cell, r):
        return own[cell, r : r + 1, :]

    fill(lay, pay, meta, SENT, row)


def fill(lay, pay, meta, count, row):
    slots = pay.shape[2] // count
    region = lax.axis_index("region")
    here = lax.axis_index("cell")
    first = region * lay.peers
    pay[...] = jnp.zeros_like(pay)

    def put(at, cell, keep):
        for r in range(count):
            value = row(cell, r)
            if keep is not None:
                value = jnp.where(keep, value, 0.0)
            pay[at, :, r * slots : (r + 1) * slots] = value

    def peer(k, carry):
        picked = meta[lay.send + k]
        put(first + k, jnp.maximum(picked, 0), picked >= 0)
        return carry

    lax.fori_loop(0, lay.peers, peer, 0)

    @pl.when(region > 0)
    def _():
        put(first - lay.peers + here, meta[lay.edge], None)

    @pl.when(first + lay.peers < pay.shape[0])
    def _():
        put(first + lay.peers + here, meta[lay.edge + 1], None)


def arrivals(lay, got):
    region = lax.axis_index("region")
    here = lax.axis_index("cell")
    last = got.shape[0] // lay.peers - 1
    return (
        region * lay.peers,
        jnp.maximum(region - 1, 0) * lay.peers + here,
        jnp.minimum(region + 1, last) * lay.peers + here,
    )


class Tiles:
    FIELDS = 7

    def __init__(self, icut, jcut, table):
        self.icut, self.jcut, self.table = icut, jcut, table
        self.count = self.blocks = jnp.int32(0)

    def push(self, a, b, w, ok, i, ni, j, nj):
        at = self.FIELDS * self.count
        for field, value in enumerate((a, b, w, i, ni, j, nj)):
            self.table[at + field] = value
        self.count = self.count + ok.astype(jnp.int32)
        self.blocks = self.blocks + jnp.where(ok, ni * nj, 0)

    def whole(self, a, b, w, ok, alive, blive):
        self.push(a, b, w, ok, 0, chunks(alive, self.icut), 0, chunks(blive, self.jcut))

    def close(self):
        self.push(0, 0, 0, jnp.bool_(False), 0, 1, 0, 1)


def local_tiles(tiles, lay, meta, both):
    cells = lay.cells
    one = jnp.int32(1)

    def key(row):
        first = meta[lay.pair + 2 * row]
        second = meta[lay.pair + 2 * row + 1]
        return jnp.minimum(first, second) * cells + jnp.maximum(first, second)

    keys = [key(row) for row in range(lay.pairs)]
    for a in range(cells):
        for b in range(a + 1, cells):
            mult = jnp.int32(0)
            for pair in keys:
                mult = mult + (pair == a * cells + b).astype(jnp.int32)
            tiles.whole(a, b, mult, mult > 0, meta[a], meta[b])
            if not both:
                tiles.whole(b, a, mult, mult > 0, meta[b], meta[a])
    if not both:
        for a in range(cells):
            tiles.whole(a, a, one, meta[a] > 0, meta[a], meta[a])
        tiles.close()
        return None
    span = tiles.jcut // tiles.icut
    for a in range(cells):
        tiles.push(a, a, one, meta[a] > tiles.jcut, 0, span, 1, chunks(meta[a], tiles.jcut) - 1)
    mutual = tiles.blocks
    for a in range(cells):
        rows = chunks(meta[a], tiles.icut)
        tiles.push(a, a, one, meta[a] > 0, 0, jnp.minimum(rows, span), 0, 1)
        tiles.push(a, a, one, meta[a] > tiles.jcut, span, rows - span, 1, 1)
    tiles.close()
    return mutual


def remote_tiles(tiles, lay, meta, live):
    one = jnp.int32(1)
    for k in range(lay.peers):
        picked = meta[lay.send + k]
        a = jnp.maximum(picked, 0)
        tiles.whole(a, k, one, (picked >= 0) & (live[k] > 0), meta[a], live[k])
    for side in range(2):
        a = meta[lay.edge + side]
        b = lay.peers + side
        tiles.whole(a, b, one, live[b] > 0, meta[a], live[b])
    tiles.close()


class Blocks:
    FIELDS = 5

    def __init__(self, tiles, ring):
        self.icut, self.jcut = tiles.icut, tiles.jcut
        self.table, self.last = tiles.table, tiles.count
        self.ring, self.total = ring, tiles.blocks

    def clear(self, entries):
        for k in range(entries * self.FIELDS):
            self.ring[k] = 0

    def write(self, slot, state):
        n, ii, jj = state
        a, b, w, i, ni, j, nj = (self.table[Tiles.FIELDS * n + k] for k in range(Tiles.FIELDS))
        for field, value in enumerate((a, b, (i + ii) * self.icut, (j + jj) * self.jcut, w)):
            self.ring[self.FIELDS * slot + field] = value
        jwrap = jj + 1 >= nj
        inext = jnp.where(jwrap, ii + 1, ii)
        iwrap = inext >= ni
        return (
            jnp.minimum(jnp.where(iwrap, n + 1, n), self.last),
            jnp.where(iwrap, 0, inext),
            jnp.where(jwrap, 0, jj + 1),
        )

    def read(self, slot):
        a, b, istart, jstart, w = (self.ring[self.FIELDS * slot + k] for k in range(self.FIELDS))
        return (
            a,
            b,
            pl.multiple_of(istart, self.icut),
            pl.multiple_of(jstart, self.jcut),
            w.astype(F32),
        )

    def distances(self, slot, left, right, out):
        a, b, istart, jstart, _ = self.read(slot)
        out[...] = jnp.dot(
            left[a, pl.ds(istart, self.icut), :DOT_K],
            right[b, :, pl.ds(jstart, self.jcut)],
            preferred_element_type=F32,
        )


def density_loop(group, blocks, total, left, right, mrow, acc, work):
    icut, jcut = blocks.icut, blocks.jcut
    dist, parts = work[:group], work[group:]
    zero = jnp.int32(0)
    state = (zero, zero, zero)
    for g in range(2 * group):
        state = blocks.write(g, state)
    for g in range(group):
        blocks.distances(g, left, right, dist[g])

    def step(k, state):
        for g in range(group):
            _, b, _, jstart, w = blocks.read(k * group + g)
            weight = mrow[b, :, pl.ds(jstart, jcut)] * w
            weight = jnp.concatenate([weight] * (STRIP // 8), axis=0)
            for row in range(0, icut, STRIP):
                s = jnp.maximum(dist[g][row : row + STRIP, :], TINY)
                q = s * lax.rsqrt(s)
                e = 1.0 - q
                u = jnp.maximum(e, 0.0)
                t = jnp.minimum(0.5 - (s * 3.0) * e, u * u * u) * weight
                part = t[:, :LANES]
                for at in range(1, jcut // LANES):
                    part = part + t[:, at * LANES : (at + 1) * LANES]
                parts[g][row : row + STRIP, :] = part

            state = blocks.write((k + 2) * group + g, state)
            blocks.distances((k + 1) * group + g, left, right, dist[g])
        for g in range(group):
            a, _, istart, _, _ = blocks.read(k * group + g)
            acc[a, pl.ds(istart, icut), :] += parts[g][...]
        return state

    lax.fori_loop(0, chunks(total, group), step, state)


def density_source(rows, right, mrow, at):
    right[at] = right_parts(right_comps(rows))
    mrow[at] = jnp.broadcast_to(rows[3:4], mrow.shape[1:])


def density_local_kernel(
    icut, jcut, group, lay, meta, own, acc, left, table, ring, right, mrow, *work
):
    slots = own.shape[2]
    for k in range(lay.cells):
        rows = own[k]
        inv = 1.0 / rows[4:5]
        parts = left_parts(left_comps(rows) * (inv * inv))
        pad = jnp.zeros((COLS - DOT_K, LANES), F32)
        for at in range(slots // LANES):
            block = jnp.concatenate([parts[:, at * LANES : (at + 1) * LANES], pad], axis=0)
            left[k, pl.ds(at * LANES, LANES), :] = block.T.astype(BF16)
        density_source(rows, right, mrow, k)
        acc[k] = jnp.zeros((slots, LANES), F32)
    tiles = Tiles(icut, jcut, table)
    local_tiles(tiles, lay, meta, False)
    blocks = Blocks(tiles, ring)
    density_loop(group, blocks, tiles.blocks, left, right, mrow, acc, work)


def density_remote_kernel(
    icut, jcut, group, lay,
    meta, own, rec, acc_in, left, energy_in,
    rho_out, term_out, pay, far, live,
    table, ring, right, mrow, acc, energy, sem, *work,
):
    cells, peers = lay.cells, lay.peers
    slots = own.shape[2]
    copy = pltpu.make_async_copy(energy_in, energy, sem)
    copy.start()
    first, below, above = arrivals(lay, rec)
    ids = row_ids((8, slots))

    def receive(at, k):
        rows = jnp.zeros((8, slots), F32)
        for r in range(SENT):
            rows = jnp.where(ids == r, rec[at, :, r * slots : (r + 1) * slots], rows)
        far[k] = rows
        density_source(rows, right, mrow, k)

    def rec_cell(k, carry):
        receive(first + k, k)
        return carry

    lax.fori_loop(0, peers, rec_cell, 0, unroll=4)
    receive(below, peers)
    receive(above, peers + 1)
    occupied = jnp.sum(jnp.where(far[:, 3, :] > 0.0, 1.0, 0.0), axis=1, keepdims=True)
    for k in range(peers + 2):
        live[k] = occupied[k, 0].astype(jnp.int32)
    acc[...] = acc_in[...]
    tiles = Tiles(icut, jcut, table)
    remote_tiles(tiles, lay, meta, live)
    blocks = Blocks(tiles, ring)
    density_loop(group, blocks, tiles.blocks, left, right, mrow, acc, work)

    copy.wait()
    lane = lax.broadcasted_iota(jnp.int32, (1, slots), 1)
    ones = jnp.ones((8, LANES), BF16)
    for k in range(cells):
        one, two, three = split3(acc[k])
        total_row = jnp.zeros((8, slots), F32)
        for part in (three, two, one):
            total_row = total_row + lax.dot_general(
                ones, part.astype(BF16), (((1,), (1,)), ((), ())), preferred_element_type=F32
            )
        inv = 1.0 / own[k, 4:5, :]
        rho = total_row[0:1] * (16.0 / math.pi) * (inv * inv * inv)
        occupied = jnp.where(lane < meta[k], 1.0, 0.0)
        rho_out[k : k + 1, :] = rho * occupied
        term_out[k] = occupied * (GAMMA - 1.0) * energy[k : k + 1, :] / (rho + 1.0 - occupied)

    def row(cell, r):
        return term_out[cell] if r == 0 else own[cell, 3 + r : 4 + r, :]

    fill(lay, pay, meta, SENT_LATER, row)


def force_source(rows, pressure, right, weights, scale, at):
    slots = rows.shape[1]
    right[at] = right_parts(right_comps(rows))
    h = rows[4:5]
    inv = 1.0 / jnp.where(h > 0.0, h, 1.0)
    b = math.sqrt(24.0 / math.pi) * (inv * inv)
    scales = jnp.concatenate(
        [jnp.broadcast_to(b, (8, slots)), jnp.broadcast_to(b * inv, (8, slots))], axis=0
    )
    scale[at] = scales
    m = rows[3:4]
    mp = m * pressure
    xv = rows[0:1] * rows[5:6] + rows[1:2] * rows[6:7] + rows[2:3] * rows[7:8]
    ids = row_ids((8, slots))
    base = jnp.where(ids == 3, 1.0, jnp.where(ids == 4, xv, rows))
    sums = jnp.concatenate([base * m, jnp.where(ids < 4, base, 0.0) * mp], axis=0)
    one, two, three = split3(sums)
    weights[at] = jnp.concatenate([one, two, three], axis=0).astype(BF16)
    return scales


def force_loop(group, blocks, total, local, left, right, weights, scale, bcol, ccol, acc, work):
    icut, jcut = blocks.icut, blocks.jcut
    dist, upper, lower = work[:group], work[group : 2 * group], work[2 * group :]
    blocks.clear(group)
    for ref in (*upper, *lower):
        ref[...] = jnp.zeros_like(ref)
    zero = jnp.int32(0)
    state = (zero, zero, zero)
    for g in range(2 * group):
        state = blocks.write(group + g, state)
    for g in range(group):
        blocks.distances(group + g, left, right, dist[g])

    def sums_of(rows, columns, k, g):
        a, b, istart, jstart, w = blocks.read(k * group + g)
        adds = []
        if rows:
            wt = weights[b, :, pl.ds(jstart, jcut)]
            spec = (((1,), (1,)), ((), ()))
            part = lax.dot_general(wt, upper[g][...], spec, preferred_element_type=F32)
            part = part + lax.dot_general(wt, lower[g][...], spec, preferred_element_type=F32)
            keep = w
            if columns:
                keep = jnp.where(k * group + g < local + group, w, 0.0)
            adds.append((a, istart, part * keep))
        if columns:
            wt = weights[a, :, pl.ds(istart, icut)]
            part = jnp.dot(wt, upper[g][...], preferred_element_type=F32)
            part = part + jnp.dot(wt, lower[g][...], preferred_element_type=F32)
            adds.append((b, jstart, part * w))
        return adds

    def store(adds):
        for cell, start, part in adds:
            acc[cell, :, pl.ds(start, part.shape[1])] += part

    def step(rows, columns, k, state):
        adds = []
        for g in range(group):
            adds += sums_of(rows, columns, k, g)

            a, b, istart, jstart, _ = blocks.read((k + 1) * group + g)
            bj = jnp.concatenate([scale[b, 0:8, pl.ds(jstart, jcut)]] * (STRIP // 8), axis=0)
            cj = jnp.concatenate([scale[b, 8:16, pl.ds(jstart, jcut)]] * (STRIP // 8), axis=0)
            for row in range(0, icut, STRIP):
                s = jnp.maximum(dist[g][row : row + STRIP, :], TINY)
                r = lax.rsqrt(s)
                d = s * r
                bi = bcol[a, pl.ds(istart + row, STRIP), :]
                ci = ccol[a, pl.ds(istart + row, STRIP), :]
                bi = jnp.concatenate([bi] * (jcut // LANES), axis=1)
                ci = jnp.concatenate([ci] * (jcut // LANES), axis=1)
                t = ci * d
                u = jnp.maximum(bi - t, 0.0)
                v = jnp.minimum(t, u)
                slope = (u + u - v) * v
                t = cj * d
                u = jnp.maximum(bj - t, 0.0)
                v = jnp.minimum(t, u)
                slope = (slope + (u + u - v) * v) * r
                rounded = slope.astype(BF16)
                upper[g][row : row + STRIP, :] = rounded
                lower[g][row : row + STRIP, :] = (slope - rounded.astype(F32)).astype(BF16)

            state = blocks.write((k + 3) * group + g, state)
            blocks.distances((k + 2) * group + g, left, right, dist[g])
        store(adds)
        return state

    steps = chunks(total, group)
    adds = []
    if local is None:
        lax.fori_loop(0, steps, functools.partial(step, True, False), state)
        for g in range(group):
            adds += sums_of(True, False, steps, g)
    else:
        first = jnp.minimum(chunks(local, group) + 1, steps)
        state = lax.fori_loop(0, first, functools.partial(step, True, True), state)
        lax.fori_loop(first, steps, functools.partial(step, False, True), state)
        for g in range(group):
            adds += sums_of(True, True, steps, g)
    store(adds)


def force_local_kernel(
    icut, jcut, group, lay,
    meta, own, term,
    acc_out, left, bcol, ccol,
    table, ring, right, weights, scale, acc, *work,
):
    slots = own.shape[2]
    for k in range(lay.cells):
        rows = own[k]
        scales = force_source(rows, term[k], right, weights, scale, k)
        parts = left_parts(left_comps(rows))
        acc[k] = jnp.zeros((DOT_K, slots), F32)
        block = jnp.concatenate([parts, scales], axis=0)
        for at in range(slots // LANES):
            cols = block[:, at * LANES : (at + 1) * LANES].T
            here = pl.ds(at * LANES, LANES)
            left[k, here, :] = cols.astype(BF16)
            bcol[k, here, :] = jnp.broadcast_to(cols[:, DOT_K : DOT_K + 1], (LANES, LANES))
            ccol[k, here, :] = jnp.broadcast_to(cols[:, DOT_K + 8 : DOT_K + 9], (LANES, LANES))
    tiles = Tiles(icut, jcut, table)
    local = local_tiles(tiles, lay, meta, True)
    blocks = Blocks(tiles, ring)
    force_loop(
        group, blocks, tiles.blocks, local, left, right, weights, scale, bcol, ccol, acc, work
    )
    for k in range(lay.cells):
        acc_out[k] = acc[k, 0:16, :] + (acc[k, 16:32, :] + acc[k, 32:48, :])


def force_remote_kernel(
    icut, jcut, group, lay,
    meta, live, own, far, term, rterm, acc_in, left, bcol, ccol,
    accel_out, heat_out,
    table, ring, right, weights, scale, acc, *work,
):
    cells, peers = lay.cells, lay.peers
    slots = own.shape[2]
    first, below, above = arrivals(lay, rterm)
    ids = row_ids((8, slots))

    def receive(at, k):
        rows = far[k]
        for r in range(1, SENT_LATER):
            rows = jnp.where(ids == 3 + r, rterm[at, :, r * slots : (r + 1) * slots], rows)
        force_source(rows, rterm[at, :, :slots], right, weights, scale, k)

    def rec_cell(k, carry):
        receive(first + k, k)
        return carry

    lax.fori_loop(0, peers, rec_cell, 0, unroll=4)
    receive(below, peers)
    receive(above, peers + 1)
    acc[...] = jnp.zeros_like(acc)
    tiles = Tiles(icut, jcut, table)
    remote_tiles(tiles, lay, meta, live)
    blocks = Blocks(tiles, ring)
    force_loop(
        group, blocks, tiles.blocks, None, left, right, weights, scale, bcol, ccol, acc, work
    )

    lane = lax.broadcasted_iota(jnp.int32, (1, slots), 1)
    for k in range(cells):
        occupied = jnp.where(lane < meta[k], 1.0, 0.0)
        sums = acc_in[k] + acc[k, 0:16, :] + (acc[k, 16:32, :] + acc[k, 32:48, :])
        pressure = term[k]
        x = [own[k, d : d + 1, :] for d in range(3)]
        v = [own[k, 5 + d : 6 + d, :] for d in range(3)]
        both = pressure * sums[3:4] + sums[11:12]
        for d in range(3):
            accel_out[d, k : k + 1, :] = occupied * (
                x[d] * both - pressure * sums[d : d + 1] - sums[8 + d : 9 + d]
            )
        xv = x[0] * v[0] + x[1] * v[1] + x[2] * v[2]
        total_heat = xv * sums[3:4] + sums[4:5]
        for d in range(3):
            total_heat = total_heat - v[d] * sums[d : d + 1] - x[d] * sums[5 + d : 6 + d]
        heat_out[k : k + 1, :] = -occupied * pressure * total_heat


def on_device(positions, velocities, mass, smoothing, energy, counts, send, pairs, edge):
    cells, slots = mass.shape
    peers = send.shape[2]
    regions = lax.axis_size("region")
    lay = Meta(cells, peers, pairs.shape[2])
    others = peers + 2
    most = max(cells * (cells - 1) // 2 + 3 * cells, cells * cells, others) + 1
    icut, jcut, group = 128, slots // 2, 4
    ring = Blocks.FIELDS * (most * (slots // icut) * (slots // jcut) + 6 * group)
    shape = jax.ShapeDtypeStruct
    params = pltpu.CompilerParams(vmem_limit_bytes=20 * 1024 * 1024)
    send = send.reshape(peers)
    pairs = jnp.transpose(pairs, (0, 1, 3, 2))
    integers = (counts, send, pairs, edge)
    floats = (positions, velocities, mass, smoothing)
    integers, floats, energy = jax.tree.map(
        lambda x: pltpu.with_memory_space_constraint(x, pltpu.HBM), (integers, floats, energy)
    )
    lists = [pltpu.SMEM((Tiles.FIELDS * most,), jnp.int32), pltpu.SMEM((ring,), jnp.int32)]
    density_work = [pltpu.VMEM((icut, jcut), F32)] * group + [pltpu.VMEM((icut, LANES), F32)] * group
    force_work = [pltpu.VMEM((icut, jcut), F32)] * group + [pltpu.VMEM((icut, jcut), BF16)] * (2 * group)
    wide = shape((cells, slots, LANES), F32)
    left_shape = shape((cells, slots, COLS), BF16)
    weight_shape = lambda count: pltpu.VMEM((count, DOT_K, slots), BF16)

    own, pay, meta = pl.pallas_call(
        functools.partial(prep_kernel, lay),
        out_shape=[
            shape((cells, ROWS, slots), F32),
            shape((regions * peers, 1, SENT * slots), F32),
            shape((lay.size,), jnp.int32),
        ],
        in_specs=[HBM] * 8,
        out_specs=[VMEM] * 2 + [SMEM],
        scratch_shapes=[pltpu.SMEM(x.shape, jnp.int32) for x in integers]
        + [pltpu.VMEM(x.shape, F32) for x in floats]
        + [pltpu.SemaphoreType.DMA((8,))],
        compiler_params=params,
        name="prep",
    )(*integers, *floats)

    rec = lax.all_to_all(pay, ("region", "cell"), split_axis=0, concat_axis=0, tiled=True)

    acc, left = pl.pallas_call(
        functools.partial(density_local_kernel, icut, jcut, group, lay),
        out_shape=[wide, left_shape],
        in_specs=[SMEM, VMEM],
        out_specs=[VMEM] * 2,
        scratch_shapes=lists + [weight_shape(cells), pltpu.VMEM((cells, 8, slots), F32)] + density_work,
        compiler_params=params,
        name="density_local",
    )(meta, own)

    density, term, pay, far, live = pl.pallas_call(
        functools.partial(density_remote_kernel, icut, jcut, group, lay),
        out_shape=[
            shape((cells, slots), F32),
            shape((cells, 1, slots), F32),
            shape((regions * peers, 1, SENT_LATER * slots), F32),
            shape((others, ROWS, slots), F32),
            shape((others,), jnp.int32),
        ],
        in_specs=[SMEM] + [VMEM] * 4 + [HBM],
        out_specs=[VMEM] * 4 + [SMEM],
        scratch_shapes=lists
        + [
            weight_shape(others),
            pltpu.VMEM((others, 8, slots), F32),
            pltpu.VMEM((cells, slots, LANES), F32),
            pltpu.VMEM(energy.shape, F32),
            pltpu.SemaphoreType.DMA,
        ]
        + density_work,
        compiler_params=params,
        name="density_remote",
    )(meta, own, rec, acc, left, energy)

    rterm = lax.all_to_all(pay, ("region", "cell"), split_axis=0, concat_axis=0, tiled=True)

    acc, left, bcol, ccol = pl.pallas_call(
        functools.partial(force_local_kernel, icut, jcut, group, lay),
        out_shape=[shape((cells, 16, slots), F32), left_shape, wide, wide],
        in_specs=[SMEM] + [VMEM] * 2,
        out_specs=[VMEM] * 4,
        scratch_shapes=lists
        + [
            weight_shape(cells),
            weight_shape(cells),
            pltpu.VMEM((cells, 16, slots), F32),
            pltpu.VMEM((cells, DOT_K, slots), F32),
        ]
        + force_work,
        compiler_params=params,
        name="force_local",
    )(meta, own, term)

    accel, heat = pl.pallas_call(
        functools.partial(force_remote_kernel, icut, jcut, group, lay),
        out_shape=[shape((3, cells, slots), F32), shape((cells, slots), F32)],
        in_specs=[SMEM] * 2 + [VMEM] * 8,
        out_specs=[VMEM] * 2,
        scratch_shapes=lists
        + [
            weight_shape(others),
            weight_shape(others),
            pltpu.VMEM((others, 16, slots), F32),
            pltpu.VMEM((cells, DOT_K, slots), F32),
        ]
        + force_work,
        compiler_params=params,
        name="force_remote",
    )(meta, live, own, far, term, rterm, acc, left, bcol, ccol)
    return density, accel, heat


def solution(mesh):
    placed = (
        P(None, ("region", "cell"), None),
        P(None, ("region", "cell"), None),
        P(("region", "cell"), None),
        P(("region", "cell"), None),
        P(("region", "cell"), None),
        P(("region", "cell")),
        P("region", "cell", None, None),
        P("region", "cell", None, None),
        P("region", "cell", None),
    )
    return jax.shard_map(
        on_device,
        mesh=mesh,
        in_specs=placed,
        out_specs=(
            P(("region", "cell"), None),
            P(None, ("region", "cell"), None),
            P(("region", "cell"), None),
        ),
        check_vma=False,
    )
```

```python
import functools
import math

import jax
import jax.numpy as jnp
from jax import lax
from jax.experimental import pallas as pl
from jax.experimental.pallas import tpu as pltpu
from jax.sharding import PartitionSpec as P

GAMMA = 5.0 / 3.0
LANES = 128
BF16 = jnp.bfloat16
F32 = jnp.float32

ROWS = 8
TINY = 1e-12
DOT_K = 48
COLS = 64
STRIP = 16
SENT = 4
SENT_LATER = 5

VMEM = pl.BlockSpec(memory_space=pltpu.VMEM)
SMEM = pl.BlockSpec(memory_space=pltpu.SMEM)
HBM = pl.BlockSpec(memory_space=pltpu.HBM)


def row_ids(shape):
    return lax.broadcasted_iota(jnp.int32, shape, 0)


def split3(value):
    first = value.astype(BF16).astype(F32)
    rest = value - first
    second = rest.astype(BF16).astype(F32)
    return first, second, rest - second


def left_parts(value):
    a, b, c = split3(value)
    return jnp.concatenate([a, a, b, b, a, c], axis=0)


def right_parts(value):
    a, b, c = split3(value)
    return jnp.concatenate([a, b, a, b, c, a], axis=0).astype(BF16)


def norm_row(rows):
    return rows[0:1] * rows[0:1] + rows[1:2] * rows[1:2] + rows[2:3] * rows[2:3]


def left_comps(rows):
    ids = row_ids(rows.shape)
    return jnp.where(ids < 3, rows, jnp.where(ids == 3, norm_row(rows), jnp.where(ids == 4, 1.0, 0.0)))


def right_comps(rows):
    ids = row_ids(rows.shape)
    return jnp.where(ids < 3, -2.0 * rows, jnp.where(ids == 3, 1.0, jnp.where(ids == 4, norm_row(rows), 0.0)))


def chunks(count, size):
    return lax.shift_right_logical(count + (size - 1), jnp.int32(size.bit_length() - 1))


class Meta:
    def __init__(self, cells, peers, pairs):
        self.cells, self.peers, self.pairs = cells, peers, pairs
        self.send = cells
        self.pair = cells + peers
        self.edge = self.pair + 2 * pairs
        self.size = self.edge + 2


def prep_kernel(
    lay,
    counts_in, send_in, pairs_in, edge_in, pos_in, vel_in, mass_in, smooth_in,
    own, pay, odd, meta,
    counts, send, pairs, edge, pos, vel, mass, smooth, sems,
):
    inputs = (counts_in, send_in, pairs_in, edge_in, pos_in, vel_in, mass_in, smooth_in)
    buffers = (counts, send, pairs, edge, pos, vel, mass, smooth)
    copies = [
        pltpu.make_async_copy(source, target, sems.at[k])
        for k, (source, target) in enumerate(zip(inputs, buffers))
    ]
    for copy in copies:
        copy.start()
    for copy in copies:
        copy.wait()
    cells = mass.shape[0]
    slots = mass.shape[1]
    for k in range(cells):
        meta[k] = counts[k]
    for k in range(lay.peers):
        meta[lay.send + k] = send[k]
    for k in range(lay.pairs):
        for side in range(2):
            meta[lay.pair + 2 * k + side] = pairs[0, 0, side, k]
    for side in range(2):
        meta[lay.edge + side] = edge[0, 0, side]

    lane = lax.broadcasted_iota(jnp.int32, (1, slots), 1)
    for k in range(cells):
        live = lane < counts[k]
        for d in range(3):
            own[k, d : d + 1, :] = pos[d, k : k + 1, :] - 0.5
            own[k, 5 + d : 6 + d, :] = vel[d, k : k + 1, :]
        own[k, 3:4, :] = jnp.where(live, mass[k : k + 1, :], 0.0)
        own[k, 4:5, :] = smooth[k : k + 1, :]

    def row(cell, r):
        return own[cell, r : r + 1, :]

    fill(lay, pay, odd, meta, SENT, row)


def fill(lay, pay, odd, meta, count, row):
    slots = pay.shape[2] // count
    side = lax.axis_index("side")
    first = side * lay.peers
    pay[...] = jnp.zeros_like(pay)

    def put(out, at, cell, keep):
        for r in range(count):
            value = row(cell, r)
            if keep is not None:
                value = jnp.where(keep, value, 0.0)
            out[at, :, r * slots : (r + 1) * slots] = value

    def peer(k, carry):
        picked = meta[lay.send + k]
        put(pay, first + k, jnp.maximum(picked, 0), picked >= 0)
        return carry

    lax.fori_loop(0, lay.peers, peer, 0)
    put(pay, lay.peers - first + lax.axis_index("cell"), meta[lay.edge + 1 - side], None)
    put(odd, 0, meta[lay.edge + side], None)


def arrivals(lay):
    first = lax.axis_index("side") * lay.peers
    return first, lay.peers - first + lax.axis_index("cell")


class Tiles:
    FIELDS = 7

    def __init__(self, icut, jcut, table):
        self.icut, self.jcut, self.table = icut, jcut, table
        self.count = self.blocks = jnp.int32(0)

    def push(self, a, b, w, ok, i, ni, j, nj):
        at = self.FIELDS * self.count
        for field, value in enumerate((a, b, w, i, ni, j, nj)):
            self.table[at + field] = value
        self.count = self.count + ok.astype(jnp.int32)
        self.blocks = self.blocks + jnp.where(ok, ni * nj, 0)

    def whole(self, a, b, w, ok, alive, blive):
        self.push(a, b, w, ok, 0, chunks(alive, self.icut), 0, chunks(blive, self.jcut))

    def close(self):
        self.push(0, 0, 0, jnp.bool_(False), 0, 1, 0, 1)


def local_tiles(tiles, lay, meta, both):
    cells = lay.cells
    one = jnp.int32(1)

    def key(row):
        first = meta[lay.pair + 2 * row]
        second = meta[lay.pair + 2 * row + 1]
        return jnp.minimum(first, second) * cells + jnp.maximum(first, second)

    keys = [key(row) for row in range(lay.pairs)]
    for a in range(cells):
        for b in range(a + 1, cells):
            mult = jnp.int32(0)
            for pair in keys:
                mult = mult + (pair == a * cells + b).astype(jnp.int32)
            tiles.whole(a, b, mult, mult > 0, meta[a], meta[b])
            if not both:
                tiles.whole(b, a, mult, mult > 0, meta[b], meta[a])
    if not both:
        for a in range(cells):
            tiles.whole(a, a, one, meta[a] > 0, meta[a], meta[a])
        tiles.close()
        return None
    span = tiles.jcut // tiles.icut
    for a in range(cells):
        tiles.push(a, a, one, meta[a] > tiles.jcut, 0, span, 1, chunks(meta[a], tiles.jcut) - 1)
    mutual = tiles.blocks
    for a in range(cells):
        rows = chunks(meta[a], tiles.icut)
        tiles.push(a, a, one, meta[a] > 0, 0, jnp.minimum(rows, span), 0, 1)
        tiles.push(a, a, one, meta[a] > tiles.jcut, span, rows - span, 1, 1)
    tiles.close()
    return mutual


def remote_tiles(tiles, lay, meta, live):
    one = jnp.int32(1)
    for k in range(lay.peers):
        picked = meta[lay.send + k]
        a = jnp.maximum(picked, 0)
        tiles.whole(a, k, one, (picked >= 0) & (live[k] > 0), meta[a], live[k])
    side = lax.axis_index("side")
    for b, edge in ((lay.peers, 1 - side), (lay.peers + 1, side)):
        a = meta[lay.edge + edge]
        tiles.whole(a, b, one, live[b] > 0, meta[a], live[b])
    tiles.close()


class Blocks:
    FIELDS = 5

    def __init__(self, tiles, ring):
        self.icut, self.jcut = tiles.icut, tiles.jcut
        self.table, self.last = tiles.table, tiles.count
        self.ring, self.total = ring, tiles.blocks

    def clear(self, entries):
        for k in range(entries * self.FIELDS):
            self.ring[k] = 0

    def write(self, slot, state):
        n, ii, jj = state
        a, b, w, i, ni, j, nj = (self.table[Tiles.FIELDS * n + k] for k in range(Tiles.FIELDS))
        for field, value in enumerate((a, b, (i + ii) * self.icut, (j + jj) * self.jcut, w)):
            self.ring[self.FIELDS * slot + field] = value
        jwrap = jj + 1 >= nj
        inext = jnp.where(jwrap, ii + 1, ii)
        iwrap = inext >= ni
        return (
            jnp.minimum(jnp.where(iwrap, n + 1, n), self.last),
            jnp.where(iwrap, 0, inext),
            jnp.where(jwrap, 0, jj + 1),
        )

    def read(self, slot):
        a, b, istart, jstart, w = (self.ring[self.FIELDS * slot + k] for k in range(self.FIELDS))
        return (
            a,
            b,
            pl.multiple_of(istart, self.icut),
            pl.multiple_of(jstart, self.jcut),
            w.astype(F32),
        )

    def distances(self, slot, left, right, out):
        a, b, istart, jstart, _ = self.read(slot)
        out[...] = jnp.dot(
            left[a, pl.ds(istart, self.icut), :DOT_K],
            right[b, :, pl.ds(jstart, self.jcut)],
            preferred_element_type=F32,
        )


def density_loop(group, blocks, total, left, right, mrow, acc, work):
    icut, jcut = blocks.icut, blocks.jcut
    dist, parts = work[:group], work[group:]
    zero = jnp.int32(0)
    state = (zero, zero, zero)
    for g in range(2 * group):
        state = blocks.write(g, state)
    for g in range(group):
        blocks.distances(g, left, right, dist[g])

    def step(k, state):
        for g in range(group):
            _, b, _, jstart, w = blocks.read(k * group + g)
            weight = mrow[b, :, pl.ds(jstart, jcut)] * w
            weight = jnp.concatenate([weight] * (STRIP // 8), axis=0)
            for row in range(0, icut, STRIP):
                s = jnp.maximum(dist[g][row : row + STRIP, :], TINY)
                q = s * lax.rsqrt(s)
                e = 1.0 - q
                u = jnp.maximum(e, 0.0)
                t = jnp.minimum(0.5 - (s * 3.0) * e, u * u * u) * weight
                part = t[:, :LANES]
                for at in range(1, jcut // LANES):
                    part = part + t[:, at * LANES : (at + 1) * LANES]
                parts[g][row : row + STRIP, :] = part

            state = blocks.write((k + 2) * group + g, state)
            blocks.distances((k + 1) * group + g, left, right, dist[g])
        for g in range(group):
            a, _, istart, _, _ = blocks.read(k * group + g)
            acc[a, pl.ds(istart, icut), :] += parts[g][...]
        return state

    lax.fori_loop(0, chunks(total, group), step, state)


def density_source(rows, right, mrow, at):
    right[at] = right_parts(right_comps(rows))
    mrow[at] = jnp.broadcast_to(rows[3:4], mrow.shape[1:])


def spread_left(parts, left, cell):
    for at in range(parts.shape[1] // LANES):
        left[cell, pl.ds(at * LANES, LANES), :] = parts[:, at * LANES : (at + 1) * LANES].T.astype(BF16)


def force_scales(rows):
    h = rows[4:5]
    inv = 1.0 / jnp.where(h > 0.0, h, 1.0)
    b = math.sqrt(24.0 / math.pi) * (inv * inv)
    return b, b * inv


def density_local_kernel(
    icut, jcut, group, lay, meta, own, acc, left, force_left, table, ring, right, mrow, *work
):
    slots = own.shape[2]
    ids = row_ids((8, slots))
    empty = jnp.zeros((8, slots), F32)
    for k in range(lay.cells):
        rows = own[k]
        inv = 1.0 / rows[4:5]
        comps = left_comps(rows)
        spread_left(jnp.concatenate([left_parts(comps * (inv * inv)), empty, empty], axis=0), left, k)
        scales = empty
        for at, part in enumerate(x for scale in force_scales(rows) for x in split3(scale)):
            scales = jnp.where(ids == at, part, scales)
        spread_left(jnp.concatenate([left_parts(comps), scales, empty], axis=0), force_left, k)
        density_source(rows, right, mrow, k)
        acc[k] = jnp.zeros((slots, LANES), F32)
    tiles = Tiles(icut, jcut, table)
    local_tiles(tiles, lay, meta, False)
    blocks = Blocks(tiles, ring)
    density_loop(group, blocks, tiles.blocks, left, right, mrow, acc, work)


def density_remote_kernel(
    icut, jcut, group, lay,
    meta, own, rec, rec_odd, acc_in, left, energy_in,
    rho_out, term_out, pay, odd, far, live,
    table, ring, right, mrow, acc, energy, sem, *work,
):
    cells, peers = lay.cells, lay.peers
    slots = own.shape[2]
    copy = pltpu.make_async_copy(energy_in, energy, sem)
    copy.start()
    first, face = arrivals(lay)
    ids = row_ids((8, slots))

    def receive(got, at, k):
        rows = jnp.zeros((8, slots), F32)
        for r in range(SENT):
            rows = jnp.where(ids == r, got[at, :, r * slots : (r + 1) * slots], rows)
        far[k] = rows
        density_source(rows, right, mrow, k)

    def rec_cell(k, carry):
        receive(rec, first + k, k)
        return carry

    lax.fori_loop(0, peers, rec_cell, 0, unroll=4)
    receive(rec, face, peers)
    receive(rec_odd, 0, peers + 1)
    occupied = jnp.sum(jnp.where(far[:, 3, :] > 0.0, 1.0, 0.0), axis=1, keepdims=True)
    for k in range(peers + 2):
        live[k] = occupied[k, 0].astype(jnp.int32)
    acc[...] = acc_in[...]
    tiles = Tiles(icut, jcut, table)
    remote_tiles(tiles, lay, meta, live)
    blocks = Blocks(tiles, ring)
    density_loop(group, blocks, tiles.blocks, left, right, mrow, acc, work)

    copy.wait()
    lane = lax.broadcasted_iota(jnp.int32, (1, slots), 1)
    ones = jnp.ones((8, LANES), BF16)
    for k in range(cells):
        one, two, three = split3(acc[k])
        total_row = jnp.zeros((8, slots), F32)
        for part in (three, two, one):
            total_row = total_row + lax.dot_general(
                ones, part.astype(BF16), (((1,), (1,)), ((), ())), preferred_element_type=F32
            )
        inv = 1.0 / own[k, 4:5, :]
        rho = total_row[0:1] * (16.0 / math.pi) * (inv * inv * inv)
        occupied = jnp.where(lane < meta[k], 1.0, 0.0)
        rho_out[k : k + 1, :] = rho * occupied
        term_out[k] = occupied * (GAMMA - 1.0) * energy[k : k + 1, :] / (rho + 1.0 - occupied)

    def row(cell, r):
        return term_out[cell] if r == 0 else own[cell, 3 + r : 4 + r, :]

    fill(lay, pay, odd, meta, SENT_LATER, row)


def force_source(rows, pressure, right, weights, scale, at):
    slots = rows.shape[1]
    right[at] = right_parts(right_comps(rows))
    b, c = force_scales(rows)
    scale[at] = jnp.concatenate([jnp.broadcast_to(b, (8, slots)), jnp.broadcast_to(c, (8, slots))], axis=0)
    m = rows[3:4]
    mp = m * pressure
    xv = rows[0:1] * rows[5:6] + rows[1:2] * rows[6:7] + rows[2:3] * rows[7:8]
    ids = row_ids((8, slots))
    base = jnp.where(ids == 3, 1.0, jnp.where(ids == 4, xv, rows))
    sums = jnp.concatenate([base * m, jnp.where(ids < 4, base, 0.0) * mp], axis=0)
    one, two, three = split3(sums)
    weights[at] = jnp.concatenate([one, two, three], axis=0).astype(BF16)


def force_loop(group, blocks, total, local, left, right, weights, scale, bcol, ccol, acc, work):
    icut, jcut = blocks.icut, blocks.jcut
    dist, upper, lower = work[:group], work[group : 2 * group], work[2 * group :]
    blocks.clear(group)
    for ref in (*upper, *lower):
        ref[...] = jnp.zeros_like(ref)
    zero = jnp.int32(0)
    state = (zero, zero, zero)
    for g in range(2 * group):
        state = blocks.write(group + g, state)
    for g in range(group):
        blocks.distances(group + g, left, right, dist[g])

    def sums_of(rows, columns, k, g):
        a, b, istart, jstart, w = blocks.read(k * group + g)
        adds = []
        if rows:
            wt = weights[b, :, pl.ds(jstart, jcut)]
            spec = (((1,), (1,)), ((), ()))
            part = lax.dot_general(wt, upper[g][...], spec, preferred_element_type=F32)
            part = part + lax.dot_general(wt, lower[g][...], spec, preferred_element_type=F32)
            keep = w
            if columns:
                keep = jnp.where(k * group + g < local + group, w, 0.0)
            adds.append((a, istart, part * keep))
        if columns:
            wt = weights[a, :, pl.ds(istart, icut)]
            part = jnp.dot(wt, upper[g][...], preferred_element_type=F32)
            part = part + jnp.dot(wt, lower[g][...], preferred_element_type=F32)
            adds.append((b, jstart, part * w))
        return adds

    def store(adds):
        for cell, start, part in adds:
            acc[cell, :, pl.ds(start, part.shape[1])] += part

    def step(rows, columns, k, state):
        adds = []
        for g in range(group):
            adds += sums_of(rows, columns, k, g)

            a, b, istart, jstart, _ = blocks.read((k + 1) * group + g)
            bj = jnp.concatenate([scale[b, 0:8, pl.ds(jstart, jcut)]] * (STRIP // 8), axis=0)
            cj = jnp.concatenate([scale[b, 8:16, pl.ds(jstart, jcut)]] * (STRIP // 8), axis=0)
            for row in range(0, icut, STRIP):
                s = jnp.maximum(dist[g][row : row + STRIP, :], TINY)
                r = lax.rsqrt(s)
                d = s * r
                bi = bcol[a, pl.ds(istart + row, STRIP), :]
                ci = ccol[a, pl.ds(istart + row, STRIP), :]
                bi = jnp.concatenate([bi] * (jcut // LANES), axis=1)
                ci = jnp.concatenate([ci] * (jcut // LANES), axis=1)
                t = ci * d
                u = jnp.maximum(bi - t, 0.0)
                v = jnp.minimum(t, u)
                slope = (u + u - v) * v
                t = cj * d
                u = jnp.maximum(bj - t, 0.0)
                v = jnp.minimum(t, u)
                slope = (slope + (u + u - v) * v) * r
                rounded = slope.astype(BF16)
                upper[g][row : row + STRIP, :] = rounded
                lower[g][row : row + STRIP, :] = (slope - rounded.astype(F32)).astype(BF16)

            state = blocks.write((k + 3) * group + g, state)
            blocks.distances((k + 2) * group + g, left, right, dist[g])
        store(adds)
        return state

    steps = chunks(total, group)
    adds = []
    if local is None:
        lax.fori_loop(0, steps, functools.partial(step, True, False), state)
        for g in range(group):
            adds += sums_of(True, False, steps, g)
    else:
        first = jnp.minimum(chunks(local, group) + 1, steps)
        state = lax.fori_loop(0, first, functools.partial(step, True, True), state)
        lax.fori_loop(first, steps, functools.partial(step, False, True), state)
        for g in range(group):
            adds += sums_of(True, True, steps, g)
    store(adds)


def force_local_kernel(
    icut, jcut, group, lay,
    meta, own, term, left,
    acc_out, bcol, ccol,
    table, ring, right, weights, scale, acc, *work,
):
    slots = own.shape[2]
    part = lax.broadcasted_iota(jnp.int32, (COLS, 2 * LANES), 0) - DOT_K
    lane = lax.broadcasted_iota(jnp.int32, (COLS, 2 * LANES), 1)
    of_b = (part >= 0) & (part < 3) & (lane < LANES)
    of_c = (part >= 3) & (part < 6) & (lane >= LANES)
    pick = jnp.where(of_b | of_c, 1.0, 0.0).astype(BF16)
    for k in range(lay.cells):
        force_source(own[k], term[k], right, weights, scale, k)
        acc[k] = jnp.zeros((DOT_K, slots), F32)
        for at in range(slots // LANES):
            here = pl.ds(at * LANES, LANES)
            both = jnp.dot(left[k, here, :], pick, preferred_element_type=F32)
            bcol[k, here, :] = both[:, :LANES]
            ccol[k, here, :] = both[:, LANES:]
    tiles = Tiles(icut, jcut, table)
    local = local_tiles(tiles, lay, meta, True)
    blocks = Blocks(tiles, ring)
    force_loop(
        group, blocks, tiles.blocks, local, left, right, weights, scale, bcol, ccol, acc, work
    )
    for k in range(lay.cells):
        acc_out[k] = acc[k, 0:16, :] + (acc[k, 16:32, :] + acc[k, 32:48, :])


def force_remote_kernel(
    icut, jcut, group, lay,
    meta, live, own, far, term, rterm, odd_term, acc_in, left, bcol, ccol,
    accel_out, heat_out,
    table, ring, right, weights, scale, acc, *work,
):
    cells, peers = lay.cells, lay.peers
    slots = own.shape[2]
    first, face = arrivals(lay)
    ids = row_ids((8, slots))

    def receive(got, at, k):
        rows = far[k]
        for r in range(1, SENT_LATER):
            rows = jnp.where(ids == 3 + r, got[at, :, r * slots : (r + 1) * slots], rows)
        force_source(rows, got[at, :, :slots], right, weights, scale, k)

    def rec_cell(k, carry):
        receive(rterm, first + k, k)
        return carry

    lax.fori_loop(0, peers, rec_cell, 0, unroll=4)
    receive(rterm, face, peers)
    receive(odd_term, 0, peers + 1)
    acc[...] = jnp.zeros_like(acc)
    tiles = Tiles(icut, jcut, table)
    remote_tiles(tiles, lay, meta, live)
    blocks = Blocks(tiles, ring)
    force_loop(
        group, blocks, tiles.blocks, None, left, right, weights, scale, bcol, ccol, acc, work
    )

    lane = lax.broadcasted_iota(jnp.int32, (1, slots), 1)
    for k in range(cells):
        occupied = jnp.where(lane < meta[k], 1.0, 0.0)
        sums = acc_in[k] + acc[k, 0:16, :] + (acc[k, 16:32, :] + acc[k, 32:48, :])
        pressure = term[k]
        x = [own[k, d : d + 1, :] for d in range(3)]
        v = [own[k, 5 + d : 6 + d, :] for d in range(3)]
        both = pressure * sums[3:4] + sums[11:12]
        for d in range(3):
            accel_out[d, k : k + 1, :] = occupied * (
                x[d] * both - pressure * sums[d : d + 1] - sums[8 + d : 9 + d]
            )
        xv = x[0] * v[0] + x[1] * v[1] + x[2] * v[2]
        total_heat = xv * sums[3:4] + sums[4:5]
        for d in range(3):
            total_heat = total_heat - v[d] * sums[d : d + 1] - x[d] * sums[5 + d : 6 + d]
        heat_out[k : k + 1, :] = -occupied * pressure * total_heat


def on_device(positions, velocities, mass, smoothing, energy, counts, send, pairs, edge):
    cells, slots = mass.shape
    peers = send.shape[2]
    regions = 2 * lax.axis_size("pair")
    lay = Meta(cells, peers, pairs.shape[2])
    others = peers + 2
    most = max(cells * (cells - 1) // 2 + 3 * cells, cells * cells, others) + 1
    icut, jcut, group = 128, slots // 2, 4
    ring = Blocks.FIELDS * (most * (slots // icut) * (slots // jcut) + 6 * group)
    shape = jax.ShapeDtypeStruct
    params = pltpu.CompilerParams(vmem_limit_bytes=20 * 1024 * 1024)
    send = send.reshape(peers)
    pairs = jnp.transpose(pairs, (0, 1, 3, 2))
    integers = (counts, send, pairs, edge)
    floats = (positions, velocities, mass, smoothing)
    integers, floats, energy = jax.tree.map(
        lambda x: pltpu.with_memory_space_constraint(x, pltpu.HBM), (integers, floats, energy)
    )
    lists = [pltpu.SMEM((Tiles.FIELDS * most,), jnp.int32), pltpu.SMEM((ring,), jnp.int32)]
    density_work = [pltpu.VMEM((icut, jcut), F32)] * group + [pltpu.VMEM((icut, LANES), F32)] * group
    force_work = [pltpu.VMEM((icut, jcut), F32)] * group + [pltpu.VMEM((icut, jcut), BF16)] * (2 * group)
    wide = shape((cells, slots, LANES), F32)
    left_shape = shape((cells, slots, COLS), BF16)
    weight_shape = lambda count: pltpu.VMEM((count, DOT_K, slots), BF16)

    def exchange(pay, odd):
        between = [(r, r + 1) for r in range(1, regions - 1, 2)]
        swap = between + [(b, a) for a, b in between]
        got_odd = lax.ppermute(odd, ("pair", "side"), swap)
        return lax.all_to_all(pay, ("side", "cell"), split_axis=0, concat_axis=0, tiled=True), got_odd

    own, pay, odd, meta = pl.pallas_call(
        functools.partial(prep_kernel, lay),
        out_shape=[
            shape((cells, ROWS, slots), F32),
            shape((2 * peers, 1, SENT * slots), F32),
            shape((1, 1, SENT * slots), F32),
            shape((lay.size,), jnp.int32),
        ],
        in_specs=[HBM] * 8,
        out_specs=[VMEM] * 3 + [SMEM],
        scratch_shapes=[pltpu.SMEM(x.shape, jnp.int32) for x in integers]
        + [pltpu.VMEM(x.shape, F32) for x in floats]
        + [pltpu.SemaphoreType.DMA((8,))],
        compiler_params=params,
        name="prep",
    )(*integers, *floats)

    rec, rec_odd = exchange(pay, odd)

    acc, left, force_left = pl.pallas_call(
        functools.partial(density_local_kernel, icut, jcut, group, lay),
        out_shape=[wide, left_shape, left_shape],
        in_specs=[SMEM, VMEM],
        out_specs=[VMEM] * 3,
        scratch_shapes=lists + [weight_shape(cells), pltpu.VMEM((cells, 8, slots), F32)] + density_work,
        compiler_params=params,
        name="density_local",
    )(meta, own)

    density, term, pay, odd, far, live = pl.pallas_call(
        functools.partial(density_remote_kernel, icut, jcut, group, lay),
        out_shape=[
            shape((cells, slots), F32),
            shape((cells, 1, slots), F32),
            shape((2 * peers, 1, SENT_LATER * slots), F32),
            shape((1, 1, SENT_LATER * slots), F32),
            shape((others, ROWS, slots), F32),
            shape((others,), jnp.int32),
        ],
        in_specs=[SMEM] + [VMEM] * 5 + [HBM],
        out_specs=[VMEM] * 5 + [SMEM],
        scratch_shapes=lists
        + [
            weight_shape(others),
            pltpu.VMEM((others, 8, slots), F32),
            pltpu.VMEM((cells, slots, LANES), F32),
            pltpu.VMEM(energy.shape, F32),
            pltpu.SemaphoreType.DMA,
        ]
        + density_work,
        compiler_params=params,
        name="density_remote",
    )(meta, own, rec, rec_odd, acc, left, energy)

    rterm, odd_term = exchange(pay, odd)

    acc, bcol, ccol = pl.pallas_call(
        functools.partial(force_local_kernel, icut, jcut, group, lay),
        out_shape=[shape((cells, 16, slots), F32), wide, wide],
        in_specs=[SMEM] + [VMEM] * 3,
        out_specs=[VMEM] * 3,
        scratch_shapes=lists
        + [
            weight_shape(cells),
            weight_shape(cells),
            pltpu.VMEM((cells, 16, slots), F32),
            pltpu.VMEM((cells, DOT_K, slots), F32),
        ]
        + force_work,
        compiler_params=params,
        name="force_local",
    )(meta, own, term, force_left)

    accel, heat = pl.pallas_call(
        functools.partial(force_remote_kernel, icut, jcut, group, lay),
        out_shape=[shape((3, cells, slots), F32), shape((cells, slots), F32)],
        in_specs=[SMEM] * 2 + [VMEM] * 9,
        out_specs=[VMEM] * 2,
        scratch_shapes=lists
        + [
            weight_shape(others),
            weight_shape(others),
            pltpu.VMEM((others, 16, slots), F32),
            pltpu.VMEM((cells, DOT_K, slots), F32),
        ]
        + force_work,
        compiler_params=params,
        name="force_remote",
    )(meta, live, own, far, term, rterm, odd_term, acc, force_left, bcol, ccol)
    return density, accel, heat


def solution(mesh):
    regions, peers = mesh.devices.shape
    mesh = jax.sharding.Mesh(mesh.devices.reshape(regions // 2, 2, peers), ("pair", "side", "cell"))
    region = ("pair", "side")
    every = (*region, "cell")
    placed = (
        P(None, every, None),
        P(None, every, None),
        P(every, None),
        P(every, None),
        P(every, None),
        P(every),
        P(region, "cell", None, None),
        P(region, "cell", None, None),
        P(region, "cell", None),
    )
    return jax.shard_map(
        on_device,
        mesh=mesh,
        in_specs=placed,
        out_specs=(P(every, None), P(None, every, None), P(every, None)),
        check_vma=False,
    )
```

```python
import functools
import math

import jax
import jax.numpy as jnp
from jax import lax
from jax.experimental import pallas as pl
from jax.experimental.pallas import tpu as pltpu
from jax.sharding import PartitionSpec as P

GAMMA = 5.0 / 3.0
LANES = 128
BF16 = jnp.bfloat16
F32 = jnp.float32

ROWS = 8
TINY = 1e-12
DOT_K = 48
COLS = 64
STRIP = 16
SENT = 4
SENT_LATER = 5

VMEM = pl.BlockSpec(memory_space=pltpu.VMEM)
SMEM = pl.BlockSpec(memory_space=pltpu.SMEM)
HBM = pl.BlockSpec(memory_space=pltpu.HBM)


def row_ids(shape):
    return lax.broadcasted_iota(jnp.int32, shape, 0)


def split3(value):
    first = value.astype(BF16).astype(F32)
    rest = value - first
    second = rest.astype(BF16).astype(F32)
    return first, second, rest - second


def left_parts(value):
    a, b, c = split3(value)
    return jnp.concatenate([a, a, b, b, a, c], axis=0)


def right_parts(value):
    a, b, c = split3(value)
    return jnp.concatenate([a, b, a, b, c, a], axis=0).astype(BF16)


def norm_row(rows):
    return rows[0:1] * rows[0:1] + rows[1:2] * rows[1:2] + rows[2:3] * rows[2:3]


def left_comps(rows):
    ids = row_ids(rows.shape)
    return jnp.where(ids < 3, rows, jnp.where(ids == 3, norm_row(rows), jnp.where(ids == 4, 1.0, 0.0)))


def right_comps(rows):
    ids = row_ids(rows.shape)
    return jnp.where(ids < 3, -2.0 * rows, jnp.where(ids == 3, 1.0, jnp.where(ids == 4, norm_row(rows), 0.0)))


def chunks(count, size):
    return lax.shift_right_logical(count + (size - 1), jnp.int32(size.bit_length() - 1))


class Meta:
    def __init__(self, cells, peers, pairs):
        self.cells, self.peers, self.pairs = cells, peers, pairs
        self.send = cells
        self.pair = cells + peers
        self.edge = self.pair + 2 * pairs
        self.size = self.edge + 2


def prep_kernel(
    lay,
    counts_in, send_in, pairs_in, edge_in, pos_in, vel_in, mass_in, smooth_in,
    own, pay, odd, meta,
    counts, send, pairs, edge, pos, vel, mass, smooth, sems,
):
    inputs = (counts_in, send_in, pairs_in, edge_in, pos_in, vel_in, mass_in, smooth_in)
    buffers = (counts, send, pairs, edge, pos, vel, mass, smooth)
    copies = [
        pltpu.make_async_copy(source, target, sems.at[k])
        for k, (source, target) in enumerate(zip(inputs, buffers))
    ]
    for copy in copies:
        copy.start()
    for copy in copies:
        copy.wait()
    cells = mass.shape[0]
    slots = mass.shape[1]
    for k in range(cells):
        meta[k] = counts[k]
    for k in range(lay.peers):
        meta[lay.send + k] = send[k]
    for k in range(lay.pairs):
        for side in range(2):
            meta[lay.pair + 2 * k + side] = pairs[0, 0, side, k]
    for side in range(2):
        meta[lay.edge + side] = edge[0, 0, side]

    lane = lax.broadcasted_iota(jnp.int32, (1, slots), 1)
    for k in range(cells):
        live = lane < counts[k]
        for d in range(3):
            own[k, d : d + 1, :] = pos[d, k : k + 1, :] - 0.5
            own[k, 5 + d : 6 + d, :] = vel[d, k : k + 1, :]
        own[k, 3:4, :] = jnp.where(live, mass[k : k + 1, :], 0.0)
        own[k, 4:5, :] = smooth[k : k + 1, :]

    def row(cell, r):
        return own[cell, r : r + 1, :]

    fill(lay, pay, odd, meta, SENT, row)


def fill(lay, pay, odd, meta, count, row):
    slots = pay.shape[2] // count
    side = lax.axis_index("side")
    first = side * lay.peers
    pay[...] = jnp.zeros_like(pay)

    def put(out, at, cell, keep):
        for r in range(count):
            value = row(cell, r)
            if keep is not None:
                value = jnp.where(keep, value, 0.0)
            out[at, :, r * slots : (r + 1) * slots] = value

    def peer(k, carry):
        picked = meta[lay.send + k]
        put(pay, first + k, jnp.maximum(picked, 0), picked >= 0)
        return carry

    lax.fori_loop(0, lay.peers, peer, 0)
    put(pay, lay.peers - first + lax.axis_index("cell"), meta[lay.edge + 1 - side], None)
    put(odd, 0, meta[lay.edge + side], None)


def arrivals(lay):
    first = lax.axis_index("side") * lay.peers
    return first, lay.peers - first + lax.axis_index("cell")


class Tiles:
    FIELDS = 7

    def __init__(self, icut, jcut, table):
        self.icut, self.jcut, self.table = icut, jcut, table
        self.count = self.blocks = jnp.int32(0)

    def push(self, a, b, w, ok, i, ni, j, nj):
        at = self.FIELDS * self.count
        for field, value in enumerate((a, b, w, i, ni, j, nj)):
            self.table[at + field] = value
        self.count = self.count + ok.astype(jnp.int32)
        self.blocks = self.blocks + jnp.where(ok, ni * nj, 0)

    def whole(self, a, b, w, ok, alive, blive):
        self.push(a, b, w, ok, 0, chunks(alive, self.icut), 0, chunks(blive, self.jcut))

    def close(self):
        self.push(0, 0, 0, jnp.bool_(False), 0, 1, 0, 1)


def local_tiles(tiles, lay, meta, both):
    cells = lay.cells
    one = jnp.int32(1)

    def key(row):
        first = meta[lay.pair + 2 * row]
        second = meta[lay.pair + 2 * row + 1]
        return jnp.minimum(first, second) * cells + jnp.maximum(first, second)

    keys = [key(row) for row in range(lay.pairs)]
    for a in range(cells):
        for b in range(a + 1, cells):
            mult = jnp.int32(0)
            for pair in keys:
                mult = mult + (pair == a * cells + b).astype(jnp.int32)
            tiles.whole(a, b, mult, mult > 0, meta[a], meta[b])
            if not both:
                tiles.whole(b, a, mult, mult > 0, meta[b], meta[a])
    if not both:
        for a in range(cells):
            tiles.whole(a, a, one, meta[a] > 0, meta[a], meta[a])
        tiles.close()
        return None
    span = tiles.jcut // tiles.icut
    for a in range(cells):
        tiles.push(a, a, one, meta[a] > tiles.jcut, 0, span, 1, chunks(meta[a], tiles.jcut) - 1)
    mutual = tiles.blocks
    for a in range(cells):
        rows = chunks(meta[a], tiles.icut)
        tiles.push(a, a, one, meta[a] > 0, 0, jnp.minimum(rows, span), 0, 1)
        tiles.push(a, a, one, meta[a] > tiles.jcut, span, rows - span, 1, 1)
    tiles.close()
    return mutual


def remote_tiles(tiles, lay, meta, live):
    one = jnp.int32(1)
    for k in range(lay.peers):
        picked = meta[lay.send + k]
        a = jnp.maximum(picked, 0)
        tiles.whole(a, k, one, (picked >= 0) & (live[k] > 0), meta[a], live[k])
    side = lax.axis_index("side")
    for b, edge in ((lay.peers, 1 - side), (lay.peers + 1, side)):
        a = meta[lay.edge + edge]
        tiles.whole(a, b, one, live[b] > 0, meta[a], live[b])
    tiles.close()


class Blocks:
    FIELDS = 5

    def __init__(self, tiles, ring):
        self.icut, self.jcut = tiles.icut, tiles.jcut
        self.table, self.last = tiles.table, tiles.count
        self.ring, self.total = ring, tiles.blocks

    def clear(self, entries):
        for k in range(entries * self.FIELDS):
            self.ring[k] = 0

    def write(self, slot, state):
        n, ii, jj = state
        a, b, w, i, ni, j, nj = (self.table[Tiles.FIELDS * n + k] for k in range(Tiles.FIELDS))
        for field, value in enumerate((a, b, (i + ii) * self.icut, (j + jj) * self.jcut, w)):
            self.ring[self.FIELDS * slot + field] = value
        jwrap = jj + 1 >= nj
        inext = jnp.where(jwrap, ii + 1, ii)
        iwrap = inext >= ni
        return (
            jnp.minimum(jnp.where(iwrap, n + 1, n), self.last),
            jnp.where(iwrap, 0, inext),
            jnp.where(jwrap, 0, jj + 1),
        )

    def read(self, slot):
        a, b, istart, jstart, w = (self.ring[self.FIELDS * slot + k] for k in range(self.FIELDS))
        return (
            a,
            b,
            pl.multiple_of(istart, self.icut),
            pl.multiple_of(jstart, self.jcut),
            w.astype(F32),
        )

    def distances(self, slot, left, right, out):
        a, b, istart, jstart, _ = self.read(slot)
        out[...] = jnp.dot(
            left[a, pl.ds(istart, self.icut), :DOT_K],
            right[b, :, pl.ds(jstart, self.jcut)],
            preferred_element_type=F32,
        )


def density_loop(group, blocks, total, left, right, mrow, acc, work):
    icut, jcut = blocks.icut, blocks.jcut
    dist, parts = work[:group], work[group:]
    zero = jnp.int32(0)
    state = (zero, zero, zero)
    for g in range(2 * group):
        state = blocks.write(g, state)
    for g in range(group):
        blocks.distances(g, left, right, dist[g])

    def step(k, state):
        for g in range(group):
            _, b, _, jstart, w = blocks.read(k * group + g)
            weight = mrow[b, :, pl.ds(jstart, jcut)] * w
            weight = jnp.concatenate([weight] * (STRIP // 8), axis=0)
            for row in range(0, icut, STRIP):
                s = jnp.maximum(dist[g][row : row + STRIP, :], TINY)
                q = s * lax.rsqrt(s)
                e = 1.0 - q
                u = jnp.maximum(e, 0.0)
                t = jnp.minimum(0.5 - (s * 3.0) * e, u * u * u) * weight
                part = t[:, :LANES]
                for at in range(1, jcut // LANES):
                    part = part + t[:, at * LANES : (at + 1) * LANES]
                parts[g][row : row + STRIP, :] = part

            state = blocks.write((k + 2) * group + g, state)
            blocks.distances((k + 1) * group + g, left, right, dist[g])
        for g in range(group):
            a, _, istart, _, _ = blocks.read(k * group + g)
            acc[a, pl.ds(istart, icut), :] += parts[g][...]
        return state

    lax.fori_loop(0, chunks(total, group), step, state)


def density_source(rows, right, mrow, at):
    right[at] = right_parts(right_comps(rows))
    mrow[at] = jnp.broadcast_to(rows[3:4], mrow.shape[1:])


def spread_left(parts, left, cell):
    for at in range(parts.shape[1] // LANES):
        left[cell, pl.ds(at * LANES, LANES), :] = parts[:, at * LANES : (at + 1) * LANES].T.astype(BF16)


def force_scales(rows):
    h = rows[4:5]
    inv = 1.0 / jnp.where(h > 0.0, h, 1.0)
    b = math.sqrt(24.0 / math.pi) * (inv * inv)
    return b, b * inv


def density_local_kernel(
    icut, jcut, group, lay, meta, own, acc, left, force_left, table, ring, right, mrow, *work
):
    slots = own.shape[2]
    ids = row_ids((8, slots))
    empty = jnp.zeros((8, slots), F32)
    for k in range(lay.cells):
        rows = own[k]
        inv = 1.0 / rows[4:5]
        comps = left_comps(rows)
        spread_left(jnp.concatenate([left_parts(comps * (inv * inv)), empty, empty], axis=0), left, k)
        scales = empty
        for at, part in enumerate(x for scale in force_scales(rows) for x in split3(scale)):
            scales = jnp.where(ids == at, part, scales)
        spread_left(jnp.concatenate([left_parts(comps), scales, empty], axis=0), force_left, k)
        density_source(rows, right, mrow, k)
        acc[k] = jnp.zeros((slots, LANES), F32)
    tiles = Tiles(icut, jcut, table)
    local_tiles(tiles, lay, meta, False)
    blocks = Blocks(tiles, ring)
    density_loop(group, blocks, tiles.blocks, left, right, mrow, acc, work)


def density_remote_kernel(
    icut, jcut, group, lay,
    meta, own, rec, rec_odd, acc_in, left, energy_in,
    rho_out, term_out, pay, odd, far, live,
    table, ring, right, mrow, acc, energy, sem, *work,
):
    cells, peers = lay.cells, lay.peers
    slots = own.shape[2]
    copy = pltpu.make_async_copy(energy_in, energy, sem)
    copy.start()
    first, face = arrivals(lay)
    ids = row_ids((8, slots))

    def receive(got, at, k):
        rows = jnp.zeros((8, slots), F32)
        for r in range(SENT):
            rows = jnp.where(ids == r, got[at, :, r * slots : (r + 1) * slots], rows)
        far[k] = rows
        density_source(rows, right, mrow, k)

    def rec_cell(k, carry):
        receive(rec, first + k, k)
        return carry

    lax.fori_loop(0, peers, rec_cell, 0, unroll=4)
    receive(rec, face, peers)
    receive(rec_odd, 0, peers + 1)
    occupied = jnp.sum(jnp.where(far[:, 3, :] > 0.0, 1.0, 0.0), axis=1, keepdims=True)
    for k in range(peers + 2):
        live[k] = occupied[k, 0].astype(jnp.int32)
    acc[...] = acc_in[...]
    tiles = Tiles(icut, jcut, table)
    remote_tiles(tiles, lay, meta, live)
    blocks = Blocks(tiles, ring)
    density_loop(group, blocks, tiles.blocks, left, right, mrow, acc, work)

    copy.wait()
    lane = lax.broadcasted_iota(jnp.int32, (1, slots), 1)
    ones = jnp.ones((8, LANES), BF16)
    for k in range(cells):
        one, two, three = split3(acc[k])
        total_row = jnp.zeros((8, slots), F32)
        for part in (three, two, one):
            total_row = total_row + lax.dot_general(
                ones, part.astype(BF16), (((1,), (1,)), ((), ())), preferred_element_type=F32
            )
        inv = 1.0 / own[k, 4:5, :]
        rho = total_row[0:1] * (16.0 / math.pi) * (inv * inv * inv)
        occupied = jnp.where(lane < meta[k], 1.0, 0.0)
        rho_out[k : k + 1, :] = rho * occupied
        term_out[k] = occupied * (GAMMA - 1.0) * energy[k : k + 1, :] / (rho + 1.0 - occupied)

    def row(cell, r):
        return term_out[cell] if r == 0 else own[cell, 3 + r : 4 + r, :]

    fill(lay, pay, odd, meta, SENT_LATER, row)


def force_source(rows, pressure, right, weights, scale, at):
    slots = rows.shape[1]
    right[at] = right_parts(right_comps(rows))
    b, c = force_scales(rows)
    scale[at] = jnp.concatenate([jnp.broadcast_to(b, (8, slots)), jnp.broadcast_to(c, (8, slots))], axis=0)
    m = rows[3:4]
    mp = m * pressure
    xv = rows[0:1] * rows[5:6] + rows[1:2] * rows[6:7] + rows[2:3] * rows[7:8]
    ids = row_ids((8, slots))
    base = jnp.where(ids == 3, 1.0, jnp.where(ids == 4, xv, rows))
    sums = jnp.concatenate([base * m, jnp.where(ids < 4, base, 0.0) * mp], axis=0)
    one, two, three = split3(sums)
    weights[at] = jnp.concatenate([one, two, three], axis=0).astype(BF16)


def force_loop(group, blocks, total, local, left, right, weights, scale, bcol, ccol, acc, work):
    icut, jcut = blocks.icut, blocks.jcut
    dist, upper, lower = work[:group], work[group : 2 * group], work[2 * group :]
    blocks.clear(group)
    for ref in (*upper, *lower):
        ref[...] = jnp.zeros_like(ref)
    zero = jnp.int32(0)
    state = (zero, zero, zero)
    for g in range(2 * group):
        state = blocks.write(group + g, state)
    for g in range(group):
        blocks.distances(group + g, left, right, dist[g])

    def sums_of(rows, columns, k, g):
        a, b, istart, jstart, w = blocks.read(k * group + g)
        adds = []
        if rows:
            wt = weights[b, :, pl.ds(jstart, jcut)]
            spec = (((1,), (1,)), ((), ()))
            part = lax.dot_general(wt, upper[g][...], spec, preferred_element_type=F32)
            part = part + lax.dot_general(wt, lower[g][...], spec, preferred_element_type=F32)
            keep = w
            if columns:
                keep = jnp.where(k * group + g < local + group, w, 0.0)
            adds.append((a, istart, part * keep))
        if columns:
            wt = weights[a, :, pl.ds(istart, icut)]
            part = jnp.dot(wt, upper[g][...], preferred_element_type=F32)
            part = part + jnp.dot(wt, lower[g][...], preferred_element_type=F32)
            adds.append((b, jstart, part * w))
        return adds

    def store(adds):
        for cell, start, part in adds:
            acc[cell, :, pl.ds(start, part.shape[1])] += part

    def step(rows, columns, k, state):
        adds = []
        for g in range(group):
            adds += sums_of(rows, columns, k, g)

            a, b, istart, jstart, _ = blocks.read((k + 1) * group + g)
            bj = jnp.concatenate([scale[b, 0:8, pl.ds(jstart, jcut)]] * (STRIP // 8), axis=0)
            cj = jnp.concatenate([scale[b, 8:16, pl.ds(jstart, jcut)]] * (STRIP // 8), axis=0)
            for row in range(0, icut, STRIP):
                s = jnp.maximum(dist[g][row : row + STRIP, :], TINY)
                r = lax.rsqrt(s)
                d = s * r
                bi = bcol[a, pl.ds(istart + row, STRIP), :]
                ci = ccol[a, pl.ds(istart + row, STRIP), :]
                bi = jnp.concatenate([bi] * (jcut // LANES), axis=1)
                ci = jnp.concatenate([ci] * (jcut // LANES), axis=1)
                t = ci * d
                u = jnp.maximum(bi - t, 0.0)
                v = jnp.minimum(t, u)
                slope = (u + u - v) * v
                t = cj * d
                u = jnp.maximum(bj - t, 0.0)
                v = jnp.minimum(t, u)
                slope = (slope + (u + u - v) * v) * r
                rounded = slope.astype(BF16)
                upper[g][row : row + STRIP, :] = rounded
                lower[g][row : row + STRIP, :] = (slope - rounded.astype(F32)).astype(BF16)

            state = blocks.write((k + 3) * group + g, state)
            blocks.distances((k + 2) * group + g, left, right, dist[g])
        store(adds)
        return state

    steps = chunks(total, group)
    adds = []
    if local is None:
        lax.fori_loop(0, steps, functools.partial(step, True, False), state)
        for g in range(group):
            adds += sums_of(True, False, steps, g)
    else:
        first = jnp.minimum(chunks(local, group) + 1, steps)
        state = lax.fori_loop(0, first, functools.partial(step, True, True), state)
        lax.fori_loop(first, steps, functools.partial(step, False, True), state)
        for g in range(group):
            adds += sums_of(True, True, steps, g)
    store(adds)


def force_local_kernel(
    icut, jcut, group, lay,
    meta, own, term, left,
    acc_out, bcol, ccol,
    table, ring, right, weights, scale, acc, *work,
):
    slots = own.shape[2]
    part = lax.broadcasted_iota(jnp.int32, (COLS, 2 * LANES), 0) - DOT_K
    lane = lax.broadcasted_iota(jnp.int32, (COLS, 2 * LANES), 1)
    of_b = (part >= 0) & (part < 3) & (lane < LANES)
    of_c = (part >= 3) & (part < 6) & (lane >= LANES)
    pick = jnp.where(of_b | of_c, 1.0, 0.0).astype(BF16)
    for k in range(lay.cells):
        force_source(own[k], term[k], right, weights, scale, k)
        acc[k] = jnp.zeros((DOT_K, slots), F32)
        for at in range(slots // LANES):
            here = pl.ds(at * LANES, LANES)
            both = jnp.dot(left[k, here, :], pick, preferred_element_type=F32)
            bcol[k, here, :] = both[:, :LANES]
            ccol[k, here, :] = both[:, LANES:]
    tiles = Tiles(icut, jcut, table)
    local = local_tiles(tiles, lay, meta, True)
    blocks = Blocks(tiles, ring)
    force_loop(
        group, blocks, tiles.blocks, local, left, right, weights, scale, bcol, ccol, acc, work
    )
    for k in range(lay.cells):
        acc_out[k] = acc[k, 0:16, :] + (acc[k, 16:32, :] + acc[k, 32:48, :])


def force_remote_kernel(
    icut, jcut, group, lay,
    meta, live, own, far, term, rterm, odd_term, acc_in, left, bcol, ccol,
    accel_out, heat_out,
    table, ring, right, weights, scale, acc, *work,
):
    cells, peers = lay.cells, lay.peers
    slots = own.shape[2]
    first, face = arrivals(lay)
    ids = row_ids((8, slots))

    def receive(got, at, k):
        rows = far[k]
        for r in range(1, SENT_LATER):
            rows = jnp.where(ids == 3 + r, got[at, :, r * slots : (r + 1) * slots], rows)
        force_source(rows, got[at, :, :slots], right, weights, scale, k)

    def rec_cell(k, carry):
        receive(rterm, first + k, k)
        return carry

    lax.fori_loop(0, peers, rec_cell, 0, unroll=4)
    receive(rterm, face, peers)
    receive(odd_term, 0, peers + 1)
    acc[...] = jnp.zeros_like(acc)
    tiles = Tiles(icut, jcut, table)
    remote_tiles(tiles, lay, meta, live)
    blocks = Blocks(tiles, ring)
    force_loop(
        group, blocks, tiles.blocks, None, left, right, weights, scale, bcol, ccol, acc, work
    )

    lane = lax.broadcasted_iota(jnp.int32, (1, slots), 1)
    for k in range(cells):
        occupied = jnp.where(lane < meta[k], 1.0, 0.0)
        sums = acc_in[k] + acc[k, 0:16, :] + (acc[k, 16:32, :] + acc[k, 32:48, :])
        pressure = term[k]
        x = [own[k, d : d + 1, :] for d in range(3)]
        v = [own[k, 5 + d : 6 + d, :] for d in range(3)]
        both = pressure * sums[3:4] + sums[11:12]
        for d in range(3):
            accel_out[d, k : k + 1, :] = occupied * (
                x[d] * both - pressure * sums[d : d + 1] - sums[8 + d : 9 + d]
            )
        xv = x[0] * v[0] + x[1] * v[1] + x[2] * v[2]
        total_heat = xv * sums[3:4] + sums[4:5]
        for d in range(3):
            total_heat = total_heat - v[d] * sums[d : d + 1] - x[d] * sums[5 + d : 6 + d]
        heat_out[k : k + 1, :] = -occupied * pressure * total_heat


def on_device(positions, velocities, mass, smoothing, energy, counts, send, pairs, edge):
    cells, slots = mass.shape
    peers = send.shape[2]
    regions = 2 * lax.axis_size("pair")
    lay = Meta(cells, peers, pairs.shape[2])
    others = peers + 2
    most = max(cells * (cells - 1) // 2 + 3 * cells, cells * cells, others) + 1
    icut, jcut, group = 128, slots // 2, 8
    ring = Blocks.FIELDS * (most * (slots // icut) * (slots // jcut) + 6 * group)
    shape = jax.ShapeDtypeStruct
    params = pltpu.CompilerParams(vmem_limit_bytes=20 * 1024 * 1024)
    send = send.reshape(peers)
    pairs = jnp.transpose(pairs, (0, 1, 3, 2))
    integers = (counts, send, pairs, edge)
    floats = (positions, velocities, mass, smoothing)
    integers, floats, energy = jax.tree.map(
        lambda x: pltpu.with_memory_space_constraint(x, pltpu.HBM), (integers, floats, energy)
    )
    lists = [pltpu.SMEM((Tiles.FIELDS * most,), jnp.int32), pltpu.SMEM((ring,), jnp.int32)]
    density_work = [pltpu.VMEM((icut, jcut), F32)] * group + [pltpu.VMEM((icut, LANES), F32)] * group
    force_work = [pltpu.VMEM((icut, jcut), F32)] * group + [pltpu.VMEM((icut, jcut), BF16)] * (2 * group)
    wide = shape((cells, slots, LANES), F32)
    left_shape = shape((cells, slots, COLS), BF16)
    weight_shape = lambda count: pltpu.VMEM((count, DOT_K, slots), BF16)

    def exchange(pay, odd):
        between = [(r, r + 1) for r in range(1, regions - 1, 2)]
        swap = between + [(b, a) for a, b in between]
        got_odd = lax.ppermute(odd, ("pair", "side"), swap)
        return lax.all_to_all(pay, ("side", "cell"), split_axis=0, concat_axis=0, tiled=True), got_odd

    own, pay, odd, meta = pl.pallas_call(
        functools.partial(prep_kernel, lay),
        out_shape=[
            shape((cells, ROWS, slots), F32),
            shape((2 * peers, 1, SENT * slots), F32),
            shape((1, 1, SENT * slots), F32),
            shape((lay.size,), jnp.int32),
        ],
        in_specs=[HBM] * 8,
        out_specs=[VMEM] * 3 + [SMEM],
        scratch_shapes=[pltpu.SMEM(x.shape, jnp.int32) for x in integers]
        + [pltpu.VMEM(x.shape, F32) for x in floats]
        + [pltpu.SemaphoreType.DMA((8,))],
        compiler_params=params,
        name="prep",
    )(*integers, *floats)

    rec, rec_odd = exchange(pay, odd)

    acc, left, force_left = pl.pallas_call(
        functools.partial(density_local_kernel, icut, jcut, group, lay),
        out_shape=[wide, left_shape, left_shape],
        in_specs=[SMEM, VMEM],
        out_specs=[VMEM] * 3,
        scratch_shapes=lists + [weight_shape(cells), pltpu.VMEM((cells, 8, slots), F32)] + density_work,
        compiler_params=params,
        name="density_local",
    )(meta, own)

    density, term, pay, odd, far, live = pl.pallas_call(
        functools.partial(density_remote_kernel, icut, jcut, group, lay),
        out_shape=[
            shape((cells, slots), F32),
            shape((cells, 1, slots), F32),
            shape((2 * peers, 1, SENT_LATER * slots), F32),
            shape((1, 1, SENT_LATER * slots), F32),
            shape((others, ROWS, slots), F32),
            shape((others,), jnp.int32),
        ],
        in_specs=[SMEM] + [VMEM] * 5 + [HBM],
        out_specs=[VMEM] * 5 + [SMEM],
        scratch_shapes=lists
        + [
            weight_shape(others),
            pltpu.VMEM((others, 8, slots), F32),
            pltpu.VMEM((cells, slots, LANES), F32),
            pltpu.VMEM(energy.shape, F32),
            pltpu.SemaphoreType.DMA,
        ]
        + density_work,
        compiler_params=params,
        name="density_remote",
    )(meta, own, rec, rec_odd, acc, left, energy)

    rterm, odd_term = exchange(pay, odd)

    acc, bcol, ccol = pl.pallas_call(
        functools.partial(force_local_kernel, icut, jcut, group, lay),
        out_shape=[shape((cells, 16, slots), F32), wide, wide],
        in_specs=[SMEM] + [VMEM] * 3,
        out_specs=[VMEM] * 3,
        scratch_shapes=lists
        + [
            weight_shape(cells),
            weight_shape(cells),
            pltpu.VMEM((cells, 16, slots), F32),
            pltpu.VMEM((cells, DOT_K, slots), F32),
        ]
        + force_work,
        compiler_params=params,
        name="force_local",
    )(meta, own, term, force_left)

    accel, heat = pl.pallas_call(
        functools.partial(force_remote_kernel, icut, jcut, group, lay),
        out_shape=[shape((3, cells, slots), F32), shape((cells, slots), F32)],
        in_specs=[SMEM] * 2 + [VMEM] * 9,
        out_specs=[VMEM] * 2,
        scratch_shapes=lists
        + [
            weight_shape(others),
            weight_shape(others),
            pltpu.VMEM((others, 16, slots), F32),
            pltpu.VMEM((cells, DOT_K, slots), F32),
        ]
        + force_work,
        compiler_params=params,
        name="force_remote",
    )(meta, live, own, far, term, rterm, odd_term, acc, force_left, bcol, ccol)
    return density, accel, heat


def solution(mesh):
    regions, peers = mesh.devices.shape
    mesh = jax.sharding.Mesh(mesh.devices.reshape(regions // 2, 2, peers), ("pair", "side", "cell"))
    region = ("pair", "side")
    every = (*region, "cell")
    placed = (
        P(None, every, None),
        P(None, every, None),
        P(every, None),
        P(every, None),
        P(every, None),
        P(every),
        P(region, "cell", None, None),
        P(region, "cell", None, None),
        P(region, "cell", None),
    )
    return jax.shard_map(
        on_device,
        mesh=mesh,
        in_specs=placed,
        out_specs=(P(every, None), P(None, every, None), P(every, None)),
        check_vma=False,
    )
```

```python
import functools
import math

import jax
import jax.numpy as jnp
from jax import lax
from jax.experimental import pallas as pl
from jax.experimental.pallas import tpu as pltpu
from jax.sharding import PartitionSpec as P

GAMMA = 5.0 / 3.0
LANES = 128
BF16 = jnp.bfloat16
F32 = jnp.float32

ROWS = 8
TINY = 1e-12
DOT_K = 48
COLS = 64
STRIP = 16
SENT = 4
SENT_LATER = 5

VMEM = pl.BlockSpec(memory_space=pltpu.VMEM)
SMEM = pl.BlockSpec(memory_space=pltpu.SMEM)
HBM = pl.BlockSpec(memory_space=pltpu.HBM)


def row_ids(shape):
    return lax.broadcasted_iota(jnp.int32, shape, 0)


def split3(value):
    first = value.astype(BF16).astype(F32)
    rest = value - first
    second = rest.astype(BF16).astype(F32)
    return first, second, rest - second


def left_parts(value):
    a, b, c = split3(value)
    return jnp.concatenate([a, a, b, b, a, c], axis=0)


def right_parts(value):
    a, b, c = split3(value)
    return jnp.concatenate([a, b, a, b, c, a], axis=0).astype(BF16)


def norm_row(rows):
    return rows[0:1] * rows[0:1] + rows[1:2] * rows[1:2] + rows[2:3] * rows[2:3]


def left_comps(rows):
    ids = row_ids(rows.shape)
    return jnp.where(ids < 3, rows, jnp.where(ids == 3, norm_row(rows), jnp.where(ids == 4, 1.0, 0.0)))


def right_comps(rows):
    ids = row_ids(rows.shape)
    return jnp.where(ids < 3, -2.0 * rows, jnp.where(ids == 3, 1.0, jnp.where(ids == 4, norm_row(rows), 0.0)))


def chunks(count, size):
    return lax.shift_right_logical(count + (size - 1), jnp.int32(size.bit_length() - 1))


class Meta:
    def __init__(self, cells, peers, pairs):
        self.cells, self.peers, self.pairs = cells, peers, pairs
        self.send = cells
        self.pair = cells + peers
        self.edge = self.pair + 2 * pairs
        self.size = self.edge + 2


def prep_kernel(
    lay,
    counts_in, send_in, pairs_in, edge_in, pos_in, vel_in, mass_in, smooth_in,
    own, pay, odd, meta,
    counts, send, pairs, edge, pos, vel, mass, smooth, sems,
):
    inputs = (counts_in, send_in, pairs_in, edge_in, pos_in, vel_in, mass_in, smooth_in)
    buffers = (counts, send, pairs, edge, pos, vel, mass, smooth)
    copies = [
        pltpu.make_async_copy(source, target, sems.at[k])
        for k, (source, target) in enumerate(zip(inputs, buffers))
    ]
    for copy in copies:
        copy.start()
    for copy in copies:
        copy.wait()
    cells = mass.shape[0]
    slots = mass.shape[1]
    for k in range(cells):
        meta[k] = counts[k]
    for k in range(lay.peers):
        meta[lay.send + k] = send[k]
    for k in range(lay.pairs):
        for side in range(2):
            meta[lay.pair + 2 * k + side] = pairs[0, 0, side, k]
    for side in range(2):
        meta[lay.edge + side] = edge[0, 0, side]

    lane = lax.broadcasted_iota(jnp.int32, (1, slots), 1)
    for k in range(cells):
        live = lane < counts[k]
        for d in range(3):
            own[k, d : d + 1, :] = pos[d, k : k + 1, :] - 0.5
            own[k, 5 + d : 6 + d, :] = vel[d, k : k + 1, :]
        own[k, 3:4, :] = jnp.where(live, mass[k : k + 1, :], 0.0)
        own[k, 4:5, :] = smooth[k : k + 1, :]

    def row(cell, r):
        return own[cell, r : r + 1, :]

    fill(lay, pay, odd, meta, SENT, row)


def fill(lay, pay, odd, meta, count, row):
    slots = pay.shape[2] // count
    side = lax.axis_index("side")
    first = side * lay.peers
    pay[...] = jnp.zeros_like(pay)

    def put(out, at, cell, keep):
        for r in range(count):
            value = row(cell, r)
            if keep is not None:
                value = jnp.where(keep, value, 0.0)
            out[at, :, r * slots : (r + 1) * slots] = value

    def peer(k, carry):
        picked = meta[lay.send + k]
        put(pay, first + k, jnp.maximum(picked, 0), picked >= 0)
        return carry

    lax.fori_loop(0, lay.peers, peer, 0)
    put(pay, lay.peers - first + lax.axis_index("cell"), meta[lay.edge + 1 - side], None)
    put(odd, 0, meta[lay.edge + side], None)


def arrivals(lay):
    first = lax.axis_index("side") * lay.peers
    return first, lay.peers - first + lax.axis_index("cell")


class Tiles:
    FIELDS = 7

    def __init__(self, icut, jcut, table):
        self.icut, self.jcut, self.table = icut, jcut, table
        self.count = self.blocks = jnp.int32(0)

    def push(self, a, b, w, ok, i, ni, j, nj):
        at = self.FIELDS * self.count
        for field, value in enumerate((a, b, w, i, ni, j, nj)):
            self.table[at + field] = value
        self.count = self.count + ok.astype(jnp.int32)
        self.blocks = self.blocks + jnp.where(ok, ni * nj, 0)

    def whole(self, a, b, w, ok, alive, blive):
        self.push(a, b, w, ok, 0, chunks(alive, self.icut), 0, chunks(blive, self.jcut))

    def close(self):
        self.push(0, 0, 0, jnp.bool_(False), 0, 1, 0, 1)


def local_tiles(tiles, lay, meta, both):
    cells = lay.cells
    one = jnp.int32(1)

    def key(row):
        first = meta[lay.pair + 2 * row]
        second = meta[lay.pair + 2 * row + 1]
        return jnp.minimum(first, second) * cells + jnp.maximum(first, second)

    keys = [key(row) for row in range(lay.pairs)]
    for a in range(cells):
        for b in range(a + 1, cells):
            mult = jnp.int32(0)
            for pair in keys:
                mult = mult + (pair == a * cells + b).astype(jnp.int32)
            tiles.whole(a, b, mult, mult > 0, meta[a], meta[b])
            if not both:
                tiles.whole(b, a, mult, mult > 0, meta[b], meta[a])
    if not both:
        for a in range(cells):
            tiles.whole(a, a, one, meta[a] > 0, meta[a], meta[a])
        tiles.close()
        return None
    span = tiles.jcut // tiles.icut
    for a in range(cells):
        tiles.push(a, a, one, meta[a] > tiles.jcut, 0, span, 1, chunks(meta[a], tiles.jcut) - 1)
    mutual = tiles.blocks
    for a in range(cells):
        rows = chunks(meta[a], tiles.icut)
        tiles.push(a, a, one, meta[a] > 0, 0, jnp.minimum(rows, span), 0, 1)
        tiles.push(a, a, one, meta[a] > tiles.jcut, span, rows - span, 1, 1)
    tiles.close()
    return mutual


def remote_tiles(tiles, lay, meta, live, across):
    one = jnp.int32(1)

    def add(own, k, ok):
        if across:
            tiles.whole(k, own, one, ok, live[k], meta[own])
        else:
            tiles.whole(own, k, one, ok, meta[own], live[k])

    for k in range(lay.peers):
        picked = meta[lay.send + k]
        add(jnp.maximum(picked, 0), k, (picked >= 0) & (live[k] > 0))
    side = lax.axis_index("side")
    for k, edge in ((lay.peers, 1 - side), (lay.peers + 1, side)):
        add(meta[lay.edge + edge], k, live[k] > 0)
    tiles.close()


class Blocks:
    FIELDS = 5

    def __init__(self, tiles, ring):
        self.icut, self.jcut = tiles.icut, tiles.jcut
        self.table, self.last = tiles.table, tiles.count
        self.ring, self.total = ring, tiles.blocks

    def clear(self, entries):
        for k in range(entries * self.FIELDS):
            self.ring[k] = 0

    def write(self, slot, state):
        n, ii, jj = state
        a, b, w, i, ni, j, nj = (self.table[Tiles.FIELDS * n + k] for k in range(Tiles.FIELDS))
        for field, value in enumerate((a, b, (i + ii) * self.icut, (j + jj) * self.jcut, w)):
            self.ring[self.FIELDS * slot + field] = value
        jwrap = jj + 1 >= nj
        inext = jnp.where(jwrap, ii + 1, ii)
        iwrap = inext >= ni
        return (
            jnp.minimum(jnp.where(iwrap, n + 1, n), self.last),
            jnp.where(iwrap, 0, inext),
            jnp.where(jwrap, 0, jj + 1),
        )

    def read(self, slot):
        a, b, istart, jstart, w = (self.ring[self.FIELDS * slot + k] for k in range(self.FIELDS))
        return (
            a,
            b,
            pl.multiple_of(istart, self.icut),
            pl.multiple_of(jstart, self.jcut),
            w.astype(F32),
        )

    def distances(self, slot, left, right, out):
        a, b, istart, jstart, _ = self.read(slot)
        out[...] = jnp.dot(
            left[a, pl.ds(istart, self.icut), :DOT_K],
            right[b, :, pl.ds(jstart, self.jcut)],
            preferred_element_type=F32,
        )


def density_loop(group, blocks, total, left, right, mrow, acc, work):
    icut, jcut = blocks.icut, blocks.jcut
    dist, parts = work[:group], work[group:]
    zero = jnp.int32(0)
    state = (zero, zero, zero)
    for g in range(2 * group):
        state = blocks.write(g, state)
    for g in range(group):
        blocks.distances(g, left, right, dist[g])

    def step(k, state):
        for g in range(group):
            _, b, _, jstart, w = blocks.read(k * group + g)
            weight = mrow[b, :, pl.ds(jstart, jcut)] * w
            weight = jnp.concatenate([weight] * (STRIP // 8), axis=0)
            for row in range(0, icut, STRIP):
                s = jnp.maximum(dist[g][row : row + STRIP, :], TINY)
                q = s * lax.rsqrt(s)
                e = 1.0 - q
                u = jnp.maximum(e, 0.0)
                t = jnp.minimum(0.5 - (s * 3.0) * e, u * u * u) * weight
                part = t[:, :LANES]
                for at in range(1, jcut // LANES):
                    part = part + t[:, at * LANES : (at + 1) * LANES]
                parts[g][row : row + STRIP, :] = part

            state = blocks.write((k + 2) * group + g, state)
            blocks.distances((k + 1) * group + g, left, right, dist[g])
        for g in range(group):
            a, _, istart, _, _ = blocks.read(k * group + g)
            acc[a, pl.ds(istart, icut), :] += parts[g][...]
        return state

    lax.fori_loop(0, chunks(total, group), step, state)


def density_source(rows, right, mrow, at):
    right[at] = right_parts(right_comps(rows))
    mrow[at] = jnp.broadcast_to(rows[3:4], mrow.shape[1:])


def spread_left(parts, left, cell):
    for at in range(parts.shape[1] // LANES):
        left[cell, pl.ds(at * LANES, LANES), :] = parts[:, at * LANES : (at + 1) * LANES].T.astype(BF16)


def force_scales(rows):
    h = rows[4:5]
    inv = 1.0 / jnp.where(h > 0.0, h, 1.0)
    b = math.sqrt(24.0 / math.pi) * (inv * inv)
    return b, b * inv


def force_columns(rows, left, at):
    empty = jnp.zeros(rows.shape, F32)
    ids = row_ids(rows.shape)
    scales = empty
    for field, part in enumerate(x for scale in force_scales(rows) for x in split3(scale)):
        scales = jnp.where(ids == field, part, scales)
    spread_left(jnp.concatenate([left_parts(left_comps(rows)), scales, empty], axis=0), left, at)


def scale_picker():
    part = lax.broadcasted_iota(jnp.int32, (COLS, 2 * LANES), 0) - DOT_K
    lane = lax.broadcasted_iota(jnp.int32, (COLS, 2 * LANES), 1)
    of_b = (part >= 0) & (part < 3) & (lane < LANES)
    of_c = (part >= 3) & (part < 6) & (lane >= LANES)
    return jnp.where(of_b | of_c, 1.0, 0.0).astype(BF16)


def scale_columns(left, pick, bcol, ccol, at):
    for chunk in range(left.shape[1] // LANES):
        here = pl.ds(chunk * LANES, LANES)
        both = jnp.dot(left[at, here, :], pick, preferred_element_type=F32)
        bcol[at, here, :] = both[:, :LANES]
        ccol[at, here, :] = both[:, LANES:]


def density_local_kernel(
    icut, jcut, group, lay, meta, own, acc, left, force_left, table, ring, right, mrow, *work
):
    slots = own.shape[2]
    empty = jnp.zeros((8, slots), F32)
    for k in range(lay.cells):
        rows = own[k]
        inv = 1.0 / rows[4:5]
        parts = left_parts(left_comps(rows) * (inv * inv))
        spread_left(jnp.concatenate([parts, empty, empty], axis=0), left, k)
        force_columns(rows, force_left, k)
        density_source(rows, right, mrow, k)
        acc[k] = jnp.zeros((slots, LANES), F32)
    tiles = Tiles(icut, jcut, table)
    local_tiles(tiles, lay, meta, False)
    blocks = Blocks(tiles, ring)
    density_loop(group, blocks, tiles.blocks, left, right, mrow, acc, work)


def density_remote_kernel(
    icut, jcut, group, lay,
    meta, own, rec, rec_odd, acc_in, left, energy_in,
    rho_out, term_out, pay, odd, far, live,
    table, ring, right, mrow, acc, energy, sem, *work,
):
    cells, peers = lay.cells, lay.peers
    slots = own.shape[2]
    copy = pltpu.make_async_copy(energy_in, energy, sem)
    copy.start()
    first, face = arrivals(lay)
    ids = row_ids((8, slots))

    def receive(got, at, k):
        rows = jnp.zeros((8, slots), F32)
        for r in range(SENT):
            rows = jnp.where(ids == r, got[at, :, r * slots : (r + 1) * slots], rows)
        far[k] = rows
        density_source(rows, right, mrow, k)

    def rec_cell(k, carry):
        receive(rec, first + k, k)
        return carry

    lax.fori_loop(0, peers, rec_cell, 0, unroll=4)
    receive(rec, face, peers)
    receive(rec_odd, 0, peers + 1)
    occupied = jnp.sum(jnp.where(far[:, 3, :] > 0.0, 1.0, 0.0), axis=1, keepdims=True)
    for k in range(peers + 2):
        live[k] = occupied[k, 0].astype(jnp.int32)
    acc[...] = acc_in[...]
    tiles = Tiles(icut, jcut, table)
    remote_tiles(tiles, lay, meta, live, False)
    blocks = Blocks(tiles, ring)
    density_loop(group, blocks, tiles.blocks, left, right, mrow, acc, work)

    copy.wait()
    lane = lax.broadcasted_iota(jnp.int32, (1, slots), 1)
    ones = jnp.ones((8, LANES), BF16)
    for k in range(cells):
        one, two, three = split3(acc[k])
        total_row = jnp.zeros((8, slots), F32)
        for part in (three, two, one):
            total_row = total_row + lax.dot_general(
                ones, part.astype(BF16), (((1,), (1,)), ((), ())), preferred_element_type=F32
            )
        inv = 1.0 / own[k, 4:5, :]
        rho = total_row[0:1] * (16.0 / math.pi) * (inv * inv * inv)
        occupied = jnp.where(lane < meta[k], 1.0, 0.0)
        rho_out[k : k + 1, :] = rho * occupied
        term_out[k] = occupied * (GAMMA - 1.0) * energy[k : k + 1, :] / (rho + 1.0 - occupied)

    def row(cell, r):
        return term_out[cell] if r == 0 else own[cell, 3 + r : 4 + r, :]

    fill(lay, pay, odd, meta, SENT_LATER, row)


def force_lanes(rows, right, scale, at):
    slots = rows.shape[1]
    right[at] = right_parts(right_comps(rows))
    b, c = force_scales(rows)
    scale[at] = jnp.concatenate([jnp.broadcast_to(b, (8, slots)), jnp.broadcast_to(c, (8, slots))], axis=0)


def force_weights(rows, pressure, weights, at):
    m = rows[3:4]
    mp = m * pressure
    xv = rows[0:1] * rows[5:6] + rows[1:2] * rows[6:7] + rows[2:3] * rows[7:8]
    ids = row_ids(rows.shape)
    base = jnp.where(ids == 3, 1.0, jnp.where(ids == 4, xv, rows))
    sums = jnp.concatenate([base * m, jnp.where(ids < 4, base, 0.0) * mp], axis=0)
    one, two, three = split3(sums)
    weights[at] = jnp.concatenate([one, two, three], axis=0).astype(BF16)


def force_loop(group, blocks, total, local, left, right, weights, scale, bcol, ccol, acc, work):
    icut, jcut = blocks.icut, blocks.jcut
    dist, upper, lower = work[:group], work[group : 2 * group], work[2 * group :]
    blocks.clear(group)
    for ref in (*upper, *lower):
        ref[...] = jnp.zeros_like(ref)
    zero = jnp.int32(0)
    state = (zero, zero, zero)
    for g in range(2 * group):
        state = blocks.write(group + g, state)
    for g in range(group):
        blocks.distances(group + g, left, right, dist[g])

    def sums_of(rows, columns, k, g):
        a, b, istart, jstart, w = blocks.read(k * group + g)
        adds = []
        if rows:
            wt = weights[b, :, pl.ds(jstart, jcut)]
            spec = (((1,), (1,)), ((), ()))
            part = lax.dot_general(wt, upper[g][...], spec, preferred_element_type=F32)
            part = part + lax.dot_general(wt, lower[g][...], spec, preferred_element_type=F32)
            keep = w
            if columns:
                keep = jnp.where(k * group + g < local + group, w, 0.0)
            adds.append((a, istart, part * keep))
        if columns:
            wt = weights[a, :, pl.ds(istart, icut)]
            part = jnp.dot(wt, upper[g][...], preferred_element_type=F32)
            part = part + jnp.dot(wt, lower[g][...], preferred_element_type=F32)
            adds.append((b, jstart, part * w))
        return adds

    def store(adds):
        for cell, start, part in adds:
            acc[cell, :, pl.ds(start, part.shape[1])] += part

    def step(rows, columns, k, state):
        adds = []
        for g in range(group):
            adds += sums_of(rows, columns, k, g)

            a, b, istart, jstart, _ = blocks.read((k + 1) * group + g)
            bj = jnp.concatenate([scale[b, 0:8, pl.ds(jstart, jcut)]] * (STRIP // 8), axis=0)
            cj = jnp.concatenate([scale[b, 8:16, pl.ds(jstart, jcut)]] * (STRIP // 8), axis=0)
            for row in range(0, icut, STRIP):
                s = jnp.maximum(dist[g][row : row + STRIP, :], TINY)
                r = lax.rsqrt(s)
                d = s * r
                bi = bcol[a, pl.ds(istart + row, STRIP), :]
                ci = ccol[a, pl.ds(istart + row, STRIP), :]
                bi = jnp.concatenate([bi] * (jcut // LANES), axis=1)
                ci = jnp.concatenate([ci] * (jcut // LANES), axis=1)
                t = ci * d
                u = jnp.maximum(bi - t, 0.0)
                v = jnp.minimum(t, u)
                slope = (u + u - v) * v
                t = cj * d
                u = jnp.maximum(bj - t, 0.0)
                v = jnp.minimum(t, u)
                slope = (slope + (u + u - v) * v) * r
                rounded = slope.astype(BF16)
                upper[g][row : row + STRIP, :] = rounded
                lower[g][row : row + STRIP, :] = (slope - rounded.astype(F32)).astype(BF16)

            state = blocks.write((k + 3) * group + g, state)
            blocks.distances((k + 2) * group + g, left, right, dist[g])
        store(adds)
        return state

    steps = chunks(total, group)
    adds = []
    if local is None:
        lax.fori_loop(0, steps, functools.partial(step, False, True), state)
        for g in range(group):
            adds += sums_of(False, True, steps, g)
    else:
        first = jnp.minimum(chunks(local, group) + 1, steps)
        state = lax.fori_loop(0, first, functools.partial(step, True, True), state)
        lax.fori_loop(first, steps, functools.partial(step, False, True), state)
        for g in range(group):
            adds += sums_of(True, True, steps, g)
    store(adds)


def force_local_kernel(
    icut, jcut, group, lay,
    meta, own, term, left,
    acc_out,
    table, ring, right, weights, scale, bcol, ccol, acc, *work,
):
    slots = own.shape[2]
    pick = scale_picker()
    for k in range(lay.cells):
        force_lanes(own[k], right, scale, k)
        force_weights(own[k], term[k], weights, k)
        scale_columns(left, pick, bcol, ccol, k)
        acc[k] = jnp.zeros((DOT_K, slots), F32)
    tiles = Tiles(icut, jcut, table)
    local = local_tiles(tiles, lay, meta, True)
    blocks = Blocks(tiles, ring)
    force_loop(
        group, blocks, tiles.blocks, local, left, right, weights, scale, bcol, ccol, acc, work
    )
    for k in range(lay.cells):
        acc_out[k] = acc[k, 0:16, :] + (acc[k, 16:32, :] + acc[k, 32:48, :])


def force_remote_kernel(
    icut, jcut, group, lay,
    meta, live, own, far, term, rterm, odd_term, acc_in,
    accel_out, heat_out,
    table, ring, left, right, weights, scale, bcol, ccol, acc, *work,
):
    cells, peers = lay.cells, lay.peers
    slots = own.shape[2]
    first, face = arrivals(lay)
    ids = row_ids((8, slots))

    pick = scale_picker()
    for k in range(cells):
        force_lanes(own[k], right, scale, k)

    def receive(got, at, k):
        rows = far[k]
        for r in range(1, SENT_LATER):
            rows = jnp.where(ids == 3 + r, got[at, :, r * slots : (r + 1) * slots], rows)
        force_weights(rows, got[at, :, :slots], weights, k)
        force_columns(rows, left, k)
        scale_columns(left, pick, bcol, ccol, k)

    def rec_cell(k, carry):
        receive(rterm, first + k, k)
        return carry

    lax.fori_loop(0, peers, rec_cell, 0, unroll=2)
    receive(rterm, face, peers)
    receive(odd_term, 0, peers + 1)
    acc[...] = jnp.zeros_like(acc)
    tiles = Tiles(icut, jcut, table)
    remote_tiles(tiles, lay, meta, live, True)
    blocks = Blocks(tiles, ring)
    force_loop(
        group, blocks, tiles.blocks, None, left, right, weights, scale, bcol, ccol, acc, work
    )

    lane = lax.broadcasted_iota(jnp.int32, (1, slots), 1)
    for k in range(cells):
        occupied = jnp.where(lane < meta[k], 1.0, 0.0)
        sums = acc_in[k] + acc[k, 0:16, :] + (acc[k, 16:32, :] + acc[k, 32:48, :])
        pressure = term[k]
        x = [own[k, d : d + 1, :] for d in range(3)]
        v = [own[k, 5 + d : 6 + d, :] for d in range(3)]
        both = pressure * sums[3:4] + sums[11:12]
        for d in range(3):
            accel_out[d, k : k + 1, :] = occupied * (
                x[d] * both - pressure * sums[d : d + 1] - sums[8 + d : 9 + d]
            )
        xv = x[0] * v[0] + x[1] * v[1] + x[2] * v[2]
        total_heat = xv * sums[3:4] + sums[4:5]
        for d in range(3):
            total_heat = total_heat - v[d] * sums[d : d + 1] - x[d] * sums[5 + d : 6 + d]
        heat_out[k : k + 1, :] = -occupied * pressure * total_heat


def on_device(positions, velocities, mass, smoothing, energy, counts, send, pairs, edge):
    cells, slots = mass.shape
    peers = send.shape[2]
    regions = 2 * lax.axis_size("pair")
    lay = Meta(cells, peers, pairs.shape[2])
    others = peers + 2
    most = max(cells * (cells - 1) // 2 + 3 * cells, cells * cells, others) + 1
    icut, jcut, group = 128, slots // 2, 8
    ring = Blocks.FIELDS * (most * (slots // icut) * (slots // jcut) + 6 * group)
    shape = jax.ShapeDtypeStruct
    params = pltpu.CompilerParams(vmem_limit_bytes=48 * 1024 * 1024)
    send = send.reshape(peers)
    pairs = jnp.transpose(pairs, (0, 1, 3, 2))
    integers = (counts, send, pairs, edge)
    floats = (positions, velocities, mass, smoothing)
    integers, floats, energy = jax.tree.map(
        lambda x: pltpu.with_memory_space_constraint(x, pltpu.HBM), (integers, floats, energy)
    )
    lists = [pltpu.SMEM((Tiles.FIELDS * most,), jnp.int32), pltpu.SMEM((ring,), jnp.int32)]
    density_work = [pltpu.VMEM((icut, jcut), F32)] * group + [pltpu.VMEM((icut, LANES), F32)] * group
    force_work = [pltpu.VMEM((icut, jcut), F32)] * group + [pltpu.VMEM((icut, jcut), BF16)] * (2 * group)
    wide = shape((cells, slots, LANES), F32)
    left_shape = shape((cells, slots, COLS), BF16)
    weight_shape = lambda count: pltpu.VMEM((count, DOT_K, slots), BF16)

    def exchange(pay, odd):
        between = [(r, r + 1) for r in range(1, regions - 1, 2)]
        swap = between + [(b, a) for a, b in between]
        got_odd = lax.ppermute(odd, ("pair", "side"), swap)
        return lax.all_to_all(pay, ("side", "cell"), split_axis=0, concat_axis=0, tiled=True), got_odd

    own, pay, odd, meta = pl.pallas_call(
        functools.partial(prep_kernel, lay),
        out_shape=[
            shape((cells, ROWS, slots), F32),
            shape((2 * peers, 1, SENT * slots), F32),
            shape((1, 1, SENT * slots), F32),
            shape((lay.size,), jnp.int32),
        ],
        in_specs=[HBM] * 8,
        out_specs=[VMEM] * 3 + [SMEM],
        scratch_shapes=[pltpu.SMEM(x.shape, jnp.int32) for x in integers]
        + [pltpu.VMEM(x.shape, F32) for x in floats]
        + [pltpu.SemaphoreType.DMA((8,))],
        compiler_params=params,
        name="prep",
    )(*integers, *floats)

    rec, rec_odd = exchange(pay, odd)

    acc, left, force_left = pl.pallas_call(
        functools.partial(density_local_kernel, icut, jcut, group, lay),
        out_shape=[wide, left_shape, left_shape],
        in_specs=[SMEM, VMEM],
        out_specs=[VMEM] * 3,
        scratch_shapes=lists + [weight_shape(cells), pltpu.VMEM((cells, 8, slots), F32)] + density_work,
        compiler_params=params,
        name="density_local",
    )(meta, own)

    density, term, pay, odd, far, live = pl.pallas_call(
        functools.partial(density_remote_kernel, icut, jcut, group, lay),
        out_shape=[
            shape((cells, slots), F32),
            shape((cells, 1, slots), F32),
            shape((2 * peers, 1, SENT_LATER * slots), F32),
            shape((1, 1, SENT_LATER * slots), F32),
            shape((others, ROWS, slots), F32),
            shape((others,), jnp.int32),
        ],
        in_specs=[SMEM] + [VMEM] * 5 + [HBM],
        out_specs=[VMEM] * 5 + [SMEM],
        scratch_shapes=lists
        + [
            weight_shape(others),
            pltpu.VMEM((others, 8, slots), F32),
            pltpu.VMEM((cells, slots, LANES), F32),
            pltpu.VMEM(energy.shape, F32),
            pltpu.SemaphoreType.DMA,
        ]
        + density_work,
        compiler_params=params,
        name="density_remote",
    )(meta, own, rec, rec_odd, acc, left, energy)

    rterm, odd_term = exchange(pay, odd)

    acc = pl.pallas_call(
        functools.partial(force_local_kernel, icut, jcut, group, lay),
        out_shape=shape((cells, 16, slots), F32),
        in_specs=[SMEM] + [VMEM] * 3,
        out_specs=VMEM,
        scratch_shapes=lists
        + [
            weight_shape(cells),
            weight_shape(cells),
            pltpu.VMEM((cells, 16, slots), F32),
            pltpu.VMEM((cells, slots, LANES), F32),
            pltpu.VMEM((cells, slots, LANES), F32),
            pltpu.VMEM((cells, DOT_K, slots), F32),
        ]
        + force_work,
        compiler_params=params,
        name="force_local",
    )(meta, own, term, force_left)

    accel, heat = pl.pallas_call(
        functools.partial(force_remote_kernel, icut, jcut, group, lay),
        out_shape=[shape((3, cells, slots), F32), shape((cells, slots), F32)],
        in_specs=[SMEM] * 2 + [VMEM] * 6,
        out_specs=[VMEM] * 2,
        scratch_shapes=lists
        + [
            pltpu.VMEM((others, slots, COLS), BF16),
            weight_shape(cells),
            weight_shape(others),
            pltpu.VMEM((cells, 16, slots), F32),
            pltpu.VMEM((others, slots, LANES), F32),
            pltpu.VMEM((others, slots, LANES), F32),
            pltpu.VMEM((cells, DOT_K, slots), F32),
        ]
        + force_work,
        compiler_params=params,
        name="force_remote",
    )(meta, live, own, far, term, rterm, odd_term, acc)
    return density, accel, heat


def solution(mesh):
    regions, peers = mesh.devices.shape
    mesh = jax.sharding.Mesh(mesh.devices.reshape(regions // 2, 2, peers), ("pair", "side", "cell"))
    region = ("pair", "side")
    every = (*region, "cell")
    placed = (
        P(None, every, None),
        P(None, every, None),
        P(every, None),
        P(every, None),
        P(every, None),
        P(every),
        P(region, "cell", None, None),
        P(region, "cell", None, None),
        P(region, "cell", None),
    )
    return jax.shard_map(
        on_device,
        mesh=mesh,
        in_specs=placed,
        out_specs=(P(every, None), P(None, every, None), P(every, None)),
        check_vma=False,
    )
```

```python
import functools
import math

import jax
import jax.numpy as jnp
from jax import lax
from jax.experimental import pallas as pl
from jax.experimental.pallas import tpu as pltpu
from jax.sharding import PartitionSpec as P

GAMMA = 5.0 / 3.0
LANES = 128
BF16 = jnp.bfloat16
F32 = jnp.float32

ROWS = 8
TINY = 1e-12
DOT_K = 48
COLS = 64
STRIP = 16
SENT = 4
SENT_LATER = 5

VMEM = pl.BlockSpec(memory_space=pltpu.VMEM)
SMEM = pl.BlockSpec(memory_space=pltpu.SMEM)
HBM = pl.BlockSpec(memory_space=pltpu.HBM)


def row_ids(shape):
    return lax.broadcasted_iota(jnp.int32, shape, 0)


def split3(value):
    first = value.astype(BF16).astype(F32)
    rest = value - first
    second = rest.astype(BF16).astype(F32)
    return first, second, rest - second


def left_parts(value):
    a, b, c = split3(value)
    return jnp.concatenate([a, a, b, b, a, c], axis=0)


def right_parts(value):
    a, b, c = split3(value)
    return jnp.concatenate([a, b, a, b, c, a], axis=0).astype(BF16)


def norm_row(rows):
    return rows[0:1] * rows[0:1] + rows[1:2] * rows[1:2] + rows[2:3] * rows[2:3]


def left_comps(rows):
    ids = row_ids(rows.shape)
    return jnp.where(ids < 3, rows, jnp.where(ids == 3, norm_row(rows), jnp.where(ids == 4, 1.0, 0.0)))


def right_comps(rows):
    ids = row_ids(rows.shape)
    return jnp.where(ids < 3, -2.0 * rows, jnp.where(ids == 3, 1.0, jnp.where(ids == 4, norm_row(rows), 0.0)))


def chunks(count, size):
    return lax.shift_right_logical(count + (size - 1), jnp.int32(size.bit_length() - 1))


class Meta:
    def __init__(self, cells, peers, pairs):
        self.cells, self.peers, self.pairs = cells, peers, pairs
        self.send = cells
        self.pair = cells + peers
        self.edge = self.pair + 2 * pairs
        self.size = self.edge + 2


def prep_kernel(
    lay,
    counts_in, send_in, pairs_in, edge_in, pos_in, vel_in, mass_in, smooth_in,
    own, pay, odd, meta,
    counts, send, pairs, edge, pos, vel, mass, smooth, sems,
):
    inputs = (counts_in, send_in, pairs_in, edge_in, pos_in, vel_in, mass_in, smooth_in)
    buffers = (counts, send, pairs, edge, pos, vel, mass, smooth)
    copies = [
        pltpu.make_async_copy(source, target, sems.at[k])
        for k, (source, target) in enumerate(zip(inputs, buffers))
    ]
    for copy in copies:
        copy.start()
    for copy in copies:
        copy.wait()
    cells = mass.shape[0]
    slots = mass.shape[1]
    for k in range(cells):
        meta[k] = counts[k]
    for k in range(lay.peers):
        meta[lay.send + k] = send[k]
    for k in range(lay.pairs):
        for side in range(2):
            meta[lay.pair + 2 * k + side] = pairs[0, 0, side, k]
    for side in range(2):
        meta[lay.edge + side] = edge[0, 0, side]

    lane = lax.broadcasted_iota(jnp.int32, (1, slots), 1)
    for k in range(cells):
        live = lane < counts[k]
        for d in range(3):
            own[k, d : d + 1, :] = pos[d, k : k + 1, :] - 0.5
            own[k, 5 + d : 6 + d, :] = vel[d, k : k + 1, :]
        own[k, 3:4, :] = jnp.where(live, mass[k : k + 1, :], 0.0)
        own[k, 4:5, :] = smooth[k : k + 1, :]

    def row(cell, r):
        return own[cell, r : r + 1, :]

    fill(lay, pay, odd, meta, SENT, row)


def fill(lay, pay, odd, meta, count, row):
    slots = pay.shape[2] // count
    side = lax.axis_index("side")
    first = side * lay.peers
    pay[...] = jnp.zeros_like(pay)

    def put(out, at, cell, keep):
        for r in range(count):
            value = row(cell, r)
            if keep is not None:
                value = jnp.where(keep, value, 0.0)
            out[at, :, r * slots : (r + 1) * slots] = value

    def peer(k, carry):
        picked = meta[lay.send + k]
        put(pay, first + k, jnp.maximum(picked, 0), picked >= 0)
        return carry

    lax.fori_loop(0, lay.peers, peer, 0)
    put(pay, lay.peers - first + lax.axis_index("cell"), meta[lay.edge + 1 - side], None)
    put(odd, 0, meta[lay.edge + side], None)


def arrivals(lay):
    first = lax.axis_index("side") * lay.peers
    return first, lay.peers - first + lax.axis_index("cell")


class Tiles:
    FIELDS = 7

    def __init__(self, icut, jcut, table):
        self.icut, self.jcut, self.table = icut, jcut, table
        self.count = self.blocks = jnp.int32(0)

    def push(self, a, b, w, ok, i, ni, j, nj):
        at = self.FIELDS * self.count
        for field, value in enumerate((a, b, w, i, ni, j, nj)):
            self.table[at + field] = value
        self.count = self.count + ok.astype(jnp.int32)
        self.blocks = self.blocks + jnp.where(ok, ni * nj, 0)

    def whole(self, a, b, w, ok, alive, blive):
        self.push(a, b, w, ok, 0, chunks(alive, self.icut), 0, chunks(blive, self.jcut))

    def close(self):
        self.push(0, 0, 0, jnp.bool_(False), 0, 1, 0, 1)


def local_tiles(tiles, lay, meta, both):
    cells = lay.cells
    one = jnp.int32(1)

    def key(row):
        first = meta[lay.pair + 2 * row]
        second = meta[lay.pair + 2 * row + 1]
        return jnp.minimum(first, second) * cells + jnp.maximum(first, second)

    keys = [key(row) for row in range(lay.pairs)]
    for a in range(cells):
        for b in range(a + 1, cells):
            mult = jnp.int32(0)
            for pair in keys:
                mult = mult + (pair == a * cells + b).astype(jnp.int32)
            tiles.whole(a, b, mult, mult > 0, meta[a], meta[b])
            if not both:
                tiles.whole(b, a, mult, mult > 0, meta[b], meta[a])
    if not both:
        for a in range(cells):
            tiles.whole(a, a, one, meta[a] > 0, meta[a], meta[a])
        tiles.close()
        return None
    span = tiles.jcut // tiles.icut
    for a in range(cells):
        tiles.push(a, a, one, meta[a] > tiles.jcut, 0, span, 1, chunks(meta[a], tiles.jcut) - 1)
    mutual = tiles.blocks
    for a in range(cells):
        rows = chunks(meta[a], tiles.icut)
        tiles.push(a, a, one, meta[a] > 0, 0, jnp.minimum(rows, span), 0, 1)
        tiles.push(a, a, one, meta[a] > tiles.jcut, span, rows - span, 1, 1)
    tiles.close()
    return mutual


def remote_tiles(tiles, lay, meta, live):
    one = jnp.int32(1)
    for k in range(lay.peers):
        picked = meta[lay.send + k]
        a = jnp.maximum(picked, 0)
        tiles.whole(a, k, one, (picked >= 0) & (live[k] > 0), meta[a], live[k])
    side = lax.axis_index("side")
    for b, edge in ((lay.peers, 1 - side), (lay.peers + 1, side)):
        a = meta[lay.edge + edge]
        tiles.whole(a, b, one, live[b] > 0, meta[a], live[b])
    tiles.close()


class Blocks:
    FIELDS = 5

    def __init__(self, tiles, ring):
        self.icut, self.jcut = tiles.icut, tiles.jcut
        self.table, self.last = tiles.table, tiles.count
        self.ring, self.total = ring, tiles.blocks

    def clear(self, entries):
        for k in range(entries * self.FIELDS):
            self.ring[k] = 0

    def write(self, slot, state):
        n, ii, jj = state
        a, b, w, i, ni, j, nj = (self.table[Tiles.FIELDS * n + k] for k in range(Tiles.FIELDS))
        for field, value in enumerate((a, b, (i + ii) * self.icut, (j + jj) * self.jcut, w)):
            self.ring[self.FIELDS * slot + field] = value
        jwrap = jj + 1 >= nj
        inext = jnp.where(jwrap, ii + 1, ii)
        iwrap = inext >= ni
        return (
            jnp.minimum(jnp.where(iwrap, n + 1, n), self.last),
            jnp.where(iwrap, 0, inext),
            jnp.where(jwrap, 0, jj + 1),
        )

    def read(self, slot):
        a, b, istart, jstart, w = (self.ring[self.FIELDS * slot + k] for k in range(self.FIELDS))
        return (
            a,
            b,
            pl.multiple_of(istart, self.icut),
            pl.multiple_of(jstart, self.jcut),
            w.astype(F32),
        )

    def distances(self, slot, left, right, out):
        a, b, istart, jstart, _ = self.read(slot)
        out[...] = jnp.dot(
            left[a, pl.ds(istart, self.icut), :DOT_K],
            right[b, :, pl.ds(jstart, self.jcut)],
            preferred_element_type=F32,
        )


def density_loop(group, blocks, total, left, right, mrow, acc, work):
    icut, jcut = blocks.icut, blocks.jcut
    dist, parts = work[:group], work[group:]
    zero = jnp.int32(0)
    state = (zero, zero, zero)
    for g in range(2 * group):
        state = blocks.write(g, state)
    for g in range(group):
        blocks.distances(g, left, right, dist[g])

    def step(k, state):
        for g in range(group):
            _, b, _, jstart, w = blocks.read(k * group + g)
            weight = mrow[b, :, pl.ds(jstart, jcut)] * w
            weight = jnp.concatenate([weight] * (STRIP // 8), axis=0)
            for row in range(0, icut, STRIP):
                s = jnp.maximum(dist[g][row : row + STRIP, :], TINY)
                q = s * lax.rsqrt(s)
                e = 1.0 - q
                u = jnp.maximum(e, 0.0)
                t = jnp.minimum(0.5 - (s * 3.0) * e, u * u * u) * weight
                part = t[:, :LANES]
                for at in range(1, jcut // LANES):
                    part = part + t[:, at * LANES : (at + 1) * LANES]
                parts[g][row : row + STRIP, :] = part

            state = blocks.write((k + 2) * group + g, state)
            blocks.distances((k + 1) * group + g, left, right, dist[g])
        for g in range(group):
            a, _, istart, _, _ = blocks.read(k * group + g)
            acc[a, pl.ds(istart, icut), :] += parts[g][...]
        return state

    lax.fori_loop(0, chunks(total, group), step, state)


def density_source(rows, right, mrow, at):
    right[at] = right_parts(right_comps(rows))
    mrow[at] = jnp.broadcast_to(rows[3:4], mrow.shape[1:])


def spread_left(parts, left, cell):
    for at in range(parts.shape[1] // LANES):
        left[cell, pl.ds(at * LANES, LANES), :] = parts[:, at * LANES : (at + 1) * LANES].T.astype(BF16)


def force_scales(rows):
    h = rows[4:5]
    inv = 1.0 / jnp.where(h > 0.0, h, 1.0)
    b = math.sqrt(24.0 / math.pi) * (inv * inv)
    return b, b * inv


def density_local_kernel(
    icut, jcut, group, lay, meta, own, acc, left, force_left, table, ring, right, mrow, *work
):
    slots = own.shape[2]
    ids = row_ids((8, slots))
    empty = jnp.zeros((8, slots), F32)
    for k in range(lay.cells):
        rows = own[k]
        inv = 1.0 / rows[4:5]
        comps = left_comps(rows)
        spread_left(jnp.concatenate([left_parts(comps * (inv * inv)), empty, empty], axis=0), left, k)
        scales = empty
        for at, part in enumerate(x for scale in force_scales(rows) for x in split3(scale)):
            scales = jnp.where(ids == at, part, scales)
        spread_left(jnp.concatenate([left_parts(comps), scales, empty], axis=0), force_left, k)
        density_source(rows, right, mrow, k)
        acc[k] = jnp.zeros((slots, LANES), F32)
    tiles = Tiles(icut, jcut, table)
    local_tiles(tiles, lay, meta, False)
    blocks = Blocks(tiles, ring)
    density_loop(group, blocks, tiles.blocks, left, right, mrow, acc, work)


def density_remote_kernel(
    icut, jcut, group, lay,
    meta, own, rec, rec_odd, acc_in, left, energy_in,
    rho_out, term_out, pay, odd, far, live,
    table, ring, right, mrow, acc, energy, sem, *work,
):
    cells, peers = lay.cells, lay.peers
    slots = own.shape[2]
    copy = pltpu.make_async_copy(energy_in, energy, sem)
    copy.start()
    first, face = arrivals(lay)
    ids = row_ids((8, slots))

    def receive(got, at, k):
        rows = jnp.zeros((8, slots), F32)
        for r in range(SENT):
            rows = jnp.where(ids == r, got[at, :, r * slots : (r + 1) * slots], rows)
        far[k] = rows
        density_source(rows, right, mrow, k)

    def rec_cell(k, carry):
        receive(rec, first + k, k)
        return carry

    lax.fori_loop(0, peers, rec_cell, 0, unroll=4)
    receive(rec, face, peers)
    receive(rec_odd, 0, peers + 1)
    occupied = jnp.sum(jnp.where(far[:, 3, :] > 0.0, 1.0, 0.0), axis=1, keepdims=True)
    for k in range(peers + 2):
        live[k] = occupied[k, 0].astype(jnp.int32)
    acc[...] = acc_in[...]
    tiles = Tiles(icut, jcut, table)
    remote_tiles(tiles, lay, meta, live)
    blocks = Blocks(tiles, ring)
    density_loop(group, blocks, tiles.blocks, left, right, mrow, acc, work)

    copy.wait()
    lane = lax.broadcasted_iota(jnp.int32, (1, slots), 1)
    ones = jnp.ones((8, LANES), BF16)
    for k in range(cells):
        one, two, three = split3(acc[k])
        total_row = jnp.zeros((8, slots), F32)
        for part in (three, two, one):
            total_row = total_row + lax.dot_general(
                ones, part.astype(BF16), (((1,), (1,)), ((), ())), preferred_element_type=F32
            )
        inv = 1.0 / own[k, 4:5, :]
        rho = total_row[0:1] * (16.0 / math.pi) * (inv * inv * inv)
        occupied = jnp.where(lane < meta[k], 1.0, 0.0)
        rho_out[k : k + 1, :] = rho * occupied
        term_out[k] = occupied * (GAMMA - 1.0) * energy[k : k + 1, :] / (rho + 1.0 - occupied)

    def row(cell, r):
        return term_out[cell] if r == 0 else own[cell, 3 + r : 4 + r, :]

    fill(lay, pay, odd, meta, SENT_LATER, row)


def force_source(rows, pressure, right, weights, scale, at):
    slots = rows.shape[1]
    right[at] = right_parts(right_comps(rows))
    b, c = force_scales(rows)
    scale[at] = jnp.concatenate([jnp.broadcast_to(b, (8, slots)), jnp.broadcast_to(c, (8, slots))], axis=0)
    m = rows[3:4]
    mp = m * pressure
    xv = rows[0:1] * rows[5:6] + rows[1:2] * rows[6:7] + rows[2:3] * rows[7:8]
    ids = row_ids((8, slots))
    base = jnp.where(ids == 3, 1.0, jnp.where(ids == 4, xv, rows))
    sums = jnp.concatenate([base * m, jnp.where(ids < 4, base, 0.0) * mp], axis=0)
    one, two, three = split3(sums)
    weights[at] = jnp.concatenate([one, two, three], axis=0).astype(BF16)


def force_loop(group, blocks, total, local, left, right, weights, scale, bcol, ccol, acc, work):
    icut, jcut = blocks.icut, blocks.jcut
    dist, slopes = work[:group], work[group:]
    blocks.clear(group)
    for ref in slopes:
        ref[...] = jnp.zeros_like(ref)
    zero = jnp.int32(0)
    state = (zero, zero, zero)
    for g in range(2 * group):
        state = blocks.write(group + g, state)
    for g in range(group):
        blocks.distances(group + g, left, right, dist[g])

    def sums_of(rows, columns, k, g):
        a, b, istart, jstart, w = blocks.read(k * group + g)
        adds = []
        if rows:
            wt = weights[b, :, pl.ds(jstart, jcut)]
            spec = (((1,), (1,)), ((), ()))
            part = lax.dot_general(wt, slopes[g][...], spec, preferred_element_type=F32)
            part = part[:, :icut] + part[:, icut:]
            keep = w
            if columns:
                keep = jnp.where(k * group + g < local + group, w, 0.0)
            adds.append((a, istart, part * keep))
        if columns:
            wt = weights[a, :, pl.ds(istart, icut)]
            wt = jnp.concatenate([wt, wt], axis=1)
            part = jnp.dot(wt, slopes[g][...], preferred_element_type=F32)
            adds.append((b, jstart, part * w))
        return adds

    def store(adds):
        for cell, start, part in adds:
            acc[cell, :, pl.ds(start, part.shape[1])] += part

    def step(rows, columns, k, state):
        adds = []
        for g in range(group):
            adds += sums_of(rows, columns, k, g)

            a, b, istart, jstart, _ = blocks.read((k + 1) * group + g)
            bj = jnp.concatenate([scale[b, 0:8, pl.ds(jstart, jcut)]] * (STRIP // 8), axis=0)
            cj = jnp.concatenate([scale[b, 8:16, pl.ds(jstart, jcut)]] * (STRIP // 8), axis=0)
            for row in range(0, icut, STRIP):
                s = jnp.maximum(dist[g][row : row + STRIP, :], TINY)
                r = lax.rsqrt(s)
                d = s * r
                bi = bcol[a, pl.ds(istart + row, STRIP), :]
                ci = ccol[a, pl.ds(istart + row, STRIP), :]
                bi = jnp.concatenate([bi] * (jcut // LANES), axis=1)
                ci = jnp.concatenate([ci] * (jcut // LANES), axis=1)
                t = ci * d
                u = jnp.maximum(bi - t, 0.0)
                v = jnp.minimum(t, u)
                slope = (u + u - v) * v
                t = cj * d
                u = jnp.maximum(bj - t, 0.0)
                v = jnp.minimum(t, u)
                slope = (slope + (u + u - v) * v) * r
                rounded = slope.astype(BF16)
                rest = slope - rounded.astype(F32)
                slopes[g][row : row + STRIP, :] = rounded
                slopes[g][icut + row : icut + row + STRIP, :] = rest.astype(BF16)

            state = blocks.write((k + 3) * group + g, state)
            blocks.distances((k + 2) * group + g, left, right, dist[g])
        store(adds)
        return state

    steps = chunks(total, group)
    adds = []
    if local is None:
        lax.fori_loop(0, steps, functools.partial(step, True, False), state)
        for g in range(group):
            adds += sums_of(True, False, steps, g)
    else:
        first = jnp.minimum(chunks(local, group) + 1, steps)
        state = lax.fori_loop(0, first, functools.partial(step, True, True), state)
        lax.fori_loop(first, steps, functools.partial(step, False, True), state)
        for g in range(group):
            adds += sums_of(True, True, steps, g)
    store(adds)


def force_local_kernel(
    icut, jcut, group, lay,
    meta, own, term, left,
    acc_out, bcol, ccol,
    table, ring, right, weights, scale, acc, *work,
):
    slots = own.shape[2]
    part = lax.broadcasted_iota(jnp.int32, (COLS, 2 * LANES), 0) - DOT_K
    lane = lax.broadcasted_iota(jnp.int32, (COLS, 2 * LANES), 1)
    of_b = (part >= 0) & (part < 3) & (lane < LANES)
    of_c = (part >= 3) & (part < 6) & (lane >= LANES)
    pick = jnp.where(of_b | of_c, 1.0, 0.0).astype(BF16)
    for k in range(lay.cells):
        force_source(own[k], term[k], right, weights, scale, k)
        acc[k] = jnp.zeros((DOT_K, slots), F32)
        for at in range(slots // LANES):
            here = pl.ds(at * LANES, LANES)
            both = jnp.dot(left[k, here, :], pick, preferred_element_type=F32)
            bcol[k, here, :] = both[:, :LANES]
            ccol[k, here, :] = both[:, LANES:]
    tiles = Tiles(icut, jcut, table)
    local = local_tiles(tiles, lay, meta, True)
    blocks = Blocks(tiles, ring)
    force_loop(
        group, blocks, tiles.blocks, local, left, right, weights, scale, bcol, ccol, acc, work
    )
    for k in range(lay.cells):
        acc_out[k] = acc[k, 0:16, :] + (acc[k, 16:32, :] + acc[k, 32:48, :])


def force_remote_kernel(
    icut, jcut, group, lay,
    meta, live, own, far, term, rterm, odd_term, acc_in, left, bcol, ccol,
    accel_out, heat_out,
    table, ring, right, weights, scale, acc, *work,
):
    cells, peers = lay.cells, lay.peers
    slots = own.shape[2]
    first, face = arrivals(lay)
    ids = row_ids((8, slots))

    def receive(got, at, k):
        rows = far[k]
        for r in range(1, SENT_LATER):
            rows = jnp.where(ids == 3 + r, got[at, :, r * slots : (r + 1) * slots], rows)
        force_source(rows, got[at, :, :slots], right, weights, scale, k)

    def rec_cell(k, carry):
        receive(rterm, first + k, k)
        return carry

    lax.fori_loop(0, peers, rec_cell, 0, unroll=4)
    receive(rterm, face, peers)
    receive(odd_term, 0, peers + 1)
    acc[...] = jnp.zeros_like(acc)
    tiles = Tiles(icut, jcut, table)
    remote_tiles(tiles, lay, meta, live)
    blocks = Blocks(tiles, ring)
    force_loop(
        group, blocks, tiles.blocks, None, left, right, weights, scale, bcol, ccol, acc, work
    )

    lane = lax.broadcasted_iota(jnp.int32, (1, slots), 1)
    for k in range(cells):
        occupied = jnp.where(lane < meta[k], 1.0, 0.0)
        sums = acc_in[k] + acc[k, 0:16, :] + (acc[k, 16:32, :] + acc[k, 32:48, :])
        pressure = term[k]
        x = [own[k, d : d + 1, :] for d in range(3)]
        v = [own[k, 5 + d : 6 + d, :] for d in range(3)]
        both = pressure * sums[3:4] + sums[11:12]
        for d in range(3):
            accel_out[d, k : k + 1, :] = occupied * (
                x[d] * both - pressure * sums[d : d + 1] - sums[8 + d : 9 + d]
            )
        xv = x[0] * v[0] + x[1] * v[1] + x[2] * v[2]
        total_heat = xv * sums[3:4] + sums[4:5]
        for d in range(3):
            total_heat = total_heat - v[d] * sums[d : d + 1] - x[d] * sums[5 + d : 6 + d]
        heat_out[k : k + 1, :] = -occupied * pressure * total_heat


def on_device(positions, velocities, mass, smoothing, energy, counts, send, pairs, edge):
    cells, slots = mass.shape
    peers = send.shape[2]
    regions = 2 * lax.axis_size("pair")
    lay = Meta(cells, peers, pairs.shape[2])
    others = peers + 2
    most = max(cells * (cells - 1) // 2 + 3 * cells, cells * cells, others) + 1
    icut, jcut, group = 128, slots // 2, 8
    ring = Blocks.FIELDS * (most * (slots // icut) * (slots // jcut) + 6 * group)
    shape = jax.ShapeDtypeStruct
    params = pltpu.CompilerParams(vmem_limit_bytes=20 * 1024 * 1024)
    send = send.reshape(peers)
    pairs = jnp.transpose(pairs, (0, 1, 3, 2))
    integers = (counts, send, pairs, edge)
    floats = (positions, velocities, mass, smoothing)
    integers, floats, energy = jax.tree.map(
        lambda x: pltpu.with_memory_space_constraint(x, pltpu.HBM), (integers, floats, energy)
    )
    lists = [pltpu.SMEM((Tiles.FIELDS * most,), jnp.int32), pltpu.SMEM((ring,), jnp.int32)]
    density_work = [pltpu.VMEM((icut, jcut), F32)] * group + [pltpu.VMEM((icut, LANES), F32)] * group
    force_work = [pltpu.VMEM((icut, jcut), F32)] * group + [pltpu.VMEM((2 * icut, jcut), BF16)] * group
    wide = shape((cells, slots, LANES), F32)
    left_shape = shape((cells, slots, COLS), BF16)
    weight_shape = lambda count: pltpu.VMEM((count, DOT_K, slots), BF16)

    def exchange(pay, odd):
        between = [(r, r + 1) for r in range(1, regions - 1, 2)]
        swap = between + [(b, a) for a, b in between]
        got_odd = lax.ppermute(odd, ("pair", "side"), swap)
        return lax.all_to_all(pay, ("side", "cell"), split_axis=0, concat_axis=0, tiled=True), got_odd

    own, pay, odd, meta = pl.pallas_call(
        functools.partial(prep_kernel, lay),
        out_shape=[
            shape((cells, ROWS, slots), F32),
            shape((2 * peers, 1, SENT * slots), F32),
            shape((1, 1, SENT * slots), F32),
            shape((lay.size,), jnp.int32),
        ],
        in_specs=[HBM] * 8,
        out_specs=[VMEM] * 3 + [SMEM],
        scratch_shapes=[pltpu.SMEM(x.shape, jnp.int32) for x in integers]
        + [pltpu.VMEM(x.shape, F32) for x in floats]
        + [pltpu.SemaphoreType.DMA((8,))],
        compiler_params=params,
        name="prep",
    )(*integers, *floats)

    rec, rec_odd = exchange(pay, odd)

    acc, left, force_left = pl.pallas_call(
        functools.partial(density_local_kernel, icut, jcut, group, lay),
        out_shape=[wide, left_shape, left_shape],
        in_specs=[SMEM, VMEM],
        out_specs=[VMEM] * 3,
        scratch_shapes=lists + [weight_shape(cells), pltpu.VMEM((cells, 8, slots), F32)] + density_work,
        compiler_params=params,
        name="density_local",
    )(meta, own)

    density, term, pay, odd, far, live = pl.pallas_call(
        functools.partial(density_remote_kernel, icut, jcut, group, lay),
        out_shape=[
            shape((cells, slots), F32),
            shape((cells, 1, slots), F32),
            shape((2 * peers, 1, SENT_LATER * slots), F32),
            shape((1, 1, SENT_LATER * slots), F32),
            shape((others, ROWS, slots), F32),
            shape((others,), jnp.int32),
        ],
        in_specs=[SMEM] + [VMEM] * 5 + [HBM],
        out_specs=[VMEM] * 5 + [SMEM],
        scratch_shapes=lists
        + [
            weight_shape(others),
            pltpu.VMEM((others, 8, slots), F32),
            pltpu.VMEM((cells, slots, LANES), F32),
            pltpu.VMEM(energy.shape, F32),
            pltpu.SemaphoreType.DMA,
        ]
        + density_work,
        compiler_params=params,
        name="density_remote",
    )(meta, own, rec, rec_odd, acc, left, energy)

    rterm, odd_term = exchange(pay, odd)

    acc, bcol, ccol = pl.pallas_call(
        functools.partial(force_local_kernel, icut, jcut, group, lay),
        out_shape=[shape((cells, 16, slots), F32), wide, wide],
        in_specs=[SMEM] + [VMEM] * 3,
        out_specs=[VMEM] * 3,
        scratch_shapes=lists
        + [
            weight_shape(cells),
            weight_shape(cells),
            pltpu.VMEM((cells, 16, slots), F32),
            pltpu.VMEM((cells, DOT_K, slots), F32),
        ]
        + force_work,
        compiler_params=params,
        name="force_local",
    )(meta, own, term, force_left)

    accel, heat = pl.pallas_call(
        functools.partial(force_remote_kernel, icut, jcut, group, lay),
        out_shape=[shape((3, cells, slots), F32), shape((cells, slots), F32)],
        in_specs=[SMEM] * 2 + [VMEM] * 9,
        out_specs=[VMEM] * 2,
        scratch_shapes=lists
        + [
            weight_shape(others),
            weight_shape(others),
            pltpu.VMEM((others, 16, slots), F32),
            pltpu.VMEM((cells, DOT_K, slots), F32),
        ]
        + force_work,
        compiler_params=params,
        name="force_remote",
    )(meta, live, own, far, term, rterm, odd_term, acc, force_left, bcol, ccol)
    return density, accel, heat


def solution(mesh):
    regions, peers = mesh.devices.shape
    mesh = jax.sharding.Mesh(mesh.devices.reshape(regions // 2, 2, peers), ("pair", "side", "cell"))
    region = ("pair", "side")
    every = (*region, "cell")
    placed = (
        P(None, every, None),
        P(None, every, None),
        P(every, None),
        P(every, None),
        P(every, None),
        P(every),
        P(region, "cell", None, None),
        P(region, "cell", None, None),
        P(region, "cell", None),
    )
    return jax.shard_map(
        on_device,
        mesh=mesh,
        in_specs=placed,
        out_specs=(P(every, None), P(None, every, None), P(every, None)),
        check_vma=False,
    )
```

```python
import functools
import math

import jax
import jax.numpy as jnp
from jax import lax
from jax.experimental import pallas as pl
from jax.experimental.pallas import tpu as pltpu
from jax.sharding import PartitionSpec as P

GAMMA = 5.0 / 3.0
LANES = 128
BF16 = jnp.bfloat16
F32 = jnp.float32

ROWS = 8
TINY = 1e-12
DOT_K = 48
COLS = 64
STRIP = 16

VMEM = pl.BlockSpec(memory_space=pltpu.VMEM)
SMEM = pl.BlockSpec(memory_space=pltpu.SMEM)
HBM = pl.BlockSpec(memory_space=pltpu.HBM)


def row_ids(shape):
    return lax.broadcasted_iota(jnp.int32, shape, 0)


def split3(value):
    first = value.astype(BF16).astype(F32)
    rest = value - first
    second = rest.astype(BF16).astype(F32)
    return first, second, rest - second


def left_parts(value):
    a, b, c = split3(value)
    return jnp.concatenate([a, a, b, b, a, c], axis=0)


def right_parts(value):
    a, b, c = split3(value)
    return jnp.concatenate([a, b, a, b, c, a], axis=0).astype(BF16)


def norm_row(rows):
    return rows[0:1] * rows[0:1] + rows[1:2] * rows[1:2] + rows[2:3] * rows[2:3]


def left_comps(rows):
    ids = row_ids(rows.shape)
    return jnp.where(ids < 3, rows, jnp.where(ids == 3, norm_row(rows), jnp.where(ids == 4, 1.0, 0.0)))


def right_comps(rows):
    ids = row_ids(rows.shape)
    return jnp.where(ids < 3, -2.0 * rows, jnp.where(ids == 3, 1.0, jnp.where(ids == 4, norm_row(rows), 0.0)))


def chunks(count, size):
    return lax.shift_right_logical(count + (size - 1), jnp.int32(size.bit_length() - 1))


class Meta:
    def __init__(self, cells, regions, peers, pairs):
        self.cells, self.regions, self.peers, self.pairs = cells, regions, peers, pairs
        self.send = cells
        self.pair = cells + peers
        self.edge = self.pair + 2 * pairs
        self.size = self.edge + 2


def prep_kernel(
    lay,
    counts_in, send_in, pairs_in, edge_in, pos_in, vel_in, mass_in, smooth_in,
    own, pay, odd, meta,
    counts, send, pairs, edge, pos, vel, mass, smooth, sems,
):
    inputs = (counts_in, send_in, pairs_in, edge_in, pos_in, vel_in, mass_in, smooth_in)
    buffers = (counts, send, pairs, edge, pos, vel, mass, smooth)
    copies = [
        pltpu.make_async_copy(source, target, sems.at[k])
        for k, (source, target) in enumerate(zip(inputs, buffers))
    ]
    for copy in copies:
        copy.start()
    for copy in copies:
        copy.wait()
    cells = mass.shape[0]
    slots = mass.shape[1]
    for k in range(cells):
        meta[k] = counts[k]
    for k in range(lay.peers):
        meta[lay.send + k] = send[k]
    for k in range(lay.pairs):
        for side in range(2):
            meta[lay.pair + 2 * k + side] = pairs[0, 0, side, k]
    for side in range(2):
        meta[lay.edge + side] = edge[0, 0, side]

    lane = lax.broadcasted_iota(jnp.int32, (1, slots), 1)
    for k in range(cells):
        live = lane < counts[k]
        for d in range(3):
            own[k, d : d + 1, :] = pos[d, k : k + 1, :] - 0.5
            own[k, 5 + d : 6 + d, :] = vel[d, k : k + 1, :]
        own[k, 3:4, :] = jnp.where(live, mass[k : k + 1, :], 0.0)
        own[k, 4:5, :] = smooth[k : k + 1, :]

    place = Place(lay)
    pay[...] = jnp.zeros_like(pay)

    def peer(k, carry):
        picked = send[k]
        pay[place.pair_peers + k] = jnp.where(picked >= 0, own[jnp.maximum(picked, 0)], 0.0)
        return carry

    lax.fori_loop(0, lay.peers, peer, 0)
    pay[place.pair_partner] = own[meta[place.partner_edge]]
    odd[0] = own[meta[place.odd_edge]]


class Place:
    def __init__(self, lay):
        peers, regions = lay.peers, lay.regions
        self.side = lax.axis_index("side")
        here = lax.axis_index("cell")
        region = 2 * lax.axis_index("pair") + self.side
        other = region - 1 + 2 * self.side
        self.partner_edge = lay.edge + 1 - self.side
        self.odd_edge = lay.edge + self.side
        self.pair_peers = self.side * peers
        self.pair_partner = (1 - self.side) * peers + here
        self.peers = region * peers
        self.partner = (region + 1 - 2 * self.side) * peers + here
        self.has_odd = (other >= 0) & (other < regions)
        self.odd = jnp.clip(other, 0, regions - 1) * peers + here


class Tiles:
    FIELDS = 7

    def __init__(self, icut, jcut, table):
        self.icut, self.jcut, self.table = icut, jcut, table
        self.count = self.blocks = jnp.int32(0)

    def push(self, a, b, w, ok, i, ni, j, nj):
        at = self.FIELDS * self.count
        for field, value in enumerate((a, b, w, i, ni, j, nj)):
            self.table[at + field] = value
        self.count = self.count + ok.astype(jnp.int32)
        self.blocks = self.blocks + jnp.where(ok, ni * nj, 0)

    def whole(self, a, b, w, ok, alive, blive):
        self.push(a, b, w, ok, 0, chunks(alive, self.icut), 0, chunks(blive, self.jcut))

    def close(self):
        self.push(0, 0, 0, jnp.bool_(False), 0, 1, 0, 1)


def local_tiles(tiles, lay, meta, both):
    cells = lay.cells
    one = jnp.int32(1)

    def key(row):
        first = meta[lay.pair + 2 * row]
        second = meta[lay.pair + 2 * row + 1]
        return jnp.minimum(first, second) * cells + jnp.maximum(first, second)

    keys = [key(row) for row in range(lay.pairs)]
    for a in range(cells):
        for b in range(a + 1, cells):
            mult = jnp.int32(0)
            for pair in keys:
                mult = mult + (pair == a * cells + b).astype(jnp.int32)
            tiles.whole(a, b, mult, mult > 0, meta[a], meta[b])
            if not both:
                tiles.whole(b, a, mult, mult > 0, meta[b], meta[a])
    if not both:
        for a in range(cells):
            tiles.whole(a, a, one, meta[a] > 0, meta[a], meta[a])
        tiles.close()
        return None
    span = tiles.jcut // tiles.icut
    for a in range(cells):
        tiles.push(a, a, one, meta[a] > tiles.jcut, 0, span, 1, chunks(meta[a], tiles.jcut) - 1)
    mutual = tiles.blocks
    for a in range(cells):
        rows = chunks(meta[a], tiles.icut)
        tiles.push(a, a, one, meta[a] > 0, 0, jnp.minimum(rows, span), 0, 1)
        tiles.push(a, a, one, meta[a] > tiles.jcut, span, rows - span, 1, 1)
    tiles.close()
    return mutual


def remote_tiles(tiles, lay, meta, live):
    one = jnp.int32(1)
    for k in range(lay.peers):
        picked = meta[lay.send + k]
        a = jnp.maximum(picked, 0)
        tiles.whole(a, k, one, (picked >= 0) & (live[k] > 0), meta[a], live[k])
    place = Place(lay)
    for b, edge in ((lay.peers, place.partner_edge), (lay.peers + 1, place.odd_edge)):
        a = meta[edge]
        tiles.whole(a, b, one, live[b] > 0, meta[a], live[b])
    tiles.close()


class Blocks:
    FIELDS = 5

    def __init__(self, tiles, ring):
        self.icut, self.jcut = tiles.icut, tiles.jcut
        self.table, self.last = tiles.table, tiles.count
        self.ring, self.total = ring, tiles.blocks

    def clear(self, entries):
        for k in range(entries * self.FIELDS):
            self.ring[k] = 0

    def write(self, slot, state):
        n, ii, jj = state
        a, b, w, i, ni, j, nj = (self.table[Tiles.FIELDS * n + k] for k in range(Tiles.FIELDS))
        for field, value in enumerate((a, b, (i + ii) * self.icut, (j + jj) * self.jcut, w)):
            self.ring[self.FIELDS * slot + field] = value
        jwrap = jj + 1 >= nj
        inext = jnp.where(jwrap, ii + 1, ii)
        iwrap = inext >= ni
        return (
            jnp.minimum(jnp.where(iwrap, n + 1, n), self.last),
            jnp.where(iwrap, 0, inext),
            jnp.where(jwrap, 0, jj + 1),
        )

    def read(self, slot):
        a, b, istart, jstart, w = (self.ring[self.FIELDS * slot + k] for k in range(self.FIELDS))
        return (
            a,
            b,
            pl.multiple_of(istart, self.icut),
            pl.multiple_of(jstart, self.jcut),
            w.astype(F32),
        )

    def distances(self, slot, left, right, out):
        a, b, istart, jstart, _ = self.read(slot)
        out[...] = jnp.dot(
            left[a, pl.ds(istart, self.icut), :DOT_K],
            right[b, :, pl.ds(jstart, self.jcut)],
            preferred_element_type=F32,
        )


def density_loop(group, blocks, total, left, right, mrow, acc, work):
    icut, jcut = blocks.icut, blocks.jcut
    dist, parts = work[:group], work[group:]
    zero = jnp.int32(0)
    state = (zero, zero, zero)
    for g in range(2 * group):
        state = blocks.write(g, state)
    for g in range(group):
        blocks.distances(g, left, right, dist[g])

    def step(k, state):
        for g in range(group):
            _, b, _, jstart, w = blocks.read(k * group + g)
            weight = mrow[b, :, pl.ds(jstart, jcut)] * w
            weight = jnp.concatenate([weight] * (STRIP // 8), axis=0)
            for row in range(0, icut, STRIP):
                s = jnp.maximum(dist[g][row : row + STRIP, :], TINY)
                q = s * lax.rsqrt(s)
                e = 1.0 - q
                u = jnp.maximum(e, 0.0)
                t = jnp.minimum(0.5 - (s * 3.0) * e, u * u * u) * weight
                part = t[:, :LANES]
                for at in range(1, jcut // LANES):
                    part = part + t[:, at * LANES : (at + 1) * LANES]
                parts[g][row : row + STRIP, :] = part

            state = blocks.write((k + 2) * group + g, state)
            blocks.distances((k + 1) * group + g, left, right, dist[g])
        for g in range(group):
            a, _, istart, _, _ = blocks.read(k * group + g)
            acc[a, pl.ds(istart, icut), :] += parts[g][...]
        return state

    lax.fori_loop(0, chunks(total, group), step, state)


def density_source(rows, right, mrow, at):
    right[at] = right_parts(right_comps(rows))
    mrow[at] = jnp.broadcast_to(rows[3:4], mrow.shape[1:])


def spread_left(parts, left, cell):
    for at in range(parts.shape[1] // LANES):
        left[cell, pl.ds(at * LANES, LANES), :] = parts[:, at * LANES : (at + 1) * LANES].T.astype(BF16)


def force_scales(rows):
    h = rows[4:5]
    inv = 1.0 / jnp.where(h > 0.0, h, 1.0)
    b = math.sqrt(24.0 / math.pi) * (inv * inv)
    return b, b * inv


def density_local_kernel(
    icut, jcut, group, lay, meta, own, acc, left, force_left, table, ring, right, mrow, *work
):
    slots = own.shape[2]
    ids = row_ids((8, slots))
    empty = jnp.zeros((8, slots), F32)
    for k in range(lay.cells):
        rows = own[k]
        inv = 1.0 / rows[4:5]
        comps = left_comps(rows)
        spread_left(jnp.concatenate([left_parts(comps * (inv * inv)), empty, empty], axis=0), left, k)
        scales = empty
        for at, part in enumerate(x for scale in force_scales(rows) for x in split3(scale)):
            scales = jnp.where(ids == at, part, scales)
        spread_left(jnp.concatenate([left_parts(comps), scales, empty], axis=0), force_left, k)
        density_source(rows, right, mrow, k)
        acc[k] = jnp.zeros((slots, LANES), F32)
    tiles = Tiles(icut, jcut, table)
    local_tiles(tiles, lay, meta, False)
    blocks = Blocks(tiles, ring)
    density_loop(group, blocks, tiles.blocks, left, right, mrow, acc, work)


def density_remote_kernel(
    icut, jcut, group, lay,
    meta, own, rec, rec_odd, acc_in, left, energy_in,
    rho_out, term_out, pay, live,
    table, ring, right, mrow, acc, energy, sem, *work,
):
    cells, peers = lay.cells, lay.peers
    slots = own.shape[2]
    copy = pltpu.make_async_copy(energy_in, energy, sem)
    copy.start()
    place = Place(lay)
    occupied = jnp.where(rec[:, 3, :] > 0.0, 1.0, 0.0).reshape(2, peers, slots)
    occupied = jnp.sum(jnp.where(place.side == 0, occupied[0], occupied[1]), axis=1, keepdims=True)
    for k in range(peers):
        live[k] = occupied[k, 0].astype(jnp.int32)
    for k, rows in ((peers, rec[place.pair_partner]), (peers + 1, rec_odd[0])):
        live[k] = jnp.sum(jnp.where(rows[3:4] > 0.0, 1.0, 0.0)).astype(jnp.int32)

    def rec_cell(k, carry):
        density_source(rec[place.pair_peers + k], right, mrow, k)
        return carry

    lax.fori_loop(0, peers, rec_cell, 0, unroll=4)
    density_source(rec[place.pair_partner], right, mrow, peers)
    density_source(rec_odd[0], right, mrow, peers + 1)
    acc[...] = acc_in[...]
    tiles = Tiles(icut, jcut, table)
    remote_tiles(tiles, lay, meta, live)
    blocks = Blocks(tiles, ring)
    density_loop(group, blocks, tiles.blocks, left, right, mrow, acc, work)

    copy.wait()
    lane = lax.broadcasted_iota(jnp.int32, (1, slots), 1)
    ones = jnp.ones((8, LANES), BF16)
    for k in range(cells):
        one, two, three = split3(acc[k])
        total_row = jnp.zeros((8, slots), F32)
        for part in (three, two, one):
            total_row = total_row + lax.dot_general(
                ones, part.astype(BF16), (((1,), (1,)), ((), ())), preferred_element_type=F32
            )
        inv = 1.0 / own[k, 4:5, :]
        rho = total_row[0:1] * (16.0 / math.pi) * (inv * inv * inv)
        occupied = jnp.where(lane < meta[k], 1.0, 0.0)
        rho_out[k : k + 1, :] = rho * occupied
        term_out[k] = occupied * (GAMMA - 1.0) * energy[k : k + 1, :] / (rho + 1.0 - occupied)

    pay[...] = jnp.zeros_like(pay)

    def peer(k, carry):
        pay[place.peers + k] = term_out[jnp.maximum(meta[lay.send + k], 0)]
        return carry

    lax.fori_loop(0, peers, peer, 0)
    pay[place.partner] = term_out[meta[place.partner_edge]]

    @pl.when(place.has_odd)
    def _():
        pay[place.odd] = term_out[meta[place.odd_edge]]


def force_source(rows, pressure, right, weights, scale, at):
    slots = rows.shape[1]
    right[at] = right_parts(right_comps(rows))
    b, c = force_scales(rows)
    scale[at] = jnp.concatenate([jnp.broadcast_to(b, (8, slots)), jnp.broadcast_to(c, (8, slots))], axis=0)
    m = rows[3:4]
    mp = m * pressure
    xv = rows[0:1] * rows[5:6] + rows[1:2] * rows[6:7] + rows[2:3] * rows[7:8]
    ids = row_ids((8, slots))
    base = jnp.where(ids == 3, 1.0, jnp.where(ids == 4, xv, rows))
    sums = jnp.concatenate([base * m, jnp.where(ids < 4, base, 0.0) * mp], axis=0)
    one, two, three = split3(sums)
    weights[at] = jnp.concatenate([one, two, three], axis=0).astype(BF16)


def force_loop(group, blocks, total, local, left, right, weights, scale, bcol, ccol, acc, work):
    icut, jcut = blocks.icut, blocks.jcut
    dist, upper, lower = work[:group], work[group : 2 * group], work[2 * group :]
    blocks.clear(group)
    for ref in (*upper, *lower):
        ref[...] = jnp.zeros_like(ref)
    zero = jnp.int32(0)
    state = (zero, zero, zero)
    for g in range(2 * group):
        state = blocks.write(group + g, state)
    for g in range(group):
        blocks.distances(group + g, left, right, dist[g])

    def sums_of(rows, columns, k, g):
        a, b, istart, jstart, w = blocks.read(k * group + g)
        adds = []
        if rows:
            wt = weights[b, :, pl.ds(jstart, jcut)]
            spec = (((1,), (1,)), ((), ()))
            part = lax.dot_general(wt, upper[g][...], spec, preferred_element_type=F32)
            part = part + lax.dot_general(wt, lower[g][...], spec, preferred_element_type=F32)
            keep = w
            if columns:
                keep = jnp.where(k * group + g < local + group, w, 0.0)
            adds.append((a, istart, part * keep))
        if columns:
            wt = weights[a, :, pl.ds(istart, icut)]
            part = jnp.dot(wt, upper[g][...], preferred_element_type=F32)
            part = part + jnp.dot(wt, lower[g][...], preferred_element_type=F32)
            adds.append((b, jstart, part * w))
        return adds

    def store(adds):
        for cell, start, part in adds:
            acc[cell, :, pl.ds(start, part.shape[1])] += part

    def step(rows, columns, k, state):
        adds = []
        for g in range(group):
            adds += sums_of(rows, columns, k, g)

            a, b, istart, jstart, _ = blocks.read((k + 1) * group + g)
            bj = jnp.concatenate([scale[b, 0:8, pl.ds(jstart, jcut)]] * (STRIP // 8), axis=0)
            cj = jnp.concatenate([scale[b, 8:16, pl.ds(jstart, jcut)]] * (STRIP // 8), axis=0)
            for row in range(0, icut, STRIP):
                s = jnp.maximum(dist[g][row : row + STRIP, :], TINY)
                r = lax.rsqrt(s)
                d = s * r
                bi = bcol[a, pl.ds(istart + row, STRIP), :]
                ci = ccol[a, pl.ds(istart + row, STRIP), :]
                bi = jnp.concatenate([bi] * (jcut // LANES), axis=1)
                ci = jnp.concatenate([ci] * (jcut // LANES), axis=1)
                t = ci * d
                u = jnp.maximum(bi - t, 0.0)
                v = jnp.minimum(t, u)
                slope = (u + u - v) * v
                t = cj * d
                u = jnp.maximum(bj - t, 0.0)
                v = jnp.minimum(t, u)
                slope = (slope + (u + u - v) * v) * r
                rounded = slope.astype(BF16)
                upper[g][row : row + STRIP, :] = rounded
                lower[g][row : row + STRIP, :] = (slope - rounded.astype(F32)).astype(BF16)

            state = blocks.write((k + 3) * group + g, state)
            blocks.distances((k + 2) * group + g, left, right, dist[g])
        store(adds)
        return state

    steps = chunks(total, group)
    adds = []
    if local is None:
        lax.fori_loop(0, steps, functools.partial(step, True, False), state)
        for g in range(group):
            adds += sums_of(True, False, steps, g)
    else:
        first = jnp.minimum(chunks(local, group) + 1, steps)
        state = lax.fori_loop(0, first, functools.partial(step, True, True), state)
        lax.fori_loop(first, steps, functools.partial(step, False, True), state)
        for g in range(group):
            adds += sums_of(True, True, steps, g)
    store(adds)


def force_local_kernel(
    icut, jcut, group, lay,
    meta, own, term, left,
    acc_out, bcol, ccol,
    table, ring, right, weights, scale, acc, *work,
):
    slots = own.shape[2]
    part = lax.broadcasted_iota(jnp.int32, (COLS, 2 * LANES), 0) - DOT_K
    lane = lax.broadcasted_iota(jnp.int32, (COLS, 2 * LANES), 1)
    of_b = (part >= 0) & (part < 3) & (lane < LANES)
    of_c = (part >= 3) & (part < 6) & (lane >= LANES)
    pick = jnp.where(of_b | of_c, 1.0, 0.0).astype(BF16)
    for k in range(lay.cells):
        force_source(own[k], term[k], right, weights, scale, k)
        acc[k] = jnp.zeros((DOT_K, slots), F32)
        for at in range(slots // LANES):
            here = pl.ds(at * LANES, LANES)
            both = jnp.dot(left[k, here, :], pick, preferred_element_type=F32)
            bcol[k, here, :] = both[:, :LANES]
            ccol[k, here, :] = both[:, LANES:]
    tiles = Tiles(icut, jcut, table)
    local = local_tiles(tiles, lay, meta, True)
    blocks = Blocks(tiles, ring)
    force_loop(
        group, blocks, tiles.blocks, local, left, right, weights, scale, bcol, ccol, acc, work
    )
    for k in range(lay.cells):
        acc_out[k] = acc[k, 0:16, :] + (acc[k, 16:32, :] + acc[k, 32:48, :])


def force_remote_kernel(
    icut, jcut, group, lay,
    meta, live, own, rec, rec_odd, term, rterm, acc_in, left, bcol, ccol,
    accel_out, heat_out,
    table, ring, right, weights, scale, acc, *work,
):
    cells, peers = lay.cells, lay.peers
    slots = own.shape[2]
    place = Place(lay)

    def rec_cell(k, carry):
        force_source(rec[place.pair_peers + k], rterm[place.peers + k], right, weights, scale, k)
        return carry

    lax.fori_loop(0, peers, rec_cell, 0, unroll=4)
    force_source(rec[place.pair_partner], rterm[place.partner], right, weights, scale, peers)
    force_source(rec_odd[0], rterm[place.odd], right, weights, scale, peers + 1)
    acc[...] = jnp.zeros_like(acc)
    tiles = Tiles(icut, jcut, table)
    remote_tiles(tiles, lay, meta, live)
    blocks = Blocks(tiles, ring)
    force_loop(
        group, blocks, tiles.blocks, None, left, right, weights, scale, bcol, ccol, acc, work
    )

    lane = lax.broadcasted_iota(jnp.int32, (1, slots), 1)
    for k in range(cells):
        occupied = jnp.where(lane < meta[k], 1.0, 0.0)
        sums = acc_in[k] + acc[k, 0:16, :] + (acc[k, 16:32, :] + acc[k, 32:48, :])
        pressure = term[k]
        x = [own[k, d : d + 1, :] for d in range(3)]
        v = [own[k, 5 + d : 6 + d, :] for d in range(3)]
        both = pressure * sums[3:4] + sums[11:12]
        for d in range(3):
            accel_out[d, k : k + 1, :] = occupied * (
                x[d] * both - pressure * sums[d : d + 1] - sums[8 + d : 9 + d]
            )
        xv = x[0] * v[0] + x[1] * v[1] + x[2] * v[2]
        total_heat = xv * sums[3:4] + sums[4:5]
        for d in range(3):
            total_heat = total_heat - v[d] * sums[d : d + 1] - x[d] * sums[5 + d : 6 + d]
        heat_out[k : k + 1, :] = -occupied * pressure * total_heat


def on_device(positions, velocities, mass, smoothing, energy, counts, send, pairs, edge):
    cells, slots = mass.shape
    peers = send.shape[2]
    regions = 2 * lax.axis_size("pair")
    lay = Meta(cells, regions, peers, pairs.shape[2])
    others = peers + 2
    most = max(cells * (cells - 1) // 2 + 3 * cells, cells * cells, others) + 1
    icut, jcut, group = 128, slots // 2, 8
    ring = Blocks.FIELDS * (most * (slots // icut) * (slots // jcut) + 6 * group)
    shape = jax.ShapeDtypeStruct
    params = pltpu.CompilerParams(vmem_limit_bytes=20 * 1024 * 1024)
    send = send.reshape(peers)
    pairs = jnp.transpose(pairs, (0, 1, 3, 2))
    integers = (counts, send, pairs, edge)
    floats = (positions, velocities, mass, smoothing)
    integers, floats, energy = jax.tree.map(
        lambda x: pltpu.with_memory_space_constraint(x, pltpu.HBM), (integers, floats, energy)
    )
    lists = [pltpu.SMEM((Tiles.FIELDS * most,), jnp.int32), pltpu.SMEM((ring,), jnp.int32)]
    density_work = [pltpu.VMEM((icut, jcut), F32)] * group + [pltpu.VMEM((icut, LANES), F32)] * group
    force_work = [pltpu.VMEM((icut, jcut), F32)] * group + [pltpu.VMEM((icut, jcut), BF16)] * (2 * group)
    wide = shape((cells, slots, LANES), F32)
    left_shape = shape((cells, slots, COLS), BF16)
    weight_shape = lambda count: pltpu.VMEM((count, DOT_K, slots), BF16)

    own, pay, odd, meta = pl.pallas_call(
        functools.partial(prep_kernel, lay),
        out_shape=[
            shape((cells, ROWS, slots), F32),
            shape((2 * peers, ROWS, slots), F32),
            shape((1, ROWS, slots), F32),
            shape((lay.size,), jnp.int32),
        ],
        in_specs=[HBM] * 8,
        out_specs=[VMEM] * 3 + [SMEM],
        scratch_shapes=[pltpu.SMEM(x.shape, jnp.int32) for x in integers]
        + [pltpu.VMEM(x.shape, F32) for x in floats]
        + [pltpu.SemaphoreType.DMA((8,))],
        compiler_params=params,
        name="prep",
    )(*integers, *floats)

    between = [(r, r + 1) for r in range(1, regions - 1, 2)]
    swap = between + [(b, a) for a, b in between]
    rec_odd = lax.ppermute(odd, ("pair", "side"), swap)
    rec = lax.all_to_all(pay, ("side", "cell"), split_axis=0, concat_axis=0, tiled=True)

    acc, left, force_left = pl.pallas_call(
        functools.partial(density_local_kernel, icut, jcut, group, lay),
        out_shape=[wide, left_shape, left_shape],
        in_specs=[SMEM, VMEM],
        out_specs=[VMEM] * 3,
        scratch_shapes=lists + [weight_shape(cells), pltpu.VMEM((cells, 8, slots), F32)] + density_work,
        compiler_params=params,
        name="density_local",
    )(meta, own)

    density, term, pay, live = pl.pallas_call(
        functools.partial(density_remote_kernel, icut, jcut, group, lay),
        out_shape=[
            shape((cells, slots), F32),
            shape((cells, 1, slots), F32),
            shape((regions * peers, 1, slots), F32),
            shape((others,), jnp.int32),
        ],
        in_specs=[SMEM] + [VMEM] * 5 + [HBM],
        out_specs=[VMEM] * 3 + [SMEM],
        scratch_shapes=lists
        + [
            weight_shape(others),
            pltpu.VMEM((others, 8, slots), F32),
            pltpu.VMEM((cells, slots, LANES), F32),
            pltpu.VMEM(energy.shape, F32),
            pltpu.SemaphoreType.DMA,
        ]
        + density_work,
        compiler_params=params,
        name="density_remote",
    )(meta, own, rec, rec_odd, acc, left, energy)

    rterm = lax.all_to_all(pay, ("pair", "side", "cell"), split_axis=0, concat_axis=0, tiled=True)

    acc, bcol, ccol = pl.pallas_call(
        functools.partial(force_local_kernel, icut, jcut, group, lay),
        out_shape=[shape((cells, 16, slots), F32), wide, wide],
        in_specs=[SMEM] + [VMEM] * 3,
        out_specs=[VMEM] * 3,
        scratch_shapes=lists
        + [
            weight_shape(cells),
            weight_shape(cells),
            pltpu.VMEM((cells, 16, slots), F32),
            pltpu.VMEM((cells, DOT_K, slots), F32),
        ]
        + force_work,
        compiler_params=params,
        name="force_local",
    )(meta, own, term, force_left)

    accel, heat = pl.pallas_call(
        functools.partial(force_remote_kernel, icut, jcut, group, lay),
        out_shape=[shape((3, cells, slots), F32), shape((cells, slots), F32)],
        in_specs=[SMEM] * 2 + [VMEM] * 9,
        out_specs=[VMEM] * 2,
        scratch_shapes=lists
        + [
            weight_shape(others),
            weight_shape(others),
            pltpu.VMEM((others, 16, slots), F32),
            pltpu.VMEM((cells, DOT_K, slots), F32),
        ]
        + force_work,
        compiler_params=params,
        name="force_remote",
    )(meta, live, own, rec, rec_odd, term, rterm, acc, force_left, bcol, ccol)
    return density, accel, heat


def solution(mesh):
    regions, peers = mesh.devices.shape
    mesh = jax.sharding.Mesh(mesh.devices.reshape(regions // 2, 2, peers), ("pair", "side", "cell"))
    region = ("pair", "side")
    every = (*region, "cell")
    placed = (
        P(None, every, None),
        P(None, every, None),
        P(every, None),
        P(every, None),
        P(every, None),
        P(every),
        P(region, "cell", None, None),
        P(region, "cell", None, None),
        P(region, "cell", None),
    )
    return jax.shard_map(
        on_device,
        mesh=mesh,
        in_specs=placed,
        out_specs=(P(every, None), P(None, every, None), P(every, None)),
        check_vma=False,
    )
```

```python
import functools
import math

import jax
import jax.numpy as jnp
from jax import lax
from jax.experimental import pallas as pl
from jax.experimental.pallas import tpu as pltpu
from jax.sharding import PartitionSpec as P

GAMMA = 5.0 / 3.0
LANES = 128
BF16 = jnp.bfloat16
F32 = jnp.float32

ROWS = 8
TINY = 1e-12
DOT_K = 48
COLS = 64
STRIP = 16

VMEM = pl.BlockSpec(memory_space=pltpu.VMEM)
SMEM = pl.BlockSpec(memory_space=pltpu.SMEM)
HBM = pl.BlockSpec(memory_space=pltpu.HBM)


def row_ids(shape):
    return lax.broadcasted_iota(jnp.int32, shape, 0)


def split3(value):
    first = value.astype(BF16).astype(F32)
    rest = value - first
    second = rest.astype(BF16).astype(F32)
    return first, second, rest - second


def left_parts(value):
    a, b, c = split3(value)
    return jnp.concatenate([a, a, b, b, a, c], axis=0)


def right_parts(value):
    a, b, c = split3(value)
    return jnp.concatenate([a, b, a, b, c, a], axis=0).astype(BF16)


def norm_row(rows):
    return rows[0:1] * rows[0:1] + rows[1:2] * rows[1:2] + rows[2:3] * rows[2:3]


def left_comps(rows):
    ids = row_ids(rows.shape)
    return jnp.where(ids < 3, rows, jnp.where(ids == 3, norm_row(rows), jnp.where(ids == 4, 1.0, 0.0)))


def right_comps(rows):
    ids = row_ids(rows.shape)
    return jnp.where(ids < 3, -2.0 * rows, jnp.where(ids == 3, 1.0, jnp.where(ids == 4, norm_row(rows), 0.0)))


def chunks(count, size):
    return lax.shift_right_logical(count + (size - 1), jnp.int32(size.bit_length() - 1))


class Meta:
    def __init__(self, cells, regions, peers, pairs):
        self.cells, self.regions, self.peers, self.pairs = cells, regions, peers, pairs
        self.send = cells
        self.pair = cells + peers
        self.edge = self.pair + 2 * pairs
        self.size = self.edge + 2


def prep_kernel(
    lay,
    counts_in, send_in, pairs_in, edge_in, pos_in, vel_in, mass_in, smooth_in,
    own, pay, odd, meta,
    counts, send, pairs, edge, pos, vel, mass, smooth, sems,
):
    inputs = (counts_in, send_in, pairs_in, edge_in, pos_in, vel_in, mass_in, smooth_in)
    buffers = (counts, send, pairs, edge, pos, vel, mass, smooth)
    copies = [
        pltpu.make_async_copy(source, target, sems.at[k])
        for k, (source, target) in enumerate(zip(inputs, buffers))
    ]
    for copy in copies:
        copy.start()
    for copy in copies:
        copy.wait()
    cells = mass.shape[0]
    slots = mass.shape[1]
    for k in range(cells):
        meta[k] = counts[k]
    for k in range(lay.peers):
        meta[lay.send + k] = send[k]
    for k in range(lay.pairs):
        for side in range(2):
            meta[lay.pair + 2 * k + side] = pairs[0, 0, side, k]
    for side in range(2):
        meta[lay.edge + side] = edge[0, 0, side]

    lane = lax.broadcasted_iota(jnp.int32, (1, slots), 1)
    for k in range(cells):
        live = lane < counts[k]
        for d in range(3):
            own[k, d : d + 1, :] = pos[d, k : k + 1, :] - 0.5
            own[k, 5 + d : 6 + d, :] = vel[d, k : k + 1, :]
        own[k, 3:4, :] = jnp.where(live, mass[k : k + 1, :], 0.0)
        own[k, 4:5, :] = smooth[k : k + 1, :]

    place = Place(lay)
    pay[...] = jnp.zeros_like(pay)

    def peer(k, carry):
        picked = send[k]
        pay[place.pair_peers + k] = jnp.where(picked >= 0, own[jnp.maximum(picked, 0)], 0.0)
        return carry

    lax.fori_loop(0, lay.peers, peer, 0)
    pay[place.pair_partner] = own[meta[place.partner_edge]]
    odd[0] = own[meta[place.odd_edge]]


class Place:
    def __init__(self, lay):
        peers, regions = lay.peers, lay.regions
        self.side = lax.axis_index("side")
        here = lax.axis_index("cell")
        region = 2 * lax.axis_index("pair") + self.side
        other = region - 1 + 2 * self.side
        self.partner_edge = lay.edge + 1 - self.side
        self.odd_edge = lay.edge + self.side
        self.pair_peers = self.side * peers
        self.pair_partner = (1 - self.side) * peers + here
        self.peers = region * peers
        self.partner = (region + 1 - 2 * self.side) * peers + here
        self.has_odd = (other >= 0) & (other < regions)
        self.odd = jnp.clip(other, 0, regions - 1) * peers + here


class Tiles:
    FIELDS = 7

    def __init__(self, icut, jcut, table):
        self.icut, self.jcut, self.table = icut, jcut, table
        self.count = self.blocks = jnp.int32(0)

    def push(self, a, b, w, ok, i, ni, j, nj):
        at = self.FIELDS * self.count
        for field, value in enumerate((a, b, w, i, ni, j, nj)):
            self.table[at + field] = value
        self.count = self.count + ok.astype(jnp.int32)
        self.blocks = self.blocks + jnp.where(ok, ni * nj, 0)

    def whole(self, a, b, w, ok, alive, blive):
        self.push(a, b, w, ok, 0, chunks(alive, self.icut), 0, chunks(blive, self.jcut))

    def close(self):
        self.push(0, 0, 0, jnp.bool_(False), 0, 1, 0, 1)


def local_tiles(tiles, lay, meta, both):
    cells = lay.cells
    one = jnp.int32(1)

    def key(row):
        first = meta[lay.pair + 2 * row]
        second = meta[lay.pair + 2 * row + 1]
        return jnp.minimum(first, second) * cells + jnp.maximum(first, second)

    keys = [key(row) for row in range(lay.pairs)]
    for a in range(cells):
        for b in range(a + 1, cells):
            mult = jnp.int32(0)
            for pair in keys:
                mult = mult + (pair == a * cells + b).astype(jnp.int32)
            tiles.whole(a, b, mult, mult > 0, meta[a], meta[b])
            if not both:
                tiles.whole(b, a, mult, mult > 0, meta[b], meta[a])
    if not both:
        for a in range(cells):
            tiles.whole(a, a, one, meta[a] > 0, meta[a], meta[a])
        tiles.close()
        return None
    span = tiles.jcut // tiles.icut
    for a in range(cells):
        tiles.push(a, a, one, meta[a] > tiles.jcut, 0, span, 1, chunks(meta[a], tiles.jcut) - 1)
    mutual = tiles.blocks
    for a in range(cells):
        rows = chunks(meta[a], tiles.icut)
        tiles.push(a, a, one, meta[a] > 0, 0, jnp.minimum(rows, span), 0, 1)
        tiles.push(a, a, one, meta[a] > tiles.jcut, span, rows - span, 1, 1)
    tiles.close()
    return mutual


def remote_tiles(tiles, lay, meta, live):
    one = jnp.int32(1)
    for k in range(lay.peers):
        picked = meta[lay.send + k]
        a = jnp.maximum(picked, 0)
        tiles.whole(a, k, one, (picked >= 0) & (live[k] > 0), meta[a], live[k])
    place = Place(lay)
    for b, edge in ((lay.peers, place.partner_edge), (lay.peers + 1, place.odd_edge)):
        a = meta[edge]
        tiles.whole(a, b, one, live[b] > 0, meta[a], live[b])
    tiles.close()


class Blocks:
    FIELDS = 5

    def __init__(self, tiles, ring):
        self.icut, self.jcut = tiles.icut, tiles.jcut
        self.table, self.last = tiles.table, tiles.count
        self.ring, self.total = ring, tiles.blocks

    def clear(self, entries):
        for k in range(entries * self.FIELDS):
            self.ring[k] = 0

    def write(self, slot, state):
        n, ii, jj = state
        a, b, w, i, ni, j, nj = (self.table[Tiles.FIELDS * n + k] for k in range(Tiles.FIELDS))
        for field, value in enumerate((a, b, (i + ii) * self.icut, (j + jj) * self.jcut, w)):
            self.ring[self.FIELDS * slot + field] = value
        jwrap = jj + 1 >= nj
        inext = jnp.where(jwrap, ii + 1, ii)
        iwrap = inext >= ni
        return (
            jnp.minimum(jnp.where(iwrap, n + 1, n), self.last),
            jnp.where(iwrap, 0, inext),
            jnp.where(jwrap, 0, jj + 1),
        )

    def read(self, slot):
        a, b, istart, jstart, w = (self.ring[self.FIELDS * slot + k] for k in range(self.FIELDS))
        return (
            a,
            b,
            pl.multiple_of(istart, self.icut),
            pl.multiple_of(jstart, self.jcut),
            w.astype(F32),
        )

    def distances(self, slot, left, right, out):
        a, b, istart, jstart, _ = self.read(slot)
        out[...] = jnp.dot(
            left[a, pl.ds(istart, self.icut), :DOT_K],
            right[b, :, pl.ds(jstart, self.jcut)],
            preferred_element_type=F32,
        )


def density_loop(group, blocks, total, left, right, mrow, acc, work):
    icut, jcut = blocks.icut, blocks.jcut
    dist, parts = work[:group], work[group:]
    zero = jnp.int32(0)
    state = (zero, zero, zero)
    for g in range(2 * group):
        state = blocks.write(g, state)
    for g in range(group):
        blocks.distances(g, left, right, dist[g])

    def step(k, state):
        for g in range(group):
            _, b, _, jstart, _ = blocks.read(k * group + g)
            root = jnp.concatenate([mrow[b, 0:8, pl.ds(jstart, jcut)]] * (STRIP // 8), axis=0)
            half = jnp.concatenate([mrow[b, 8:16, pl.ds(jstart, jcut)]] * (STRIP // 8), axis=0)
            for row in range(0, icut, STRIP):
                s = jnp.maximum(dist[g][row : row + STRIP, :], TINY)
                e = root - s * lax.rsqrt(s)
                u = jnp.maximum(e, 0.0)
                t = jnp.minimum(half - (s * 3.0) * e, u * u * u)
                part = t[:, :LANES]
                for at in range(1, jcut // LANES):
                    part = part + t[:, at * LANES : (at + 1) * LANES]
                parts[g][row : row + STRIP, :] = part

            state = blocks.write((k + 2) * group + g, state)
            blocks.distances((k + 1) * group + g, left, right, dist[g])
        for g in range(group):
            a, _, istart, _, w = blocks.read(k * group + g)
            acc[a, pl.ds(istart, icut), :] += parts[g][...] * w
        return state

    lax.fori_loop(0, chunks(total, group), step, state)


def density_source(rows, right, mrow, at):
    m = rows[3:4]
    root = jnp.where(m > 0.0, jnp.exp(jnp.log(jnp.maximum(m, 1e-30)) * (1.0 / 3.0)), 0.0)
    right[at] = right_parts(right_comps(rows) * (root * root))
    shape = (8, rows.shape[1])
    half = 0.5 * (root * root * root)
    mrow[at] = jnp.concatenate([jnp.broadcast_to(root, shape), jnp.broadcast_to(half, shape)], axis=0)


def spread_left(parts, left, cell):
    for at in range(parts.shape[1] // LANES):
        left[cell, pl.ds(at * LANES, LANES), :] = parts[:, at * LANES : (at + 1) * LANES].T.astype(BF16)


def force_scales(rows):
    h = rows[4:5]
    inv = 1.0 / jnp.where(h > 0.0, h, 1.0)
    b = math.sqrt(24.0 / math.pi) * (inv * inv)
    return b, b * inv


def density_local_kernel(
    icut, jcut, group, lay, meta, own, acc, left, force_left, table, ring, right, mrow, *work
):
    slots = own.shape[2]
    ids = row_ids((8, slots))
    empty = jnp.zeros((8, slots), F32)
    for k in range(lay.cells):
        rows = own[k]
        inv = 1.0 / rows[4:5]
        comps = left_comps(rows)
        spread_left(jnp.concatenate([left_parts(comps * (inv * inv)), empty, empty], axis=0), left, k)
        scales = empty
        for at, part in enumerate(x for scale in force_scales(rows) for x in split3(scale)):
            scales = jnp.where(ids == at, part, scales)
        spread_left(jnp.concatenate([left_parts(comps), scales, empty], axis=0), force_left, k)
        density_source(rows, right, mrow, k)
        acc[k] = jnp.zeros((slots, LANES), F32)
    tiles = Tiles(icut, jcut, table)
    local_tiles(tiles, lay, meta, False)
    blocks = Blocks(tiles, ring)
    density_loop(group, blocks, tiles.blocks, left, right, mrow, acc, work)


def density_remote_kernel(
    icut, jcut, group, lay,
    meta, own, rec, rec_odd, acc_in, left, energy_in,
    rho_out, term_out, pay, live,
    table, ring, right, mrow, acc, energy, sem, *work,
):
    cells, peers = lay.cells, lay.peers
    slots = own.shape[2]
    copy = pltpu.make_async_copy(energy_in, energy, sem)
    copy.start()
    place = Place(lay)
    occupied = jnp.where(rec[:, 3, :] > 0.0, 1.0, 0.0).reshape(2, peers, slots)
    occupied = jnp.sum(jnp.where(place.side == 0, occupied[0], occupied[1]), axis=1, keepdims=True)
    for k in range(peers):
        live[k] = occupied[k, 0].astype(jnp.int32)
    for k, rows in ((peers, rec[place.pair_partner]), (peers + 1, rec_odd[0])):
        live[k] = jnp.sum(jnp.where(rows[3:4] > 0.0, 1.0, 0.0)).astype(jnp.int32)

    def rec_cell(k, carry):
        density_source(rec[place.pair_peers + k], right, mrow, k)
        return carry

    lax.fori_loop(0, peers, rec_cell, 0, unroll=4)
    density_source(rec[place.pair_partner], right, mrow, peers)
    density_source(rec_odd[0], right, mrow, peers + 1)
    acc[...] = acc_in[...]
    tiles = Tiles(icut, jcut, table)
    remote_tiles(tiles, lay, meta, live)
    blocks = Blocks(tiles, ring)
    density_loop(group, blocks, tiles.blocks, left, right, mrow, acc, work)

    copy.wait()
    lane = lax.broadcasted_iota(jnp.int32, (1, slots), 1)
    ones = jnp.ones((8, 2 * LANES), BF16)
    for k in range(cells):
        one = acc[k].astype(BF16)
        two = (acc[k] - one.astype(F32)).astype(BF16)
        total_row = lax.dot_general(
            ones,
            jnp.concatenate([one, two], axis=1),
            (((1,), (1,)), ((), ())),
            preferred_element_type=F32,
        )
        inv = 1.0 / own[k, 4:5, :]
        rho = total_row[0:1] * (16.0 / math.pi) * (inv * inv * inv)
        occupied = jnp.where(lane < meta[k], 1.0, 0.0)
        rho_out[k : k + 1, :] = rho * occupied
        term_out[k] = occupied * (GAMMA - 1.0) * energy[k : k + 1, :] / (rho + 1.0 - occupied)

    pay[...] = jnp.zeros_like(pay)

    def peer(k, carry):
        pay[place.peers + k] = term_out[jnp.maximum(meta[lay.send + k], 0)]
        return carry

    lax.fori_loop(0, peers, peer, 0)
    pay[place.partner] = term_out[meta[place.partner_edge]]

    @pl.when(place.has_odd)
    def _():
        pay[place.odd] = term_out[meta[place.odd_edge]]


def force_source(rows, pressure, right, weights, scale, at):
    slots = rows.shape[1]
    right[at] = right_parts(right_comps(rows))
    b, c = force_scales(rows)
    scale[at] = jnp.concatenate([jnp.broadcast_to(b, (8, slots)), jnp.broadcast_to(c, (8, slots))], axis=0)
    m = rows[3:4]
    mp = m * pressure
    xv = rows[0:1] * rows[5:6] + rows[1:2] * rows[6:7] + rows[2:3] * rows[7:8]
    ids = row_ids((8, slots))
    base = jnp.where(ids == 3, 1.0, jnp.where(ids == 4, xv, rows))
    sums = jnp.concatenate([base * m, jnp.where(ids < 4, base, 0.0) * mp], axis=0)
    one, two, three = split3(sums)
    weights[at] = jnp.concatenate([one, two, three], axis=0).astype(BF16)


def force_loop(group, blocks, total, local, left, right, weights, scale, bcol, ccol, acc, work):
    icut, jcut = blocks.icut, blocks.jcut
    dist, upper, lower = work[:group], work[group : 2 * group], work[2 * group :]
    blocks.clear(group)
    for ref in (*upper, *lower):
        ref[...] = jnp.zeros_like(ref)
    zero = jnp.int32(0)
    state = (zero, zero, zero)
    for g in range(2 * group):
        state = blocks.write(group + g, state)
    for g in range(group):
        blocks.distances(group + g, left, right, dist[g])

    def sums_of(rows, columns, k, g):
        a, b, istart, jstart, w = blocks.read(k * group + g)
        adds = []
        if rows:
            wt = weights[b, :, pl.ds(jstart, jcut)]
            spec = (((1,), (1,)), ((), ()))
            part = lax.dot_general(wt, upper[g][...], spec, preferred_element_type=F32)
            part = part + lax.dot_general(wt, lower[g][...], spec, preferred_element_type=F32)
            keep = w
            if columns:
                keep = jnp.where(k * group + g < local + group, w, 0.0)
            adds.append((a, istart, part * keep))
        if columns:
            wt = weights[a, :, pl.ds(istart, icut)]
            part = jnp.dot(wt, upper[g][...], preferred_element_type=F32)
            part = part + jnp.dot(wt, lower[g][...], preferred_element_type=F32)
            adds.append((b, jstart, part * w))
        return adds

    def store(adds):
        for cell, start, part in adds:
            acc[cell, :, pl.ds(start, part.shape[1])] += part

    def step(rows, columns, k, state):
        adds = []
        for g in range(group):
            adds += sums_of(rows, columns, k, g)

            a, b, istart, jstart, _ = blocks.read((k + 1) * group + g)
            bj = jnp.concatenate([scale[b, 0:8, pl.ds(jstart, jcut)]] * (STRIP // 8), axis=0)
            cj = jnp.concatenate([scale[b, 8:16, pl.ds(jstart, jcut)]] * (STRIP // 8), axis=0)
            for row in range(0, icut, STRIP):
                s = jnp.maximum(dist[g][row : row + STRIP, :], TINY)
                r = lax.rsqrt(s)
                d = s * r
                bi = bcol[a, pl.ds(istart + row, STRIP), :]
                ci = ccol[a, pl.ds(istart + row, STRIP), :]
                bi = jnp.concatenate([bi] * (jcut // LANES), axis=1)
                ci = jnp.concatenate([ci] * (jcut // LANES), axis=1)
                t = ci * d
                u = jnp.maximum(bi - t, 0.0)
                v = jnp.minimum(t, u)
                slope = (u + u - v) * v
                t = cj * d
                u = jnp.maximum(bj - t, 0.0)
                v = jnp.minimum(t, u)
                slope = (slope + (u + u - v) * v) * r
                rounded = slope.astype(BF16)
                upper[g][row : row + STRIP, :] = rounded
                lower[g][row : row + STRIP, :] = (slope - rounded.astype(F32)).astype(BF16)

            state = blocks.write((k + 3) * group + g, state)
            blocks.distances((k + 2) * group + g, left, right, dist[g])
        store(adds)
        return state

    steps = chunks(total, group)
    adds = []
    if local is None:
        lax.fori_loop(0, steps, functools.partial(step, True, False), state)
        for g in range(group):
            adds += sums_of(True, False, steps, g)
    else:
        first = jnp.minimum(chunks(local, group) + 1, steps)
        state = lax.fori_loop(0, first, functools.partial(step, True, True), state)
        lax.fori_loop(first, steps, functools.partial(step, False, True), state)
        for g in range(group):
            adds += sums_of(True, True, steps, g)
    store(adds)


def force_local_kernel(
    icut, jcut, group, lay,
    meta, own, term, left,
    acc_out, bcol, ccol,
    table, ring, right, weights, scale, acc, *work,
):
    slots = own.shape[2]
    part = lax.broadcasted_iota(jnp.int32, (COLS, 2 * LANES), 0) - DOT_K
    lane = lax.broadcasted_iota(jnp.int32, (COLS, 2 * LANES), 1)
    of_b = (part >= 0) & (part < 3) & (lane < LANES)
    of_c = (part >= 3) & (part < 6) & (lane >= LANES)
    pick = jnp.where(of_b | of_c, 1.0, 0.0).astype(BF16)
    for k in range(lay.cells):
        force_source(own[k], term[k], right, weights, scale, k)
        acc[k] = jnp.zeros((DOT_K, slots), F32)
        for at in range(slots // LANES):
            here = pl.ds(at * LANES, LANES)
            both = jnp.dot(left[k, here, :], pick, preferred_element_type=F32)
            bcol[k, here, :] = both[:, :LANES]
            ccol[k, here, :] = both[:, LANES:]
    tiles = Tiles(icut, jcut, table)
    local = local_tiles(tiles, lay, meta, True)
    blocks = Blocks(tiles, ring)
    force_loop(
        group, blocks, tiles.blocks, local, left, right, weights, scale, bcol, ccol, acc, work
    )
    for k in range(lay.cells):
        acc_out[k] = acc[k, 0:16, :] + (acc[k, 16:32, :] + acc[k, 32:48, :])


def force_remote_kernel(
    icut, jcut, group, lay,
    meta, live, own, rec, rec_odd, term, rterm, acc_in, left, bcol, ccol,
    accel_out, heat_out,
    table, ring, right, weights, scale, acc, *work,
):
    cells, peers = lay.cells, lay.peers
    slots = own.shape[2]
    place = Place(lay)

    def rec_cell(k, carry):
        force_source(rec[place.pair_peers + k], rterm[place.peers + k], right, weights, scale, k)
        return carry

    lax.fori_loop(0, peers, rec_cell, 0, unroll=4)
    force_source(rec[place.pair_partner], rterm[place.partner], right, weights, scale, peers)
    force_source(rec_odd[0], rterm[place.odd], right, weights, scale, peers + 1)
    acc[...] = jnp.zeros_like(acc)
    tiles = Tiles(icut, jcut, table)
    remote_tiles(tiles, lay, meta, live)
    blocks = Blocks(tiles, ring)
    force_loop(
        group, blocks, tiles.blocks, None, left, right, weights, scale, bcol, ccol, acc, work
    )

    lane = lax.broadcasted_iota(jnp.int32, (1, slots), 1)
    for k in range(cells):
        occupied = jnp.where(lane < meta[k], 1.0, 0.0)
        sums = acc_in[k] + acc[k, 0:16, :] + (acc[k, 16:32, :] + acc[k, 32:48, :])
        pressure = term[k]
        x = [own[k, d : d + 1, :] for d in range(3)]
        v = [own[k, 5 + d : 6 + d, :] for d in range(3)]
        both = pressure * sums[3:4] + sums[11:12]
        for d in range(3):
            accel_out[d, k : k + 1, :] = occupied * (
                x[d] * both - pressure * sums[d : d + 1] - sums[8 + d : 9 + d]
            )
        xv = x[0] * v[0] + x[1] * v[1] + x[2] * v[2]
        total_heat = xv * sums[3:4] + sums[4:5]
        for d in range(3):
            total_heat = total_heat - v[d] * sums[d : d + 1] - x[d] * sums[5 + d : 6 + d]
        heat_out[k : k + 1, :] = -occupied * pressure * total_heat


def on_device(positions, velocities, mass, smoothing, energy, counts, send, pairs, edge):
    cells, slots = mass.shape
    peers = send.shape[2]
    regions = 2 * lax.axis_size("pair")
    lay = Meta(cells, regions, peers, pairs.shape[2])
    others = peers + 2
    most = max(cells * (cells - 1) // 2 + 3 * cells, cells * cells, others) + 1
    icut, jcut, group = 128, slots // 2, 8
    dcut, dgroup = 64, 16
    ring = Blocks.FIELDS * (most * (slots // dcut) * (slots // jcut) + 6 * dgroup)
    shape = jax.ShapeDtypeStruct
    params = pltpu.CompilerParams(vmem_limit_bytes=20 * 1024 * 1024)
    send = send.reshape(peers)
    pairs = jnp.transpose(pairs, (0, 1, 3, 2))
    integers = (counts, send, pairs, edge)
    floats = (positions, velocities, mass, smoothing)
    integers, floats, energy = jax.tree.map(
        lambda x: pltpu.with_memory_space_constraint(x, pltpu.HBM), (integers, floats, energy)
    )
    lists = [pltpu.SMEM((Tiles.FIELDS * most,), jnp.int32), pltpu.SMEM((ring,), jnp.int32)]
    density_work = [pltpu.VMEM((dcut, jcut), F32)] * dgroup + [pltpu.VMEM((dcut, LANES), F32)] * dgroup
    force_work = [pltpu.VMEM((icut, jcut), F32)] * group + [pltpu.VMEM((icut, jcut), BF16)] * (2 * group)
    wide = shape((cells, slots, LANES), F32)
    left_shape = shape((cells, slots, COLS), BF16)
    weight_shape = lambda count: pltpu.VMEM((count, DOT_K, slots), BF16)

    own, pay, odd, meta = pl.pallas_call(
        functools.partial(prep_kernel, lay),
        out_shape=[
            shape((cells, ROWS, slots), F32),
            shape((2 * peers, ROWS, slots), F32),
            shape((1, ROWS, slots), F32),
            shape((lay.size,), jnp.int32),
        ],
        in_specs=[HBM] * 8,
        out_specs=[VMEM] * 3 + [SMEM],
        scratch_shapes=[pltpu.SMEM(x.shape, jnp.int32) for x in integers]
        + [pltpu.VMEM(x.shape, F32) for x in floats]
        + [pltpu.SemaphoreType.DMA((8,))],
        compiler_params=params,
        name="prep",
    )(*integers, *floats)

    between = [(r, r + 1) for r in range(1, regions - 1, 2)]
    swap = between + [(b, a) for a, b in between]
    rec_odd = lax.ppermute(odd, ("pair", "side"), swap)
    rec = lax.all_to_all(pay, ("side", "cell"), split_axis=0, concat_axis=0, tiled=True)

    acc, left, force_left = pl.pallas_call(
        functools.partial(density_local_kernel, dcut, jcut, dgroup, lay),
        out_shape=[wide, left_shape, left_shape],
        in_specs=[SMEM, VMEM],
        out_specs=[VMEM] * 3,
        scratch_shapes=lists + [weight_shape(cells), pltpu.VMEM((cells, 16, slots), F32)] + density_work,
        compiler_params=params,
        name="density_local",
    )(meta, own)

    density, term, pay, live = pl.pallas_call(
        functools.partial(density_remote_kernel, dcut, jcut, dgroup, lay),
        out_shape=[
            shape((cells, slots), F32),
            shape((cells, 1, slots), F32),
            shape((regions * peers, 1, slots), F32),
            shape((others,), jnp.int32),
        ],
        in_specs=[SMEM] + [VMEM] * 5 + [HBM],
        out_specs=[VMEM] * 3 + [SMEM],
        scratch_shapes=lists
        + [
            weight_shape(others),
            pltpu.VMEM((others, 16, slots), F32),
            pltpu.VMEM((cells, slots, LANES), F32),
            pltpu.VMEM(energy.shape, F32),
            pltpu.SemaphoreType.DMA,
        ]
        + density_work,
        compiler_params=params,
        name="density_remote",
    )(meta, own, rec, rec_odd, acc, left, energy)

    rterm = lax.all_to_all(pay, ("pair", "side", "cell"), split_axis=0, concat_axis=0, tiled=True)

    acc, bcol, ccol = pl.pallas_call(
        functools.partial(force_local_kernel, icut, jcut, group, lay),
        out_shape=[shape((cells, 16, slots), F32), wide, wide],
        in_specs=[SMEM] + [VMEM] * 3,
        out_specs=[VMEM] * 3,
        scratch_shapes=lists
        + [
            weight_shape(cells),
            weight_shape(cells),
            pltpu.VMEM((cells, 16, slots), F32),
            pltpu.VMEM((cells, DOT_K, slots), F32),
        ]
        + force_work,
        compiler_params=params,
        name="force_local",
    )(meta, own, term, force_left)

    accel, heat = pl.pallas_call(
        functools.partial(force_remote_kernel, icut, jcut, group, lay),
        out_shape=[shape((3, cells, slots), F32), shape((cells, slots), F32)],
        in_specs=[SMEM] * 2 + [VMEM] * 9,
        out_specs=[VMEM] * 2,
        scratch_shapes=lists
        + [
            weight_shape(others),
            weight_shape(others),
            pltpu.VMEM((others, 16, slots), F32),
            pltpu.VMEM((cells, DOT_K, slots), F32),
        ]
        + force_work,
        compiler_params=params,
        name="force_remote",
    )(meta, live, own, rec, rec_odd, term, rterm, acc, force_left, bcol, ccol)
    return density, accel, heat


def solution(mesh):
    regions, peers = mesh.devices.shape
    mesh = jax.sharding.Mesh(mesh.devices.reshape(regions // 2, 2, peers), ("pair", "side", "cell"))
    region = ("pair", "side")
    every = (*region, "cell")
    placed = (
        P(None, every, None),
        P(None, every, None),
        P(every, None),
        P(every, None),
        P(every, None),
        P(every),
        P(region, "cell", None, None),
        P(region, "cell", None, None),
        P(region, "cell", None),
    )
    return jax.shard_map(
        on_device,
        mesh=mesh,
        in_specs=placed,
        out_specs=(P(every, None), P(None, every, None), P(every, None)),
        check_vma=False,
    )
```

```python
import functools
import math

import jax
import jax.numpy as jnp
from jax import lax
from jax.experimental import pallas as pl
from jax.experimental.pallas import tpu as pltpu
from jax.sharding import PartitionSpec as P

GAMMA = 5.0 / 3.0
LANES = 128
BF16 = jnp.bfloat16
F32 = jnp.float32

ROWS = 8
TINY = 1e-12
DOT_K = 48
COLS = 64
STRIP = 16

VMEM = pl.BlockSpec(memory_space=pltpu.VMEM)
SMEM = pl.BlockSpec(memory_space=pltpu.SMEM)
HBM = pl.BlockSpec(memory_space=pltpu.HBM)


def row_ids(shape):
    return lax.broadcasted_iota(jnp.int32, shape, 0)


def split3(value):
    first = value.astype(BF16).astype(F32)
    rest = value - first
    second = rest.astype(BF16).astype(F32)
    return first, second, rest - second


def left_parts(value):
    a, b, c = split3(value)
    return jnp.concatenate([a, a, b, b, a, c], axis=0)


def right_parts(value):
    a, b, c = split3(value)
    return jnp.concatenate([a, b, a, b, c, a], axis=0).astype(BF16)


def norm_row(rows):
    return rows[0:1] * rows[0:1] + rows[1:2] * rows[1:2] + rows[2:3] * rows[2:3]


def left_comps(rows):
    ids = row_ids(rows.shape)
    return jnp.where(ids < 3, rows, jnp.where(ids == 3, norm_row(rows), jnp.where(ids == 4, 1.0, 0.0)))


def right_comps(rows):
    ids = row_ids(rows.shape)
    return jnp.where(ids < 3, -2.0 * rows, jnp.where(ids == 3, 1.0, jnp.where(ids == 4, norm_row(rows), 0.0)))


def chunks(count, size):
    return lax.shift_right_logical(count + (size - 1), jnp.int32(size.bit_length() - 1))


class Meta:
    def __init__(self, cells, regions, peers, pairs):
        self.cells, self.regions, self.peers, self.pairs = cells, regions, peers, pairs
        self.send = cells
        self.pair = cells + peers
        self.edge = self.pair + 2 * pairs
        self.size = self.edge + 2


def prep_kernel(
    lay,
    counts_in, send_in, pairs_in, edge_in, pos_in, vel_in, mass_in, smooth_in,
    own, pay, odd, meta,
    counts, send, pairs, edge, pos, vel, mass, smooth, sems,
):
    inputs = (counts_in, send_in, pairs_in, edge_in, pos_in, vel_in, mass_in, smooth_in)
    buffers = (counts, send, pairs, edge, pos, vel, mass, smooth)
    copies = [
        pltpu.make_async_copy(source, target, sems.at[k])
        for k, (source, target) in enumerate(zip(inputs, buffers))
    ]
    for copy in copies:
        copy.start()
    for copy in copies:
        copy.wait()
    cells = mass.shape[0]
    slots = mass.shape[1]
    for k in range(cells):
        meta[k] = counts[k]
    for k in range(lay.peers):
        meta[lay.send + k] = send[k]
    for k in range(lay.pairs):
        for side in range(2):
            meta[lay.pair + 2 * k + side] = pairs[0, 0, side, k]
    for side in range(2):
        meta[lay.edge + side] = edge[0, 0, side]

    lane = lax.broadcasted_iota(jnp.int32, (1, slots), 1)
    for k in range(cells):
        live = lane < counts[k]
        for d in range(3):
            own[k, d : d + 1, :] = pos[d, k : k + 1, :] - 0.5
            own[k, 5 + d : 6 + d, :] = vel[d, k : k + 1, :]
        own[k, 3:4, :] = jnp.where(live, mass[k : k + 1, :], 0.0)
        own[k, 4:5, :] = smooth[k : k + 1, :]

    place = Place(lay)
    pay[...] = jnp.zeros_like(pay)

    def peer(k, carry):
        picked = send[k]
        pay[place.pair_peers + k] = jnp.where(picked >= 0, own[jnp.maximum(picked, 0)], 0.0)
        return carry

    lax.fori_loop(0, lay.peers, peer, 0)
    pay[place.pair_partner] = own[meta[place.partner_edge]]
    odd[0] = own[meta[place.odd_edge]]


class Place:
    def __init__(self, lay):
        peers, regions = lay.peers, lay.regions
        self.side = lax.axis_index("side")
        here = lax.axis_index("cell")
        region = 2 * lax.axis_index("pair") + self.side
        other = region - 1 + 2 * self.side
        self.partner_edge = lay.edge + 1 - self.side
        self.odd_edge = lay.edge + self.side
        self.pair_peers = self.side * peers
        self.pair_partner = (1 - self.side) * peers + here
        self.peers = region * peers
        self.partner = (region + 1 - 2 * self.side) * peers + here
        self.has_odd = (other >= 0) & (other < regions)
        self.odd = jnp.clip(other, 0, regions - 1) * peers + here


class Tiles:
    FIELDS = 7

    def __init__(self, icut, jcut, table):
        self.icut, self.jcut, self.table = icut, jcut, table
        self.count = self.blocks = jnp.int32(0)

    def push(self, a, b, w, ok, i, ni, j, nj):
        at = self.FIELDS * self.count
        for field, value in enumerate((a, b, w, i, ni, j, nj)):
            self.table[at + field] = value
        self.count = self.count + ok.astype(jnp.int32)
        self.blocks = self.blocks + jnp.where(ok, ni * nj, 0)

    def whole(self, a, b, w, ok, alive, blive):
        self.push(a, b, w, ok, 0, chunks(alive, self.icut), 0, chunks(blive, self.jcut))

    def close(self):
        self.push(0, 0, 0, jnp.bool_(False), 0, 1, 0, 1)


def local_tiles(tiles, lay, meta, both):
    cells = lay.cells
    one = jnp.int32(1)

    def key(row):
        first = meta[lay.pair + 2 * row]
        second = meta[lay.pair + 2 * row + 1]
        return jnp.minimum(first, second) * cells + jnp.maximum(first, second)

    keys = [key(row) for row in range(lay.pairs)]
    for a in range(cells):
        for b in range(a + 1, cells):
            mult = jnp.int32(0)
            for pair in keys:
                mult = mult + (pair == a * cells + b).astype(jnp.int32)
            tiles.whole(a, b, mult, mult > 0, meta[a], meta[b])
            if not both:
                tiles.whole(b, a, mult, mult > 0, meta[b], meta[a])
    if not both:
        for a in range(cells):
            tiles.whole(a, a, one, meta[a] > 0, meta[a], meta[a])
        tiles.close()
        return None
    span = tiles.jcut // tiles.icut
    for a in range(cells):
        tiles.push(a, a, one, meta[a] > tiles.jcut, 0, span, 1, chunks(meta[a], tiles.jcut) - 1)
    mutual = tiles.blocks
    for a in range(cells):
        rows = chunks(meta[a], tiles.icut)
        tiles.push(a, a, one, meta[a] > 0, 0, jnp.minimum(rows, span), 0, 1)
        tiles.push(a, a, one, meta[a] > tiles.jcut, span, rows - span, 1, 1)
    tiles.close()
    return mutual


def remote_tiles(tiles, lay, meta, live):
    one = jnp.int32(1)
    for k in range(lay.peers):
        picked = meta[lay.send + k]
        a = jnp.maximum(picked, 0)
        tiles.whole(a, k, one, (picked >= 0) & (live[k] > 0), meta[a], live[k])
    place = Place(lay)
    for b, edge in ((lay.peers, place.partner_edge), (lay.peers + 1, place.odd_edge)):
        a = meta[edge]
        tiles.whole(a, b, one, live[b] > 0, meta[a], live[b])
    tiles.close()


class Blocks:
    FIELDS = 5

    def __init__(self, tiles, ring):
        self.icut, self.jcut = tiles.icut, tiles.jcut
        self.table, self.last = tiles.table, tiles.count
        self.ring, self.total = ring, tiles.blocks

    def clear(self, entries):
        for k in range(entries * self.FIELDS):
            self.ring[k] = 0

    def write(self, slot, state):
        n, ii, jj = state
        a, b, w, i, ni, j, nj = (self.table[Tiles.FIELDS * n + k] for k in range(Tiles.FIELDS))
        for field, value in enumerate((a, b, (i + ii) * self.icut, (j + jj) * self.jcut, w)):
            self.ring[self.FIELDS * slot + field] = value
        jwrap = jj + 1 >= nj
        inext = jnp.where(jwrap, ii + 1, ii)
        iwrap = inext >= ni
        return (
            jnp.minimum(jnp.where(iwrap, n + 1, n), self.last),
            jnp.where(iwrap, 0, inext),
            jnp.where(jwrap, 0, jj + 1),
        )

    def read(self, slot):
        a, b, istart, jstart, w = (self.ring[self.FIELDS * slot + k] for k in range(self.FIELDS))
        return (
            a,
            b,
            pl.multiple_of(istart, self.icut),
            pl.multiple_of(jstart, self.jcut),
            w.astype(F32),
        )

    def distances(self, slot, left, right, out):
        a, b, istart, jstart, _ = self.read(slot)
        out[...] = jnp.dot(
            left[a, pl.ds(istart, self.icut), :DOT_K],
            right[b, :, pl.ds(jstart, self.jcut)],
            preferred_element_type=F32,
        )


def density_loop(group, blocks, total, left, right, mrow, acc, work):
    icut, jcut = blocks.icut, blocks.jcut
    dist, parts = work[:group], work[group:]
    zero = jnp.int32(0)
    state = (zero, zero, zero)
    for g in range(2 * group):
        state = blocks.write(g, state)
    for g in range(group):
        blocks.distances(g, left, right, dist[g])

    def step(k, state):
        for g in range(group):
            _, b, _, jstart, _ = blocks.read(k * group + g)
            root = jnp.concatenate([mrow[b, 0:8, pl.ds(jstart, jcut)]] * (STRIP // 8), axis=0)
            half = jnp.concatenate([mrow[b, 8:16, pl.ds(jstart, jcut)]] * (STRIP // 8), axis=0)
            for row in range(0, icut, STRIP):
                s = jnp.maximum(dist[g][row : row + STRIP, :], TINY)
                e = root - s * lax.rsqrt(s)
                u = jnp.maximum(e, 0.0)
                t = jnp.minimum(half - (s * 3.0) * e, u * u * u)
                part = t[:, :LANES]
                for at in range(1, jcut // LANES):
                    part = part + t[:, at * LANES : (at + 1) * LANES]
                parts[g][row : row + STRIP, :] = part

            state = blocks.write((k + 2) * group + g, state)
            blocks.distances((k + 1) * group + g, left, right, dist[g])
        for g in range(group):
            a, _, istart, _, w = blocks.read(k * group + g)
            acc[a, pl.ds(istart, icut), :] += parts[g][...] * w
        return state

    lax.fori_loop(0, chunks(total, group), step, state)


def density_source(rows, right, mrow, at):
    m = rows[3:4]
    root = jnp.where(m > 0.0, jnp.exp(jnp.log(jnp.maximum(m, 1e-30)) * (1.0 / 3.0)), 0.0)
    right[at] = right_parts(right_comps(rows) * (root * root))
    shape = (8, rows.shape[1])
    half = 0.5 * (root * root * root)
    mrow[at] = jnp.concatenate([jnp.broadcast_to(root, shape), jnp.broadcast_to(half, shape)], axis=0)


def spread_left(parts, left, cell):
    for at in range(parts.shape[1] // LANES):
        left[cell, pl.ds(at * LANES, LANES), :] = parts[:, at * LANES : (at + 1) * LANES].T.astype(BF16)


def force_scales(rows):
    h = rows[4:5]
    inv = 1.0 / jnp.where(h > 0.0, h, 1.0)
    b = math.sqrt(24.0 / math.pi) * (inv * inv)
    return b, b * inv


def density_local_kernel(
    icut, jcut, group, lay, meta, own, acc, left, force_left, table, ring, right, mrow, *work
):
    slots = own.shape[2]
    ids = row_ids((8, slots))
    empty = jnp.zeros((8, slots), F32)
    for k in range(lay.cells):
        rows = own[k]
        inv = 1.0 / rows[4:5]
        comps = left_comps(rows)
        spread_left(jnp.concatenate([left_parts(comps * (inv * inv)), empty, empty], axis=0), left, k)
        scales = empty
        for at, part in enumerate(x for scale in force_scales(rows) for x in split3(scale)):
            scales = jnp.where(ids == at, part, scales)
        spread_left(jnp.concatenate([left_parts(comps), scales, empty], axis=0), force_left, k)
        density_source(rows, right, mrow, k)
        acc[k] = jnp.zeros((slots, LANES), F32)
    tiles = Tiles(icut, jcut, table)
    local_tiles(tiles, lay, meta, False)
    blocks = Blocks(tiles, ring)
    density_loop(group, blocks, tiles.blocks, left, right, mrow, acc, work)


def density_remote_kernel(
    icut, jcut, group, lay,
    meta, own, rec, rec_odd, acc_in, left, energy_in,
    rho_out, term_out, pay, live,
    table, ring, right, mrow, acc, energy, sem, *work,
):
    cells, peers = lay.cells, lay.peers
    slots = own.shape[2]
    copy = pltpu.make_async_copy(energy_in, energy, sem)
    copy.start()
    place = Place(lay)
    occupied = jnp.where(rec[:, 3, :] > 0.0, 1.0, 0.0).reshape(2, peers, slots)
    occupied = jnp.sum(jnp.where(place.side == 0, occupied[0], occupied[1]), axis=1, keepdims=True)
    for k in range(peers):
        live[k] = occupied[k, 0].astype(jnp.int32)
    for k, rows in ((peers, rec[place.pair_partner]), (peers + 1, rec_odd[0])):
        live[k] = jnp.sum(jnp.where(rows[3:4] > 0.0, 1.0, 0.0)).astype(jnp.int32)

    def rec_cell(k, carry):
        density_source(rec[place.pair_peers + k], right, mrow, k)
        return carry

    lax.fori_loop(0, peers, rec_cell, 0, unroll=4)
    density_source(rec[place.pair_partner], right, mrow, peers)
    density_source(rec_odd[0], right, mrow, peers + 1)
    acc[...] = acc_in[...]
    tiles = Tiles(icut, jcut, table)
    remote_tiles(tiles, lay, meta, live)
    blocks = Blocks(tiles, ring)
    density_loop(group, blocks, tiles.blocks, left, right, mrow, acc, work)

    copy.wait()
    lane = lax.broadcasted_iota(jnp.int32, (1, slots), 1)
    ones = jnp.ones((8, 2 * LANES), BF16)
    for k in range(cells):
        one = acc[k].astype(BF16)
        two = (acc[k] - one.astype(F32)).astype(BF16)
        total_row = lax.dot_general(
            ones,
            jnp.concatenate([one, two], axis=1),
            (((1,), (1,)), ((), ())),
            preferred_element_type=F32,
        )
        inv = 1.0 / own[k, 4:5, :]
        rho = total_row[0:1] * (16.0 / math.pi) * (inv * inv * inv)
        occupied = jnp.where(lane < meta[k], 1.0, 0.0)
        rho_out[k : k + 1, :] = rho * occupied
        term_out[k] = occupied * (GAMMA - 1.0) * energy[k : k + 1, :] / (rho + 1.0 - occupied)

    pay[...] = jnp.zeros_like(pay)

    def peer(k, carry):
        pay[place.peers + k] = term_out[jnp.maximum(meta[lay.send + k], 0)]
        return carry

    lax.fori_loop(0, peers, peer, 0)
    pay[place.partner] = term_out[meta[place.partner_edge]]

    @pl.when(place.has_odd)
    def _():
        pay[place.odd] = term_out[meta[place.odd_edge]]


def force_source(rows, pressure, right, weights, scale, at):
    slots = rows.shape[1]
    right[at] = right_parts(right_comps(rows))
    b, c = force_scales(rows)
    scale[at] = jnp.concatenate([jnp.broadcast_to(b, (8, slots)), jnp.broadcast_to(c, (8, slots))], axis=0)
    m = rows[3:4]
    mp = m * pressure
    xv = rows[0:1] * rows[5:6] + rows[1:2] * rows[6:7] + rows[2:3] * rows[7:8]
    ids = row_ids((8, slots))
    base = jnp.where(ids == 3, 1.0, jnp.where(ids == 4, xv, rows))
    sums = jnp.concatenate([base * m, jnp.where(ids < 4, base, 0.0) * mp], axis=0)
    one, two, three = split3(sums)
    weights[at] = jnp.concatenate([one, two, three], axis=0).astype(BF16)


def force_loop(group, blocks, total, local, left, right, weights, scale, bcol, ccol, acc, work):
    icut, jcut = blocks.icut, blocks.jcut
    dist, upper, lower = work[:group], work[group : 2 * group], work[2 * group :]
    blocks.clear(group)
    for ref in (*upper, *lower):
        ref[...] = jnp.zeros_like(ref)
    zero = jnp.int32(0)
    state = (zero, zero, zero)
    for g in range(2 * group):
        state = blocks.write(group + g, state)
    for g in range(group):
        blocks.distances(group + g, left, right, dist[g])

    def sums_of(rows, columns, k, g):
        a, b, istart, jstart, w = blocks.read(k * group + g)
        adds = []
        if rows:
            wt = weights[b, :, pl.ds(jstart, jcut)]
            spec = (((1,), (1,)), ((), ()))
            part = lax.dot_general(wt, upper[g][...], spec, preferred_element_type=F32)
            part = part + lax.dot_general(wt, lower[g][...], spec, preferred_element_type=F32)
            keep = w
            if columns:
                keep = jnp.where(k * group + g < local + group, w, 0.0)
            adds.append((a, istart, part * keep))
        if columns:
            wt = weights[a, :, pl.ds(istart, icut)]
            part = jnp.dot(wt, upper[g][...], preferred_element_type=F32)
            part = part + jnp.dot(wt, lower[g][...], preferred_element_type=F32)
            adds.append((b, jstart, part * w))
        return adds

    def store(adds):
        for cell, start, part in adds:
            acc[cell, :, pl.ds(start, part.shape[1])] += part

    def step(rows, columns, k, state):
        adds = []
        for g in range(group):
            adds += sums_of(rows, columns, k, g)

            a, b, istart, jstart, _ = blocks.read((k + 1) * group + g)
            bj = jnp.concatenate([scale[b, 0:8, pl.ds(jstart, jcut)]] * (STRIP // 8), axis=0)
            cj = jnp.concatenate([scale[b, 8:16, pl.ds(jstart, jcut)]] * (STRIP // 8), axis=0)
            for row in range(0, icut, STRIP):
                s = jnp.maximum(dist[g][row : row + STRIP, :], TINY)
                r = lax.rsqrt(s)
                d = s * r
                bi = bcol[a, pl.ds(istart + row, STRIP), :]
                ci = ccol[a, pl.ds(istart + row, STRIP), :]
                bi = jnp.concatenate([bi] * (jcut // LANES), axis=1)
                ci = jnp.concatenate([ci] * (jcut // LANES), axis=1)
                t = ci * d
                u = jnp.maximum(bi - t, 0.0)
                v = jnp.minimum(t, u)
                slope = (u + u - v) * v
                t = cj * d
                u = jnp.maximum(bj - t, 0.0)
                v = jnp.minimum(t, u)
                slope = (slope + (u + u - v) * v) * r
                rounded = slope.astype(BF16)
                upper[g][row : row + STRIP, :] = rounded
                lower[g][row : row + STRIP, :] = (slope - rounded.astype(F32)).astype(BF16)

            state = blocks.write((k + 3) * group + g, state)
            blocks.distances((k + 2) * group + g, left, right, dist[g])
        store(adds)
        return state

    steps = chunks(total, group)
    adds = []
    if local is None:
        lax.fori_loop(0, steps, functools.partial(step, True, False), state)
        for g in range(group):
            adds += sums_of(True, False, steps, g)
    else:
        first = jnp.minimum(chunks(local, group) + 1, steps)
        state = lax.fori_loop(0, first, functools.partial(step, True, True), state)
        lax.fori_loop(first, steps, functools.partial(step, False, True), state)
        for g in range(group):
            adds += sums_of(True, True, steps, g)
    store(adds)


def force_local_kernel(
    icut, jcut, group, lay,
    meta, own, term, left,
    acc_out, bcol, ccol,
    table, ring, right, weights, scale, acc, *work,
):
    slots = own.shape[2]
    part = lax.broadcasted_iota(jnp.int32, (COLS, 2 * LANES), 0) - DOT_K
    lane = lax.broadcasted_iota(jnp.int32, (COLS, 2 * LANES), 1)
    of_b = (part >= 0) & (part < 3) & (lane < LANES)
    of_c = (part >= 3) & (part < 6) & (lane >= LANES)
    pick = jnp.where(of_b | of_c, 1.0, 0.0).astype(BF16)
    for k in range(lay.cells):
        force_source(own[k], term[k], right, weights, scale, k)
        acc[k] = jnp.zeros((DOT_K, slots), F32)
        for at in range(slots // LANES):
            here = pl.ds(at * LANES, LANES)
            both = jnp.dot(left[k, here, :], pick, preferred_element_type=F32)
            bcol[k, here, :] = both[:, :LANES]
            ccol[k, here, :] = both[:, LANES:]
    tiles = Tiles(icut, jcut, table)
    local = local_tiles(tiles, lay, meta, True)
    blocks = Blocks(tiles, ring)
    force_loop(
        group, blocks, tiles.blocks, local, left, right, weights, scale, bcol, ccol, acc, work
    )
    for k in range(lay.cells):
        acc_out[k] = acc[k, 0:16, :] + (acc[k, 16:32, :] + acc[k, 32:48, :])


def force_remote_kernel(
    icut, jcut, group, lay,
    meta, live, own, rec, rec_odd, term, rterm, acc_in, left, bcol, ccol,
    accel_out, heat_out,
    table, ring, right, weights, scale, acc, *work,
):
    cells, peers = lay.cells, lay.peers
    slots = own.shape[2]
    place = Place(lay)

    def rec_cell(k, carry):
        force_source(rec[place.pair_peers + k], rterm[place.peers + k], right, weights, scale, k)
        return carry

    lax.fori_loop(0, peers, rec_cell, 0, unroll=4)
    force_source(rec[place.pair_partner], rterm[place.partner], right, weights, scale, peers)
    force_source(rec_odd[0], rterm[place.odd], right, weights, scale, peers + 1)
    acc[...] = jnp.zeros_like(acc)
    tiles = Tiles(icut, jcut, table)
    remote_tiles(tiles, lay, meta, live)
    blocks = Blocks(tiles, ring)
    force_loop(
        group, blocks, tiles.blocks, None, left, right, weights, scale, bcol, ccol, acc, work
    )

    lane = lax.broadcasted_iota(jnp.int32, (1, slots), 1)
    for k in range(cells):
        occupied = jnp.where(lane < meta[k], 1.0, 0.0)
        sums = acc_in[k] + acc[k, 0:16, :] + (acc[k, 16:32, :] + acc[k, 32:48, :])
        pressure = term[k]
        x = [own[k, d : d + 1, :] for d in range(3)]
        v = [own[k, 5 + d : 6 + d, :] for d in range(3)]
        both = pressure * sums[3:4] + sums[11:12]
        for d in range(3):
            accel_out[d, k : k + 1, :] = occupied * (
                x[d] * both - pressure * sums[d : d + 1] - sums[8 + d : 9 + d]
            )
        xv = x[0] * v[0] + x[1] * v[1] + x[2] * v[2]
        total_heat = xv * sums[3:4] + sums[4:5]
        for d in range(3):
            total_heat = total_heat - v[d] * sums[d : d + 1] - x[d] * sums[5 + d : 6 + d]
        heat_out[k : k + 1, :] = -occupied * pressure * total_heat


def on_device(positions, velocities, mass, smoothing, energy, counts, send, pairs, edge):
    cells, slots = mass.shape
    peers = send.shape[2]
    regions = 2 * lax.axis_size("pair")
    lay = Meta(cells, regions, peers, pairs.shape[2])
    others = peers + 2
    most = max(cells * (cells - 1) // 2 + 3 * cells, cells * cells, others) + 1
    icut, jcut, group = 128, slots // 2, 8
    dcut, dgroup = 128, 8
    ring = Blocks.FIELDS * (most * (slots // dcut) * (slots // jcut) + 6 * dgroup)
    shape = jax.ShapeDtypeStruct
    params = pltpu.CompilerParams(vmem_limit_bytes=20 * 1024 * 1024)
    send = send.reshape(peers)
    pairs = jnp.transpose(pairs, (0, 1, 3, 2))
    integers = (counts, send, pairs, edge)
    floats = (positions, velocities, mass, smoothing)
    integers, floats, energy = jax.tree.map(
        lambda x: pltpu.with_memory_space_constraint(x, pltpu.HBM), (integers, floats, energy)
    )
    lists = [pltpu.SMEM((Tiles.FIELDS * most,), jnp.int32), pltpu.SMEM((ring,), jnp.int32)]
    density_work = [pltpu.VMEM((dcut, jcut), F32)] * dgroup + [pltpu.VMEM((dcut, LANES), F32)] * dgroup
    force_work = [pltpu.VMEM((icut, jcut), F32)] * group + [pltpu.VMEM((icut, jcut), BF16)] * (2 * group)
    wide = shape((cells, slots, LANES), F32)
    left_shape = shape((cells, slots, COLS), BF16)
    weight_shape = lambda count: pltpu.VMEM((count, DOT_K, slots), BF16)

    own, pay, odd, meta = pl.pallas_call(
        functools.partial(prep_kernel, lay),
        out_shape=[
            shape((cells, ROWS, slots), F32),
            shape((2 * peers, ROWS, slots), F32),
            shape((1, ROWS, slots), F32),
            shape((lay.size,), jnp.int32),
        ],
        in_specs=[HBM] * 8,
        out_specs=[VMEM] * 3 + [SMEM],
        scratch_shapes=[pltpu.SMEM(x.shape, jnp.int32) for x in integers]
        + [pltpu.VMEM(x.shape, F32) for x in floats]
        + [pltpu.SemaphoreType.DMA((8,))],
        compiler_params=params,
        name="prep",
    )(*integers, *floats)

    between = [(r, r + 1) for r in range(1, regions - 1, 2)]
    swap = between + [(b, a) for a, b in between]
    rec_odd = lax.ppermute(odd, ("pair", "side"), swap)
    rec = lax.all_to_all(pay, ("side", "cell"), split_axis=0, concat_axis=0, tiled=True)

    acc, left, force_left = pl.pallas_call(
        functools.partial(density_local_kernel, dcut, jcut, dgroup, lay),
        out_shape=[wide, left_shape, left_shape],
        in_specs=[SMEM, VMEM],
        out_specs=[VMEM] * 3,
        scratch_shapes=lists + [weight_shape(cells), pltpu.VMEM((cells, 16, slots), F32)] + density_work,
        compiler_params=params,
        name="density_local",
    )(meta, own)

    density, term, pay, live = pl.pallas_call(
        functools.partial(density_remote_kernel, dcut, jcut, dgroup, lay),
        out_shape=[
            shape((cells, slots), F32),
            shape((cells, 1, slots), F32),
            shape((regions * peers, 1, slots), F32),
            shape((others,), jnp.int32),
        ],
        in_specs=[SMEM] + [VMEM] * 5 + [HBM],
        out_specs=[VMEM] * 3 + [SMEM],
        scratch_shapes=lists
        + [
            weight_shape(others),
            pltpu.VMEM((others, 16, slots), F32),
            pltpu.VMEM((cells, slots, LANES), F32),
            pltpu.VMEM(energy.shape, F32),
            pltpu.SemaphoreType.DMA,
        ]
        + density_work,
        compiler_params=params,
        name="density_remote",
    )(meta, own, rec, rec_odd, acc, left, energy)

    rterm = lax.all_to_all(pay, ("pair", "side", "cell"), split_axis=0, concat_axis=0, tiled=True)

    acc, bcol, ccol = pl.pallas_call(
        functools.partial(force_local_kernel, icut, jcut, group, lay),
        out_shape=[shape((cells, 16, slots), F32), wide, wide],
        in_specs=[SMEM] + [VMEM] * 3,
        out_specs=[VMEM] * 3,
        scratch_shapes=lists
        + [
            weight_shape(cells),
            weight_shape(cells),
            pltpu.VMEM((cells, 16, slots), F32),
            pltpu.VMEM((cells, DOT_K, slots), F32),
        ]
        + force_work,
        compiler_params=params,
        name="force_local",
    )(meta, own, term, force_left)

    accel, heat = pl.pallas_call(
        functools.partial(force_remote_kernel, icut, jcut, group, lay),
        out_shape=[shape((3, cells, slots), F32), shape((cells, slots), F32)],
        in_specs=[SMEM] * 2 + [VMEM] * 9,
        out_specs=[VMEM] * 2,
        scratch_shapes=lists
        + [
            weight_shape(others),
            weight_shape(others),
            pltpu.VMEM((others, 16, slots), F32),
            pltpu.VMEM((cells, DOT_K, slots), F32),
        ]
        + force_work,
        compiler_params=params,
        name="force_remote",
    )(meta, live, own, rec, rec_odd, term, rterm, acc, force_left, bcol, ccol)
    return density, accel, heat


def solution(mesh):
    regions, peers = mesh.devices.shape
    mesh = jax.sharding.Mesh(mesh.devices.reshape(regions // 2, 2, peers), ("pair", "side", "cell"))
    region = ("pair", "side")
    every = (*region, "cell")
    placed = (
        P(None, every, None),
        P(None, every, None),
        P(every, None),
        P(every, None),
        P(every, None),
        P(every),
        P(region, "cell", None, None),
        P(region, "cell", None, None),
        P(region, "cell", None),
    )
    return jax.shard_map(
        on_device,
        mesh=mesh,
        in_specs=placed,
        out_specs=(P(every, None), P(None, every, None), P(every, None)),
        check_vma=False,
    )
```

```python
import functools
import math

import jax
import jax.numpy as jnp
from jax import lax
from jax.experimental import pallas as pl
from jax.experimental.pallas import tpu as pltpu
from jax.sharding import PartitionSpec as P

GAMMA = 5.0 / 3.0
LANES = 128
BF16 = jnp.bfloat16
F32 = jnp.float32

ROWS = 8
TINY = 1e-12
DOT_K = 48
COLS = 64
STRIP = 16

VMEM = pl.BlockSpec(memory_space=pltpu.VMEM)
SMEM = pl.BlockSpec(memory_space=pltpu.SMEM)
HBM = pl.BlockSpec(memory_space=pltpu.HBM)


def row_ids(shape):
    return lax.broadcasted_iota(jnp.int32, shape, 0)


def split3(value):
    first = value.astype(BF16).astype(F32)
    rest = value - first
    second = rest.astype(BF16).astype(F32)
    return first, second, rest - second


def left_parts(value):
    a, b, c = split3(value)
    return jnp.concatenate([a, a, b, b, a, c], axis=0)


def right_parts(value):
    a, b, c = split3(value)
    return jnp.concatenate([a, b, a, b, c, a], axis=0).astype(BF16)


def norm_row(rows):
    return rows[0:1] * rows[0:1] + rows[1:2] * rows[1:2] + rows[2:3] * rows[2:3]


def left_comps(rows):
    ids = row_ids(rows.shape)
    return jnp.where(ids < 3, rows, jnp.where(ids == 3, norm_row(rows), jnp.where(ids == 4, 1.0, 0.0)))


def right_comps(rows):
    ids = row_ids(rows.shape)
    return jnp.where(ids < 3, -2.0 * rows, jnp.where(ids == 3, 1.0, jnp.where(ids == 4, norm_row(rows), 0.0)))


def chunks(count, size):
    return lax.shift_right_logical(count + (size - 1), jnp.int32(size.bit_length() - 1))


class Meta:
    def __init__(self, cells, regions, peers, pairs):
        self.cells, self.regions, self.peers, self.pairs = cells, regions, peers, pairs
        self.send = cells
        self.pair = cells + peers
        self.edge = self.pair + 2 * pairs
        self.size = self.edge + 2


def prep_kernel(
    lay,
    counts_in, send_in, pairs_in, edge_in, pos_in, vel_in, mass_in, smooth_in,
    own, pay, odd, meta,
    counts, send, pairs, edge, pos, vel, mass, smooth, sems,
):
    inputs = (counts_in, send_in, pairs_in, edge_in, pos_in, vel_in, mass_in, smooth_in)
    buffers = (counts, send, pairs, edge, pos, vel, mass, smooth)
    copies = [
        pltpu.make_async_copy(source, target, sems.at[k])
        for k, (source, target) in enumerate(zip(inputs, buffers))
    ]
    for copy in copies:
        copy.start()
    for copy in copies:
        copy.wait()
    cells = mass.shape[0]
    slots = mass.shape[1]
    for k in range(cells):
        meta[k] = counts[k]
    for k in range(lay.peers):
        meta[lay.send + k] = send[k]
    for k in range(lay.pairs):
        for side in range(2):
            meta[lay.pair + 2 * k + side] = pairs[0, 0, side, k]
    for side in range(2):
        meta[lay.edge + side] = edge[0, 0, side]

    lane = lax.broadcasted_iota(jnp.int32, (1, slots), 1)
    for k in range(cells):
        live = lane < counts[k]
        for d in range(3):
            own[k, d : d + 1, :] = pos[d, k : k + 1, :] - 0.5
            own[k, 5 + d : 6 + d, :] = vel[d, k : k + 1, :]
        own[k, 3:4, :] = jnp.where(live, mass[k : k + 1, :], 0.0)
        own[k, 4:5, :] = smooth[k : k + 1, :]

    place = Place(lay)
    pay[...] = jnp.zeros_like(pay)

    def peer(k, carry):
        picked = send[k]
        pay[place.pair_peers + k] = jnp.where(picked >= 0, own[jnp.maximum(picked, 0)], 0.0)
        return carry

    lax.fori_loop(0, lay.peers, peer, 0)
    pay[place.pair_partner] = own[meta[place.partner_edge]]
    odd[0] = own[meta[place.odd_edge]]


class Place:
    def __init__(self, lay):
        peers, regions = lay.peers, lay.regions
        self.side = lax.axis_index("side")
        here = lax.axis_index("cell")
        region = 2 * lax.axis_index("pair") + self.side
        other = region - 1 + 2 * self.side
        self.partner_edge = lay.edge + 1 - self.side
        self.odd_edge = lay.edge + self.side
        self.pair_peers = self.side * peers
        self.pair_partner = (1 - self.side) * peers + here
        self.peers = region * peers
        self.partner = (region + 1 - 2 * self.side) * peers + here
        self.has_odd = (other >= 0) & (other < regions)
        self.odd = jnp.clip(other, 0, regions - 1) * peers + here


class Tiles:
    FIELDS = 7

    def __init__(self, icut, jcut, table):
        self.icut, self.jcut, self.table = icut, jcut, table
        self.count = self.blocks = jnp.int32(0)

    def push(self, a, b, w, ok, i, ni, j, nj):
        at = self.FIELDS * self.count
        for field, value in enumerate((a, b, w, i, ni, j, nj)):
            self.table[at + field] = value
        self.count = self.count + ok.astype(jnp.int32)
        self.blocks = self.blocks + jnp.where(ok, ni * nj, 0)

    def whole(self, a, b, w, ok, alive, blive):
        self.push(a, b, w, ok, 0, chunks(alive, self.icut), 0, chunks(blive, self.jcut))

    def close(self):
        self.push(0, 0, 0, jnp.bool_(False), 0, 1, 0, 1)


def local_tiles(tiles, lay, meta, both):
    cells = lay.cells
    one = jnp.int32(1)

    def key(row):
        first = meta[lay.pair + 2 * row]
        second = meta[lay.pair + 2 * row + 1]
        return jnp.minimum(first, second) * cells + jnp.maximum(first, second)

    keys = [key(row) for row in range(lay.pairs)]
    for a in range(cells):
        for b in range(a + 1, cells):
            mult = jnp.int32(0)
            for pair in keys:
                mult = mult + (pair == a * cells + b).astype(jnp.int32)
            tiles.whole(a, b, mult, mult > 0, meta[a], meta[b])
            if not both:
                tiles.whole(b, a, mult, mult > 0, meta[b], meta[a])
    if not both:
        for a in range(cells):
            tiles.whole(a, a, one, meta[a] > 0, meta[a], meta[a])
        tiles.close()
        return None
    span = tiles.jcut // tiles.icut
    for a in range(cells):
        tiles.push(a, a, one, meta[a] > tiles.jcut, 0, span, 1, chunks(meta[a], tiles.jcut) - 1)
    mutual = tiles.blocks
    for a in range(cells):
        rows = chunks(meta[a], tiles.icut)
        tiles.push(a, a, one, meta[a] > 0, 0, jnp.minimum(rows, span), 0, 1)
        tiles.push(a, a, one, meta[a] > tiles.jcut, span, rows - span, 1, 1)
    tiles.close()
    return mutual


def remote_tiles(tiles, lay, meta, live):
    one = jnp.int32(1)
    for k in range(lay.peers):
        picked = meta[lay.send + k]
        a = jnp.maximum(picked, 0)
        tiles.whole(a, k, one, (picked >= 0) & (live[k] > 0), meta[a], live[k])
    place = Place(lay)
    for b, edge in ((lay.peers, place.partner_edge), (lay.peers + 1, place.odd_edge)):
        a = meta[edge]
        tiles.whole(a, b, one, live[b] > 0, meta[a], live[b])
    tiles.close()


class Blocks:
    FIELDS = 5

    def __init__(self, tiles, ring):
        self.icut, self.jcut = tiles.icut, tiles.jcut
        self.table, self.last = tiles.table, tiles.count
        self.ring, self.total = ring, tiles.blocks

    def clear(self, entries):
        for k in range(entries * self.FIELDS):
            self.ring[k] = 0

    def write(self, slot, state):
        n, ii, jj = state
        a, b, w, i, ni, j, nj = (self.table[Tiles.FIELDS * n + k] for k in range(Tiles.FIELDS))
        for field, value in enumerate((a, b, (i + ii) * self.icut, (j + jj) * self.jcut, w)):
            self.ring[self.FIELDS * slot + field] = value
        jwrap = jj + 1 >= nj
        inext = jnp.where(jwrap, ii + 1, ii)
        iwrap = inext >= ni
        return (
            jnp.minimum(jnp.where(iwrap, n + 1, n), self.last),
            jnp.where(iwrap, 0, inext),
            jnp.where(jwrap, 0, jj + 1),
        )

    def read(self, slot):
        a, b, istart, jstart, w = (self.ring[self.FIELDS * slot + k] for k in range(self.FIELDS))
        return (
            a,
            b,
            pl.multiple_of(istart, self.icut),
            pl.multiple_of(jstart, self.jcut),
            w.astype(F32),
        )

    def distances(self, slot, left, right, out):
        a, b, istart, jstart, _ = self.read(slot)
        out[...] = jnp.dot(
            left[a, pl.ds(istart, self.icut), :DOT_K],
            right[b, :, pl.ds(jstart, self.jcut)],
            preferred_element_type=F32,
        )


def density_loop(group, blocks, total, left, right, mrow, acc, parts):
    icut, jcut = blocks.icut, blocks.jcut
    zero = jnp.int32(0)
    state = (zero, zero, zero)
    for g in range(group):
        state = blocks.write(g, state)

    def step(k, state):
        for g in range(group):
            a, b, istart, jstart, w = blocks.read(k * group + g)
            square = jnp.dot(
                left[a, pl.ds(istart, icut), :DOT_K],
                right[b, :, pl.ds(jstart, jcut)],
                preferred_element_type=F32,
            )
            weight = mrow[b, :, pl.ds(jstart, jcut)] * w
            weight = jnp.concatenate([weight] * (STRIP // 8), axis=0)
            for row in range(0, icut, STRIP):
                s = jnp.maximum(square[row : row + STRIP, :], TINY)
                q = s * lax.rsqrt(s)
                e = 1.0 - q
                u = jnp.maximum(e, 0.0)
                t = jnp.minimum(0.5 - (s * 3.0) * e, u * u * u) * weight
                part = t[:, :LANES]
                for at in range(1, jcut // LANES):
                    part = part + t[:, at * LANES : (at + 1) * LANES]
                parts[g][row : row + STRIP, :] = part
            state = blocks.write((k + 1) * group + g, state)
        for g in range(group):
            a, _, istart, _, _ = blocks.read(k * group + g)
            acc[a, pl.ds(istart, icut), :] += parts[g][...]
        return state

    lax.fori_loop(0, chunks(total, group), step, state)


def density_source(rows, right, mrow, at):
    right[at] = right_parts(right_comps(rows))
    mrow[at] = jnp.broadcast_to(rows[3:4], mrow.shape[1:])


def spread_left(parts, left, cell):
    for at in range(parts.shape[1] // LANES):
        left[cell, pl.ds(at * LANES, LANES), :] = parts[:, at * LANES : (at + 1) * LANES].T.astype(BF16)


def force_scales(rows):
    h = rows[4:5]
    inv = 1.0 / jnp.where(h > 0.0, h, 1.0)
    b = math.sqrt(24.0 / math.pi) * (inv * inv)
    return b, b * inv


def density_local_kernel(
    icut, jcut, group, lay, meta, own, acc, left, force_left, table, ring, right, mrow, *work
):
    slots = own.shape[2]
    ids = row_ids((8, slots))
    empty = jnp.zeros((8, slots), F32)
    for k in range(lay.cells):
        rows = own[k]
        inv = 1.0 / rows[4:5]
        comps = left_comps(rows)
        spread_left(jnp.concatenate([left_parts(comps * (inv * inv)), empty, empty], axis=0), left, k)
        scales = empty
        for at, part in enumerate(x for scale in force_scales(rows) for x in split3(scale)):
            scales = jnp.where(ids == at, part, scales)
        spread_left(jnp.concatenate([left_parts(comps), scales, empty], axis=0), force_left, k)
        density_source(rows, right, mrow, k)
        acc[k] = jnp.zeros((slots, LANES), F32)
    tiles = Tiles(icut, jcut, table)
    local_tiles(tiles, lay, meta, False)
    blocks = Blocks(tiles, ring)
    density_loop(group, blocks, tiles.blocks, left, right, mrow, acc, work)


def density_remote_kernel(
    icut, jcut, group, lay,
    meta, own, rec, rec_odd, acc_in, left, energy_in,
    rho_out, term_out, pay, live,
    table, ring, right, mrow, acc, energy, sem, *work,
):
    cells, peers = lay.cells, lay.peers
    slots = own.shape[2]
    copy = pltpu.make_async_copy(energy_in, energy, sem)
    copy.start()
    place = Place(lay)
    occupied = jnp.where(rec[:, 3, :] > 0.0, 1.0, 0.0).reshape(2, peers, slots)
    occupied = jnp.sum(jnp.where(place.side == 0, occupied[0], occupied[1]), axis=1, keepdims=True)
    for k in range(peers):
        live[k] = occupied[k, 0].astype(jnp.int32)
    for k, rows in ((peers, rec[place.pair_partner]), (peers + 1, rec_odd[0])):
        live[k] = jnp.sum(jnp.where(rows[3:4] > 0.0, 1.0, 0.0)).astype(jnp.int32)

    def rec_cell(k, carry):
        density_source(rec[place.pair_peers + k], right, mrow, k)
        return carry

    lax.fori_loop(0, peers, rec_cell, 0, unroll=4)
    density_source(rec[place.pair_partner], right, mrow, peers)
    density_source(rec_odd[0], right, mrow, peers + 1)
    acc[...] = acc_in[...]
    tiles = Tiles(icut, jcut, table)
    remote_tiles(tiles, lay, meta, live)
    blocks = Blocks(tiles, ring)
    density_loop(group, blocks, tiles.blocks, left, right, mrow, acc, work)

    copy.wait()
    lane = lax.broadcasted_iota(jnp.int32, (1, slots), 1)
    ones = jnp.ones((8, 2 * LANES), BF16)
    for k in range(cells):
        one = acc[k].astype(BF16)
        two = (acc[k] - one.astype(F32)).astype(BF16)
        total_row = lax.dot_general(
            ones,
            jnp.concatenate([one, two], axis=1),
            (((1,), (1,)), ((), ())),
            preferred_element_type=F32,
        )
        inv = 1.0 / own[k, 4:5, :]
        rho = total_row[0:1] * (16.0 / math.pi) * (inv * inv * inv)
        occupied = jnp.where(lane < meta[k], 1.0, 0.0)
        rho_out[k : k + 1, :] = rho * occupied
        term_out[k] = occupied * (GAMMA - 1.0) * energy[k : k + 1, :] / (rho + 1.0 - occupied)

    pay[...] = jnp.zeros_like(pay)

    def peer(k, carry):
        pay[place.peers + k] = term_out[jnp.maximum(meta[lay.send + k], 0)]
        return carry

    lax.fori_loop(0, peers, peer, 0)
    pay[place.partner] = term_out[meta[place.partner_edge]]

    @pl.when(place.has_odd)
    def _():
        pay[place.odd] = term_out[meta[place.odd_edge]]


def force_source(rows, pressure, right, weights, scale, at):
    slots = rows.shape[1]
    right[at] = right_parts(right_comps(rows))
    b, c = force_scales(rows)
    scale[at] = jnp.concatenate([jnp.broadcast_to(b, (8, slots)), jnp.broadcast_to(c, (8, slots))], axis=0)
    m = rows[3:4]
    mp = m * pressure
    xv = rows[0:1] * rows[5:6] + rows[1:2] * rows[6:7] + rows[2:3] * rows[7:8]
    ids = row_ids((8, slots))
    base = jnp.where(ids == 3, 1.0, jnp.where(ids == 4, xv, rows))
    sums = jnp.concatenate([base * m, jnp.where(ids < 4, base, 0.0) * mp], axis=0)
    one, two, three = split3(sums)
    weights[at] = jnp.concatenate([one, two, three], axis=0).astype(BF16)


def force_loop(group, blocks, total, local, left, right, weights, scale, bcol, ccol, acc, work):
    icut, jcut = blocks.icut, blocks.jcut
    dist, upper, lower = work[:group], work[group : 2 * group], work[2 * group :]
    blocks.clear(group)
    for ref in (*upper, *lower):
        ref[...] = jnp.zeros_like(ref)
    zero = jnp.int32(0)
    state = (zero, zero, zero)
    for g in range(2 * group):
        state = blocks.write(group + g, state)
    for g in range(group):
        blocks.distances(group + g, left, right, dist[g])

    def sums_of(rows, columns, k, g):
        a, b, istart, jstart, w = blocks.read(k * group + g)
        adds = []
        if rows:
            wt = weights[b, :, pl.ds(jstart, jcut)]
            spec = (((1,), (1,)), ((), ()))
            part = lax.dot_general(wt, upper[g][...], spec, preferred_element_type=F32)
            part = part + lax.dot_general(wt, lower[g][...], spec, preferred_element_type=F32)
            keep = w
            if columns:
                keep = jnp.where(k * group + g < local + group, w, 0.0)
            adds.append((a, istart, part * keep))
        if columns:
            wt = weights[a, :, pl.ds(istart, icut)]
            part = jnp.dot(wt, upper[g][...], preferred_element_type=F32)
            part = part + jnp.dot(wt, lower[g][...], preferred_element_type=F32)
            adds.append((b, jstart, part * w))
        return adds

    def store(adds):
        for cell, start, part in adds:
            acc[cell, :, pl.ds(start, part.shape[1])] += part

    def step(rows, columns, k, state):
        adds = []
        for g in range(group):
            adds += sums_of(rows, columns, k, g)

            a, b, istart, jstart, _ = blocks.read((k + 1) * group + g)
            bj = jnp.concatenate([scale[b, 0:8, pl.ds(jstart, jcut)]] * (STRIP // 8), axis=0)
            cj = jnp.concatenate([scale[b, 8:16, pl.ds(jstart, jcut)]] * (STRIP // 8), axis=0)
            for row in range(0, icut, STRIP):
                s = jnp.maximum(dist[g][row : row + STRIP, :], TINY)
                r = lax.rsqrt(s)
                d = s * r
                bi = bcol[a, pl.ds(istart + row, STRIP), :]
                ci = ccol[a, pl.ds(istart + row, STRIP), :]
                bi = jnp.concatenate([bi] * (jcut // LANES), axis=1)
                ci = jnp.concatenate([ci] * (jcut // LANES), axis=1)
                t = ci * d
                u = jnp.maximum(bi - t, 0.0)
                v = jnp.minimum(t, u)
                slope = (u + u - v) * v
                t = cj * d
                u = jnp.maximum(bj - t, 0.0)
                v = jnp.minimum(t, u)
                slope = (slope + (u + u - v) * v) * r
                rounded = slope.astype(BF16)
                upper[g][row : row + STRIP, :] = rounded
                lower[g][row : row + STRIP, :] = (slope - rounded.astype(F32)).astype(BF16)

            state = blocks.write((k + 3) * group + g, state)
            blocks.distances((k + 2) * group + g, left, right, dist[g])
        store(adds)
        return state

    steps = chunks(total, group)
    adds = []
    if local is None:
        lax.fori_loop(0, steps, functools.partial(step, True, False), state)
        for g in range(group):
            adds += sums_of(True, False, steps, g)
    else:
        first = jnp.minimum(chunks(local, group) + 1, steps)
        state = lax.fori_loop(0, first, functools.partial(step, True, True), state)
        lax.fori_loop(first, steps, functools.partial(step, False, True), state)
        for g in range(group):
            adds += sums_of(True, True, steps, g)
    store(adds)


def force_local_kernel(
    icut, jcut, group, lay,
    meta, own, term, left,
    acc_out, bcol, ccol,
    table, ring, right, weights, scale, acc, *work,
):
    slots = own.shape[2]
    part = lax.broadcasted_iota(jnp.int32, (COLS, 2 * LANES), 0) - DOT_K
    lane = lax.broadcasted_iota(jnp.int32, (COLS, 2 * LANES), 1)
    of_b = (part >= 0) & (part < 3) & (lane < LANES)
    of_c = (part >= 3) & (part < 6) & (lane >= LANES)
    pick = jnp.where(of_b | of_c, 1.0, 0.0).astype(BF16)
    for k in range(lay.cells):
        force_source(own[k], term[k], right, weights, scale, k)
        acc[k] = jnp.zeros((DOT_K, slots), F32)
        for at in range(slots // LANES):
            here = pl.ds(at * LANES, LANES)
            both = jnp.dot(left[k, here, :], pick, preferred_element_type=F32)
            bcol[k, here, :] = both[:, :LANES]
            ccol[k, here, :] = both[:, LANES:]
    tiles = Tiles(icut, jcut, table)
    local = local_tiles(tiles, lay, meta, True)
    blocks = Blocks(tiles, ring)
    force_loop(
        group, blocks, tiles.blocks, local, left, right, weights, scale, bcol, ccol, acc, work
    )
    for k in range(lay.cells):
        acc_out[k] = acc[k, 0:16, :] + (acc[k, 16:32, :] + acc[k, 32:48, :])


def force_remote_kernel(
    icut, jcut, group, lay,
    meta, live, own, rec, rec_odd, term, rterm, acc_in, left, bcol, ccol,
    accel_out, heat_out,
    table, ring, right, weights, scale, acc, *work,
):
    cells, peers = lay.cells, lay.peers
    slots = own.shape[2]
    place = Place(lay)

    def rec_cell(k, carry):
        force_source(rec[place.pair_peers + k], rterm[place.peers + k], right, weights, scale, k)
        return carry

    lax.fori_loop(0, peers, rec_cell, 0, unroll=4)
    force_source(rec[place.pair_partner], rterm[place.partner], right, weights, scale, peers)
    force_source(rec_odd[0], rterm[place.odd], right, weights, scale, peers + 1)
    acc[...] = jnp.zeros_like(acc)
    tiles = Tiles(icut, jcut, table)
    remote_tiles(tiles, lay, meta, live)
    blocks = Blocks(tiles, ring)
    force_loop(
        group, blocks, tiles.blocks, None, left, right, weights, scale, bcol, ccol, acc, work
    )

    lane = lax.broadcasted_iota(jnp.int32, (1, slots), 1)
    for k in range(cells):
        occupied = jnp.where(lane < meta[k], 1.0, 0.0)
        sums = acc_in[k] + acc[k, 0:16, :] + (acc[k, 16:32, :] + acc[k, 32:48, :])
        pressure = term[k]
        x = [own[k, d : d + 1, :] for d in range(3)]
        v = [own[k, 5 + d : 6 + d, :] for d in range(3)]
        both = pressure * sums[3:4] + sums[11:12]
        for d in range(3):
            accel_out[d, k : k + 1, :] = occupied * (
                x[d] * both - pressure * sums[d : d + 1] - sums[8 + d : 9 + d]
            )
        xv = x[0] * v[0] + x[1] * v[1] + x[2] * v[2]
        total_heat = xv * sums[3:4] + sums[4:5]
        for d in range(3):
            total_heat = total_heat - v[d] * sums[d : d + 1] - x[d] * sums[5 + d : 6 + d]
        heat_out[k : k + 1, :] = -occupied * pressure * total_heat


def on_device(positions, velocities, mass, smoothing, energy, counts, send, pairs, edge):
    cells, slots = mass.shape
    peers = send.shape[2]
    regions = 2 * lax.axis_size("pair")
    lay = Meta(cells, regions, peers, pairs.shape[2])
    others = peers + 2
    most = max(cells * (cells - 1) // 2 + 3 * cells, cells * cells, others) + 1
    icut, jcut, group = 128, slots // 2, 8
    ring = Blocks.FIELDS * (most * (slots // icut) * (slots // jcut) + 6 * group)
    shape = jax.ShapeDtypeStruct
    params = pltpu.CompilerParams(vmem_limit_bytes=20 * 1024 * 1024)
    send = send.reshape(peers)
    pairs = jnp.transpose(pairs, (0, 1, 3, 2))
    integers = (counts, send, pairs, edge)
    floats = (positions, velocities, mass, smoothing)
    integers, floats, energy = jax.tree.map(
        lambda x: pltpu.with_memory_space_constraint(x, pltpu.HBM), (integers, floats, energy)
    )
    lists = [pltpu.SMEM((Tiles.FIELDS * most,), jnp.int32), pltpu.SMEM((ring,), jnp.int32)]
    density_work = [pltpu.VMEM((icut, LANES), F32)] * group
    force_work = [pltpu.VMEM((icut, jcut), F32)] * group + [pltpu.VMEM((icut, jcut), BF16)] * (2 * group)
    wide = shape((cells, slots, LANES), F32)
    left_shape = shape((cells, slots, COLS), BF16)
    weight_shape = lambda count: pltpu.VMEM((count, DOT_K, slots), BF16)

    own, pay, odd, meta = pl.pallas_call(
        functools.partial(prep_kernel, lay),
        out_shape=[
            shape((cells, ROWS, slots), F32),
            shape((2 * peers, ROWS, slots), F32),
            shape((1, ROWS, slots), F32),
            shape((lay.size,), jnp.int32),
        ],
        in_specs=[HBM] * 8,
        out_specs=[VMEM] * 3 + [SMEM],
        scratch_shapes=[pltpu.SMEM(x.shape, jnp.int32) for x in integers]
        + [pltpu.VMEM(x.shape, F32) for x in floats]
        + [pltpu.SemaphoreType.DMA((8,))],
        compiler_params=params,
        name="prep",
    )(*integers, *floats)

    between = [(r, r + 1) for r in range(1, regions - 1, 2)]
    swap = between + [(b, a) for a, b in between]
    rec_odd = lax.ppermute(odd, ("pair", "side"), swap)
    rec = lax.all_to_all(pay, ("side", "cell"), split_axis=0, concat_axis=0, tiled=True)

    acc, left, force_left = pl.pallas_call(
        functools.partial(density_local_kernel, icut, jcut, group, lay),
        out_shape=[wide, left_shape, left_shape],
        in_specs=[SMEM, VMEM],
        out_specs=[VMEM] * 3,
        scratch_shapes=lists + [weight_shape(cells), pltpu.VMEM((cells, 8, slots), F32)] + density_work,
        compiler_params=params,
        name="density_local",
    )(meta, own)

    density, term, pay, live = pl.pallas_call(
        functools.partial(density_remote_kernel, icut, jcut, group, lay),
        out_shape=[
            shape((cells, slots), F32),
            shape((cells, 1, slots), F32),
            shape((regions * peers, 1, slots), F32),
            shape((others,), jnp.int32),
        ],
        in_specs=[SMEM] + [VMEM] * 5 + [HBM],
        out_specs=[VMEM] * 3 + [SMEM],
        scratch_shapes=lists
        + [
            weight_shape(others),
            pltpu.VMEM((others, 8, slots), F32),
            pltpu.VMEM((cells, slots, LANES), F32),
            pltpu.VMEM(energy.shape, F32),
            pltpu.SemaphoreType.DMA,
        ]
        + density_work,
        compiler_params=params,
        name="density_remote",
    )(meta, own, rec, rec_odd, acc, left, energy)

    rterm = lax.all_to_all(pay, ("pair", "side", "cell"), split_axis=0, concat_axis=0, tiled=True)

    acc, bcol, ccol = pl.pallas_call(
        functools.partial(force_local_kernel, icut, jcut, group, lay),
        out_shape=[shape((cells, 16, slots), F32), wide, wide],
        in_specs=[SMEM] + [VMEM] * 3,
        out_specs=[VMEM] * 3,
        scratch_shapes=lists
        + [
            weight_shape(cells),
            weight_shape(cells),
            pltpu.VMEM((cells, 16, slots), F32),
            pltpu.VMEM((cells, DOT_K, slots), F32),
        ]
        + force_work,
        compiler_params=params,
        name="force_local",
    )(meta, own, term, force_left)

    accel, heat = pl.pallas_call(
        functools.partial(force_remote_kernel, icut, jcut, group, lay),
        out_shape=[shape((3, cells, slots), F32), shape((cells, slots), F32)],
        in_specs=[SMEM] * 2 + [VMEM] * 9,
        out_specs=[VMEM] * 2,
        scratch_shapes=lists
        + [
            weight_shape(others),
            weight_shape(others),
            pltpu.VMEM((others, 16, slots), F32),
            pltpu.VMEM((cells, DOT_K, slots), F32),
        ]
        + force_work,
        compiler_params=params,
        name="force_remote",
    )(meta, live, own, rec, rec_odd, term, rterm, acc, force_left, bcol, ccol)
    return density, accel, heat


def solution(mesh):
    regions, peers = mesh.devices.shape
    mesh = jax.sharding.Mesh(mesh.devices.reshape(regions // 2, 2, peers), ("pair", "side", "cell"))
    region = ("pair", "side")
    every = (*region, "cell")
    placed = (
        P(None, every, None),
        P(None, every, None),
        P(every, None),
        P(every, None),
        P(every, None),
        P(every),
        P(region, "cell", None, None),
        P(region, "cell", None, None),
        P(region, "cell", None),
    )
    return jax.shard_map(
        on_device,
        mesh=mesh,
        in_specs=placed,
        out_specs=(P(every, None), P(None, every, None), P(every, None)),
        check_vma=False,
    )
```

```python
import functools
import math

import jax
import jax.numpy as jnp
from jax import lax
from jax.experimental import pallas as pl
from jax.experimental.pallas import tpu as pltpu
from jax.sharding import PartitionSpec as P

GAMMA = 5.0 / 3.0
LANES = 128
BF16 = jnp.bfloat16
F32 = jnp.float32

ROWS = 8
TINY = 1e-12
DOT_K = 32
SUMS = 48
COLS = 64
STRIP = 16

VMEM = pl.BlockSpec(memory_space=pltpu.VMEM)
SMEM = pl.BlockSpec(memory_space=pltpu.SMEM)
HBM = pl.BlockSpec(memory_space=pltpu.HBM)


def row_ids(shape):
    return lax.broadcasted_iota(jnp.int32, shape, 0)


def split3(value):
    first = value.astype(BF16).astype(F32)
    rest = value - first
    second = rest.astype(BF16).astype(F32)
    return first, second, rest - second


def parts_of(comps, left):
    ids = row_ids(comps.shape)
    a, b, c = split3(comps)
    again = [pltpu.roll(x, 5, 0) for x in (a, b, c)]
    after = [pltpu.roll(x, 1, 0) for x in (a, b, c)]
    if left:
        one = jnp.where(ids < 5, a, again[0])
        two = jnp.where(ids < 5, jnp.where(ids == 3, b, a), again[2])
        three = jnp.where(ids < 5, jnp.where(ids == 3, c, b), after[0])
        four = jnp.where(ids < 5, b, after[2])
    else:
        one = jnp.where(ids < 5, a, again[2])
        two = jnp.where(ids < 5, jnp.where(ids == 3, a, b), again[0])
        three = jnp.where(ids < 5, a, after[2])
        four = jnp.where(ids < 5, b, after[0])
    three = jnp.where(ids < 6, three, 0.0)
    four = jnp.where((ids < 6) & (ids != 3), four, 0.0)
    return jnp.concatenate([one, two, three, four], axis=0)


def left_parts(comps):
    return parts_of(comps, True)


def right_parts(comps):
    return parts_of(comps, False).astype(BF16)


def norm_row(rows):
    return rows[0:1] * rows[0:1] + rows[1:2] * rows[1:2] + rows[2:3] * rows[2:3]


def left_comps(rows):
    ids = row_ids(rows.shape)
    return jnp.where(ids < 3, rows, jnp.where(ids == 3, norm_row(rows), jnp.where(ids == 4, 1.0, 0.0)))


def right_comps(rows):
    ids = row_ids(rows.shape)
    return jnp.where(ids < 3, -2.0 * rows, jnp.where(ids == 3, 1.0, jnp.where(ids == 4, norm_row(rows), 0.0)))


def chunks(count, size):
    return lax.shift_right_logical(count + (size - 1), jnp.int32(size.bit_length() - 1))


class Meta:
    def __init__(self, cells, regions, peers, pairs):
        self.cells, self.regions, self.peers, self.pairs = cells, regions, peers, pairs
        self.send = cells
        self.pair = cells + peers
        self.edge = self.pair + 2 * pairs
        self.size = self.edge + 2


def prep_kernel(
    lay,
    counts_in, send_in, pairs_in, edge_in, pos_in, vel_in, mass_in, smooth_in,
    own, pay, odd, meta,
    counts, send, pairs, edge, pos, vel, mass, smooth, sems,
):
    inputs = (counts_in, send_in, pairs_in, edge_in, pos_in, vel_in, mass_in, smooth_in)
    buffers = (counts, send, pairs, edge, pos, vel, mass, smooth)
    copies = [
        pltpu.make_async_copy(source, target, sems.at[k])
        for k, (source, target) in enumerate(zip(inputs, buffers))
    ]
    for copy in copies:
        copy.start()
    for copy in copies:
        copy.wait()
    cells = mass.shape[0]
    slots = mass.shape[1]
    for k in range(cells):
        meta[k] = counts[k]
    for k in range(lay.peers):
        meta[lay.send + k] = send[k]
    for k in range(lay.pairs):
        for side in range(2):
            meta[lay.pair + 2 * k + side] = pairs[0, 0, side, k]
    for side in range(2):
        meta[lay.edge + side] = edge[0, 0, side]

    lane = lax.broadcasted_iota(jnp.int32, (1, slots), 1)
    for k in range(cells):
        live = lane < counts[k]
        for d in range(3):
            own[k, d : d + 1, :] = pos[d, k : k + 1, :] - 0.5
            own[k, 5 + d : 6 + d, :] = vel[d, k : k + 1, :]
        own[k, 3:4, :] = jnp.where(live, mass[k : k + 1, :], 0.0)
        own[k, 4:5, :] = smooth[k : k + 1, :]

    place = Place(lay)
    pay[...] = jnp.zeros_like(pay)

    def peer(k, carry):
        picked = send[k]
        pay[place.pair_peers + k] = jnp.where(picked >= 0, own[jnp.maximum(picked, 0)], 0.0)
        return carry

    lax.fori_loop(0, lay.peers, peer, 0)
    pay[place.pair_partner] = own[meta[place.partner_edge]]
    odd[0] = own[meta[place.odd_edge]]


class Place:
    def __init__(self, lay):
        peers, regions = lay.peers, lay.regions
        self.side = lax.axis_index("side")
        here = lax.axis_index("cell")
        region = 2 * lax.axis_index("pair") + self.side
        other = region - 1 + 2 * self.side
        self.partner_edge = lay.edge + 1 - self.side
        self.odd_edge = lay.edge + self.side
        self.pair_peers = self.side * peers
        self.pair_partner = (1 - self.side) * peers + here
        self.peers = region * peers
        self.partner = (region + 1 - 2 * self.side) * peers + here
        self.has_odd = (other >= 0) & (other < regions)
        self.odd = jnp.clip(other, 0, regions - 1) * peers + here


class Tiles:
    FIELDS = 7

    def __init__(self, icut, jcut, table):
        self.icut, self.jcut, self.table = icut, jcut, table
        self.count = self.blocks = jnp.int32(0)

    def push(self, a, b, w, ok, i, ni, j, nj):
        at = self.FIELDS * self.count
        for field, value in enumerate((a, b, w, i, ni, j, nj)):
            self.table[at + field] = value
        self.count = self.count + ok.astype(jnp.int32)
        self.blocks = self.blocks + jnp.where(ok, ni * nj, 0)

    def whole(self, a, b, w, ok, alive, blive):
        self.push(a, b, w, ok, 0, chunks(alive, self.icut), 0, chunks(blive, self.jcut))

    def close(self):
        self.push(0, 0, 0, jnp.bool_(False), 0, 1, 0, 1)


def local_tiles(tiles, lay, meta, both):
    cells = lay.cells
    one = jnp.int32(1)

    def key(row):
        first = meta[lay.pair + 2 * row]
        second = meta[lay.pair + 2 * row + 1]
        return jnp.minimum(first, second) * cells + jnp.maximum(first, second)

    keys = [key(row) for row in range(lay.pairs)]
    for a in range(cells):
        for b in range(a + 1, cells):
            mult = jnp.int32(0)
            for pair in keys:
                mult = mult + (pair == a * cells + b).astype(jnp.int32)
            tiles.whole(a, b, mult, mult > 0, meta[a], meta[b])
            if not both:
                tiles.whole(b, a, mult, mult > 0, meta[b], meta[a])
    if not both:
        for a in range(cells):
            tiles.whole(a, a, one, meta[a] > 0, meta[a], meta[a])
        tiles.close()
        return None
    span = tiles.jcut // tiles.icut
    for a in range(cells):
        tiles.push(a, a, one, meta[a] > tiles.jcut, 0, span, 1, chunks(meta[a], tiles.jcut) - 1)
    mutual = tiles.blocks
    for a in range(cells):
        rows = chunks(meta[a], tiles.icut)
        tiles.push(a, a, one, meta[a] > 0, 0, jnp.minimum(rows, span), 0, 1)
        tiles.push(a, a, one, meta[a] > tiles.jcut, span, rows - span, 1, 1)
    tiles.close()
    return mutual


def remote_tiles(tiles, lay, meta, live):
    one = jnp.int32(1)
    for k in range(lay.peers):
        picked = meta[lay.send + k]
        a = jnp.maximum(picked, 0)
        tiles.whole(a, k, one, (picked >= 0) & (live[k] > 0), meta[a], live[k])
    place = Place(lay)
    for b, edge in ((lay.peers, place.partner_edge), (lay.peers + 1, place.odd_edge)):
        a = meta[edge]
        tiles.whole(a, b, one, live[b] > 0, meta[a], live[b])
    tiles.close()


class Blocks:
    FIELDS = 5

    def __init__(self, tiles, ring):
        self.icut, self.jcut = tiles.icut, tiles.jcut
        self.table, self.last = tiles.table, tiles.count
        self.ring, self.total = ring, tiles.blocks

    def clear(self, entries):
        for k in range(entries * self.FIELDS):
            self.ring[k] = 0

    def write(self, slot, state):
        n, ii, jj = state
        a, b, w, i, ni, j, nj = (self.table[Tiles.FIELDS * n + k] for k in range(Tiles.FIELDS))
        for field, value in enumerate((a, b, (i + ii) * self.icut, (j + jj) * self.jcut, w)):
            self.ring[self.FIELDS * slot + field] = value
        jwrap = jj + 1 >= nj
        inext = jnp.where(jwrap, ii + 1, ii)
        iwrap = inext >= ni
        return (
            jnp.minimum(jnp.where(iwrap, n + 1, n), self.last),
            jnp.where(iwrap, 0, inext),
            jnp.where(jwrap, 0, jj + 1),
        )

    def read(self, slot):
        a, b, istart, jstart, w = (self.ring[self.FIELDS * slot + k] for k in range(self.FIELDS))
        return (
            a,
            b,
            pl.multiple_of(istart, self.icut),
            pl.multiple_of(jstart, self.jcut),
            w.astype(F32),
        )

    def distances(self, slot, left, right, out):
        a, b, istart, jstart, _ = self.read(slot)
        out[...] = jnp.dot(
            left[a, pl.ds(istart, self.icut), :DOT_K],
            right[b, :, pl.ds(jstart, self.jcut)],
            preferred_element_type=F32,
        )


def density_loop(group, blocks, total, left, right, mrow, acc, parts):
    icut, jcut = blocks.icut, blocks.jcut
    zero = jnp.int32(0)
    state = (zero, zero, zero)
    for g in range(group):
        state = blocks.write(g, state)

    def step(k, state):
        for g in range(group):
            a, b, istart, jstart, w = blocks.read(k * group + g)
            square = jnp.dot(
                left[a, pl.ds(istart, icut), :DOT_K],
                right[b, :, pl.ds(jstart, jcut)],
                preferred_element_type=F32,
            )
            weight = mrow[b, :, pl.ds(jstart, jcut)] * w
            weight = jnp.concatenate([weight] * (STRIP // 8), axis=0)
            for row in range(0, icut, STRIP):
                s = jnp.maximum(square[row : row + STRIP, :], TINY)
                q = s * lax.rsqrt(s)
                e = 1.0 - q
                u = jnp.maximum(e, 0.0)
                t = jnp.minimum(0.5 - (s * 3.0) * e, u * u * u) * weight
                part = t[:, :LANES]
                for at in range(1, jcut // LANES):
                    part = part + t[:, at * LANES : (at + 1) * LANES]
                parts[g][row : row + STRIP, :] = part
            state = blocks.write((k + 1) * group + g, state)
        for g in range(group):
            a, _, istart, _, _ = blocks.read(k * group + g)
            acc[a, pl.ds(istart, icut), :] += parts[g][...]
        return state

    lax.fori_loop(0, chunks(total, group), step, state)


def density_source(rows, right, mrow, at):
    right[at] = right_parts(right_comps(rows))
    mrow[at] = jnp.broadcast_to(rows[3:4], mrow.shape[1:])


def spread_left(parts, left, cell):
    for at in range(parts.shape[1] // LANES):
        left[cell, pl.ds(at * LANES, LANES), :] = parts[:, at * LANES : (at + 1) * LANES].T.astype(BF16)


def force_scales(rows):
    h = rows[4:5]
    inv = 1.0 / jnp.where(h > 0.0, h, 1.0)
    b = math.sqrt(24.0 / math.pi) * (inv * inv)
    return b, b * inv


def density_local_kernel(
    icut, jcut, group, lay, meta, own, acc, left, force_left, table, ring, right, mrow, *work
):
    slots = own.shape[2]
    ids = row_ids((8, slots))
    empty = jnp.zeros((8, slots), F32)
    for k in range(lay.cells):
        rows = own[k]
        inv = 1.0 / rows[4:5]
        comps = left_comps(rows)
        spread_left(jnp.concatenate([left_parts(comps * (inv * inv))] + [empty] * 4, axis=0), left, k)
        scales = empty
        for at, part in enumerate(x for scale in force_scales(rows) for x in split3(scale)):
            scales = jnp.where(ids == at, part, scales)
        spread_left(jnp.concatenate([left_parts(comps), scales] + [empty] * 3, axis=0), force_left, k)
        density_source(rows, right, mrow, k)
        acc[k] = jnp.zeros((slots, LANES), F32)
    tiles = Tiles(icut, jcut, table)
    local_tiles(tiles, lay, meta, False)
    blocks = Blocks(tiles, ring)
    density_loop(group, blocks, tiles.blocks, left, right, mrow, acc, work)


def density_remote_kernel(
    icut, jcut, group, lay,
    meta, own, rec, rec_odd, acc_in, left, energy_in,
    rho_out, term_out, pay, live,
    table, ring, right, mrow, acc, energy, sem, *work,
):
    cells, peers = lay.cells, lay.peers
    slots = own.shape[2]
    copy = pltpu.make_async_copy(energy_in, energy, sem)
    copy.start()
    place = Place(lay)
    occupied = jnp.where(rec[:, 3, :] > 0.0, 1.0, 0.0).reshape(2, peers, slots)
    occupied = jnp.sum(jnp.where(place.side == 0, occupied[0], occupied[1]), axis=1, keepdims=True)
    for k in range(peers):
        live[k] = occupied[k, 0].astype(jnp.int32)
    for k, rows in ((peers, rec[place.pair_partner]), (peers + 1, rec_odd[0])):
        live[k] = jnp.sum(jnp.where(rows[3:4] > 0.0, 1.0, 0.0)).astype(jnp.int32)

    def rec_cell(k, carry):
        density_source(rec[place.pair_peers + k], right, mrow, k)
        return carry

    lax.fori_loop(0, peers, rec_cell, 0, unroll=4)
    density_source(rec[place.pair_partner], right, mrow, peers)
    density_source(rec_odd[0], right, mrow, peers + 1)
    acc[...] = acc_in[...]
    tiles = Tiles(icut, jcut, table)
    remote_tiles(tiles, lay, meta, live)
    blocks = Blocks(tiles, ring)
    density_loop(group, blocks, tiles.blocks, left, right, mrow, acc, work)

    copy.wait()
    lane = lax.broadcasted_iota(jnp.int32, (1, slots), 1)
    ones = jnp.ones((8, 2 * LANES), BF16)
    for k in range(cells):
        one = acc[k].astype(BF16)
        two = (acc[k] - one.astype(F32)).astype(BF16)
        total_row = lax.dot_general(
            ones,
            jnp.concatenate([one, two], axis=1),
            (((1,), (1,)), ((), ())),
            preferred_element_type=F32,
        )
        inv = 1.0 / own[k, 4:5, :]
        rho = total_row[0:1] * (16.0 / math.pi) * (inv * inv * inv)
        occupied = jnp.where(lane < meta[k], 1.0, 0.0)
        rho_out[k : k + 1, :] = rho * occupied
        term_out[k] = occupied * (GAMMA - 1.0) * energy[k : k + 1, :] / (rho + 1.0 - occupied)

    pay[...] = jnp.zeros_like(pay)

    def peer(k, carry):
        pay[place.peers + k] = term_out[jnp.maximum(meta[lay.send + k], 0)]
        return carry

    lax.fori_loop(0, peers, peer, 0)
    pay[place.partner] = term_out[meta[place.partner_edge]]

    @pl.when(place.has_odd)
    def _():
        pay[place.odd] = term_out[meta[place.odd_edge]]


def force_source(rows, pressure, right, weights, scale, at):
    slots = rows.shape[1]
    right[at] = right_parts(right_comps(rows))
    b, c = force_scales(rows)
    scale[at] = jnp.concatenate([jnp.broadcast_to(b, (8, slots)), jnp.broadcast_to(c, (8, slots))], axis=0)
    m = rows[3:4]
    mp = m * pressure
    xv = rows[0:1] * rows[5:6] + rows[1:2] * rows[6:7] + rows[2:3] * rows[7:8]
    ids = row_ids((8, slots))
    base = jnp.where(ids == 3, 1.0, jnp.where(ids == 4, xv, rows))
    sums = jnp.concatenate([base * m, jnp.where(ids < 4, base, 0.0) * mp], axis=0)
    one, two, three = split3(sums)
    weights[at] = jnp.concatenate([one, two, three], axis=0).astype(BF16)


def force_loop(group, blocks, total, local, left, right, weights, scale, bcol, ccol, acc, work):
    icut, jcut = blocks.icut, blocks.jcut
    dist, upper, lower = work[:group], work[group : 2 * group], work[2 * group :]
    blocks.clear(group)
    for ref in (*upper, *lower):
        ref[...] = jnp.zeros_like(ref)
    zero = jnp.int32(0)
    state = (zero, zero, zero)
    for g in range(2 * group):
        state = blocks.write(group + g, state)
    for g in range(group):
        blocks.distances(group + g, left, right, dist[g])

    def sums_of(rows, columns, k, g):
        a, b, istart, jstart, w = blocks.read(k * group + g)
        adds = []
        if rows:
            wt = weights[b, :, pl.ds(jstart, jcut)]
            spec = (((1,), (1,)), ((), ()))
            part = lax.dot_general(wt, upper[g][...], spec, preferred_element_type=F32)
            part = part + lax.dot_general(wt, lower[g][...], spec, preferred_element_type=F32)
            keep = w
            if columns:
                keep = jnp.where(k * group + g < local + group, w, 0.0)
            adds.append((a, istart, part * keep))
        if columns:
            wt = weights[a, :, pl.ds(istart, icut)]
            part = jnp.dot(wt, upper[g][...], preferred_element_type=F32)
            part = part + jnp.dot(wt, lower[g][...], preferred_element_type=F32)
            adds.append((b, jstart, part * w))
        return adds

    def store(adds):
        for cell, start, part in adds:
            acc[cell, :, pl.ds(start, part.shape[1])] += part

    def step(rows, columns, k, state):
        adds = []
        for g in range(group):
            adds += sums_of(rows, columns, k, g)

            a, b, istart, jstart, _ = blocks.read((k + 1) * group + g)
            bj = jnp.concatenate([scale[b, 0:8, pl.ds(jstart, jcut)]] * (STRIP // 8), axis=0)
            cj = jnp.concatenate([scale[b, 8:16, pl.ds(jstart, jcut)]] * (STRIP // 8), axis=0)
            for row in range(0, icut, STRIP):
                s = jnp.maximum(dist[g][row : row + STRIP, :], TINY)
                r = lax.rsqrt(s)
                d = s * r
                bi = bcol[a, pl.ds(istart + row, STRIP), :]
                ci = ccol[a, pl.ds(istart + row, STRIP), :]
                bi = jnp.concatenate([bi] * (jcut // LANES), axis=1)
                ci = jnp.concatenate([ci] * (jcut // LANES), axis=1)
                t = ci * d
                u = jnp.maximum(bi - t, 0.0)
                v = jnp.minimum(t, u)
                slope = (u + u - v) * v
                t = cj * d
                u = jnp.maximum(bj - t, 0.0)
                v = jnp.minimum(t, u)
                slope = (slope + (u + u - v) * v) * r
                rounded = slope.astype(BF16)
                upper[g][row : row + STRIP, :] = rounded
                lower[g][row : row + STRIP, :] = (slope - rounded.astype(F32)).astype(BF16)

            state = blocks.write((k + 3) * group + g, state)
            blocks.distances((k + 2) * group + g, left, right, dist[g])
        store(adds)
        return state

    steps = chunks(total, group)
    adds = []
    if local is None:
        lax.fori_loop(0, steps, functools.partial(step, True, False), state)
        for g in range(group):
            adds += sums_of(True, False, steps, g)
    else:
        first = jnp.minimum(chunks(local, group) + 1, steps)
        state = lax.fori_loop(0, first, functools.partial(step, True, True), state)
        lax.fori_loop(first, steps, functools.partial(step, False, True), state)
        for g in range(group):
            adds += sums_of(True, True, steps, g)
    store(adds)


def force_local_kernel(
    icut, jcut, group, lay,
    meta, own, term, left,
    acc_out, bcol, ccol,
    table, ring, right, weights, scale, acc, *work,
):
    slots = own.shape[2]
    part = lax.broadcasted_iota(jnp.int32, (COLS, 2 * LANES), 0) - DOT_K
    lane = lax.broadcasted_iota(jnp.int32, (COLS, 2 * LANES), 1)
    of_b = (part >= 0) & (part < 3) & (lane < LANES)
    of_c = (part >= 3) & (part < 6) & (lane >= LANES)
    pick = jnp.where(of_b | of_c, 1.0, 0.0).astype(BF16)
    for k in range(lay.cells):
        force_source(own[k], term[k], right, weights, scale, k)
        acc[k] = jnp.zeros((SUMS, slots), F32)
        for at in range(slots // LANES):
            here = pl.ds(at * LANES, LANES)
            both = jnp.dot(left[k, here, :], pick, preferred_element_type=F32)
            bcol[k, here, :] = both[:, :LANES]
            ccol[k, here, :] = both[:, LANES:]
    tiles = Tiles(icut, jcut, table)
    local = local_tiles(tiles, lay, meta, True)
    blocks = Blocks(tiles, ring)
    force_loop(
        group, blocks, tiles.blocks, local, left, right, weights, scale, bcol, ccol, acc, work
    )
    for k in range(lay.cells):
        acc_out[k] = acc[k, 0:16, :] + (acc[k, 16:32, :] + acc[k, 32:48, :])


def force_remote_kernel(
    icut, jcut, group, lay,
    meta, live, own, rec, rec_odd, term, rterm, acc_in, left, bcol, ccol,
    accel_out, heat_out,
    table, ring, right, weights, scale, acc, *work,
):
    cells, peers = lay.cells, lay.peers
    slots = own.shape[2]
    place = Place(lay)

    def rec_cell(k, carry):
        force_source(rec[place.pair_peers + k], rterm[place.peers + k], right, weights, scale, k)
        return carry

    lax.fori_loop(0, peers, rec_cell, 0, unroll=4)
    force_source(rec[place.pair_partner], rterm[place.partner], right, weights, scale, peers)
    force_source(rec_odd[0], rterm[place.odd], right, weights, scale, peers + 1)
    acc[...] = jnp.zeros_like(acc)
    tiles = Tiles(icut, jcut, table)
    remote_tiles(tiles, lay, meta, live)
    blocks = Blocks(tiles, ring)
    force_loop(
        group, blocks, tiles.blocks, None, left, right, weights, scale, bcol, ccol, acc, work
    )

    lane = lax.broadcasted_iota(jnp.int32, (1, slots), 1)
    for k in range(cells):
        occupied = jnp.where(lane < meta[k], 1.0, 0.0)
        sums = acc_in[k] + acc[k, 0:16, :] + (acc[k, 16:32, :] + acc[k, 32:48, :])
        pressure = term[k]
        x = [own[k, d : d + 1, :] for d in range(3)]
        v = [own[k, 5 + d : 6 + d, :] for d in range(3)]
        both = pressure * sums[3:4] + sums[11:12]
        for d in range(3):
            accel_out[d, k : k + 1, :] = occupied * (
                x[d] * both - pressure * sums[d : d + 1] - sums[8 + d : 9 + d]
            )
        xv = x[0] * v[0] + x[1] * v[1] + x[2] * v[2]
        total_heat = xv * sums[3:4] + sums[4:5]
        for d in range(3):
            total_heat = total_heat - v[d] * sums[d : d + 1] - x[d] * sums[5 + d : 6 + d]
        heat_out[k : k + 1, :] = -occupied * pressure * total_heat


def on_device(positions, velocities, mass, smoothing, energy, counts, send, pairs, edge):
    cells, slots = mass.shape
    peers = send.shape[2]
    regions = 2 * lax.axis_size("pair")
    lay = Meta(cells, regions, peers, pairs.shape[2])
    others = peers + 2
    most = max(cells * (cells - 1) // 2 + 3 * cells, cells * cells, others) + 1
    icut, jcut, group = 128, slots // 2, 8
    ring = Blocks.FIELDS * (most * (slots // icut) * (slots // jcut) + 6 * group)
    shape = jax.ShapeDtypeStruct
    params = pltpu.CompilerParams(vmem_limit_bytes=20 * 1024 * 1024)
    send = send.reshape(peers)
    pairs = jnp.transpose(pairs, (0, 1, 3, 2))
    integers = (counts, send, pairs, edge)
    floats = (positions, velocities, mass, smoothing)
    integers, floats, energy = jax.tree.map(
        lambda x: pltpu.with_memory_space_constraint(x, pltpu.HBM), (integers, floats, energy)
    )
    lists = [pltpu.SMEM((Tiles.FIELDS * most,), jnp.int32), pltpu.SMEM((ring,), jnp.int32)]
    density_work = [pltpu.VMEM((icut, LANES), F32)] * group
    force_work = [pltpu.VMEM((icut, jcut), F32)] * group + [pltpu.VMEM((icut, jcut), BF16)] * (2 * group)
    wide = shape((cells, slots, LANES), F32)
    left_shape = shape((cells, slots, COLS), BF16)
    weight_shape = lambda count: pltpu.VMEM((count, SUMS, slots), BF16)
    right_shape = lambda count: pltpu.VMEM((count, DOT_K, slots), BF16)

    own, pay, odd, meta = pl.pallas_call(
        functools.partial(prep_kernel, lay),
        out_shape=[
            shape((cells, ROWS, slots), F32),
            shape((2 * peers, ROWS, slots), F32),
            shape((1, ROWS, slots), F32),
            shape((lay.size,), jnp.int32),
        ],
        in_specs=[HBM] * 8,
        out_specs=[VMEM] * 3 + [SMEM],
        scratch_shapes=[pltpu.SMEM(x.shape, jnp.int32) for x in integers]
        + [pltpu.VMEM(x.shape, F32) for x in floats]
        + [pltpu.SemaphoreType.DMA((8,))],
        compiler_params=params,
        name="prep",
    )(*integers, *floats)

    between = [(r, r + 1) for r in range(1, regions - 1, 2)]
    swap = between + [(b, a) for a, b in between]
    rec_odd = lax.ppermute(odd, ("pair", "side"), swap)
    rec = lax.all_to_all(pay, ("side", "cell"), split_axis=0, concat_axis=0, tiled=True)

    acc, left, force_left = pl.pallas_call(
        functools.partial(density_local_kernel, icut, jcut, group, lay),
        out_shape=[wide, left_shape, left_shape],
        in_specs=[SMEM, VMEM],
        out_specs=[VMEM] * 3,
        scratch_shapes=lists + [right_shape(cells), pltpu.VMEM((cells, 8, slots), F32)] + density_work,
        compiler_params=params,
        name="density_local",
    )(meta, own)

    density, term, pay, live = pl.pallas_call(
        functools.partial(density_remote_kernel, icut, jcut, group, lay),
        out_shape=[
            shape((cells, slots), F32),
            shape((cells, 1, slots), F32),
            shape((regions * peers, 1, slots), F32),
            shape((others,), jnp.int32),
        ],
        in_specs=[SMEM] + [VMEM] * 5 + [HBM],
        out_specs=[VMEM] * 3 + [SMEM],
        scratch_shapes=lists
        + [
            right_shape(others),
            pltpu.VMEM((others, 8, slots), F32),
            pltpu.VMEM((cells, slots, LANES), F32),
            pltpu.VMEM(energy.shape, F32),
            pltpu.SemaphoreType.DMA,
        ]
        + density_work,
        compiler_params=params,
        name="density_remote",
    )(meta, own, rec, rec_odd, acc, left, energy)

    rterm = lax.all_to_all(pay, ("pair", "side", "cell"), split_axis=0, concat_axis=0, tiled=True)

    acc, bcol, ccol = pl.pallas_call(
        functools.partial(force_local_kernel, icut, jcut, group, lay),
        out_shape=[shape((cells, 16, slots), F32), wide, wide],
        in_specs=[SMEM] + [VMEM] * 3,
        out_specs=[VMEM] * 3,
        scratch_shapes=lists
        + [
            right_shape(cells),
            weight_shape(cells),
            pltpu.VMEM((cells, 16, slots), F32),
            pltpu.VMEM((cells, SUMS, slots), F32),
        ]
        + force_work,
        compiler_params=params,
        name="force_local",
    )(meta, own, term, force_left)

    accel, heat = pl.pallas_call(
        functools.partial(force_remote_kernel, icut, jcut, group, lay),
        out_shape=[shape((3, cells, slots), F32), shape((cells, slots), F32)],
        in_specs=[SMEM] * 2 + [VMEM] * 9,
        out_specs=[VMEM] * 2,
        scratch_shapes=lists
        + [
            right_shape(others),
            weight_shape(others),
            pltpu.VMEM((others, 16, slots), F32),
            pltpu.VMEM((cells, SUMS, slots), F32),
        ]
        + force_work,
        compiler_params=params,
        name="force_remote",
    )(meta, live, own, rec, rec_odd, term, rterm, acc, force_left, bcol, ccol)
    return density, accel, heat


def solution(mesh):
    regions, peers = mesh.devices.shape
    mesh = jax.sharding.Mesh(mesh.devices.reshape(regions // 2, 2, peers), ("pair", "side", "cell"))
    region = ("pair", "side")
    every = (*region, "cell")
    placed = (
        P(None, every, None),
        P(None, every, None),
        P(every, None),
        P(every, None),
        P(every, None),
        P(every),
        P(region, "cell", None, None),
        P(region, "cell", None, None),
        P(region, "cell", None),
    )
    return jax.shard_map(
        on_device,
        mesh=mesh,
        in_specs=placed,
        out_specs=(P(every, None), P(None, every, None), P(every, None)),
        check_vma=False,
    )
```

```python
import functools
import math

import jax
import jax.numpy as jnp
from jax import lax
from jax.experimental import pallas as pl
from jax.experimental.pallas import tpu as pltpu
from jax.sharding import PartitionSpec as P

GAMMA = 5.0 / 3.0
LANES = 128
BF16 = jnp.bfloat16
F32 = jnp.float32

ROWS = 8
TINY = 1e-12
DOT_K = 32
SUMS = 48
COLS = 64
STRIP = 16

VMEM = pl.BlockSpec(memory_space=pltpu.VMEM)
SMEM = pl.BlockSpec(memory_space=pltpu.SMEM)
HBM = pl.BlockSpec(memory_space=pltpu.HBM)


def row_ids(shape):
    return lax.broadcasted_iota(jnp.int32, shape, 0)


def split3(value):
    first = value.astype(BF16).astype(F32)
    rest = value - first
    second = rest.astype(BF16).astype(F32)
    return first, second, rest - second


def parts_of(comps, left):
    ids = row_ids(comps.shape)
    a, b, c = split3(comps)
    again = [pltpu.roll(x, 5, 0) for x in (a, b, c)]
    after = [pltpu.roll(x, 1, 0) for x in (a, b, c)]
    if left:
        one = jnp.where(ids < 5, a, again[0])
        two = jnp.where(ids < 5, jnp.where(ids == 3, b, a), again[2])
        three = jnp.where(ids < 5, jnp.where(ids == 3, c, b), after[0])
        four = jnp.where(ids < 5, b, after[2])
    else:
        one = jnp.where(ids < 5, a, again[2])
        two = jnp.where(ids < 5, jnp.where(ids == 3, a, b), again[0])
        three = jnp.where(ids < 5, a, after[2])
        four = jnp.where(ids < 5, b, after[0])
    three = jnp.where(ids < 6, three, 0.0)
    four = jnp.where((ids < 6) & (ids != 3), four, 0.0)
    return jnp.concatenate([one, two, three, four], axis=0)


def left_parts(comps):
    return parts_of(comps, True)


def right_parts(comps):
    return parts_of(comps, False).astype(BF16)


def norm_row(rows):
    return rows[0:1] * rows[0:1] + rows[1:2] * rows[1:2] + rows[2:3] * rows[2:3]


def left_comps(rows):
    ids = row_ids(rows.shape)
    return jnp.where(ids < 3, rows, jnp.where(ids == 3, norm_row(rows), jnp.where(ids == 4, 1.0, 0.0)))


def right_comps(rows):
    ids = row_ids(rows.shape)
    return jnp.where(ids < 3, -2.0 * rows, jnp.where(ids == 3, 1.0, jnp.where(ids == 4, norm_row(rows), 0.0)))


def chunks(count, size):
    return lax.shift_right_logical(count + (size - 1), jnp.int32(size.bit_length() - 1))


class Meta:
    def __init__(self, cells, regions, peers, pairs):
        self.cells, self.regions, self.peers, self.pairs = cells, regions, peers, pairs
        self.send = cells
        self.pair = cells + peers
        self.edge = self.pair + 2 * pairs
        self.size = self.edge + 2


def prep_kernel(
    lay,
    counts_in, send_in, pairs_in, edge_in, pos_in, vel_in, mass_in, smooth_in,
    own, pay, odd, meta,
    counts, send, pairs, edge, pos, vel, mass, smooth, sems,
):
    inputs = (counts_in, send_in, pairs_in, edge_in, pos_in, vel_in, mass_in, smooth_in)
    buffers = (counts, send, pairs, edge, pos, vel, mass, smooth)
    copies = [
        pltpu.make_async_copy(source, target, sems.at[k])
        for k, (source, target) in enumerate(zip(inputs, buffers))
    ]
    for copy in copies:
        copy.start()
    for copy in copies:
        copy.wait()
    cells = mass.shape[0]
    slots = mass.shape[1]
    for k in range(cells):
        meta[k] = counts[k]
    for k in range(lay.peers):
        meta[lay.send + k] = send[k]
    for k in range(lay.pairs):
        for side in range(2):
            meta[lay.pair + 2 * k + side] = pairs[0, 0, side, k]
    for side in range(2):
        meta[lay.edge + side] = edge[0, 0, side]

    lane = lax.broadcasted_iota(jnp.int32, (1, slots), 1)
    for k in range(cells):
        live = lane < counts[k]
        for d in range(3):
            own[k, d : d + 1, :] = pos[d, k : k + 1, :] - 0.5
            own[k, 5 + d : 6 + d, :] = vel[d, k : k + 1, :]
        own[k, 3:4, :] = jnp.where(live, mass[k : k + 1, :], 0.0)
        own[k, 4:5, :] = smooth[k : k + 1, :]

    place = Place(lay)
    pay[...] = jnp.zeros_like(pay)

    def peer(k, carry):
        picked = send[k]
        pay[place.pair_peers + k] = jnp.where(picked >= 0, own[jnp.maximum(picked, 0)], 0.0)
        return carry

    lax.fori_loop(0, lay.peers, peer, 0)
    pay[place.pair_partner] = own[meta[place.partner_edge]]
    odd[0] = own[meta[place.odd_edge]]


class Place:
    def __init__(self, lay):
        peers, regions = lay.peers, lay.regions
        self.side = lax.axis_index("side")
        here = lax.axis_index("cell")
        region = 2 * lax.axis_index("pair") + self.side
        other = region - 1 + 2 * self.side
        self.partner_edge = lay.edge + 1 - self.side
        self.odd_edge = lay.edge + self.side
        self.pair_peers = self.side * peers
        self.pair_partner = (1 - self.side) * peers + here
        self.peers = region * peers
        self.partner = (region + 1 - 2 * self.side) * peers + here
        self.has_odd = (other >= 0) & (other < regions)
        self.odd = jnp.clip(other, 0, regions - 1) * peers + here


class Tiles:
    FIELDS = 7

    def __init__(self, icut, jcut, table):
        self.icut, self.jcut, self.table = icut, jcut, table
        self.count = self.blocks = jnp.int32(0)

    def push(self, a, b, w, ok, i, ni, j, nj):
        at = self.FIELDS * self.count
        for field, value in enumerate((a, b, w, i, ni, j, nj)):
            self.table[at + field] = value
        self.count = self.count + ok.astype(jnp.int32)
        self.blocks = self.blocks + jnp.where(ok, ni * nj, 0)

    def whole(self, a, b, w, ok, alive, blive):
        self.push(a, b, w, ok, 0, chunks(alive, self.icut), 0, chunks(blive, self.jcut))

    def close(self):
        self.push(0, 0, 0, jnp.bool_(False), 0, 1, 0, 1)


def local_tiles(tiles, lay, meta, both):
    cells = lay.cells
    one = jnp.int32(1)

    def key(row):
        first = meta[lay.pair + 2 * row]
        second = meta[lay.pair + 2 * row + 1]
        return jnp.minimum(first, second) * cells + jnp.maximum(first, second)

    keys = [key(row) for row in range(lay.pairs)]
    for a in range(cells):
        for b in range(a + 1, cells):
            mult = jnp.int32(0)
            for pair in keys:
                mult = mult + (pair == a * cells + b).astype(jnp.int32)
            tiles.whole(a, b, mult, mult > 0, meta[a], meta[b])
            if not both:
                tiles.whole(b, a, mult, mult > 0, meta[b], meta[a])
    if not both:
        for a in range(cells):
            tiles.whole(a, a, one, meta[a] > 0, meta[a], meta[a])
        tiles.close()
        return None
    span = tiles.jcut // tiles.icut
    for a in range(cells):
        tiles.push(a, a, one, meta[a] > tiles.jcut, 0, span, 1, chunks(meta[a], tiles.jcut) - 1)
    mutual = tiles.blocks
    for a in range(cells):
        rows = chunks(meta[a], tiles.icut)
        tiles.push(a, a, one, meta[a] > 0, 0, jnp.minimum(rows, span), 0, 1)
        tiles.push(a, a, one, meta[a] > tiles.jcut, span, rows - span, 1, 1)
    tiles.close()
    return mutual


def remote_tiles(tiles, lay, meta, live):
    one = jnp.int32(1)
    for k in range(lay.peers):
        picked = meta[lay.send + k]
        a = jnp.maximum(picked, 0)
        tiles.whole(a, k, one, (picked >= 0) & (live[k] > 0), meta[a], live[k])
    place = Place(lay)
    for b, edge in ((lay.peers, place.partner_edge), (lay.peers + 1, place.odd_edge)):
        a = meta[edge]
        tiles.whole(a, b, one, live[b] > 0, meta[a], live[b])
    tiles.close()


class Blocks:
    FIELDS = 5

    def __init__(self, tiles, ring):
        self.icut, self.jcut = tiles.icut, tiles.jcut
        self.table, self.last = tiles.table, tiles.count
        self.ring, self.total = ring, tiles.blocks

    def clear(self, entries):
        for k in range(entries * self.FIELDS):
            self.ring[k] = 0

    def write(self, slot, state):
        n, ii, jj = state
        a, b, w, i, ni, j, nj = (self.table[Tiles.FIELDS * n + k] for k in range(Tiles.FIELDS))
        for field, value in enumerate((a, b, (i + ii) * self.icut, (j + jj) * self.jcut, w)):
            self.ring[self.FIELDS * slot + field] = value
        jwrap = jj + 1 >= nj
        inext = jnp.where(jwrap, ii + 1, ii)
        iwrap = inext >= ni
        return (
            jnp.minimum(jnp.where(iwrap, n + 1, n), self.last),
            jnp.where(iwrap, 0, inext),
            jnp.where(jwrap, 0, jj + 1),
        )

    def read(self, slot):
        a, b, istart, jstart, w = (self.ring[self.FIELDS * slot + k] for k in range(self.FIELDS))
        return (
            a,
            b,
            pl.multiple_of(istart, self.icut),
            pl.multiple_of(jstart, self.jcut),
            w.astype(F32),
        )

    def distances(self, params, left, right, out):
        a, b, istart, jstart, _ = params
        out[...] = jnp.dot(
            left[a, pl.ds(istart, self.icut), :DOT_K],
            right[b, :, pl.ds(jstart, self.jcut)],
            preferred_element_type=F32,
        )


def density_loop(group, blocks, total, left, right, mrow, acc, parts):
    icut, jcut = blocks.icut, blocks.jcut
    zero = jnp.int32(0)
    state = (zero, zero, zero)
    for g in range(group):
        state = blocks.write(g, state)

    def step(k, state):
        params = [blocks.read(k * group + g) for g in range(group)]
        for g, (a, b, istart, jstart, w) in enumerate(params):
            square = jnp.dot(
                left[a, pl.ds(istart, icut), :DOT_K],
                right[b, :, pl.ds(jstart, jcut)],
                preferred_element_type=F32,
            )
            weight = mrow[b, :, pl.ds(jstart, jcut)] * w
            weight = jnp.concatenate([weight] * (STRIP // 8), axis=0)
            for row in range(0, icut, STRIP):
                s = jnp.maximum(square[row : row + STRIP, :], TINY)
                q = s * lax.rsqrt(s)
                e = 1.0 - q
                u = jnp.maximum(e, 0.0)
                t = jnp.minimum(0.5 - (s * 3.0) * e, u * u * u) * weight
                part = t[:, :LANES]
                for at in range(1, jcut // LANES):
                    part = part + t[:, at * LANES : (at + 1) * LANES]
                parts[g][row : row + STRIP, :] = part
        for g, (a, _, istart, _, _) in enumerate(params):
            acc[a, pl.ds(istart, icut), :] += parts[g][...]
        for g in range(group):
            state = blocks.write((k + 1) * group + g, state)
        return state

    lax.fori_loop(0, chunks(total, group), step, state)


def density_source(rows, right, mrow, at):
    right[at] = right_parts(right_comps(rows))
    mrow[at] = jnp.broadcast_to(rows[3:4], mrow.shape[1:])


def spread_left(parts, left, cell):
    for at in range(parts.shape[1] // LANES):
        left[cell, pl.ds(at * LANES, LANES), :] = parts[:, at * LANES : (at + 1) * LANES].T.astype(BF16)


def force_scales(rows):
    h = rows[4:5]
    inv = 1.0 / jnp.where(h > 0.0, h, 1.0)
    b = math.sqrt(24.0 / math.pi) * (inv * inv)
    return b, b * inv


def density_local_kernel(
    icut, jcut, group, lay, meta, own, acc, left, force_left, table, ring, right, mrow, *work
):
    slots = own.shape[2]
    ids = row_ids((8, slots))
    empty = jnp.zeros((8, slots), F32)
    for k in range(lay.cells):
        rows = own[k]
        inv = 1.0 / rows[4:5]
        comps = left_comps(rows)
        spread_left(jnp.concatenate([left_parts(comps * (inv * inv))] + [empty] * 4, axis=0), left, k)
        scales = empty
        for at, part in enumerate(x for scale in force_scales(rows) for x in split3(scale)):
            scales = jnp.where(ids == at, part, scales)
        spread_left(jnp.concatenate([left_parts(comps), scales] + [empty] * 3, axis=0), force_left, k)
        density_source(rows, right, mrow, k)
        acc[k] = jnp.zeros((slots, LANES), F32)
    tiles = Tiles(icut, jcut, table)
    local_tiles(tiles, lay, meta, False)
    blocks = Blocks(tiles, ring)
    density_loop(group, blocks, tiles.blocks, left, right, mrow, acc, work)


def density_remote_kernel(
    icut, jcut, group, lay,
    meta, own, rec, rec_odd, acc_in, left, energy_in,
    rho_out, term_out, pay, live,
    table, ring, right, mrow, acc, energy, sem, *work,
):
    cells, peers = lay.cells, lay.peers
    slots = own.shape[2]
    copy = pltpu.make_async_copy(energy_in, energy, sem)
    copy.start()
    place = Place(lay)
    occupied = jnp.where(rec[:, 3, :] > 0.0, 1.0, 0.0).reshape(2, peers, slots)
    occupied = jnp.sum(jnp.where(place.side == 0, occupied[0], occupied[1]), axis=1, keepdims=True)
    for k in range(peers):
        live[k] = occupied[k, 0].astype(jnp.int32)
    for k, rows in ((peers, rec[place.pair_partner]), (peers + 1, rec_odd[0])):
        live[k] = jnp.sum(jnp.where(rows[3:4] > 0.0, 1.0, 0.0)).astype(jnp.int32)

    def rec_cell(k, carry):
        density_source(rec[place.pair_peers + k], right, mrow, k)
        return carry

    lax.fori_loop(0, peers, rec_cell, 0, unroll=4)
    density_source(rec[place.pair_partner], right, mrow, peers)
    density_source(rec_odd[0], right, mrow, peers + 1)
    acc[...] = acc_in[...]
    tiles = Tiles(icut, jcut, table)
    remote_tiles(tiles, lay, meta, live)
    blocks = Blocks(tiles, ring)
    density_loop(group, blocks, tiles.blocks, left, right, mrow, acc, work)

    copy.wait()
    lane = lax.broadcasted_iota(jnp.int32, (1, slots), 1)
    ones = jnp.ones((8, 2 * LANES), BF16)
    for k in range(cells):
        one = acc[k].astype(BF16)
        two = (acc[k] - one.astype(F32)).astype(BF16)
        total_row = lax.dot_general(
            ones,
            jnp.concatenate([one, two], axis=1),
            (((1,), (1,)), ((), ())),
            preferred_element_type=F32,
        )
        inv = 1.0 / own[k, 4:5, :]
        rho = total_row[0:1] * (16.0 / math.pi) * (inv * inv * inv)
        occupied = jnp.where(lane < meta[k], 1.0, 0.0)
        rho_out[k : k + 1, :] = rho * occupied
        term_out[k] = occupied * (GAMMA - 1.0) * energy[k : k + 1, :] / (rho + 1.0 - occupied)

    pay[...] = jnp.zeros_like(pay)

    def peer(k, carry):
        pay[place.peers + k] = term_out[jnp.maximum(meta[lay.send + k], 0)]
        return carry

    lax.fori_loop(0, peers, peer, 0)
    pay[place.partner] = term_out[meta[place.partner_edge]]

    @pl.when(place.has_odd)
    def _():
        pay[place.odd] = term_out[meta[place.odd_edge]]


def force_source(rows, pressure, right, weights, scale, at):
    slots = rows.shape[1]
    right[at] = right_parts(right_comps(rows))
    b, c = force_scales(rows)
    scale[at] = jnp.concatenate([jnp.broadcast_to(b, (8, slots)), jnp.broadcast_to(c, (8, slots))], axis=0)
    m = rows[3:4]
    mp = m * pressure
    xv = rows[0:1] * rows[5:6] + rows[1:2] * rows[6:7] + rows[2:3] * rows[7:8]
    ids = row_ids((8, slots))
    base = jnp.where(ids == 3, 1.0, jnp.where(ids == 4, xv, rows))
    sums = jnp.concatenate([base * m, jnp.where(ids < 4, base, 0.0) * mp], axis=0)
    one, two, three = split3(sums)
    weights[at] = jnp.concatenate([one, two, three], axis=0).astype(BF16)


def force_loop(group, blocks, total, local, left, right, weights, scale, bcol, ccol, acc, work):
    icut, jcut = blocks.icut, blocks.jcut
    dist, upper, lower = work[:group], work[group : 2 * group], work[2 * group :]
    blocks.clear(group)
    for ref in (*upper, *lower):
        ref[...] = jnp.zeros_like(ref)
    zero = jnp.int32(0)
    state = (zero, zero, zero)
    for g in range(2 * group):
        state = blocks.write(group + g, state)
    for g in range(group):
        blocks.distances(blocks.read(group + g), left, right, dist[g])

    def sums_of(rows, columns, params, k, g):
        a, b, istart, jstart, w = params
        adds = []
        if rows:
            wt = weights[b, :, pl.ds(jstart, jcut)]
            spec = (((1,), (1,)), ((), ()))
            part = lax.dot_general(wt, upper[g][...], spec, preferred_element_type=F32)
            part = part + lax.dot_general(wt, lower[g][...], spec, preferred_element_type=F32)
            keep = w
            if columns:
                keep = jnp.where(k * group + g < local + group, w, 0.0)
            adds.append((a, istart, part * keep))
        if columns:
            wt = weights[a, :, pl.ds(istart, icut)]
            part = jnp.dot(wt, upper[g][...], preferred_element_type=F32)
            part = part + jnp.dot(wt, lower[g][...], preferred_element_type=F32)
            adds.append((b, jstart, part * w))
        return adds

    def store(adds):
        for cell, start, part in adds:
            acc[cell, :, pl.ds(start, part.shape[1])] += part

    def step(rows, columns, k, state):
        adds = []
        summed, worked, ahead = (
            [blocks.read((k + stage) * group + g) for g in range(group)] for stage in range(3)
        )
        for g in range(group):
            adds += sums_of(rows, columns, summed[g], k, g)

            a, b, istart, jstart, _ = worked[g]
            bj = jnp.concatenate([scale[b, 0:8, pl.ds(jstart, jcut)]] * (STRIP // 8), axis=0)
            cj = jnp.concatenate([scale[b, 8:16, pl.ds(jstart, jcut)]] * (STRIP // 8), axis=0)
            for row in range(0, icut, STRIP):
                s = jnp.maximum(dist[g][row : row + STRIP, :], TINY)
                r = lax.rsqrt(s)
                d = s * r
                bi = bcol[a, pl.ds(istart + row, STRIP), :]
                ci = ccol[a, pl.ds(istart + row, STRIP), :]
                bi = jnp.concatenate([bi] * (jcut // LANES), axis=1)
                ci = jnp.concatenate([ci] * (jcut // LANES), axis=1)
                t = ci * d
                u = jnp.maximum(bi - t, 0.0)
                v = jnp.minimum(t, u)
                slope = (u + u - v) * v
                t = cj * d
                u = jnp.maximum(bj - t, 0.0)
                v = jnp.minimum(t, u)
                slope = (slope + (u + u - v) * v) * r
                rounded = slope.astype(BF16)
                upper[g][row : row + STRIP, :] = rounded
                lower[g][row : row + STRIP, :] = (slope - rounded.astype(F32)).astype(BF16)

            blocks.distances(ahead[g], left, right, dist[g])
        store(adds)
        for g in range(group):
            state = blocks.write((k + 3) * group + g, state)
        return state

    steps = chunks(total, group)
    adds = []
    if local is None:
        lax.fori_loop(0, steps, functools.partial(step, True, False), state)
        for g in range(group):
            adds += sums_of(True, False, blocks.read(steps * group + g), steps, g)
    else:
        first = jnp.minimum(chunks(local, group) + 1, steps)
        state = lax.fori_loop(0, first, functools.partial(step, True, True), state)
        lax.fori_loop(first, steps, functools.partial(step, False, True), state)
        for g in range(group):
            adds += sums_of(True, True, blocks.read(steps * group + g), steps, g)
    store(adds)


def force_local_kernel(
    icut, jcut, group, lay,
    meta, own, term, left,
    acc_out, bcol, ccol,
    table, ring, right, weights, scale, acc, *work,
):
    slots = own.shape[2]
    part = lax.broadcasted_iota(jnp.int32, (COLS, 2 * LANES), 0) - DOT_K
    lane = lax.broadcasted_iota(jnp.int32, (COLS, 2 * LANES), 1)
    of_b = (part >= 0) & (part < 3) & (lane < LANES)
    of_c = (part >= 3) & (part < 6) & (lane >= LANES)
    pick = jnp.where(of_b | of_c, 1.0, 0.0).astype(BF16)
    for k in range(lay.cells):
        force_source(own[k], term[k], right, weights, scale, k)
        acc[k] = jnp.zeros((SUMS, slots), F32)
        for at in range(slots // LANES):
            here = pl.ds(at * LANES, LANES)
            both = jnp.dot(left[k, here, :], pick, preferred_element_type=F32)
            bcol[k, here, :] = both[:, :LANES]
            ccol[k, here, :] = both[:, LANES:]
    tiles = Tiles(icut, jcut, table)
    local = local_tiles(tiles, lay, meta, True)
    blocks = Blocks(tiles, ring)
    force_loop(
        group, blocks, tiles.blocks, local, left, right, weights, scale, bcol, ccol, acc, work
    )
    for k in range(lay.cells):
        acc_out[k] = acc[k, 0:16, :] + (acc[k, 16:32, :] + acc[k, 32:48, :])


def force_remote_kernel(
    icut, jcut, group, lay,
    meta, live, own, rec, rec_odd, term, rterm, acc_in, left, bcol, ccol,
    accel_out, heat_out,
    table, ring, right, weights, scale, acc, *work,
):
    cells, peers = lay.cells, lay.peers
    slots = own.shape[2]
    place = Place(lay)

    def rec_cell(k, carry):
        force_source(rec[place.pair_peers + k], rterm[place.peers + k], right, weights, scale, k)
        return carry

    lax.fori_loop(0, peers, rec_cell, 0, unroll=4)
    force_source(rec[place.pair_partner], rterm[place.partner], right, weights, scale, peers)
    force_source(rec_odd[0], rterm[place.odd], right, weights, scale, peers + 1)
    acc[...] = jnp.zeros_like(acc)
    tiles = Tiles(icut, jcut, table)
    remote_tiles(tiles, lay, meta, live)
    blocks = Blocks(tiles, ring)
    force_loop(
        group, blocks, tiles.blocks, None, left, right, weights, scale, bcol, ccol, acc, work
    )

    lane = lax.broadcasted_iota(jnp.int32, (1, slots), 1)
    for k in range(cells):
        occupied = jnp.where(lane < meta[k], 1.0, 0.0)
        sums = acc_in[k] + acc[k, 0:16, :] + (acc[k, 16:32, :] + acc[k, 32:48, :])
        pressure = term[k]
        x = [own[k, d : d + 1, :] for d in range(3)]
        v = [own[k, 5 + d : 6 + d, :] for d in range(3)]
        both = pressure * sums[3:4] + sums[11:12]
        for d in range(3):
            accel_out[d, k : k + 1, :] = occupied * (
                x[d] * both - pressure * sums[d : d + 1] - sums[8 + d : 9 + d]
            )
        xv = x[0] * v[0] + x[1] * v[1] + x[2] * v[2]
        total_heat = xv * sums[3:4] + sums[4:5]
        for d in range(3):
            total_heat = total_heat - v[d] * sums[d : d + 1] - x[d] * sums[5 + d : 6 + d]
        heat_out[k : k + 1, :] = -occupied * pressure * total_heat


def on_device(positions, velocities, mass, smoothing, energy, counts, send, pairs, edge):
    cells, slots = mass.shape
    peers = send.shape[2]
    regions = 2 * lax.axis_size("pair")
    lay = Meta(cells, regions, peers, pairs.shape[2])
    others = peers + 2
    most = max(cells * (cells - 1) // 2 + 3 * cells, cells * cells, others) + 1
    icut, jcut, group = 128, slots // 2, 8
    ring = Blocks.FIELDS * (most * (slots // icut) * (slots // jcut) + 6 * group)
    shape = jax.ShapeDtypeStruct
    params = pltpu.CompilerParams(vmem_limit_bytes=20 * 1024 * 1024)
    send = send.reshape(peers)
    pairs = jnp.transpose(pairs, (0, 1, 3, 2))
    integers = (counts, send, pairs, edge)
    floats = (positions, velocities, mass, smoothing)
    integers, floats, energy = jax.tree.map(
        lambda x: pltpu.with_memory_space_constraint(x, pltpu.HBM), (integers, floats, energy)
    )
    lists = [pltpu.SMEM((Tiles.FIELDS * most,), jnp.int32), pltpu.SMEM((ring,), jnp.int32)]
    density_work = [pltpu.VMEM((icut, LANES), F32)] * group
    force_work = [pltpu.VMEM((icut, jcut), F32)] * group + [pltpu.VMEM((icut, jcut), BF16)] * (2 * group)
    wide = shape((cells, slots, LANES), F32)
    left_shape = shape((cells, slots, COLS), BF16)
    weight_shape = lambda count: pltpu.VMEM((count, SUMS, slots), BF16)
    right_shape = lambda count: pltpu.VMEM((count, DOT_K, slots), BF16)

    own, pay, odd, meta = pl.pallas_call(
        functools.partial(prep_kernel, lay),
        out_shape=[
            shape((cells, ROWS, slots), F32),
            shape((2 * peers, ROWS, slots), F32),
            shape((1, ROWS, slots), F32),
            shape((lay.size,), jnp.int32),
        ],
        in_specs=[HBM] * 8,
        out_specs=[VMEM] * 3 + [SMEM],
        scratch_shapes=[pltpu.SMEM(x.shape, jnp.int32) for x in integers]
        + [pltpu.VMEM(x.shape, F32) for x in floats]
        + [pltpu.SemaphoreType.DMA((8,))],
        compiler_params=params,
        name="prep",
    )(*integers, *floats)

    between = [(r, r + 1) for r in range(1, regions - 1, 2)]
    swap = between + [(b, a) for a, b in between]
    rec_odd = lax.ppermute(odd, ("pair", "side"), swap)
    rec = lax.all_to_all(pay, ("side", "cell"), split_axis=0, concat_axis=0, tiled=True)

    acc, left, force_left = pl.pallas_call(
        functools.partial(density_local_kernel, icut, jcut, group, lay),
        out_shape=[wide, left_shape, left_shape],
        in_specs=[SMEM, VMEM],
        out_specs=[VMEM] * 3,
        scratch_shapes=lists + [right_shape(cells), pltpu.VMEM((cells, 8, slots), F32)] + density_work,
        compiler_params=params,
        name="density_local",
    )(meta, own)

    density, term, pay, live = pl.pallas_call(
        functools.partial(density_remote_kernel, icut, jcut, group, lay),
        out_shape=[
            shape((cells, slots), F32),
            shape((cells, 1, slots), F32),
            shape((regions * peers, 1, slots), F32),
            shape((others,), jnp.int32),
        ],
        in_specs=[SMEM] + [VMEM] * 5 + [HBM],
        out_specs=[VMEM] * 3 + [SMEM],
        scratch_shapes=lists
        + [
            right_shape(others),
            pltpu.VMEM((others, 8, slots), F32),
            pltpu.VMEM((cells, slots, LANES), F32),
            pltpu.VMEM(energy.shape, F32),
            pltpu.SemaphoreType.DMA,
        ]
        + density_work,
        compiler_params=params,
        name="density_remote",
    )(meta, own, rec, rec_odd, acc, left, energy)

    rterm = lax.all_to_all(pay, ("pair", "side", "cell"), split_axis=0, concat_axis=0, tiled=True)

    acc, bcol, ccol = pl.pallas_call(
        functools.partial(force_local_kernel, icut, jcut, group, lay),
        out_shape=[shape((cells, 16, slots), F32), wide, wide],
        in_specs=[SMEM] + [VMEM] * 3,
        out_specs=[VMEM] * 3,
        scratch_shapes=lists
        + [
            right_shape(cells),
            weight_shape(cells),
            pltpu.VMEM((cells, 16, slots), F32),
            pltpu.VMEM((cells, SUMS, slots), F32),
        ]
        + force_work,
        compiler_params=params,
        name="force_local",
    )(meta, own, term, force_left)

    accel, heat = pl.pallas_call(
        functools.partial(force_remote_kernel, icut, jcut, group, lay),
        out_shape=[shape((3, cells, slots), F32), shape((cells, slots), F32)],
        in_specs=[SMEM] * 2 + [VMEM] * 9,
        out_specs=[VMEM] * 2,
        scratch_shapes=lists
        + [
            right_shape(others),
            weight_shape(others),
            pltpu.VMEM((others, 16, slots), F32),
            pltpu.VMEM((cells, SUMS, slots), F32),
        ]
        + force_work,
        compiler_params=params,
        name="force_remote",
    )(meta, live, own, rec, rec_odd, term, rterm, acc, force_left, bcol, ccol)
    return density, accel, heat


def solution(mesh):
    regions, peers = mesh.devices.shape
    mesh = jax.sharding.Mesh(mesh.devices.reshape(regions // 2, 2, peers), ("pair", "side", "cell"))
    region = ("pair", "side")
    every = (*region, "cell")
    placed = (
        P(None, every, None),
        P(None, every, None),
        P(every, None),
        P(every, None),
        P(every, None),
        P(every),
        P(region, "cell", None, None),
        P(region, "cell", None, None),
        P(region, "cell", None),
    )
    return jax.shard_map(
        on_device,
        mesh=mesh,
        in_specs=placed,
        out_specs=(P(every, None), P(None, every, None), P(every, None)),
        check_vma=False,
    )
```
